128 devices in a mesh: clip: 4 (over y), frame: 8 (over x_hi, z), tensor: 4 (over x_lo, core).
Axes of the slice: x: 4 (x_hi: 2, x_lo: 2; x = x_hi * 2 + x_lo), y: 4, z: 4, core: 2. Of those that a mesh axis runs over, the one named last changes fastest.
Arguments:
- features: bfloat16 [4, 8, 256, 1408], P('clip', 'frame', None, 'tensor'), may hold values from -6 to 6
- cond_values: float32 [4, 8, 2, 7], P('clip', 'frame'), may hold values from -6 to 6
- cond_live: int32 [4, 8, 2], P('clip'), may hold values 0 or 1
- in_weight: bfloat16 [1408, 1024], P('tensor'), may hold values from -0.15625 to 0.15625
- in_bias: float32 [1024], replicated, may hold values from -1.75 to 1.75
- act_weight: float32 [7, 1024], replicated, may hold values from -2 to 2
- act_bias: float32 [1024], replicated, may hold values from -1.75 to 1.75
- state_weight: float32 [7, 1024], replicated, may hold values from -2 to 2
- state_bias: float32 [1024], replicated, may hold values from -1.75 to 1.75
- attn_gain: float32 [2, 1024], replicated, may hold values from 0.1 to 1.9
- attn_shift: float32 [2, 1024], replicated, may hold values from -1.25 to 1.25
- qkv_weight: bfloat16 [2, 1024, 3, 1024], P(None, None, None, 'tensor'), may hold values from -0.1875 to 0.1875
- qkv_bias: float32 [2, 3, 1024], P(None, None, 'tensor'), may hold values from -1.75 to 1.75
- proj_weight: bfloat16 [2, 1024, 1024], P(None, 'tensor'), may hold values from -0.5 to 0.5
- proj_bias: float32 [2, 1024], replicated, may hold values from -1.25 to 1.25
- mlp_gain: float32 [2, 1024], replicated, may hold values from 0.1 to 1.9
- mlp_shift: float32 [2, 1024], replicated, may hold values from -1.25 to 1.25
- up_weight: bfloat16 [2, 1024, 4096], P(None, None, 'tensor'), may hold values from -0.1875 to 0.1875
- up_bias: float32 [2, 4096], P(None, 'tensor'), may hold values from -1.75 to 1.75
- down_weight: bfloat16 [2, 4096, 1024], P(None, 'tensor'), may hold values from -0.125 to 0.125
- down_bias: float32 [2, 1024], replicated, may hold values from -1.25 to 1.25
- out_grad: bfloat16 [4, 8, 258, 1024], P('clip', 'frame'), may hold values from -6 to 6
Outputs:
- block_out: bfloat16 [4, 8, 258, 1024], P('clip', 'frame')
- grad_features: float32 [4, 8, 256, 1408], P('clip', 'frame', None, 'tensor')
- grad_in_weight: float32 [1408, 1024], P('tensor')
- grad_in_bias: float32 [1024], replicated
- grad_act_weight: float32 [7, 1024], replicated
- grad_act_bias: float32 [1024], replicated
- grad_state_weight: float32 [7, 1024], replicated
- grad_state_bias: float32 [1024], replicated
- grad_attn_gain: float32 [2, 1024], replicated
- grad_attn_shift: float32 [2, 1024], replicated
- grad_qkv_weight: float32 [2, 1024, 3, 1024], P(None, None, None, 'tensor')
- grad_qkv_bias: float32 [2, 3, 1024], P(None, None, 'tensor')
- grad_proj_weight: float32 [2, 1024, 1024], P(None, 'tensor')
- grad_proj_bias: float32 [2, 1024], replicated
- grad_mlp_gain: float32 [2, 1024], replicated
- grad_mlp_shift: float32 [2, 1024], replicated
- grad_up_weight: float32 [2, 1024, 4096], P(None, None, 'tensor')
- grad_up_bias: float32 [2, 4096], P(None, 'tensor')
- grad_down_weight: float32 [2, 4096, 1024], P(None, 'tensor')
- grad_down_bias: float32 [2, 1024], replicated
The draws below stay inside these ranges and needn't reach their ends.
Inputs may be any that keep to these rules, and one draw needn't show every extreme that they name: `cond_live`: patch rows are always live; each slot is live or padding.
All inputs are finite; a program needn't handle non-finite values. No bound on the sum of `cond_live` on one device may be relied on, other than what follows from the above.
Results may differ from the reference program's by a relative error of at most 0.015.
Values may be sent and summed in bfloat16 or wider, within the bound.
No kernel may reach another device: no remote copies, remote signals or barrier semaphores. Data moves between devices by JAX's collectives and lax.ppermute only.
A program may use at most 320 MiB of HBM per device.

```python
import jax
import jax.numpy as jnp
import numpy as np
from jax import lax

D = 1024
HEADS = 16
HEAD = 64
MLP = 4096
FEAT = 1408
ACT = 7
LAYERS = 2
FRAMES = 8
GRID_W = 16
COND = 2
PATCH = 256
ROWS = 258
CLIPS = 4


def place_ends(drawn, rng, smallest, top_value):
    dims = drawn.shape
    spot = [jax.random.randint(jax.random.fold_in(rng, axis), (), 0, dims[axis]) for axis in range(len(dims))]
    drawn = drawn.at[tuple(spot)].set(smallest)
    longest = dims.index(max(dims))
    spot[longest] = (spot[longest] + 1) % dims[longest]
    return drawn.at[tuple(spot)].set(top_value)


def levels(stream_key, shape, cuts, smallest, top_value):
    def one(position, shards_of):
        steps = jax.random.uniform(jax.random.fold_in(jax.random.fold_in(stream_key, 6), position), (shards_of,), jnp.float32, smallest / len(cuts), top_value / len(cuts))
        return jnp.repeat(jnp.exp(steps), shape[position] // shards_of).reshape((-1,) + (1,) * (len(shape) - position - 1))

    loudness = one(*cuts[0])
    for cut in cuts[1:]:
        loudness = loudness * one(*cut)
    return loudness


def gaussian(key, extent, scale, reach, split=(), held_as=jnp.bfloat16):
    factor_of = levels(key, extent, split, -0.22, 0.18) if split else 1.0
    entries = jax.random.normal(key, extent, jnp.float32) * scale * factor_of
    return jnp.minimum(jnp.maximum(entries, -reach), reach).astype(held_as)


def setup_inputs(seed: int = 0) -> dict:
    seeds = jax.random.split(jax.random.key(seed), 23)
    features = gaussian(seeds[0], (CLIPS, FRAMES, PATCH, FEAT), 1.0, 6.0, ((0, 4), (1, 8), (3, 4)))
    cond_values = gaussian(seeds[1], (CLIPS, FRAMES, COND, ACT), 1.0, 6.0, ((0, 4), (1, 8)), jnp.float32)
    cond_live = place_ends((jax.random.randint(seeds[2], (CLIPS, FRAMES, COND), 0, 8) < 7).astype(jnp.int32), jax.random.fold_in(seeds[2], 1), 0, 1)
    in_weight = gaussian(seeds[3], (FEAT, D), FEAT ** -0.5, 0.15625, ((0, 4),))
    in_bias = gaussian(seeds[4], (D,), 0.3, 1.75, (), jnp.float32)
    act_weight = gaussian(seeds[5], (ACT, D), ACT ** -0.5, 2.0, (), jnp.float32)
    act_bias = gaussian(seeds[6], (D,), 0.3, 1.75, (), jnp.float32)
    state_weight = gaussian(seeds[7], (ACT, D), ACT ** -0.5, 2.0, (), jnp.float32)
    state_bias = gaussian(seeds[8], (D,), 0.3, 1.75, (), jnp.float32)
    attn_gain = jnp.clip(1.0 + 0.18 * jax.random.normal(seeds[9], (LAYERS, D), jnp.float32), 0.1, 1.9)
    attn_shift = gaussian(seeds[10], (LAYERS, D), 0.2, 1.25, (), jnp.float32)
    qkv_weight = gaussian(seeds[11], (LAYERS, D, 3, D), D ** -0.5, 0.1875, ((3, 4),))
    qkv_bias = gaussian(seeds[12], (LAYERS, 3, D), 0.3, 1.75, ((2, 4),), jnp.float32)
    proj_weight = gaussian(seeds[13], (LAYERS, D, D), (max(1, D // 8)) ** -0.5, 0.5, ((1, 4),))
    proj_bias = gaussian(seeds[14], (LAYERS, D), 0.2, 1.25, (), jnp.float32)
    mlp_gain = jnp.clip(1.0 + 0.18 * jax.random.normal(seeds[15], (LAYERS, D), jnp.float32), 0.1, 1.9)
    mlp_shift = gaussian(seeds[16], (LAYERS, D), 0.2, 1.25, (), jnp.float32)
    up_weight = gaussian(seeds[17], (LAYERS, D, MLP), D ** -0.5, 0.1875, ((2, 4),))
    up_bias = gaussian(seeds[18], (LAYERS, MLP), 0.3, 1.75, ((1, 4),), jnp.float32)
    down_weight = gaussian(seeds[19], (LAYERS, MLP, D), (MLP // 2) ** -0.5, 0.125, ((1, 4),))
    down_bias = gaussian(seeds[20], (LAYERS, D), 0.2, 1.25, (), jnp.float32)
    out_grad = gaussian(seeds[21], (CLIPS, FRAMES, ROWS, D), 1.0, 6.0, ((0, 4), (1, 8)))
    return {"features": features, "cond_values": cond_values, "cond_live": cond_live, "in_weight": in_weight, "in_bias": in_bias, "act_weight": act_weight, "act_bias": act_bias, "state_weight": state_weight, "state_bias": state_bias, "attn_gain": attn_gain, "attn_shift": attn_shift, "qkv_weight": qkv_weight, "qkv_bias": qkv_bias, "proj_weight": proj_weight, "proj_bias": proj_bias, "mlp_gain": mlp_gain, "mlp_shift": mlp_shift, "up_weight": up_weight, "up_bias": up_bias, "down_weight": down_weight, "down_bias": down_bias, "out_grad": out_grad}


@jax.custom_vjp
def low(v):
    return lax.optimization_barrier(v.astype(jnp.bfloat16)).astype(jnp.float32)

@jax.custom_vjp
def low_back(v):
    return v

def low_keep(v):
    return (low(v), None)

def low_pass(kept, grad):
    return (grad,)

def back_keep(v):
    return (v, None)

def back_low(kept, grad):
    return (low(grad),)
low.defvjp(low_keep, low_pass)
low_back.defvjp(back_keep, back_low)
highest_precision = lax.Precision.HIGHEST
norm_epsilon = 1e-06
masked_score = -1000000000.0

def rotary_tables(head_size, head_count):
    group_size = 2 * (head_size // 3 // 2)
    half_size = group_size // 2
    total_width = head_size * head_count
    perm_table = np.arange(total_width)
    sign_table = np.zeros(total_width, np.float32)
    rate_table = np.zeros((3, total_width), np.float32)
    for head_at in range(head_count):
        for axis_at in range(3):
            for pair_at in range(half_size):
                lower_at = head_at * head_size + axis_at * group_size + pair_at
                upper_at = lower_at + half_size
                perm_table[lower_at] = upper_at
                perm_table[upper_at] = lower_at
                sign_table[lower_at] = -1.0
                sign_table[upper_at] = 1.0
                rate_value = 10000.0 ** (-2.0 * pair_at / group_size)
                rate_table[axis_at, lower_at] = rate_value
                rate_table[axis_at, upper_at] = rate_value
    return (perm_table, sign_table, rate_table)

def row_angles(frame_ids, frames_here, patch_rows, frame_rows, rate_table):
    within = jnp.arange(frame_rows, dtype=jnp.int32)
    is_patch = within < patch_rows
    height = jnp.where(is_patch, within // GRID_W, 0).astype(jnp.float32)
    across = jnp.where(is_patch, within % GRID_W, 0).astype(jnp.float32)
    height_rows = jnp.tile(height, frames_here)
    across_rows = jnp.tile(across, frames_here)
    time_rows = frame_ids.astype(jnp.float32)
    return time_rows[:, None] * rate_table[0] + height_rows[:, None] * rate_table[1] + across_rows[:, None] * rate_table[2]

def rotate(values, cosine_rows, sine_rows, perm_table, sign_table):
    return values * cosine_rows + values[:, perm_table] * (sign_table * sine_rows)

def layer_norm(values, gain_row, shift_row):
    row_mean = lax.optimization_barrier(jnp.mean(values, axis=-1, keepdims=True))
    centred = values - row_mean
    spread = lax.optimization_barrier(jnp.mean(centred * centred, axis=-1, keepdims=True))
    return centred * lax.rsqrt(spread + norm_epsilon) * gain_row + shift_row

def exact_gelu(values):
    return jax.nn.gelu(values, approximate=False)

def head_attention(query_head, key_head, value_head, mask_bias):
    raw_scores = low_back(jnp.dot(query_head, key_head.T, precision=highest_precision))
    scores = raw_scores * HEAD ** (-0.5) + mask_bias
    row_max = lax.optimization_barrier(jnp.max(scores, axis=1, keepdims=True))
    shifted = jnp.exp(scores - row_max)
    weights_soft = shifted / lax.optimization_barrier(jnp.sum(shifted, axis=1, keepdims=True))
    return jnp.dot(low(weights_soft), value_head, precision=highest_precision)

def block_forward(params, feat_rows, cond_here, live_here):
    in_weight, in_bias, act_weight, act_bias, state_weight, state_bias, attn_gain, attn_shift, qkv_weight, qkv_bias, proj_weight, proj_bias, mlp_gain, mlp_shift, up_weight, up_bias, down_weight, down_bias = params
    row_total = FRAMES * ROWS
    patch_x = low_back(jnp.dot(feat_rows, in_weight, precision=highest_precision) + in_bias)
    even_slot = (jnp.arange(COND) % 2 == 0)[None, :, None]
    act_rows = jnp.dot(cond_here, act_weight, precision=highest_precision) + act_bias
    state_rows = jnp.dot(cond_here, state_weight, precision=highest_precision) + state_bias
    cond_x = jnp.where(even_slot, act_rows, state_rows) * live_here[:, :, None]
    stream = jnp.concatenate([patch_x, cond_x], axis=1).reshape(row_total, D)
    key_live = jnp.concatenate([jnp.ones((FRAMES, PATCH), live_here.dtype), live_here], axis=1).reshape(row_total)
    key_frame = jnp.repeat(jnp.arange(FRAMES, dtype=jnp.int32), ROWS)
    mask_bias = jnp.where((key_frame[None, :] <= key_frame[:, None]) & (key_live[None, :] > 0.5), 0.0, masked_score)
    perm_table, sign_table, rate_table = rotary_tables(HEAD, HEADS)
    angles = row_angles(key_frame, FRAMES, PATCH, ROWS, rate_table)
    cosine_rows = jnp.cos(angles)
    sine_rows = jnp.sin(angles)
    attend = jax.checkpoint(lambda head_trio: head_attention(head_trio[0], head_trio[1], head_trio[2], mask_bias))
    for layer_at in range(LAYERS):
        normed = low(layer_norm(stream, attn_gain[layer_at], attn_shift[layer_at]))
        projected = low_back(jnp.einsum('rd,dce->rce', normed, qkv_weight[layer_at], precision=highest_precision) + qkv_bias[layer_at])
        query_rot = low(rotate(projected[:, 0], cosine_rows, sine_rows, perm_table, sign_table))
        key_rot = low(rotate(projected[:, 1], cosine_rows, sine_rows, perm_table, sign_table))
        value_low = low(projected[:, 2])
        heads_first = tuple((member.reshape(row_total, HEADS, HEAD).transpose(1, 0, 2) for member in (query_rot, key_rot, value_low)))
        heads_out = lax.map(attend, heads_first)
        attn_low = low(low_back(heads_out.transpose(1, 0, 2).reshape(row_total, D)))
        middle = stream + low_back(jnp.dot(attn_low, proj_weight[layer_at], precision=highest_precision) + proj_bias[layer_at])
        normed_two = low(layer_norm(middle, mlp_gain[layer_at], mlp_shift[layer_at]))
        hidden = low_back(jnp.dot(normed_two, up_weight[layer_at], precision=highest_precision) + up_bias[layer_at])
        active = low(exact_gelu(hidden))
        stream = middle + low_back(jnp.dot(active, down_weight[layer_at], precision=highest_precision) + down_bias[layer_at])
    return stream * key_live[:, None]

def reference(features, cond_values, cond_live, in_weight, in_bias, act_weight, act_bias, state_weight, state_bias, attn_gain, attn_shift, qkv_weight, qkv_bias, proj_weight, proj_bias, mlp_gain, mlp_shift, up_weight, up_bias, down_weight, down_bias, out_grad):
    params = (in_weight.astype(jnp.float32), in_bias, act_weight, act_bias, state_weight, state_bias, attn_gain, attn_shift, qkv_weight.astype(jnp.float32), qkv_bias, proj_weight.astype(jnp.float32), proj_bias, mlp_gain, mlp_shift, up_weight.astype(jnp.float32), up_bias, down_weight.astype(jnp.float32), down_bias)

    def one_clip(totals, clip_item):
        feat_rows, cond_here, live_here, cotangent = clip_item

        def forward_clip(param_set, feat_in):
            return block_forward(param_set, feat_in, cond_here, live_here)
        out_rows, pull_back = jax.vjp(forward_clip, params, feat_rows)
        grad_params, grad_feat = pull_back(cotangent.reshape(FRAMES * ROWS, D))
        totals = jax.tree.map(lambda running, addend: running + addend, totals, grad_params)
        return (totals, (out_rows.reshape(FRAMES, ROWS, D).astype(jnp.bfloat16), grad_feat))
    zero_grads = jax.tree.map(jnp.zeros_like, params)
    totals, (block_out, grad_features) = lax.scan(one_clip, zero_grads, (features.astype(jnp.float32), cond_values, cond_live.astype(jnp.float32), out_grad.astype(jnp.float32)))
    return (block_out, grad_features, totals[0], totals[1], totals[2], totals[3], totals[4], totals[5], totals[6], totals[7], totals[8], totals[9], totals[10], totals[11], totals[12], totals[13], totals[14], totals[15], totals[16], totals[17])
```

```python
import functools

import jax
import jax.numpy as jnp
import numpy as np
from jax import lax
from jax.experimental import pallas as pl
from jax.experimental.pallas import tpu as pltpu
from jax.sharding import PartitionSpec as P

HEAD = 64
GRID_W = 16
EXTRA = 8

highest_precision = lax.Precision.HIGHEST
norm_epsilon = 1e-06
masked_score = -1000000000.0
low_type = jnp.bfloat16
wide_type = jnp.float32

CORE_SWAP = [(0, 1), (1, 0), (2, 3), (3, 2)]
CHIP_SWAP = [(0, 2), (2, 0), (1, 3), (3, 1)]
HALF_SWAP = [(i, (i + 4) % 8) for i in range(8)]


def clip_shift(step):
    return [(i, (i + step) % 4) for i in range(4)]


def frame_shift(halves, step):
    return [
        (4 * half + i, 4 * ((half + halves) % 2) + (i + step) % 4)
        for half in range(2)
        for i in range(4)
    ]


FRAME_MOVES = [(halves, step) for halves in range(2) for step in range(4)]


def core_swap(value):
    return lax.ppermute(value, "tensor", CORE_SWAP)


def chip_swap(value):
    return lax.ppermute(value, "tensor", CHIP_SWAP)


def sum_rows_tensor(part):
    half = part.shape[0] // 2
    pair = part[:half] + core_swap(part[half:])
    quarter = half // 2
    return pair[:quarter] + chip_swap(pair[quarter:])


def join_rows_tensor(chunk):
    pair = jnp.concatenate([chunk, chip_swap(chunk)], axis=0)
    return jnp.concatenate([pair, core_swap(pair)], axis=0)


def spread_frames(value, later):
    blocks = [value]
    for halves, step in FRAME_MOVES[1:]:
        pairs = [
            (src, dst)
            for src, dst in frame_shift(halves, step)
            if (src > dst if later else src < dst)
        ]
        blocks.append(lax.ppermute(value, "frame", pairs))
    return blocks


def join_clips(value):
    return jnp.concatenate(
        [value] + [lax.ppermute(value, "clip", clip_shift(step)) for step in range(1, 4)], axis=0
    )


def swap_clips(pick, place):
    got = [pick(place)]
    for step in range(1, 4):
        got.append(lax.ppermute(pick((place + step) % 4), "clip", clip_shift(step)))
    return jnp.concatenate(got, axis=0)


def sum_over_frames(part, half, ring):
    rows = part.shape[0]
    block = rows // 4
    mine = lax.dynamic_slice_in_dim(part, ring * block, block, 0)
    for step in range(1, 4):
        sent = lax.dynamic_slice_in_dim(part, ((ring + step) % 4) * block, block, 0)
        got = lax.ppermute(sent.astype(low_type), "frame", frame_shift(0, step))
        mine = mine + got.astype(wide_type)
    share = block // 2
    sent = lax.dynamic_slice_in_dim(mine, (1 - half) * share, share, 0)
    kept = lax.dynamic_slice_in_dim(mine, half * share, share, 0)
    total = (kept + lax.ppermute(sent, "frame", HALF_SWAP)).astype(low_type)
    other = lax.ppermute(total, "frame", HALF_SWAP)
    first = half == 0
    pair = jnp.concatenate([jnp.where(first, total, other), jnp.where(first, other, total)], axis=0)
    joined = jnp.zeros((rows, part.shape[1]), low_type)
    joined = lax.dynamic_update_slice_in_dim(joined, pair, ring * block, 0)
    for step in range(1, 4):
        got = lax.ppermute(pair, "frame", frame_shift(0, step))
        joined = lax.dynamic_update_slice_in_dim(joined, got, ((ring - step) % 4) * block, 0)
    return joined


def clip_pieces(joined, place):
    pieces = [(place, joined)]
    for step in range(1, 4):
        pieces.append(((place - step) % 4, lax.ppermute(joined, "clip", clip_shift(step))))
    return pieces


def sum_everywhere(value):
    value = value + core_swap(value)
    value = value + chip_swap(value)
    value = value + lax.ppermute(value, "frame", HALF_SWAP)
    for bit in (1, 2):
        value = value + lax.ppermute(value, "frame", [(i, i ^ bit) for i in range(8)])
        value = value + lax.ppermute(value, "clip", [(i, i ^ bit) for i in range(4)])
    return value


def rotary_tables(head_size, head_count):
    group_size = 2 * (head_size // 3 // 2)
    half_size = group_size // 2
    total_width = head_size * head_count
    swap_table = np.zeros((total_width, total_width), np.float32)
    rate_table = np.zeros((3, total_width), np.float32)
    for head_at in range(head_count):
        for axis_at in range(3):
            for pair_at in range(half_size):
                lower_at = head_at * head_size + axis_at * group_size + pair_at
                upper_at = lower_at + half_size
                swap_table[upper_at, lower_at] = -1.0
                swap_table[lower_at, upper_at] = 1.0
                rate_value = 10000.0 ** (-2.0 * pair_at / group_size)
                rate_table[axis_at, lower_at] = rate_value
                rate_table[axis_at, upper_at] = rate_value
    return swap_table, rate_table


def norm_parts(values):
    row_mean = jnp.mean(values, axis=-1, keepdims=True)
    centred = values - row_mean
    spread = jnp.mean(centred * centred, axis=-1, keepdims=True)
    inverse = lax.rsqrt(spread + norm_epsilon)
    return centred * inverse, inverse


def norm_back(grad, gain_row, hat, inverse):
    scaled = grad * gain_row
    first = jnp.mean(scaled, axis=-1, keepdims=True)
    second = jnp.mean(scaled * hat, axis=-1, keepdims=True)
    return (
        (scaled - first - hat * second) * inverse,
        jnp.sum(grad * hat, axis=0),
        jnp.sum(grad, axis=0),
    )


def exact_gelu(values):
    return jax.nn.gelu(values, approximate=False)


def dot_wide(left, right):
    return jnp.dot(left, right, preferred_element_type=wide_type)


def dot_dims(left, right, left_dim, right_dim):
    return lax.dot_general(
        left, right, (((left_dim,), (right_dim,)), ((), ())), preferred_element_type=wide_type
    )


def head_cols(at):
    return slice(at * HEAD, (at + 1) * HEAD)


def attend_kernel(heads, blocks, query_ref, bias_ref, *refs):
    pair_refs = refs[:blocks]
    out_ref, total_ref, score_ref = refs[blocks:]
    rows = query_ref.shape[0]
    width = heads * HEAD
    total_ref[...] = jnp.zeros_like(total_ref)
    for head in range(heads):
        query = query_ref[:, head_cols(head)]
        top = jnp.full((1, rows), 2.0 * masked_score, wide_type)
        for at in range(blocks):
            key = pair_refs[at][:, head_cols(head)]
            scores = dot_dims(key, query, 1, 1) + bias_ref[:, at : at + 1]
            score_ref[at * rows : (at + 1) * rows, :] = scores
            top = jnp.maximum(top, jnp.max(scores, axis=0, keepdims=True))
        mass = jnp.zeros((1, rows), wide_type)
        out = jnp.zeros((HEAD, rows), wide_type)
        for at in range(blocks):
            weights = jnp.exp(score_ref[at * rows : (at + 1) * rows, :] - top)
            mass = mass + jnp.sum(weights, axis=0, keepdims=True)
            value = pair_refs[at][:, width + head * HEAD : width + (head + 1) * HEAD]
            out = out + dot_dims(value, weights.astype(low_type), 0, 0)
        out_ref[head_cols(head), :] = out / mass
        total_ref[head : head + 1, :] = top + jnp.log(mass)


def query_grad_kernel(heads, blocks, query_ref, bias_ref, total_ref, centre_ref, grad_ref, *refs):
    pair_refs = refs[:blocks]
    out_ref = refs[blocks]
    rows = query_ref.shape[0]
    width = heads * HEAD
    for head in range(heads):
        query = query_ref[:, head_cols(head)]
        grad = grad_ref[:, head_cols(head)]
        total = total_ref[head : head + 1, :]
        centre = centre_ref[head : head + 1, :]
        out = jnp.zeros((HEAD, rows), wide_type)
        for at in range(blocks):
            key = pair_refs[at][:, head_cols(head)]
            value = pair_refs[at][:, width + head * HEAD : width + (head + 1) * HEAD]
            scores = dot_dims(key, query, 1, 1) + bias_ref[:, at : at + 1]
            weights = jnp.exp(scores - total)
            soft = dot_dims(value, grad, 1, 1)
            back = (weights * (soft - centre)).astype(low_type)
            out = out + dot_dims(key, back, 0, 0)
        out_ref[head_cols(head), :] = out


def key_grad_kernel(
    heads, blocks, source_ref, hidden_ref, pair_ref, bias_ref, query_ref, total_ref, *refs
):
    grad_refs = refs[:blocks]
    centre_refs = refs[blocks : 2 * blocks]
    key_out, value_out = refs[2 * blocks :]
    rows = pair_ref.shape[0]
    width = heads * HEAD
    for head in range(heads):
        key = pair_ref[:, head_cols(head)]
        value = pair_ref[:, width + head * HEAD : width + (head + 1) * HEAD]
        key_sum = jnp.zeros((rows, HEAD), wide_type)
        value_sum = jnp.zeros((rows, HEAD), wide_type)
        for at in range(blocks):
            frame = source_ref[at]
            query = query_ref[frame, :, head_cols(head)]
            grad = grad_refs[at][:, head_cols(head)]
            total = total_ref[frame, head : head + 1, :]
            centre = centre_refs[at][head : head + 1, :]
            scores = dot_dims(key, query, 1, 1) + bias_ref[...]
            weights = jnp.exp(scores - total + hidden_ref[at])
            value_sum = value_sum + dot_wide(weights.astype(low_type), grad)
            soft = dot_dims(value, grad, 1, 1)
            back = (weights * (soft - centre)).astype(low_type)
            key_sum = key_sum + dot_wide(back, query)
        key_out[:, head_cols(head)] = key_sum
        value_out[:, head_cols(head)] = value_sum


def call_kernel(kernel, args, in_smem, outs, scratch, flops, exps):
    specs = [
        pl.BlockSpec(memory_space=pltpu.SMEM if at in in_smem else pltpu.VMEM)
        for at in range(len(args))
    ]
    moved = sum(a.size * a.dtype.itemsize for a in args)
    return pl.pallas_call(
        kernel,
        out_shape=outs,
        in_specs=specs,
        out_specs=jax.tree.map(lambda _: pl.BlockSpec(memory_space=pltpu.VMEM), outs),
        scratch_shapes=scratch,
        compiler_params=pltpu.CompilerParams(vmem_limit_bytes=40 * 1024 * 1024),
        cost_estimate=pl.CostEstimate(flops=flops, bytes_accessed=moved, transcendentals=exps),
    )(*args)


def on_device(
    features,
    cond_values,
    cond_live,
    in_weight,
    in_bias,
    act_weight,
    act_bias,
    state_weight,
    state_bias,
    attn_gain,
    attn_shift,
    qkv_weight,
    qkv_bias,
    proj_weight,
    proj_bias,
    mlp_gain,
    mlp_shift,
    up_weight,
    up_bias,
    down_weight,
    down_bias,
    out_grad,
):
    patch_rows = features.shape[2]
    feat_width = features.shape[3]
    slot_count = cond_values.shape[2]
    all_frames = cond_live.shape[1]
    model_width = in_weight.shape[1]
    width = qkv_weight.shape[3]
    heads = width // HEAD
    level_count = attn_gain.shape[0]
    patches = patch_rows // 4
    chunk_rows = patches + EXTRA
    rows = 4 * chunk_rows
    hidden_width = up_weight.shape[2]

    tensor_at = lax.axis_index("tensor")
    chip_at, core_at = tensor_at // 2, tensor_at % 2
    frame_at = lax.axis_index("frame")
    half_at, ring_at = frame_at // 4, frame_at % 4
    clip_at = lax.axis_index("clip")

    chunk_ids = [
        2 * jnp.bitwise_xor(core_at, core_step) + jnp.bitwise_xor(chip_at, chip_step)
        for core_step in range(2)
        for chip_step in range(2)
    ]
    own_chunk = chunk_ids[0]
    sources = jnp.stack(
        [4 * ((half_at + halves) % 2) + (ring_at - step) % 4 for halves, step in FRAME_MOVES]
    ).astype(jnp.int32)

    within = lax.broadcasted_iota(jnp.int32, (chunk_rows, 1), 0)
    is_patch = within < patches
    heights, columns = [], []
    for chunk_id in chunk_ids:
        patch_id = chunk_id * patches + within
        heights.append(jnp.where(is_patch, patch_id // GRID_W, 0))
        columns.append(jnp.where(is_patch, patch_id % GRID_W, 0))
    heights = jnp.concatenate(heights, axis=0).astype(wide_type)
    columns = jnp.concatenate(columns, axis=0).astype(wide_type)
    swap_table, rate_table = rotary_tables(HEAD, heads)
    angles = (
        frame_at.astype(wide_type) * rate_table[0][None, :]
        + heights * rate_table[1]
        + columns * rate_table[2]
    )
    cosine_rows = jnp.cos(angles)
    sine_rows = jnp.sin(angles)
    swap_low = jnp.asarray(swap_table, low_type)
    swap_wide = jnp.asarray(swap_table, wide_type)

    live_all = cond_live[0].astype(wide_type)
    own_slots = lax.dynamic_index_in_dim(live_all, frame_at, 0, False)

    def live_rows(slots, chunk_id):
        picked = jnp.where(
            chunk_id < slot_count,
            lax.dynamic_index_in_dim(slots, jnp.minimum(chunk_id, slot_count - 1), 1, False),
            0.0,
        )
        return jnp.where(is_patch, 1.0, jnp.where(within == patches, picked[None, :], 0.0))

    source_live = jnp.take(live_all, sources, axis=0)
    key_live = jnp.concatenate([live_rows(source_live, c) for c in chunk_ids], axis=0)
    key_bias = jnp.where(
        (key_live > 0.5) & (sources <= frame_at)[None, :], 0.0, masked_score
    ).astype(wide_type)
    own_bias = key_bias[:, :1]
    hidden_query = jnp.where(sources >= frame_at, 0.0, masked_score).astype(wide_type)
    own_live = live_rows(own_slots[None, :], own_chunk)

    def extra_rows(slot_rows):
        picked = lax.dynamic_slice_in_dim(
            slot_rows, jnp.minimum(own_chunk, slot_count - 1), 1, 0
        )
        picked = jnp.where(own_chunk < slot_count, picked, jnp.zeros_like(picked))
        return jnp.pad(picked, ((0, EXTRA - 1), (0, 0)))

    cond_here = cond_values[0, 0]
    act_rows = jnp.dot(cond_here, act_weight, precision=highest_precision) + act_bias
    state_rows = jnp.dot(cond_here, state_weight, precision=highest_precision) + state_bias
    even_slot = (jnp.arange(slot_count) % 2 == 0)[:, None]
    cond_x = jnp.where(even_slot, act_rows, state_rows) * own_slots[:, None]

    flat_feat = jnp.concatenate(
        [
            lax.dynamic_slice_in_dim(features[0, 0], c * patches, patches, 0)
            for c in chunk_ids
        ],
        axis=0,
    )
    patch_x = sum_rows_tensor(dot_wide(flat_feat, in_weight)) + in_bias
    stream = jnp.concatenate([patch_x, extra_rows(cond_x)], axis=0)

    feat_all = join_clips(flat_feat)
    score_scale = HEAD ** (-0.5)
    pair_work = 2 * blocks_work(rows, all_frames, heads)

    stored = []
    for layer in range(level_count):
        hat_one, inverse_one = norm_parts(stream)
        first_chunk = (hat_one * attn_gain[layer] + attn_shift[layer]).astype(low_type)
        first_in = join_rows_tensor(first_chunk)
        weight = qkv_weight[layer]
        turned = [dot_wide(weight[:, at], swap_low).astype(low_type) for at in range(2)]
        bias = qkv_bias[layer]
        bias_turned = jnp.dot(bias[:2], swap_wide, precision=highest_precision)
        straight = [dot_wide(first_in, weight[:, at]) + bias[at] for at in range(3)]
        crossed = [dot_wide(first_in, turned[at]) + bias_turned[at] for at in range(2)]
        key_low = (straight[1] * cosine_rows + crossed[1] * sine_rows).astype(low_type)
        value_low = straight[2].astype(low_type)
        pair = jnp.concatenate([key_low, value_low], axis=1)
        pairs = spread_frames(pair, False)
        query_low = (straight[0] * cosine_rows + crossed[0] * sine_rows).astype(low_type)
        query_low = query_low * jnp.asarray(score_scale, low_type)
        out_turned, log_total = call_kernel(
            functools.partial(attend_kernel, heads, all_frames),
            (query_low, key_bias, *pairs),
            (),
            (
                jax.ShapeDtypeStruct((width, rows), wide_type),
                jax.ShapeDtypeStruct((8, rows), wide_type),
            ),
            [pltpu.VMEM((all_frames * rows, rows), wide_type)],
            2 * pair_work,
            rows * rows * all_frames * heads,
        )
        attn_wide = out_turned.T
        attn_low = attn_wide.astype(low_type)
        query_all = lax.all_gather(query_low, "frame")
        total_all = lax.all_gather(log_total, "frame")
        middle = stream + (
            sum_rows_tensor(dot_wide(attn_low, proj_weight[layer])) + proj_bias[layer]
        )
        hat_two, inverse_two = norm_parts(middle)
        second_chunk = (hat_two * mlp_gain[layer] + mlp_shift[layer]).astype(low_type)
        second_in = join_rows_tensor(second_chunk)
        hidden = dot_wide(second_in, up_weight[layer]) + up_bias[layer]
        active_low = exact_gelu(hidden).astype(low_type)
        stream = middle + (
            sum_rows_tensor(dot_wide(active_low, down_weight[layer])) + down_bias[layer]
        )
        first_all = join_clips(jnp.concatenate([first_in, attn_low], axis=1))
        second_all = join_clips(jnp.concatenate([second_in, active_low], axis=1))
        stored.append(
            (
                hat_one,
                inverse_one,
                query_low,
                pairs,
                log_total,
                query_all,
                total_all,
                attn_wide,
                hat_two,
                inverse_two,
                hidden,
                first_all,
                second_all,
            )
        )

    def in_order(full, count):
        out = jnp.zeros((4 * count,) + full.shape[1:], full.dtype)
        size = full.shape[0] // 4
        for at, chunk_id in enumerate(chunk_ids):
            out = lax.dynamic_update_slice_in_dim(
                out, full[at * size : at * size + count], chunk_id * count, 0
            )
        return out

    block_full = join_rows_tensor((stream * own_live).astype(low_type))
    slot_full = jnp.concatenate(
        [
            block_full[at * chunk_rows + patches : at * chunk_rows + patches + 1]
            for at in range(4)
        ],
        axis=0,
    )
    block_out = jnp.concatenate(
        [in_order(block_full, patches), in_order(slot_full, 1)[:slot_count]], axis=0
    )[None, None]

    own_out = lax.dynamic_slice_in_dim(out_grad[0, 0], own_chunk * patches, patches, 0)
    grad_stream = (
        jnp.concatenate(
            [
                own_out.astype(wide_type),
                extra_rows(out_grad[0, 0, patch_rows:].astype(wide_type)),
            ],
            axis=0,
        )
        * own_live
    )

    small = {}
    grad_qkv = jnp.zeros((level_count, model_width, 3, width), wide_type)
    grad_proj = jnp.zeros((level_count, width, model_width), wide_type)
    grad_up = jnp.zeros((level_count, model_width, hidden_width), wide_type)
    grad_down = jnp.zeros((level_count, hidden_width, model_width), wide_type)
    wide_part = model_width // 4
    up_part = hidden_width // 4
    head_part = width // 4

    def columns_of(value, size):
        return lambda place: lax.dynamic_slice_in_dim(value, place * size, size, value.ndim - 1)

    for layer in reversed(range(level_count)):
        (
            hat_one,
            inverse_one,
            query_low,
            pairs,
            log_total,
            query_all,
            total_all,
            attn_wide,
            hat_two,
            inverse_two,
            hidden,
            first_all,
            second_all,
        ) = stored[layer]
        branch_chunk = grad_stream.astype(low_type)
        small["down", layer] = jnp.sum(branch_chunk.astype(wide_type), axis=0)
        branch = join_rows_tensor(branch_chunk)
        _, gelu_pull = jax.vjp(exact_gelu, hidden)
        grad_hidden = gelu_pull(dot_dims(branch, down_weight[layer], 1, 1))[0].astype(low_type)
        small["up", layer] = jnp.sum(grad_hidden.astype(wide_type), axis=0)
        grad_two = sum_rows_tensor(dot_dims(grad_hidden, up_weight[layer], 1, 1))
        from_norm, small["mlp_gain", layer], small["mlp_shift", layer] = norm_back(
            grad_two, mlp_gain[layer], hat_two, inverse_two
        )
        grad_middle = grad_stream + from_norm
        proj_chunk = grad_middle.astype(low_type)
        small["proj", layer] = jnp.sum(proj_chunk.astype(wide_type), axis=0)
        proj_out = join_rows_tensor(proj_chunk)
        grad_attn = dot_dims(proj_out, proj_weight[layer], 1, 1).astype(low_type)
        centre = jnp.sum(
            (grad_attn.astype(wide_type) * attn_wide).reshape(rows, heads, HEAD), axis=2
        ).T
        centre = jnp.pad(centre, ((0, 8 - heads), (0, 0)))
        grads = spread_frames(grad_attn, True)
        centres = spread_frames(centre, True)
        query_turned = call_kernel(
            functools.partial(query_grad_kernel, heads, all_frames),
            (query_low, key_bias, log_total, centre, grad_attn, *pairs),
            (),
            jax.ShapeDtypeStruct((width, rows), wide_type),
            [],
            3 * pair_work,
            rows * rows * all_frames * heads,
        )
        key_sum, value_sum = call_kernel(
            functools.partial(key_grad_kernel, heads, all_frames),
            (
                sources,
                hidden_query,
                pairs[0],
                own_bias,
                query_all,
                total_all,
                *grads,
                *centres,
            ),
            (0, 1),
            (
                jax.ShapeDtypeStruct((rows, width), wide_type),
                jax.ShapeDtypeStruct((rows, width), wide_type),
            ),
            [],
            4 * pair_work,
            rows * rows * all_frames * heads,
        )
        query_sum = query_turned.T * score_scale
        both = jnp.concatenate([query_sum, key_sum], axis=0)
        both_turned = jnp.dot(both, swap_wide, precision=highest_precision)
        mixed = [
            (query_sum * cosine_rows - both_turned[:rows] * sine_rows).astype(low_type),
            (key_sum * cosine_rows - both_turned[rows:] * sine_rows).astype(low_type),
            value_sum.astype(low_type),
        ]
        small["qkv", layer] = jnp.stack([jnp.sum(m.astype(wide_type), axis=0) for m in mixed])
        normed_part = sum(
            dot_dims(mixed[at], qkv_weight[layer, :, at], 1, 1) for at in range(3)
        )
        grad_one = sum_rows_tensor(normed_part)
        from_norm, small["attn_gain", layer], small["attn_shift", layer] = norm_back(
            grad_one, attn_gain[layer], hat_one, inverse_one
        )
        grad_stream = grad_middle + from_norm

        packed = swap_clips(
            lambda place: jnp.concatenate(
                [
                    columns_of(branch, wide_part)(place),
                    columns_of(grad_hidden, up_part)(place),
                    columns_of(proj_out, wide_part)(place),
                ],
                axis=1,
            ),
            clip_at,
        )
        attn_all = first_all[:, model_width:]
        first_in_all = first_all[:, :model_width]
        second_in_all = second_all[:, :model_width]
        active_all = second_all[:, model_width:]
        down_q = dot_dims(active_all, packed[:, :wide_part], 0, 0)
        up_q = dot_dims(second_in_all, packed[:, wide_part : wide_part + up_part], 0, 0)
        proj_q = dot_dims(attn_all, packed[:, wide_part + up_part :], 0, 0)
        joined = jnp.concatenate(
            [
                jnp.concatenate([down_q, up_q], axis=1),
                jnp.concatenate([proj_q[: width // 2], proj_q[width // 2 :]], axis=1),
            ],
            axis=0,
        )
        for place, piece in clip_pieces(sum_over_frames(joined, half_at, ring_at), clip_at):
            wide = piece.astype(wide_type)[None]
            grad_down = lax.dynamic_update_slice(
                grad_down, wide[:, :hidden_width, :wide_part], (layer, 0, place * wide_part)
            )
            grad_up = lax.dynamic_update_slice(
                grad_up, wide[:, :model_width, wide_part:], (layer, 0, place * up_part)
            )
            grad_proj = lax.dynamic_update_slice(
                grad_proj, wide[:, model_width:, :wide_part], (layer, 0, place * wide_part)
            )
            grad_proj = lax.dynamic_update_slice(
                grad_proj,
                wide[:, model_width:, wide_part:],
                (layer, width // 2, place * wide_part),
            )

        packed = swap_clips(
            lambda place: jnp.concatenate(
                [columns_of(m, head_part)(place) for m in mixed], axis=1
            ),
            clip_at,
        )
        qkv_q = dot_dims(first_in_all, packed, 0, 0)
        for place, piece in clip_pieces(sum_over_frames(qkv_q, half_at, ring_at), clip_at):
            wide = piece.astype(wide_type).reshape(1, model_width, 3, head_part)
            grad_qkv = lax.dynamic_update_slice(
                grad_qkv, wide, (layer, 0, 0, place * head_part)
            )

    patch_chunk = grad_stream[:patches].astype(low_type)
    in_bias_part = jnp.sum(patch_chunk.astype(wide_type), axis=0)
    grad_patch = join_rows_tensor(patch_chunk)
    grad_features = in_order(dot_dims(grad_patch, in_weight, 1, 1), patches)[None, None]
    packed = swap_clips(columns_of(grad_patch, wide_part), clip_at)
    in_q = dot_dims(feat_all, packed, 0, 0)
    in_rows = -(-feat_width // 64) * 64
    in_q = jnp.pad(in_q, ((0, in_rows - feat_width), (0, 0)))
    grad_in = jnp.zeros((feat_width, model_width), wide_type)
    for place, piece in clip_pieces(sum_over_frames(in_q, half_at, ring_at), clip_at):
        grad_in = lax.dynamic_update_slice(
            grad_in, piece[:feat_width].astype(wide_type), (0, place * wide_part)
        )

    slot_row = grad_stream[patches : patches + 1] * own_live[patches : patches + 1]
    own_cond = lax.dynamic_slice_in_dim(
        cond_here, jnp.minimum(own_chunk, slot_count - 1), 1, 0
    )
    slot_part = jnp.concatenate([own_cond.T * slot_row, slot_row], axis=0)
    here = own_chunk < slot_count
    is_act = here & (own_chunk % 2 == 0)
    is_state = here & (own_chunk % 2 == 1)
    act_part = jnp.where(is_act, slot_part, 0.0)
    state_part = jnp.where(is_state, slot_part, 0.0)

    def at_tensor(value, total):
        return lax.dynamic_update_slice(
            jnp.zeros((value.shape[0], total), wide_type),
            value,
            (0, tensor_at * value.shape[1]),
        )

    names = ("attn_gain", "attn_shift", "proj", "mlp_gain", "mlp_shift", "down")
    layers = range(level_count)
    parts = [in_bias_part[None], act_part, state_part]
    parts += [jnp.stack([small[name, layer] for layer in layers]) for name in names]
    parts.append(
        at_tensor(jnp.concatenate([small["qkv", layer] for layer in layers], axis=0), 4 * width)
    )
    ups = at_tensor(jnp.stack([small["up", layer] for layer in layers]), 4 * hidden_width)
    parts.append(ups.reshape(-1, model_width))
    counts = [part.shape[0] for part in parts]
    vector = jnp.concatenate(parts, axis=0)
    pad = -vector.shape[0] % 8
    vector = sum_everywhere(jnp.pad(vector, ((0, pad), (0, 0))))
    starts = np.cumsum([0] + counts)
    got = [vector[a : a + n] for a, n in zip(starts, counts)]
    by_name = dict(zip(names, got[3:9]))
    grad_qkv_bias = lax.dynamic_slice_in_dim(got[9], tensor_at * width, width, 1)
    grad_qkv_bias = grad_qkv_bias.reshape(level_count, 3, width)
    grad_up_bias = lax.dynamic_slice_in_dim(
        got[10].reshape(level_count, 4 * hidden_width), tensor_at * hidden_width, hidden_width, 1
    )
    act_count = cond_here.shape[1]
    return (
        block_out,
        grad_features,
        grad_in,
        got[0][0],
        got[1][:act_count],
        got[1][act_count],
        got[2][:act_count],
        got[2][act_count],
        by_name["attn_gain"],
        by_name["attn_shift"],
        grad_qkv,
        grad_qkv_bias,
        grad_proj,
        by_name["proj"],
        by_name["mlp_gain"],
        by_name["mlp_shift"],
        grad_up,
        grad_up_bias,
        grad_down,
        by_name["down"],
    )


def blocks_work(rows, frames, heads):
    return rows * rows * frames * heads * HEAD


def solution(mesh):
    return jax.shard_map(
        on_device,
        mesh=mesh,
        in_specs=(
            P("clip", "frame", None, "tensor"),
            P("clip", "frame", None, None),
            P("clip", None, None),
            P("tensor", None),
            P(),
            P(),
            P(),
            P(),
            P(),
            P(),
            P(),
            P(None, None, None, "tensor"),
            P(None, None, "tensor"),
            P(None, "tensor", None),
            P(),
            P(),
            P(),
            P(None, None, "tensor"),
            P(None, "tensor"),
            P(None, "tensor", None),
            P(),
            P("clip", "frame", None, None),
        ),
        out_specs=(
            P("clip", "frame", None, None),
            P("clip", "frame", None, "tensor"),
            P("tensor", None),
            P(),
            P(),
            P(),
            P(),
            P(),
            P(),
            P(),
            P(None, None, None, "tensor"),
            P(None, None, "tensor"),
            P(None, "tensor", None),
            P(),
            P(),
            P(),
            P(None, None, "tensor"),
            P(None, "tensor"),
            P(None, "tensor", None),
            P(),
        ),
        check_vma=False,
    )
```

```python
import functools

import jax
import jax.numpy as jnp
import numpy as np
from jax import lax
from jax.experimental import pallas as pl
from jax.experimental.pallas import tpu as pltpu
from jax.sharding import PartitionSpec as P

HEAD = 64
GRID_W = 16
EXTRA = 8

highest_precision = lax.Precision.HIGHEST
norm_epsilon = 1e-06
masked_score = -1000000000.0
low_type = jnp.bfloat16
wide_type = jnp.float32

CORE_SWAP = [(0, 1), (1, 0), (2, 3), (3, 2)]
CHIP_SWAP = [(0, 2), (2, 0), (1, 3), (3, 1)]
HALF_SWAP = [(i, (i + 4) % 8) for i in range(8)]


def clip_shift(step):
    return [(i, (i + step) % 4) for i in range(4)]


def frame_shift(halves, step):
    return [
        (4 * half + i, 4 * ((half + halves) % 2) + (i + step) % 4)
        for half in range(2)
        for i in range(4)
    ]


def core_swap(value):
    return lax.ppermute(value, "tensor", CORE_SWAP)


def chip_swap(value):
    return lax.ppermute(value, "tensor", CHIP_SWAP)


def halves_tensor(part):
    half = part.shape[0] // 2
    pair = part[:half] + core_swap(part[half:])
    quarter = half // 2
    return pair[:quarter], chip_swap(pair[quarter:])


def join_rows_tensor(chunk):
    pair = jnp.concatenate([chunk, chip_swap(chunk)], axis=0)
    return jnp.concatenate([pair, core_swap(pair)], axis=0)


def to_heads(blocks):
    return [blocks[0]] + [
        lax.ppermute(blocks[step], "frame", frame_shift(0, step)) for step in range(1, 4)
    ]


def to_frames(blocks):
    return [blocks[0]] + [
        lax.ppermute(blocks[step], "frame", frame_shift(0, -step)) for step in range(1, 4)
    ]


def pairs_to_later_half(blocks):
    return [
        lax.ppermute(
            blocks[step],
            "frame",
            [(src, dst) for src, dst in frame_shift(1, step) if src < dst],
        )
        for step in range(4)
    ]


DOWN_HALF = [(i + 4, i) for i in range(4)]


def swap_clips(packs):
    return [packs[0]] + [
        lax.ppermute(packs[step], "clip", clip_shift(step)) for step in range(1, 4)
    ]


def ring_pieces(value):
    return [value] + [
        lax.ppermute(value, "frame", frame_shift(0, step)) for step in range(1, 4)
    ]


def ring_sends(part, ring):
    block = part.shape[0] // 4
    got = []
    for step in range(1, 4):
        sent = lax.dynamic_slice_in_dim(part, ((ring + step) % 4) * block, block, 0)
        got.append(lax.ppermute(sent.astype(low_type), "frame", frame_shift(0, step)))
    return got


def clip_pieces(joined):
    return [joined] + [
        lax.ppermute(joined, "clip", clip_shift(step)) for step in range(1, 4)
    ]


def sum_everywhere(value):
    value = value + core_swap(value)
    value = value + chip_swap(value)
    value = value + lax.ppermute(value, "frame", HALF_SWAP)
    for bit in (1, 2):
        value = value + lax.ppermute(value, "frame", [(i, i ^ bit) for i in range(8)])
        value = value + lax.ppermute(value, "clip", [(i, i ^ bit) for i in range(4)])
    return value


def rotary_tables(head_size, head_count):
    group_size = 2 * (head_size // 3 // 2)
    half_size = group_size // 2
    total_width = head_size * head_count
    swap_table = np.zeros((total_width, total_width), np.float32)
    rate_table = np.zeros((3, total_width), np.float32)
    for head_at in range(head_count):
        for axis_at in range(3):
            for pair_at in range(half_size):
                lower_at = head_at * head_size + axis_at * group_size + pair_at
                upper_at = lower_at + half_size
                swap_table[upper_at, lower_at] = -1.0
                swap_table[lower_at, upper_at] = 1.0
                rate_value = 10000.0 ** (-2.0 * pair_at / group_size)
                rate_table[axis_at, lower_at] = rate_value
                rate_table[axis_at, upper_at] = rate_value
    return swap_table, rate_table


def norm_rows(values):
    row_mean = jnp.mean(values, axis=-1, keepdims=True)
    centred = values - row_mean
    spread = jnp.mean(centred * centred, axis=-1, keepdims=True)
    inverse = lax.rsqrt(spread + norm_epsilon)
    return centred * inverse, inverse


def norm_kernel(gain_ref, shift_ref, *refs):
    terms, (stream_ref, hat_ref, inverse_ref, low_ref) = refs[:-4], refs[-4:]
    values = terms[0][...]
    if len(terms) > 1:
        values = values + (terms[1][...] + terms[2][...] + terms[3][...])
    hat, inverse = norm_rows(values)
    stream_ref[...] = values
    hat_ref[...] = hat
    inverse_ref[...] = jnp.broadcast_to(inverse, inverse_ref.shape)
    low_ref[...] = (hat * gain_ref[...] + shift_ref[...]).astype(low_type)


def norm_back_kernel(count, kept_ref, got_ref, gain_ref, hat_ref, inverse_ref, grad_ref, out_ref, low_ref, sums_ref):
    grad = kept_ref[...] + got_ref[...]
    hat = hat_ref[...]
    scaled = grad * gain_ref[...]
    first = jnp.mean(scaled, axis=-1, keepdims=True)
    second = jnp.mean(scaled * hat, axis=-1, keepdims=True)
    out = grad_ref[...] + (scaled - first - hat * second) * inverse_ref[:, 0:1]
    low = out.astype(low_type)
    out_ref[...] = out
    low_ref[...] = low
    sums_ref[...] = jnp.zeros_like(sums_ref)
    sums_ref[0:1, :] = jnp.sum(grad * hat, axis=0, keepdims=True)
    sums_ref[1:2, :] = jnp.sum(grad, axis=0, keepdims=True)
    sums_ref[2:3, :] = jnp.sum(low[:count].astype(wide_type), axis=0, keepdims=True)


def exact_gelu(values):
    return jax.nn.gelu(values, approximate=False)


def dot_wide(left, right):
    return jnp.dot(left, right, preferred_element_type=wide_type)


def dot_dims(left, right, left_dim, right_dim):
    return lax.dot_general(
        left, right, (((left_dim,), (right_dim,)), ((), ())), preferred_element_type=wide_type
    )


def head_cols(at):
    return slice(at * HEAD, (at + 1) * HEAD)


def ring_back(place, step):
    return lax.rem(place - step + 4, 4)


def ring_ahead(place, step):
    return lax.rem(place + step, 4)


def project_kernel(heads, at_ref, rows_ref, key_w, value_w, query_w, bias_ref, cos_ref, sin_ref, swap_ref, *out_refs):
    rows = rows_ref[...]
    swap = swap_ref[...]
    cosine, sine = cos_ref[...], sin_ref[...]

    def turned(weight, bias):
        value = dot_wide(rows, weight[...]) + bias
        crossed = jnp.dot(value, swap, precision=highest_precision, preferred_element_type=wide_type)
        return value * cosine + crossed * sine

    key = turned(key_w, bias_ref[1:2, :]).astype(low_type)
    value = (dot_wide(rows, value_w[...]) + bias_ref[2:3, :]).astype(low_type)
    query = (turned(query_w, bias_ref[0:1, :]).astype(low_type).astype(wide_type) * HEAD ** (-0.5)).astype(low_type)

    def write(head, step):
        for at, part in enumerate((key, value, query)):
            out_refs[step][:, head_cols(at)] = part[:, head_cols(head)]
            if at < 2:
                out_refs[4 + step][:, head_cols(at)] = part[:, head_cols(head)]

    for ring in range(4):

        @pl.when(at_ref[0] == ring)
        def _(ring=ring):
            for step in range(4):
                write((ring + step) % 4, step)


def lane_tiles(total):
    size = 384 if total % 384 == 0 else total
    return [slice(at * size, (at + 1) * size) for at in range(total // size)]


def attend_kernel(bias_ref, mask_ref, *refs):
    own_refs, cross_refs = refs[:4], refs[4:8]
    out_ref, low_ref, total_ref, query_ref, score_ref = refs[8:]
    rows = own_refs[0].shape[0]
    total_rows = 4 * rows
    for at in range(4):
        query_ref[at * rows : (at + 1) * rows, :] = own_refs[at][:, head_cols(2)]
    total_ref[...] = jnp.zeros_like(total_ref)

    def pair(at, part):
        if at < 4:
            return own_refs[at][:, head_cols(part)]
        return cross_refs[at - 4][:, head_cols(part)]

    for tile in lane_tiles(total_rows):
        query = query_ref[tile, :]
        wide = tile.stop - tile.start
        top = jnp.full((1, wide), 2.0 * masked_score, wide_type)
        for at in range(8):
            scores = dot_dims(pair(at, 0), query, 1, 1) + bias_ref[:, at : at + 1]
            if at < 4:
                scores = scores + mask_ref[at : at + 1, tile]
            score_ref[at * rows : (at + 1) * rows, :] = scores
            top = jnp.maximum(top, jnp.max(scores, axis=0, keepdims=True))
        mass = jnp.zeros((1, wide), wide_type)
        out = jnp.zeros((HEAD, wide), wide_type)
        for at in range(8):
            weights = jnp.exp(score_ref[at * rows : (at + 1) * rows, :] - top)
            mass = mass + jnp.sum(weights, axis=0, keepdims=True)
            out = out + dot_dims(pair(at, 1), weights.astype(low_type), 0, 0)
        total_ref[0:1, tile] = top + jnp.log(mass)
        rows_out = (out / mass).T
        out_ref[tile, :] = rows_out
        low_ref[tile, :] = rows_out.astype(low_type)


def attend_back_kernel(own, bias_ref, mask_ref, total_ref, out_ref, *refs):
    own_refs, grad_refs = refs[:4], refs[4:8]
    cross_refs = refs[8:-4]
    pair_sum, query_sum, query_ref, grad_ref = refs[-4:]
    rows = own_refs[0].shape[0]
    for at in range(4):
        query_ref[at * rows : (at + 1) * rows, :] = own_refs[at][:, head_cols(2)]
        grad_ref[at * rows : (at + 1) * rows, :] = grad_refs[at][...]
    ones = jnp.ones((8, HEAD), wide_type)
    pair_sum[...] = jnp.zeros_like(pair_sum)
    for tile in lane_tiles(4 * rows):
        query = query_ref[tile, :]
        grad = grad_ref[tile, :]
        centre = lax.dot_general(
            ones,
            grad.astype(wide_type) * out_ref[tile, :],
            (((1,), (1,)), ((), ())),
            precision=highest_precision,
            preferred_element_type=wide_type,
        )[0:1, :]
        total = total_ref[0:1, tile]
        query_part = jnp.zeros((HEAD, tile.stop - tile.start), wide_type)
        for at in range(4):
            block = slice(at * rows, (at + 1) * rows)
            if own:
                key, value = own_refs[at][:, head_cols(0)], own_refs[at][:, head_cols(1)]
                scores = dot_dims(key, query, 1, 1) + bias_ref[:, at : at + 1] + mask_ref[at : at + 1, tile]
            else:
                key, value = cross_refs[at][:, head_cols(0)], cross_refs[at][:, head_cols(1)]
                scores = dot_dims(key, query, 1, 1) + bias_ref[:, at + 4 : at + 5]
            weights = jnp.exp(scores - total)
            pair_sum[block, head_cols(1)] += dot_wide(weights.astype(low_type), grad)
            soft = dot_dims(value, grad, 1, 1)
            back = (weights * (soft - centre)).astype(low_type)
            pair_sum[block, head_cols(0)] += dot_wide(back, query)
            query_part = query_part + dot_dims(key, back, 0, 0)
        query_sum[tile, :] = query_part.T * HEAD ** (-0.5)


def turn_back_kernel(own_pair, other_pair, own_query, other_query, cos_ref, sin_ref, swap_ref, *out_refs):
    rows = out_refs[0].shape[0]
    swap = swap_ref[...]
    for at in range(4):
        block = slice(at * rows, (at + 1) * rows)
        cosine, sine = cos_ref[block, :], sin_ref[block, :]

        def turned(value):
            crossed = jnp.dot(value, swap, precision=highest_precision, preferred_element_type=wide_type)
            return (value * cosine - crossed * sine).astype(low_type)

        pair = own_pair[block, :] + other_pair[block, :]
        out_refs[at][:, head_cols(0)] = turned(pair[:, head_cols(0)])
        out_refs[at][:, head_cols(1)] = pair[:, head_cols(1)].astype(low_type)
        out_refs[at][:, head_cols(2)] = turned(own_query[block, :] + other_query[block, :])


def mix_back_kernel(at_ref, place_ref, key_w, value_w, query_w, *refs):
    mixed_refs = refs[:4]
    out_ref, stack_ref, bias_ref = refs[4:]
    ring, clip = at_ref[0], at_ref[1]
    place = place_ref[...]
    total = None
    bias_ref[...] = jnp.zeros_like(bias_ref)
    for part, weight in ((0, key_w), (1, value_w), (2, query_w)):
        relative = jnp.concatenate([ref[:, head_cols(part)] for ref in mixed_refs], axis=1)
        ordered = dot_wide(relative, place)
        bias_ref[part : part + 1, :] = jnp.sum(ordered, axis=0, keepdims=True)
        term = dot_dims(ordered.astype(low_type), weight[...], 1, 1)
        total = term if total is None else total + term
    out_ref[...] = total
    for at in range(4):
        stack_ref[lax.rem(ring + at - clip + 4, 4)] = mixed_refs[at][...]


def clip_products(at_ref, first_ref, second_ref, pack_refs, columns):
    out = None
    half = first_ref.shape[1]
    for step in range(4):
        place = ring_back(at_ref[0], step)
        pack = pack_refs[step]
        term = dot_dims(first_ref[place], pack[:half, columns], 0, 0)
        term = term + dot_dims(second_ref[place], pack[half : 2 * half, columns], 0, 0)
        out = term if out is None else out + term
    return out


def layer_grad_kernel(at_ref, act_a, act_b, norm_a, norm_b, *refs):
    head_refs, pack_refs, out_ref = refs[:-5], refs[-5:-1], refs[-1]
    part = out_ref.shape[1] // 2
    tiles = pl.num_programs(0) - (1 if head_refs else 0)

    @pl.when(pl.program_id(0) < tiles)
    def _():
        out_ref[:, :part] = clip_products(at_ref, act_a, act_b, pack_refs, slice(0, part))
        out_ref[:, part:] = clip_products(at_ref, norm_a, norm_b, pack_refs, slice(part, 2 * part))

    if head_refs:

        @pl.when(pl.program_id(0) == tiles)
        def _():
            columns = slice(2 * part, 3 * part)
            out_ref[:, :part] = clip_products(at_ref, head_refs[0], head_refs[2], pack_refs, columns)
            out_ref[:, part:] = clip_products(at_ref, head_refs[1], head_refs[3], pack_refs, columns)


def plain_grad_kernel(at_ref, rows_a, rows_b, *refs):
    pack_refs, out_ref = refs[:4], refs[4]
    out_ref[...] = clip_products(at_ref, rows_a, rows_b, pack_refs, slice(None))


def last_grad_kernel(tiles, at_ref, head_a, head_b, *refs):
    feat_refs, pack_refs, out_ref = refs[:4], refs[4:8], refs[8]
    head_rows = 2 * head_a.shape[1]

    @pl.when(pl.program_id(0) < tiles)
    def _():
        out = None
        for step in range(4):
            term = dot_dims(feat_refs[step][...], pack_refs[step][head_rows:, :], 0, 0)
            out = term if out is None else out + term
        out_ref[...] = out

    @pl.when(pl.program_id(0) >= tiles)
    def _():
        out_ref[...] = clip_products(at_ref, head_a, head_b, pack_refs, slice(None))


def ring_sum_kernel(at_ref, part_ref, *refs):
    got_refs, out_ref = refs[:3], refs[3]
    block = out_ref.shape[0]
    out = part_ref[pl.ds(pl.multiple_of(at_ref[0] * block, 8), block), :]
    for got in got_refs:
        out = out + got[...].astype(wide_type)
    out_ref[...] = out


def ring_sum(ring_at, part, got, after):
    shape = (part.shape[0] // 4, part.shape[1])
    return call_kernel(
        ring_sum_kernel,
        (ring_at[None], part, *got),
        (0,),
        jax.ShapeDtypeStruct(shape, wide_type),
        [],
        4 * shape[0] * shape[1],
        0,
        after,
    )


def half_sum_kernel(own_ref, got_ref, out_ref):
    out_ref[...] = (own_ref[...] + got_ref[...]).astype(low_type)


def half_sum(own, after):
    got = lax.ppermute(own, "frame", HALF_SWAP)
    return call_kernel(
        half_sum_kernel,
        (own, got),
        (),
        jax.ShapeDtypeStruct(own.shape, low_type),
        [],
        own.size,
        0,
        after,
    )


def join_kernel(at_ref, *refs):
    out_ref = refs[4]
    block = refs[0].shape[0]
    for step in range(4):
        start = pl.multiple_of(ring_back(at_ref[0], step) * block, 16)
        out_ref[pl.ds(start, block), :] = refs[step][...]


def join_frames(ring_at, total, after):
    pieces = ring_pieces(total)
    return call_kernel(
        join_kernel,
        (ring_at[None], *pieces),
        (0,),
        jax.ShapeDtypeStruct((4 * total.shape[0], total.shape[1]), low_type),
        [],
        0,
        0,
        after,
    )


def beside_kernel(first_ref, second_ref, out_ref):
    half, wide, other = first_ref.shape[0] // 2, first_ref.shape[1], second_ref.shape[1]
    out_ref[:, :wide] = first_ref[:half, :]
    out_ref[:, wide : wide + other] = second_ref[:half, :]
    out_ref[:, wide + other :] = second_ref[half:, :]


def gather_clips(first, second, after):
    half, wide = first.shape[0] // 2, first.shape[1]
    beside = call_kernel(
        beside_kernel,
        (first, second),
        (),
        jax.ShapeDtypeStruct((half, wide + 2 * second.shape[1]), low_type),
        [],
        0,
        0,
        after,
    )
    whole = lax.all_gather(beside, "clip")
    return whole, core_swap(whole[:, :, :wide])


def smem_spec():
    return pl.BlockSpec(memory_space=pltpu.SMEM)


def kernel_params():
    return pltpu.CompilerParams(vmem_limit_bytes=48 * 1024 * 1024)


def held_spec():
    return pl.BlockSpec(memory_space=pltpu.VMEM)


def any_specs(arrays):
    return [pl.BlockSpec(memory_space=pl.ANY)] * len(arrays)


def without(kernel, count, after):
    return lambda *refs: kernel(*refs[:count], *refs[count + len(after) :])


def layer_grad(clip_at, second_all, packs, first_all, after):
    whole, other = second_all
    half, wide = other.shape[1:]
    tiles = wide // 128
    part = 256
    block = (4, half, 128)
    heads = () if first_all is None else (first_all[0],) * 4
    held = [
        pl.BlockSpec(block, lambda i, at=at: (0, 0, tiles + at)) for at in range(len(heads))
    ]

    def moving(start):
        return pl.BlockSpec(block, lambda i: (0, 0, start + jnp.minimum(i, tiles - 1)))

    return pl.pallas_call(
        without(layer_grad_kernel, 9 + len(heads), after),
        grid=(tiles + (1 if heads else 0),),
        out_shape=jax.ShapeDtypeStruct((wide + (128 if heads else 0), 2 * part), wide_type),
        in_specs=[smem_spec(), moving(tiles), moving(2 * tiles), moving(0), moving(0)]
        + held
        + [held_spec()] * 4
        + any_specs(after),
        out_specs=pl.BlockSpec((128, 2 * part), lambda i: (i, 0)),
        compiler_params=kernel_params(),
        cost_estimate=pl.CostEstimate(
            flops=32 * half * wide * part,
            bytes_accessed=2 * whole.size + 8 * wide * part,
            transcendentals=0,
        ),
    )(clip_at[None], whole, whole, whole, other, *heads, *packs, *after)


def plain_grad(clip_at, rows_all, packs, after):
    whole, other = rows_all
    half, count = other.shape[1:]
    part = packs[0].shape[1]
    block = pl.BlockSpec((4, half, 128), lambda i: (0, 0, i))
    return pl.pallas_call(
        without(plain_grad_kernel, 7, after),
        grid=(count // 128,),
        out_shape=jax.ShapeDtypeStruct((count, part), wide_type),
        in_specs=[smem_spec(), block, block] + [held_spec()] * 4 + any_specs(after),
        out_specs=pl.BlockSpec((128, part), lambda i: (i, 0)),
        compiler_params=kernel_params(),
        cost_estimate=pl.CostEstimate(
            flops=16 * half * count * part,
            bytes_accessed=16 * half * count + 4 * count * part,
            transcendentals=0,
        ),
    )(clip_at[None], whole, other, *packs, *after)


def last_grad(clip_at, first_all, feats, packs, after):
    whole, other = first_all
    half, part = other.shape[1], packs[0].shape[1]
    first_block = other.shape[2] // 128
    tiles = feats[0].shape[1] // 128
    kernel = functools.partial(last_grad_kernel, tiles)

    def moving(start):
        return pl.BlockSpec(
            (4, half, 128), lambda i: (0, 0, start + jnp.maximum(i - tiles, 0))
        )

    return pl.pallas_call(
        without(kernel, 11, after),
        grid=(tiles + 2,),
        out_shape=jax.ShapeDtypeStruct(((tiles + 2) * 128, part), wide_type),
        in_specs=[smem_spec(), moving(first_block), moving(first_block + 2)]
        + [pl.BlockSpec((feats[0].shape[0], 128), lambda i: (0, jnp.minimum(i, tiles - 1)))] * 4
        + [held_spec()] * 4
        + any_specs(after),
        out_specs=pl.BlockSpec((128, part), lambda i: (i, 0)),
        compiler_params=kernel_params(),
    )(clip_at[None], whole, whole, *feats, *packs, *after)


def by_clip(clip_at, write):
    for place in range(4):

        @pl.when(clip_at == place)
        def _(place=place):
            for step in range(4):
                write((place - step) % 4, step)


def place_layer_kernel(tiles, at_ref, *refs):
    pieces = refs[:4]
    outs = refs[-3:] if pl.num_programs(0) > tiles else refs[-2:]
    part = pieces[0].shape[1] // 2
    is_last = pl.program_id(0) == tiles

    def write(place, step):
        columns = slice(place * part, (place + 1) * part)
        left = pieces[step][:, :part].astype(wide_type)
        right = pieces[step][:, part:].astype(wide_type)

        @pl.when(jnp.logical_not(is_last))
        def _():
            outs[0][0, :, columns] = left
            outs[1][0, :, columns] = right

        if len(outs) > 2:

            @pl.when(is_last)
            def _():
                outs[2][0, : outs[2].shape[1] // 2, columns] = left
                outs[2][0, outs[2].shape[1] // 2 :, columns] = right

    by_clip(at_ref[0], write)


def place_layer(clip_at, layer, levels, pieces, earlier, heads_layer, after):
    part = pieces[0].shape[1] // 2
    rows = 4 * part
    tiles = rows // 128
    heads = pieces[0].shape[0] > rows
    out = [(levels, rows, 4 * part)] * 2 + [(levels, 256, 4 * part)] * heads
    tall = pl.BlockSpec((1, 128, 4 * part), lambda i: (layer, jnp.minimum(i, tiles - 1), 0))
    wide = pl.BlockSpec((1, 256, 4 * part), lambda i: (heads_layer, 0, 0))
    return pl.pallas_call(
        without(functools.partial(place_layer_kernel, tiles), 5, (*earlier, *after)),
        grid=(tiles + (1 if heads else 0),),
        out_shape=tuple(jax.ShapeDtypeStruct(shape, wide_type) for shape in out),
        in_specs=[smem_spec()]
        + [pl.BlockSpec((128, 2 * part), lambda i: (i, 0))] * 4
        + any_specs(earlier)
        + any_specs(after),
        out_specs=(tall, tall) + ((wide,) if heads else ()),
        input_output_aliases={5 + at: at for at in range(len(earlier))},
        compiler_params=kernel_params(),
    )(clip_at[None], *pieces, *earlier, *after)


def place_last_kernel(skip, at_ref, *refs):
    pieces = refs[:4]
    in_ref, proj_ref = refs[-2:]
    part = pieces[0].shape[1]

    def write(place, step):
        columns = slice(place * part, (place + 1) * part)
        in_ref[:, columns] = pieces[step][: in_ref.shape[0], :].astype(wide_type)
        proj_ref[0, :, columns] = pieces[step][skip:, :].astype(wide_type)

    by_clip(at_ref[0], write)


def place_last(clip_at, feat_rows, skip, levels, pieces, earlier):
    part = pieces[0].shape[1]
    return pl.pallas_call(
        functools.partial(place_last_kernel, skip),
        grid=(1,),
        out_shape=(
            jax.ShapeDtypeStruct((feat_rows, 4 * part), wide_type),
            jax.ShapeDtypeStruct((levels, 256, 4 * part), wide_type),
        ),
        in_specs=[smem_spec()]
        + [pl.BlockSpec(pieces[0].shape, lambda i: (0, 0))] * 4
        + [pl.BlockSpec(memory_space=pl.ANY)],
        out_specs=(
            pl.BlockSpec((feat_rows, 4 * part), lambda i: (0, 0)),
            pl.BlockSpec((1, 256, 4 * part), lambda i: (0, 0, 0)),
        ),
        input_output_aliases={5: 1},
        compiler_params=kernel_params(),
    )(clip_at[None], *pieces, earlier)


def pack_kernel(by_rows, count, at_ref, *refs):
    parts, outs = refs[:count], refs[count:]
    for clip in range(4):

        @pl.when(at_ref[0] == clip)
        def _(clip=clip):
            for step in range(4):
                place, start = (clip + step) % 4, 0
                for part in parts:
                    size = part.shape[1] // 4
                    value = part[:, place * size : (place + 1) * size]
                    if by_rows:
                        outs[step][start : start + part.shape[0], :] = value
                        start += part.shape[0]
                    else:
                        outs[step][:, start : start + size] = value
                        start += size


def pack_parts(clip_at, parts, by_rows, after):
    sizes = [part.shape[1] // 4 for part in parts]
    if by_rows:
        shape = (sum(part.shape[0] for part in parts), sizes[0])
    else:
        shape = (parts[0].shape[0], sum(sizes))
    return call_kernel(
        functools.partial(pack_kernel, by_rows, len(parts)),
        (clip_at[None], *parts),
        (0,),
        tuple(jax.ShapeDtypeStruct(shape, low_type) for _ in range(4)),
        [],
        0,
        0,
        after,
    )


def place_heads_kernel(at_ref, *refs):
    pieces, out_ref = refs[:4], refs[-1]

    def write(place, step):
        piece = pieces[step][...].astype(wide_type)
        for at, part in ((1, 0), (2, 1), (0, 2)):
            out_ref[0, at, :, head_cols(place)] = piece[:, head_cols(part)]

    by_clip(at_ref[0], write)


def place_heads(clip_at, layer, levels, pieces, earlier, after):
    rows = pieces[0].shape[0]
    tile = 256
    count = 5
    return pl.pallas_call(
        without(place_heads_kernel, count, (*earlier, *after)),
        grid=(rows // tile,),
        out_shape=jax.ShapeDtypeStruct((levels, 3, rows, 4 * HEAD), wide_type),
        in_specs=[smem_spec()]
        + [pl.BlockSpec((tile, 3 * HEAD), lambda i: (i, 0))] * 4
        + any_specs(earlier)
        + any_specs(after),
        out_specs=pl.BlockSpec((1, 3, tile, 4 * HEAD), lambda i: (layer, 0, i, 0)),
        input_output_aliases={count + at: at for at in range(len(earlier))},
        compiler_params=kernel_params(),
    )(clip_at[None], *pieces, *earlier, *after)


def stack_kernel(*refs):
    out_ref = refs[-1]
    for at, ref in enumerate(refs[:-1]):
        out_ref[8 * at : 8 * (at + 1), :] = ref[...]


def call_kernel(kernel, args, in_smem, outs, scratch, flops, exps, after=()):
    count = len(args)
    specs = [
        pl.BlockSpec(memory_space=pltpu.SMEM if at in in_smem else pltpu.VMEM)
        for at in range(count)
    ]
    specs += [pl.BlockSpec(memory_space=pl.ANY)] * len(after)
    moved = sum(a.size * a.dtype.itemsize for a in args)
    return pl.pallas_call(
        without(kernel, count, after),
        out_shape=outs,
        in_specs=specs,
        out_specs=jax.tree.map(lambda _: pl.BlockSpec(memory_space=pltpu.VMEM), outs),
        scratch_shapes=scratch,
        compiler_params=kernel_params(),
        cost_estimate=pl.CostEstimate(flops=flops, bytes_accessed=moved, transcendentals=exps),
    )(*args, *after)


def on_device(
    features,
    cond_values,
    cond_live,
    in_weight,
    in_bias,
    act_weight,
    act_bias,
    state_weight,
    state_bias,
    attn_gain,
    attn_shift,
    qkv_weight,
    qkv_bias,
    proj_weight,
    proj_bias,
    mlp_gain,
    mlp_shift,
    up_weight,
    up_bias,
    down_weight,
    down_bias,
    out_grad,
):
    patch_rows = features.shape[2]
    feat_width = features.shape[3]
    slot_count = cond_values.shape[2]
    all_frames = cond_live.shape[1]
    model_width = in_weight.shape[1]
    width = qkv_weight.shape[3]
    heads = width // HEAD
    level_count = attn_gain.shape[0]
    patches = patch_rows // 4
    chunk_rows = patches + EXTRA
    rows = 4 * chunk_rows
    hidden_width = up_weight.shape[2]

    tensor_at = lax.axis_index("tensor")
    chip_at, core_at = tensor_at // 2, tensor_at % 2
    frame_at = lax.axis_index("frame")
    half_at, ring_at = frame_at // 4, frame_at % 4
    clip_at = lax.axis_index("clip")

    chunk_ids = [
        2 * jnp.bitwise_xor(core_at, core_step) + jnp.bitwise_xor(chip_at, chip_step)
        for core_step in range(2)
        for chip_step in range(2)
    ]
    own_chunk = chunk_ids[0]
    own_frames = jnp.stack([4 * half_at + (ring_at - step) % 4 for step in range(4)])
    cross_frames = jnp.stack([4 * (1 - half_at) + (ring_at - step) % 4 for step in range(4)])

    within = lax.broadcasted_iota(jnp.int32, (chunk_rows, 1), 0)
    is_patch = within < patches
    heights, columns = [], []
    for chunk_id in chunk_ids:
        patch_id = chunk_id * patches + within
        heights.append(jnp.where(is_patch, patch_id // GRID_W, 0))
        columns.append(jnp.where(is_patch, patch_id % GRID_W, 0))
    heights = jnp.concatenate(heights, axis=0).astype(wide_type)
    columns = jnp.concatenate(columns, axis=0).astype(wide_type)
    swap_table, rate_table = rotary_tables(HEAD, heads)
    swap_heads = jnp.asarray(swap_table)
    swap_one = jnp.asarray(swap_table[:HEAD, :HEAD])
    rates = rate_table[:, :HEAD]
    place_angles = heights * rates[1] + columns * rates[2]
    angles = jnp.concatenate(
        [
            own_frames[step].astype(wide_type) * rates[0][None, :] + place_angles
            for step in range(4)
        ],
        axis=0,
    )
    cosine_four, sine_four = jnp.cos(angles), jnp.sin(angles)
    cosine_rows = jnp.tile(cosine_four[:rows], (1, heads))
    sine_rows = jnp.tile(sine_four[:rows], (1, heads))
    head_from = jnp.arange(width)
    head_to = ((head_from // HEAD + ring_at) % 4) * HEAD + head_from % HEAD
    head_place = (head_to[:, None] == head_from[None, :]).astype(low_type)
    proj_turned = [
        lax.dynamic_slice_in_dim(
            jnp.concatenate([proj_weight[layer], proj_weight[layer]], axis=0),
            ring_at * HEAD,
            width,
            0,
        )
        for layer in range(level_count)
    ]
    ring_scalar = ring_at.astype(jnp.int32)
    clip_scalar = clip_at.astype(jnp.int32)

    live_all = cond_live[0].astype(wide_type)
    own_slots = lax.dynamic_index_in_dim(live_all, frame_at, 0, False)

    def live_rows(slots, chunk_id):
        picked = jnp.where(
            chunk_id < slot_count,
            lax.dynamic_index_in_dim(slots, jnp.minimum(chunk_id, slot_count - 1), 1, False),
            0.0,
        )
        return jnp.where(is_patch, 1.0, jnp.where(within == patches, picked[None, :], 0.0))

    sources = jnp.concatenate([own_frames, cross_frames])
    source_live = jnp.take(live_all, sources, axis=0)
    key_live = jnp.concatenate([live_rows(source_live, c) for c in chunk_ids], axis=0)
    reached = jnp.concatenate([jnp.ones((4,), jnp.bool_), jnp.full((4,), half_at == 1)])
    key_bias = jnp.where((key_live > 0.5) & reached[None, :], 0.0, masked_score).astype(wide_type)
    seen = own_frames[:, None] <= own_frames[None, :]
    causal = jnp.where(seen, 0.0, masked_score).astype(wide_type)
    causal = jnp.pad(jnp.repeat(causal, rows, axis=1), ((0, 4), (0, 0)))
    own_live = live_rows(own_slots[None, :], own_chunk)

    def extra_rows(slot_rows):
        picked = lax.dynamic_slice_in_dim(
            slot_rows, jnp.minimum(own_chunk, slot_count - 1), 1, 0
        )
        picked = jnp.where(own_chunk < slot_count, picked, jnp.zeros_like(picked))
        return jnp.pad(picked, ((0, EXTRA - 1), (0, 0)))

    cond_here = cond_values[0, 0]
    act_rows = jnp.dot(cond_here, act_weight, precision=highest_precision) + act_bias
    state_rows = jnp.dot(cond_here, state_weight, precision=highest_precision) + state_bias
    even_slot = (jnp.arange(slot_count) % 2 == 0)[:, None]
    cond_x = jnp.where(even_slot, act_rows, state_rows) * own_slots[:, None]

    flat_feat = jnp.concatenate(
        [
            lax.dynamic_slice_in_dim(features[0, 0], c * patches, patches, 0)
            for c in chunk_ids
        ],
        axis=0,
    )
    kept, got = halves_tensor(dot_wide(flat_feat, in_weight))
    stream = jnp.concatenate([kept + got + in_bias, extra_rows(cond_x)], axis=0)

    feat_wide = -(-feat_width // 128) * 128
    feat_low = jnp.pad(flat_feat, ((0, 0), (0, feat_wide - feat_width)))
    feats = [feat_low] + [
        lax.ppermute(feat_low, "clip", clip_shift(step)) for step in range(1, 4)
    ]
    pair_work = 2 * 32 * rows * rows * HEAD
    pair_exps = 32 * rows * rows
    weight_parts = [
        [qkv_weight[layer, :, at] for at in (1, 2, 0)] for layer in range(level_count)
    ]

    def norm(terms, gain, shift, after=()):
        chunk = jax.ShapeDtypeStruct((chunk_rows, model_width), wide_type)
        return call_kernel(
            norm_kernel,
            (gain[None], shift[None], *terms),
            (),
            (
                chunk,
                chunk,
                jax.ShapeDtypeStruct((chunk_rows, 128), wide_type),
                jax.ShapeDtypeStruct((chunk_rows, model_width), low_type),
            ),
            [],
            12 * chunk_rows * model_width,
            0,
            after,
        )

    def norm_back(part, gain, hat, inverse, grad, count, after=()):
        kept, got = halves_tensor(part)
        return call_kernel(
            functools.partial(norm_back_kernel, count),
            (kept, got, gain[None], hat, inverse, grad),
            (),
            (
                jax.ShapeDtypeStruct((chunk_rows, model_width), wide_type),
                jax.ShapeDtypeStruct((chunk_rows, model_width), low_type),
                jax.ShapeDtypeStruct((8, model_width), wide_type),
            ),
            [],
            16 * chunk_rows * model_width,
            0,
            after,
        )

    stored = []
    terms = (stream,)
    before = None
    for layer in range(level_count):
        stream, hat_one, inverse_one, first_chunk = norm(terms, attn_gain[layer], attn_shift[layer])
        first_in = join_rows_tensor(first_chunk)
        bias = jnp.pad(qkv_bias[layer], ((0, 5), (0, 0)))
        heads_out = call_kernel(
            functools.partial(project_kernel, heads),
            (
                ring_scalar[None],
                first_in,
                *weight_parts[layer],
                bias,
                cosine_rows,
                sine_rows,
                swap_heads,
            ),
            (0,),
            tuple(
                jax.ShapeDtypeStruct((rows, count * HEAD), low_type)
                for count in (3, 3, 3, 3, 2, 2, 2, 2)
            ),
            [],
            6 * rows * model_width * width,
            0,
            () if before is None else (before[0][0],),
        )
        blocks = to_heads(heads_out[:4])
        cross = pairs_to_later_half(heads_out[4:])
        attn_wide, attn_turned, log_total = call_kernel(
            attend_kernel,
            (key_bias, causal, *blocks, *cross),
            (),
            (
                jax.ShapeDtypeStruct((4 * rows, HEAD), wide_type),
                jax.ShapeDtypeStruct((4 * rows, HEAD), low_type),
                jax.ShapeDtypeStruct((8, 4 * rows), wide_type),
            ),
            [
                pltpu.VMEM((4 * rows, HEAD), low_type),
                pltpu.VMEM((8 * rows, lane_tiles(4 * rows)[0].stop), wide_type),
            ],
            2 * pair_work,
            pair_exps,
        )
        attn_relative = jnp.concatenate(
            to_frames([attn_turned[at * rows : (at + 1) * rows] for at in range(4)]), axis=1
        )
        attn_low = dot_wide(attn_relative, head_place).astype(low_type)
        if layer < level_count - 1:
            first_all = gather_clips(first_in, attn_low, ())
        kept, got = halves_tensor(dot_wide(attn_relative, proj_turned[layer]))
        middle, hat_two, inverse_two, second_chunk = norm(
            (stream, kept, got, proj_bias[layer][None]), mlp_gain[layer], mlp_shift[layer],
            () if before is None else (before[1][0],),
        )
        second_in = join_rows_tensor(second_chunk)
        hidden = dot_wide(second_in, up_weight[layer]) + up_bias[layer]
        active_low = exact_gelu(hidden).astype(low_type)
        second_all = gather_clips(second_in, active_low, ())
        if layer == level_count - 1:
            first_all = gather_clips(first_in, attn_low, (second_all[0],))
        before = (first_all, second_all)
        kept, got = halves_tensor(dot_wide(active_low, down_weight[layer]))
        terms = (middle, kept, got, down_bias[layer][None])
        stored.append(
            (
                hat_one,
                inverse_one,
                blocks,
                cross,
                log_total,
                attn_wide,
                hat_two,
                inverse_two,
                hidden,
                first_all,
                second_all,
            )
        )
    stream = terms[0] + (terms[1] + terms[2] + terms[3])

    def in_order(full, count):
        out = jnp.zeros((4 * count,) + full.shape[1:], full.dtype)
        size = full.shape[0] // 4
        for at, chunk_id in enumerate(chunk_ids):
            out = lax.dynamic_update_slice_in_dim(
                out, full[at * size : at * size + count], chunk_id * count, 0
            )
        return out

    block_full = join_rows_tensor((stream * own_live).astype(low_type))
    slot_full = jnp.concatenate(
        [
            block_full[at * chunk_rows + patches : at * chunk_rows + patches + 1]
            for at in range(4)
        ],
        axis=0,
    )
    block_out = jnp.concatenate(
        [in_order(block_full, patches), in_order(slot_full, 1)[:slot_count]], axis=0
    )[None, None]

    own_out = lax.dynamic_slice_in_dim(out_grad[0, 0], own_chunk * patches, patches, 0)
    grad_stream = (
        jnp.concatenate(
            [
                own_out.astype(wide_type),
                extra_rows(out_grad[0, 0, patch_rows:].astype(wide_type)),
            ],
            axis=0,
        )
        * own_live
    )

    small = {}
    branch_chunk = grad_stream.astype(low_type)
    small["down", level_count - 1] = jnp.sum(branch_chunk.astype(wide_type), axis=0)
    sums_list = []
    later = None
    for layer in reversed(range(level_count)):
        (
            hat_one,
            inverse_one,
            blocks,
            cross,
            log_total,
            attn_wide,
            hat_two,
            inverse_two,
            hidden,
            first_all,
            second_all,
        ) = stored[layer]
        branch = join_rows_tensor(branch_chunk)
        _, gelu_pull = jax.vjp(exact_gelu, hidden)
        grad_hidden = gelu_pull(dot_dims(branch, down_weight[layer], 1, 1))[0].astype(low_type)
        small["up", layer] = jnp.sum(grad_hidden.astype(wide_type), axis=0)
        grad_middle, proj_chunk, sums = norm_back(
            dot_dims(grad_hidden, up_weight[layer], 1, 1),
            mlp_gain[layer],
            hat_two,
            inverse_two,
            grad_stream,
            chunk_rows,
            () if later is None else (later["tall_join"], later["heads_sum"]),
        )
        sums_list.append(sums)
        proj_out = join_rows_tensor(proj_chunk)
        grad_attn = dot_dims(proj_out, proj_turned[layer], 1, 1).astype(low_type)
        grads = to_heads([grad_attn[:, head_cols(at)] for at in range(4)])

        parts = [branch, grad_hidden] + ([] if later is None else [later["proj_out"]])
        packs = swap_clips(pack_parts(clip_scalar, parts, False, ()))
        if later is not None:
            later["heads_ring"] = ring_sum(
                ring_scalar, later["heads_sum"], later["heads_got"], (proj_chunk,)
            )

        def attend_back(own, after):
            return call_kernel(
                functools.partial(attend_back_kernel, own),
                (key_bias, causal, log_total, attn_wide, *blocks, *grads)
                + (() if own else tuple(cross)),
                (),
                (
                    jax.ShapeDtypeStruct((4 * rows, 2 * HEAD), wide_type),
                    jax.ShapeDtypeStruct((4 * rows, HEAD), wide_type),
                ),
                [
                    pltpu.VMEM((4 * rows, HEAD), low_type),
                    pltpu.VMEM((4 * rows, HEAD), low_type),
                ],
                5 * pair_work // 2,
                pair_exps // 2,
                after,
            )

        cross_pair, cross_query = attend_back(
            False, () if later is None else (later["heads_ring"],)
        )
        got_pair = lax.ppermute(cross_pair, "frame", DOWN_HALF)
        tall_sum = layer_grad(
            clip_scalar,
            second_all,
            packs,
            None if later is None else later["first_all"],
            (cross_pair,),
        )
        own_pair, own_query = attend_back(True, (tall_sum,))
        tall_got = ring_sends(tall_sum, ring_at)
        if later is not None:
            later["heads_total"] = half_sum(later["heads_ring"], (own_pair,))
        turned = call_kernel(
            turn_back_kernel,
            (own_pair, got_pair, own_query, cross_query, cosine_four, sine_four, swap_one),
            (),
            tuple(jax.ShapeDtypeStruct((rows, 3 * HEAD), low_type) for _ in range(4)),
            [],
            24 * rows * HEAD * HEAD,
            0,
            () if later is None else (later["heads_total"],),
        )
        mixed = to_frames(list(turned))
        tall_ring = ring_sum(ring_scalar, tall_sum, tall_got, (turned[0],))
        if later is not None:
            later["heads_join"] = join_frames(ring_scalar, later["heads_total"], (turned[0],))
            placed = place_layer(
                clip_scalar, layer + 1, level_count, clip_pieces(later["tall_join"]), (), 0, (turned[0],)
            )
        normed_part, mixed_stack, bias_sums = call_kernel(
            mix_back_kernel,
            (
                jnp.stack([ring_scalar, clip_scalar]),
                head_place,
                *weight_parts[layer],
                *mixed,
            ),
            (0,),
            (
                jax.ShapeDtypeStruct((rows, model_width), wide_type),
                jax.ShapeDtypeStruct((4, rows, 3 * HEAD), low_type),
                jax.ShapeDtypeStruct((8, width), wide_type),
            ),
            [],
            6 * rows * model_width * width,
            0,
            (tall_ring,) if later is None else (tall_ring, later["heads_join"], placed[0]),
        )
        small["qkv", layer] = jnp.concatenate([bias_sums[2:3], bias_sums[:2]], axis=0)
        tall_total = half_sum(tall_ring, (normed_part,))
        grad_stream, branch_chunk, sums = norm_back(
            normed_part,
            attn_gain[layer],
            hat_one,
            inverse_one,
            grad_middle,
            patches if layer == 0 else chunk_rows,
            (tall_total,),
        )
        sums_list.append(sums)

        packs = swap_clips([mixed_stack[step] for step in range(4)])
        heads_sum = plain_grad(clip_scalar, first_all, packs, (branch_chunk,))
        heads_got = ring_sends(heads_sum, ring_at)
        tall_join = join_frames(ring_scalar, tall_total, (branch_chunk,))
        if layer > 0:
            later = {
                "proj_out": proj_out,
                "first_all": first_all,
                "tall_join": tall_join,
                "heads_sum": heads_sum,
                "heads_got": heads_got,
            }

    patch_chunk = branch_chunk[:patches]
    grad_patch = join_rows_tensor(patch_chunk)
    grad_features = in_order(dot_dims(grad_patch, in_weight, 1, 1), patches)[None, None]
    packs = swap_clips(pack_parts(clip_scalar, [proj_out, grad_patch], True, ()))
    heads_ring = ring_sum(ring_scalar, heads_sum, heads_got, (packs[0],))
    last_sum = last_grad(clip_scalar, first_all, feats, packs, (tall_join, heads_ring))
    last_ring = ring_sum(ring_scalar, last_sum, ring_sends(last_sum, ring_at), ())
    heads_total = half_sum(heads_ring, (last_sum,))
    heads_join = join_frames(ring_scalar, heads_total, ())
    tall_pieces = clip_pieces(tall_join)
    last_join = join_frames(ring_scalar, half_sum(last_ring, ()), ())
    last_pieces = clip_pieces(last_join)
    grad_down, grad_up, grad_proj = place_layer(
        clip_scalar, 0, level_count, tall_pieces, placed, level_count - 1, ()
    )
    grad_in, grad_proj = place_last(
        clip_scalar, feat_width, feat_wide, level_count, last_pieces, grad_proj
    )
    grad_heads = place_heads(
        clip_scalar,
        level_count - 1,
        level_count,
        clip_pieces(later["heads_join"]),
        (),
        (last_sum,),
    )
    grad_heads = (
        place_heads(clip_scalar, 0, level_count, clip_pieces(heads_join), (grad_heads,), ()),
    )

    slot_row = grad_stream[patches : patches + 1] * own_live[patches : patches + 1]
    own_cond = lax.dynamic_slice_in_dim(
        cond_here, jnp.minimum(own_chunk, slot_count - 1), 1, 0
    )
    slot_part = jnp.concatenate([own_cond.T * slot_row, slot_row], axis=0)
    here = own_chunk < slot_count
    is_act = here & (own_chunk % 2 == 0)
    is_state = here & (own_chunk % 2 == 1)
    act_part = jnp.where(is_act, slot_part, 0.0)
    state_part = jnp.where(is_state, slot_part, 0.0)

    def at_tensor(value, total):
        return lax.dynamic_update_slice(
            jnp.zeros((value.shape[0], total), wide_type),
            value,
            (0, tensor_at * value.shape[1]),
        )

    layers = range(level_count)
    qkv_rows = at_tensor(
        jnp.concatenate([small["qkv", layer] for layer in layers], axis=0), 4 * width
    )
    mixed_rows = jnp.concatenate(
        [qkv_rows, small["down", level_count - 1][None], jnp.zeros_like(qkv_rows[:1])], axis=0
    )
    ups = at_tensor(jnp.stack([small["up", layer] for layer in layers]), 4 * hidden_width)
    parts = [*sums_list, act_part, state_part, mixed_rows, ups.reshape(-1, model_width)]
    vector = call_kernel(
        stack_kernel,
        tuple(parts),
        (),
        jax.ShapeDtypeStruct((8 * len(parts), model_width), wide_type),
        [],
        0,
        0,
    )
    vector = sum_everywhere(vector)

    def norm_sums(layer, first, row):
        return vector[8 * (2 * (level_count - 1 - layer) + first) + row]

    grad_mlp_gain = jnp.stack([norm_sums(layer, 0, 0) for layer in layers])
    grad_mlp_shift = jnp.stack([norm_sums(layer, 0, 1) for layer in layers])
    grad_proj_bias = jnp.stack([norm_sums(layer, 0, 2) for layer in layers])
    grad_attn_gain = jnp.stack([norm_sums(layer, 1, 0) for layer in layers])
    grad_attn_shift = jnp.stack([norm_sums(layer, 1, 1) for layer in layers])
    rest = vector[16 * level_count :]
    grad_down_bias = jnp.stack(
        [norm_sums(layer + 1, 1, 2) for layer in range(level_count - 1)]
        + [rest[16 + 3 * level_count]]
    )
    grad_qkv_bias = lax.dynamic_slice_in_dim(
        rest[16 : 16 + 3 * level_count], tensor_at * width, width, 1
    )
    grad_qkv_bias = grad_qkv_bias.reshape(level_count, 3, width)
    grad_up_bias = lax.dynamic_slice_in_dim(
        rest[24:].reshape(level_count, 4 * hidden_width), tensor_at * hidden_width, hidden_width, 1
    )
    act_count = cond_here.shape[1]
    return (
        block_out,
        grad_features,
        grad_in,
        norm_sums(0, 1, 2),
        rest[:act_count],
        rest[act_count],
        rest[8 : 8 + act_count],
        rest[8 + act_count],
        grad_attn_gain,
        grad_attn_shift,
        jnp.swapaxes(grad_heads[0], 1, 2),
        grad_qkv_bias,
        grad_proj,
        grad_proj_bias,
        grad_mlp_gain,
        grad_mlp_shift,
        grad_up,
        grad_up_bias,
        grad_down,
        grad_down_bias,
    )


def solution(mesh):
    return jax.shard_map(
        on_device,
        mesh=mesh,
        in_specs=(
            P("clip", "frame", None, "tensor"),
            P("clip", "frame", None, None),
            P("clip", None, None),
            P("tensor", None),
            P(),
            P(),
            P(),
            P(),
            P(),
            P(),
            P(),
            P(None, None, None, "tensor"),
            P(None, None, "tensor"),
            P(None, "tensor", None),
            P(),
            P(),
            P(),
            P(None, None, "tensor"),
            P(None, "tensor"),
            P(None, "tensor", None),
            P(),
            P("clip", "frame", None, None),
        ),
        out_specs=(
            P("clip", "frame", None, None),
            P("clip", "frame", None, "tensor"),
            P("tensor", None),
            P(),
            P(),
            P(),
            P(),
            P(),
            P(),
            P(),
            P(None, None, None, "tensor"),
            P(None, None, "tensor"),
            P(None, "tensor", None),
            P(),
            P(),
            P(),
            P(None, None, "tensor"),
            P(None, "tensor"),
            P(None, "tensor", None),
            P(),
        ),
        check_vma=False,
    )
```

```python
import functools

import jax
import jax.numpy as jnp
import numpy as np
from jax import lax
from jax.experimental import pallas as pl
from jax.experimental.pallas import tpu as pltpu
from jax.sharding import PartitionSpec as P

HEAD = 64
GRID_W = 16
EXTRA = 8

highest_precision = lax.Precision.HIGHEST
norm_epsilon = 1e-06
masked_score = -1000000000.0
low_type = jnp.bfloat16
wide_type = jnp.float32

CORE_SWAP = [(0, 1), (1, 0), (2, 3), (3, 2)]
CHIP_SWAP = [(0, 2), (2, 0), (1, 3), (3, 1)]
HALF_SWAP = [(i, (i + 4) % 8) for i in range(8)]


def clip_shift(step):
    return [(i, (i + step) % 4) for i in range(4)]


def frame_shift(halves, step):
    return [
        (4 * half + i, 4 * ((half + halves) % 2) + (i + step) % 4)
        for half in range(2)
        for i in range(4)
    ]


def core_swap(value):
    return lax.ppermute(value, "tensor", CORE_SWAP)


def chip_swap(value):
    return lax.ppermute(value, "tensor", CHIP_SWAP)


def halves_tensor(part):
    half = part.shape[0] // 2
    pair = part[:half] + core_swap(part[half:])
    quarter = half // 2
    return pair[:quarter], chip_swap(pair[quarter:])


def join_rows_tensor(chunk):
    pair = jnp.concatenate([chunk, chip_swap(chunk)], axis=0)
    return jnp.concatenate([pair, core_swap(pair)], axis=0)


def to_heads(blocks):
    return [blocks[0]] + [
        lax.ppermute(blocks[step], "frame", frame_shift(0, step)) for step in range(1, 4)
    ]


def to_frames(blocks):
    return [blocks[0]] + [
        lax.ppermute(blocks[step], "frame", frame_shift(0, -step)) for step in range(1, 4)
    ]


def pairs_to_later_half(blocks):
    return [
        lax.ppermute(
            blocks[step],
            "frame",
            [(src, dst) for src, dst in frame_shift(1, step) if src < dst],
        )
        for step in range(4)
    ]


DOWN_HALF = [(i + 4, i) for i in range(4)]


def swap_clips(packs):
    return [packs[0]] + [
        lax.ppermute(packs[step], "clip", clip_shift(step)) for step in range(1, 4)
    ]


def ring_pieces(value):
    return [value] + [
        lax.ppermute(value, "frame", frame_shift(0, step)) for step in range(1, 4)
    ]


def ring_sends(part, ring):
    block = part.shape[0] // 4
    got = []
    for step in range(1, 4):
        sent = lax.dynamic_slice_in_dim(part, ((ring + step) % 4) * block, block, 0)
        got.append(lax.ppermute(sent.astype(low_type), "frame", frame_shift(0, step)))
    return got


def clip_pieces(joined):
    return [joined] + [
        lax.ppermute(joined, "clip", clip_shift(step)) for step in range(1, 4)
    ]


def rotary_tables(head_size, head_count):
    group_size = 2 * (head_size // 3 // 2)
    half_size = group_size // 2
    total_width = head_size * head_count
    swap_table = np.zeros((total_width, total_width), np.float32)
    rate_table = np.zeros((3, total_width), np.float32)
    for head_at in range(head_count):
        for axis_at in range(3):
            for pair_at in range(half_size):
                lower_at = head_at * head_size + axis_at * group_size + pair_at
                upper_at = lower_at + half_size
                swap_table[upper_at, lower_at] = -1.0
                swap_table[lower_at, upper_at] = 1.0
                rate_value = 10000.0 ** (-2.0 * pair_at / group_size)
                rate_table[axis_at, lower_at] = rate_value
                rate_table[axis_at, upper_at] = rate_value
    return swap_table, rate_table


def norm_rows(values):
    row_mean = jnp.mean(values, axis=-1, keepdims=True)
    centred = values - row_mean
    spread = jnp.mean(centred * centred, axis=-1, keepdims=True)
    inverse = lax.rsqrt(spread + norm_epsilon)
    return centred * inverse, inverse


def norm_kernel(gain_ref, shift_ref, *refs):
    terms, (stream_ref, hat_ref, inverse_ref, low_ref) = refs[:-4], refs[-4:]
    values = terms[0][...]
    if len(terms) > 1:
        values = values + (terms[1][...] + terms[2][...] + terms[3][...])
    hat, inverse = norm_rows(values)
    stream_ref[...] = values
    hat_ref[...] = hat
    inverse_ref[...] = jnp.broadcast_to(inverse, inverse_ref.shape)
    low_ref[...] = (hat * gain_ref[...] + shift_ref[...]).astype(low_type)


def norm_back_kernel(count, kept_ref, got_ref, gain_ref, hat_ref, inverse_ref, grad_ref, out_ref, low_ref, sums_ref):
    grad = kept_ref[...] + got_ref[...]
    hat = hat_ref[...]
    scaled = grad * gain_ref[...]
    first = jnp.mean(scaled, axis=-1, keepdims=True)
    second = jnp.mean(scaled * hat, axis=-1, keepdims=True)
    out = grad_ref[...] + (scaled - first - hat * second) * inverse_ref[:, 0:1]
    low = out.astype(low_type)
    out_ref[...] = out
    low_ref[...] = low
    sums_ref[...] = jnp.zeros_like(sums_ref)
    sums_ref[0:1, :] = jnp.sum(grad * hat, axis=0, keepdims=True)
    sums_ref[1:2, :] = jnp.sum(grad, axis=0, keepdims=True)
    sums_ref[2:3, :] = jnp.sum(low[:count].astype(wide_type), axis=0, keepdims=True)


def exact_gelu(values):
    return jax.nn.gelu(values, approximate=False)


def dot_wide(left, right):
    return jnp.dot(left, right, preferred_element_type=wide_type)


def dot_dims(left, right, left_dim, right_dim):
    return lax.dot_general(
        left, right, (((left_dim,), (right_dim,)), ((), ())), preferred_element_type=wide_type
    )


def head_cols(at):
    return slice(at * HEAD, (at + 1) * HEAD)


def ring_back(place, step):
    return lax.rem(place - step + 4, 4)


def ring_ahead(place, step):
    return lax.rem(place + step, 4)


def project_kernel(heads, at_ref, rows_ref, key_w, value_w, query_w, bias_ref, cos_ref, sin_ref, swap_ref, *out_refs):
    rows = rows_ref[...]
    swap = swap_ref[...]
    cosine, sine = cos_ref[...], sin_ref[...]

    def turned(weight, bias):
        value = dot_wide(rows, weight[...]) + bias
        crossed = jnp.dot(value, swap, precision=highest_precision, preferred_element_type=wide_type)
        return value * cosine + crossed * sine

    key = turned(key_w, bias_ref[1:2, :]).astype(low_type)
    value = (dot_wide(rows, value_w[...]) + bias_ref[2:3, :]).astype(low_type)
    query = (turned(query_w, bias_ref[0:1, :]).astype(low_type).astype(wide_type) * HEAD ** (-0.5)).astype(low_type)

    def write(head, step):
        for at, part in enumerate((key, value, query)):
            out_refs[step][:, head_cols(at)] = part[:, head_cols(head)]
            if at < 2:
                out_refs[4 + step][:, head_cols(at)] = part[:, head_cols(head)]

    for ring in range(4):

        @pl.when(at_ref[0] == ring)
        def _(ring=ring):
            for step in range(4):
                write((ring + step) % 4, step)


def lane_tiles(total):
    size = 384 if total % 384 == 0 else total
    return [slice(at * size, (at + 1) * size) for at in range(total // size)]


def attend_kernel(bias_ref, mask_ref, *refs):
    own_refs, cross_refs = refs[:4], refs[4:8]
    out_ref, low_ref, total_ref, query_ref, score_ref = refs[8:]
    rows = own_refs[0].shape[0]
    total_rows = 4 * rows
    for at in range(4):
        query_ref[at * rows : (at + 1) * rows, :] = own_refs[at][:, head_cols(2)]
    total_ref[...] = jnp.zeros_like(total_ref)

    def pair(at, part):
        if at < 4:
            return own_refs[at][:, head_cols(part)]
        return cross_refs[at - 4][:, head_cols(part)]

    for tile in lane_tiles(total_rows):
        query = query_ref[tile, :]
        wide = tile.stop - tile.start
        top = jnp.full((1, wide), 2.0 * masked_score, wide_type)
        for at in range(8):
            scores = dot_dims(pair(at, 0), query, 1, 1) + bias_ref[:, at : at + 1]
            if at < 4:
                scores = scores + mask_ref[at : at + 1, tile]
            score_ref[at * rows : (at + 1) * rows, :] = scores
            top = jnp.maximum(top, jnp.max(scores, axis=0, keepdims=True))
        mass = jnp.zeros((1, wide), wide_type)
        out = jnp.zeros((HEAD, wide), wide_type)
        for at in range(8):
            weights = jnp.exp(score_ref[at * rows : (at + 1) * rows, :] - top)
            mass = mass + jnp.sum(weights, axis=0, keepdims=True)
            out = out + dot_dims(pair(at, 1), weights.astype(low_type), 0, 0)
        total_ref[0:1, tile] = top + jnp.log(mass)
        rows_out = (out / mass).T
        out_ref[tile, :] = rows_out
        low_ref[tile, :] = rows_out.astype(low_type)


def attend_back_kernel(own, bias_ref, mask_ref, total_ref, out_ref, *refs):
    own_refs, grad_refs = refs[:4], refs[4:8]
    cross_refs = refs[8:-4]
    pair_sum, query_sum, query_ref, grad_ref = refs[-4:]
    rows = own_refs[0].shape[0]
    for at in range(4):
        query_ref[at * rows : (at + 1) * rows, :] = own_refs[at][:, head_cols(2)]
        grad_ref[at * rows : (at + 1) * rows, :] = grad_refs[at][...]
    ones = jnp.ones((8, HEAD), wide_type)
    pair_sum[...] = jnp.zeros_like(pair_sum)
    for tile in lane_tiles(4 * rows):
        query = query_ref[tile, :]
        grad = grad_ref[tile, :]
        centre = lax.dot_general(
            ones,
            grad.astype(wide_type) * out_ref[tile, :],
            (((1,), (1,)), ((), ())),
            precision=highest_precision,
            preferred_element_type=wide_type,
        )[0:1, :]
        total = total_ref[0:1, tile]
        query_part = jnp.zeros((HEAD, tile.stop - tile.start), wide_type)
        for at in range(4):
            block = slice(at * rows, (at + 1) * rows)
            if own:
                key, value = own_refs[at][:, head_cols(0)], own_refs[at][:, head_cols(1)]
                scores = dot_dims(key, query, 1, 1) + bias_ref[:, at : at + 1] + mask_ref[at : at + 1, tile]
            else:
                key, value = cross_refs[at][:, head_cols(0)], cross_refs[at][:, head_cols(1)]
                scores = dot_dims(key, query, 1, 1) + bias_ref[:, at + 4 : at + 5]
            weights = jnp.exp(scores - total)
            pair_sum[block, head_cols(1)] += dot_wide(weights.astype(low_type), grad)
            soft = dot_dims(value, grad, 1, 1)
            back = (weights * (soft - centre)).astype(low_type)
            pair_sum[block, head_cols(0)] += dot_wide(back, query)
            query_part = query_part + dot_dims(key, back, 0, 0)
        query_sum[tile, :] = query_part.T * HEAD ** (-0.5)


def turn_back_kernel(own_pair, other_pair, own_query, other_query, cos_ref, sin_ref, swap_ref, *out_refs):
    rows = out_refs[0].shape[0]
    swap = swap_ref[...]
    for at in range(4):
        block = slice(at * rows, (at + 1) * rows)
        cosine, sine = cos_ref[block, :], sin_ref[block, :]

        def turned(value):
            crossed = jnp.dot(value, swap, precision=highest_precision, preferred_element_type=wide_type)
            return (value * cosine - crossed * sine).astype(low_type)

        pair = own_pair[block, :] + other_pair[block, :]
        out_refs[at][:, head_cols(0)] = turned(pair[:, head_cols(0)])
        out_refs[at][:, head_cols(1)] = pair[:, head_cols(1)].astype(low_type)
        out_refs[at][:, head_cols(2)] = turned(own_query[block, :] + other_query[block, :])


def mix_back_kernel(at_ref, place_ref, key_w, value_w, query_w, *refs):
    mixed_refs = refs[:4]
    out_ref, stack_ref, bias_ref = refs[4:]
    ring, clip = at_ref[0], at_ref[1]
    place = place_ref[...]
    total = None
    bias_ref[...] = jnp.zeros_like(bias_ref)
    for part, weight in ((0, key_w), (1, value_w), (2, query_w)):
        relative = jnp.concatenate([ref[:, head_cols(part)] for ref in mixed_refs], axis=1)
        ordered = dot_wide(relative, place)
        bias_ref[part : part + 1, :] = jnp.sum(ordered, axis=0, keepdims=True)
        term = dot_dims(ordered.astype(low_type), weight[...], 1, 1)
        total = term if total is None else total + term
    out_ref[...] = total
    for at in range(4):
        stack_ref[lax.rem(ring + at - clip + 4, 4)] = mixed_refs[at][...]


def clip_products(at_ref, first_ref, second_ref, pack_refs, columns):
    out = None
    half = first_ref.shape[1]
    for step in range(4):
        place = ring_back(at_ref[0], step)
        pack = pack_refs[step]
        term = dot_dims(first_ref[place], pack[:half, columns], 0, 0)
        term = term + dot_dims(second_ref[place], pack[half : 2 * half, columns], 0, 0)
        out = term if out is None else out + term
    return out


def layer_grad_kernel(at_ref, act_a, act_b, norm_a, norm_b, *refs):
    head_refs, pack_refs, out_ref = refs[:-5], refs[-5:-1], refs[-1]
    part = out_ref.shape[1] // 2
    tiles = pl.num_programs(0) - (1 if head_refs else 0)

    @pl.when(pl.program_id(0) < tiles)
    def _():
        out_ref[:, :part] = clip_products(at_ref, act_a, act_b, pack_refs, slice(0, part))
        out_ref[:, part:] = clip_products(at_ref, norm_a, norm_b, pack_refs, slice(part, 2 * part))

    if head_refs:

        @pl.when(pl.program_id(0) == tiles)
        def _():
            columns = slice(2 * part, 3 * part)
            out_ref[:, :part] = clip_products(at_ref, head_refs[0], head_refs[2], pack_refs, columns)
            out_ref[:, part:] = clip_products(at_ref, head_refs[1], head_refs[3], pack_refs, columns)


def plain_grad_kernel(at_ref, rows_a, rows_b, *refs):
    pack_refs, out_ref = refs[:4], refs[4]
    out_ref[...] = clip_products(at_ref, rows_a, rows_b, pack_refs, slice(None))


def last_grad_kernel(tiles, at_ref, head_a, head_b, *refs):
    feat_refs, pack_refs, out_ref = refs[:4], refs[4:8], refs[8]
    head_rows = 2 * head_a.shape[1]
    feat_rows = head_rows + feat_refs[0].shape[0]

    @pl.when(pl.program_id(0) < tiles)
    def _():
        out = None
        for step in range(4):
            term = dot_dims(feat_refs[step][...], pack_refs[step][head_rows:feat_rows, :], 0, 0)
            out = term if out is None else out + term
        out_ref[...] = out

    @pl.when(pl.program_id(0) == tiles + 2)
    def _():
        out = None
        small = (pack_refs[0].shape[0] - feat_rows) // 2
        for step in range(4):
            high = pack_refs[step][feat_rows : feat_rows + small, :].astype(wide_type)
            term = high + pack_refs[step][feat_rows + small :, :].astype(wide_type)
            out = term if out is None else out + term
        high = out.astype(low_type).astype(wide_type)
        out_ref[:small, :] = high
        out_ref[small:, :] = out - high

    @pl.when((pl.program_id(0) >= tiles) & (pl.program_id(0) < tiles + 2))
    def _():
        out_ref[...] = clip_products(at_ref, head_a, head_b, pack_refs, slice(None))


def ring_sum_kernel(at_ref, part_ref, *refs):
    got_refs, out_ref = refs[:3], refs[3]
    block = out_ref.shape[0]
    out = part_ref[pl.ds(pl.multiple_of(at_ref[0] * block, 8), block), :]
    for got in got_refs:
        out = out + got[...].astype(wide_type)
    out_ref[...] = out


def ring_sum(ring_at, part, got, after):
    shape = (part.shape[0] // 4, part.shape[1])
    return call_kernel(
        ring_sum_kernel,
        (ring_at[None], part, *got),
        (0,),
        jax.ShapeDtypeStruct(shape, wide_type),
        [],
        4 * shape[0] * shape[1],
        0,
        after,
    )


def half_sum_kernel(own_ref, got_ref, out_ref):
    out_ref[...] = (own_ref[...] + got_ref[...]).astype(low_type)


def half_sum(own, after):
    got = lax.ppermute(own, "frame", HALF_SWAP)
    return call_kernel(
        half_sum_kernel,
        (own, got),
        (),
        jax.ShapeDtypeStruct(own.shape, low_type),
        [],
        own.size,
        0,
        after,
    )


def join_kernel(at_ref, *refs):
    out_ref = refs[4]
    block = refs[0].shape[0]
    for step in range(4):
        start = pl.multiple_of(ring_back(at_ref[0], step) * block, 16)
        out_ref[pl.ds(start, block), :] = refs[step][...]


def join_frames(ring_at, total, after):
    pieces = ring_pieces(total)
    return call_kernel(
        join_kernel,
        (ring_at[None], *pieces),
        (0,),
        jax.ShapeDtypeStruct((4 * total.shape[0], total.shape[1]), low_type),
        [],
        0,
        0,
        after,
    )


def beside_kernel(first_ref, second_ref, out_ref):
    half, wide, other = first_ref.shape[0] // 2, first_ref.shape[1], second_ref.shape[1]
    out_ref[:, :wide] = first_ref[:half, :]
    out_ref[:, wide : wide + other] = second_ref[:half, :]
    out_ref[:, wide + other :] = second_ref[half:, :]


def gather_clips(first, second, after):
    half, wide = first.shape[0] // 2, first.shape[1]
    beside = call_kernel(
        beside_kernel,
        (first, second),
        (),
        jax.ShapeDtypeStruct((half, wide + 2 * second.shape[1]), low_type),
        [],
        0,
        0,
        after,
    )
    whole = lax.all_gather(beside, "clip")
    return whole, core_swap(whole[:, :, :wide])


def smem_spec():
    return pl.BlockSpec(memory_space=pltpu.SMEM)


def kernel_params():
    return pltpu.CompilerParams(vmem_limit_bytes=48 * 1024 * 1024)


def held_spec():
    return pl.BlockSpec(memory_space=pltpu.VMEM)


def any_specs(arrays):
    return [pl.BlockSpec(memory_space=pl.ANY)] * len(arrays)


def without(kernel, count, after):
    return lambda *refs: kernel(*refs[:count], *refs[count + len(after) :])


def layer_grad(clip_at, second_all, packs, first_all, after):
    whole, other = second_all
    half, wide = other.shape[1:]
    tiles = wide // 128
    part = 256
    block = (4, half, 128)
    heads = () if first_all is None else (first_all[0],) * 4
    held = [
        pl.BlockSpec(block, lambda i, at=at: (0, 0, tiles + at)) for at in range(len(heads))
    ]

    def moving(start):
        return pl.BlockSpec(block, lambda i: (0, 0, start + jnp.minimum(i, tiles - 1)))

    return pl.pallas_call(
        without(layer_grad_kernel, 9 + len(heads), after),
        grid=(tiles + (1 if heads else 0),),
        out_shape=jax.ShapeDtypeStruct((wide + (128 if heads else 0), 2 * part), wide_type),
        in_specs=[smem_spec(), moving(tiles), moving(2 * tiles), moving(0), moving(0)]
        + held
        + [held_spec()] * 4
        + any_specs(after),
        out_specs=pl.BlockSpec((128, 2 * part), lambda i: (i, 0)),
        compiler_params=kernel_params(),
        cost_estimate=pl.CostEstimate(
            flops=32 * half * wide * part,
            bytes_accessed=2 * whole.size + 8 * wide * part,
            transcendentals=0,
        ),
    )(clip_at[None], whole, whole, whole, other, *heads, *packs, *after)


def plain_grad(clip_at, rows_all, packs, after):
    whole, other = rows_all
    half, count = other.shape[1:]
    part = packs[0].shape[1]
    block = pl.BlockSpec((4, half, 128), lambda i: (0, 0, i))
    return pl.pallas_call(
        without(plain_grad_kernel, 7, after),
        grid=(count // 128,),
        out_shape=jax.ShapeDtypeStruct((count, part), wide_type),
        in_specs=[smem_spec(), block, block] + [held_spec()] * 4 + any_specs(after),
        out_specs=pl.BlockSpec((128, part), lambda i: (i, 0)),
        compiler_params=kernel_params(),
        cost_estimate=pl.CostEstimate(
            flops=16 * half * count * part,
            bytes_accessed=16 * half * count + 4 * count * part,
            transcendentals=0,
        ),
    )(clip_at[None], whole, other, *packs, *after)


def last_grad(clip_at, first_all, feats, packs, after):
    whole, other = first_all
    half, part = other.shape[1], packs[0].shape[1]
    first_block = other.shape[2] // 128
    tiles = feats[0].shape[1] // 128
    kernel = functools.partial(last_grad_kernel, tiles)

    def moving(start):
        return pl.BlockSpec(
            (4, half, 128), lambda i: (0, 0, start + jnp.clip(i - tiles, 0, 1))
        )

    return pl.pallas_call(
        without(kernel, 11, after),
        grid=(tiles + 3,),
        out_shape=jax.ShapeDtypeStruct(((tiles + 3) * 128, part), wide_type),
        in_specs=[smem_spec(), moving(first_block), moving(first_block + 2)]
        + [pl.BlockSpec((feats[0].shape[0], 128), lambda i: (0, jnp.minimum(i, tiles - 1)))] * 4
        + [held_spec()] * 4
        + any_specs(after),
        out_specs=pl.BlockSpec((128, part), lambda i: (i, 0)),
        compiler_params=kernel_params(),
    )(clip_at[None], whole, whole, *feats, *packs, *after)


def by_clip(clip_at, write):
    for place in range(4):

        @pl.when(clip_at == place)
        def _(place=place):
            for step in range(4):
                write((place - step) % 4, step)


def place_layer_kernel(tiles, at_ref, all_ref, *outs):
    part = all_ref.shape[2] // 2
    is_last = pl.program_id(0) == tiles

    for place in range(4):
        columns = slice(place * part, (place + 1) * part)
        left = all_ref[place, :, :part].astype(wide_type)
        right = all_ref[place, :, part:].astype(wide_type)

        @pl.when(jnp.logical_not(is_last))
        def _(columns=columns, left=left, right=right):
            outs[0][0, :, columns] = left
            outs[1][0, :, columns] = right

        if len(outs) > 2:

            @pl.when(is_last)
            def _(columns=columns, left=left, right=right):
                outs[2][0, : outs[2].shape[1] // 2, columns] = left
                outs[2][0, outs[2].shape[1] // 2 :, columns] = right


def place_layer(clip_at, layer, levels, joined, earlier, heads_layer, after):
    joined = lax.all_gather(joined, "clip")
    part = joined.shape[2] // 2
    rows = 4 * part
    tiles = rows // 128
    heads = joined.shape[1] > rows
    out = [(levels, rows, 4 * part)] * 2 + [(levels, 256, 4 * part)] * heads
    tall = pl.BlockSpec((1, 128, 4 * part), lambda i: (layer, jnp.minimum(i, tiles - 1), 0))
    wide = pl.BlockSpec((1, 256, 4 * part), lambda i: (heads_layer, 0, 0))
    return pl.pallas_call(
        without(functools.partial(place_layer_kernel, tiles), 2, (*earlier, *after)),
        grid=(tiles + (1 if heads else 0),),
        out_shape=tuple(jax.ShapeDtypeStruct(shape, wide_type) for shape in out),
        in_specs=[smem_spec(), pl.BlockSpec((4, 128, 2 * part), lambda i: (0, i, 0))]
        + any_specs(earlier)
        + any_specs(after),
        out_specs=(tall, tall) + ((wide,) if heads else ()),
        input_output_aliases={2 + at: at for at in range(len(earlier))},
        compiler_params=kernel_params(),
    )(clip_at[None], joined, *earlier, *after)


def place_last_kernel(skip, at_ref, *refs):
    pieces = refs[:4]
    in_ref, small_ref, proj_ref = refs[-3:]
    part = pieces[0].shape[1]
    heads = skip + proj_ref.shape[1]
    small = small_ref.shape[0]

    def write(place, step):
        columns = slice(place * part, (place + 1) * part)
        piece = pieces[step]
        in_ref[:, columns] = piece[: in_ref.shape[0], :].astype(wide_type)
        proj_ref[0, :, columns] = piece[skip:heads, :].astype(wide_type)
        small_ref[:, columns] = piece[heads : heads + small, :].astype(wide_type) + piece[
            heads + small :, :
        ].astype(wide_type)

    by_clip(at_ref[0], write)


def place_last(clip_at, feat_rows, skip, levels, pieces, earlier):
    part = pieces[0].shape[1]
    return pl.pallas_call(
        functools.partial(place_last_kernel, skip),
        grid=(1,),
        out_shape=(
            jax.ShapeDtypeStruct((feat_rows, 4 * part), wide_type),
            jax.ShapeDtypeStruct((64, 4 * part), wide_type),
            jax.ShapeDtypeStruct((levels, 256, 4 * part), wide_type),
        ),
        in_specs=[smem_spec()]
        + [pl.BlockSpec(pieces[0].shape, lambda i: (0, 0))] * 4
        + [pl.BlockSpec(memory_space=pl.ANY)],
        out_specs=(
            pl.BlockSpec((feat_rows, 4 * part), lambda i: (0, 0)),
            pl.BlockSpec((64, 4 * part), lambda i: (0, 0)),
            pl.BlockSpec((1, 256, 4 * part), lambda i: (0, 0, 0)),
        ),
        input_output_aliases={5: 2},
        compiler_params=kernel_params(),
    )(clip_at[None], *pieces, earlier)


def pack_kernel(by_rows, count, at_ref, *refs):
    parts, outs = refs[:count], refs[count:]
    for clip in range(4):

        @pl.when(at_ref[0] == clip)
        def _(clip=clip):
            for step in range(4):
                place, start = (clip + step) % 4, 0
                for part in parts:
                    size = part.shape[1] // 4
                    value = part[:, place * size : (place + 1) * size]
                    if by_rows:
                        outs[step][start : start + part.shape[0], :] = value
                        start += part.shape[0]
                    else:
                        outs[step][:, start : start + size] = value
                        start += size


def pack_parts(clip_at, parts, by_rows, after):
    sizes = [part.shape[1] // 4 for part in parts]
    if by_rows:
        shape = (sum(part.shape[0] for part in parts), sizes[0])
    else:
        shape = (parts[0].shape[0], sum(sizes))
    return call_kernel(
        functools.partial(pack_kernel, by_rows, len(parts)),
        (clip_at[None], *parts),
        (0,),
        tuple(jax.ShapeDtypeStruct(shape, low_type) for _ in range(4)),
        [],
        0,
        0,
        after,
    )


def place_heads_kernel(at_ref, all_ref, *refs):
    out_ref = refs[-1]
    for place in range(4):
        piece = all_ref[place].astype(wide_type)
        for at, part in ((1, 0), (2, 1), (0, 2)):
            out_ref[0, at, :, head_cols(place)] = piece[:, head_cols(part)]


def place_heads(clip_at, layer, levels, joined, earlier, after):
    joined = lax.all_gather(joined, "clip")
    rows = joined.shape[1]
    tile = 256
    count = 2
    return pl.pallas_call(
        without(place_heads_kernel, count, (*earlier, *after)),
        grid=(rows // tile,),
        out_shape=jax.ShapeDtypeStruct((levels, 3, rows, 4 * HEAD), wide_type),
        in_specs=[smem_spec(), pl.BlockSpec((4, tile, 3 * HEAD), lambda i: (0, i, 0))]
        + any_specs(earlier)
        + any_specs(after),
        out_specs=pl.BlockSpec((1, 3, tile, 4 * HEAD), lambda i: (layer, 0, i, 0)),
        input_output_aliases={count + at: at for at in range(len(earlier))},
        compiler_params=kernel_params(),
    )(clip_at[None], joined, *earlier, *after)


def stack_kernel(*refs):
    out_ref = refs[-1]
    for at, ref in enumerate(refs[:-1]):
        out_ref[8 * at : 8 * (at + 1), :] = ref[...]


def last_pack_kernel(at_ref, head_ref, patch_ref, small_a, small_b, *outs):
    heads, patches, small = head_ref.shape[0], patch_ref.shape[0], small_a.shape[0]
    values = small_a[...] + small_b[...]
    high = values.astype(low_type)
    rest = (values - high.astype(wide_type)).astype(low_type)
    for clip in range(4):

        @pl.when(at_ref[0] == clip)
        def _(clip=clip):
            for step in range(4):
                size = outs[step].shape[1]
                place = (clip + step) % 4
                columns = slice(place * size, (place + 1) * size)
                outs[step][:heads, :] = head_ref[:, columns]
                outs[step][heads : heads + patches, :] = patch_ref[:, columns]
                outs[step][heads + patches : heads + patches + small, :] = high[:, columns]
                outs[step][heads + patches + small :, :] = rest[:, columns]


def call_kernel(kernel, args, in_smem, outs, scratch, flops, exps, after=(), after_far=()):
    count = len(args)
    specs = [
        pl.BlockSpec(memory_space=pltpu.SMEM if at in in_smem else pltpu.VMEM)
        for at in range(count)
    ]
    specs += any_specs(after) + [pl.BlockSpec(memory_space=pltpu.HBM)] * len(after_far)
    after = (*after, *after_far)
    moved = sum(a.size * a.dtype.itemsize for a in args)
    return pl.pallas_call(
        without(kernel, count, after),
        out_shape=outs,
        in_specs=specs,
        out_specs=jax.tree.map(lambda _: pl.BlockSpec(memory_space=pltpu.VMEM), outs),
        scratch_shapes=scratch,
        compiler_params=kernel_params(),
        cost_estimate=pl.CostEstimate(flops=flops, bytes_accessed=moved, transcendentals=exps),
    )(*args, *after)


def on_device(
    features,
    cond_values,
    cond_live,
    in_weight,
    in_bias,
    act_weight,
    act_bias,
    state_weight,
    state_bias,
    attn_gain,
    attn_shift,
    qkv_weight,
    qkv_bias,
    proj_weight,
    proj_bias,
    mlp_gain,
    mlp_shift,
    up_weight,
    up_bias,
    down_weight,
    down_bias,
    out_grad,
):
    patch_rows = features.shape[2]
    feat_width = features.shape[3]
    slot_count = cond_values.shape[2]
    all_frames = cond_live.shape[1]
    model_width = in_weight.shape[1]
    width = qkv_weight.shape[3]
    heads = width // HEAD
    level_count = attn_gain.shape[0]
    patches = patch_rows // 4
    chunk_rows = patches + EXTRA
    rows = 4 * chunk_rows
    hidden_width = up_weight.shape[2]

    tensor_at = lax.axis_index("tensor")
    chip_at, core_at = tensor_at // 2, tensor_at % 2
    frame_at = lax.axis_index("frame")
    half_at, ring_at = frame_at // 4, frame_at % 4
    clip_at = lax.axis_index("clip")

    chunk_ids = [
        2 * jnp.bitwise_xor(core_at, core_step) + jnp.bitwise_xor(chip_at, chip_step)
        for core_step in range(2)
        for chip_step in range(2)
    ]
    own_chunk = chunk_ids[0]
    own_frames = jnp.stack([4 * half_at + (ring_at - step) % 4 for step in range(4)])
    cross_frames = jnp.stack([4 * (1 - half_at) + (ring_at - step) % 4 for step in range(4)])

    within = lax.broadcasted_iota(jnp.int32, (chunk_rows, 1), 0)
    is_patch = within < patches
    heights, columns = [], []
    for chunk_id in chunk_ids:
        patch_id = chunk_id * patches + within
        heights.append(jnp.where(is_patch, patch_id // GRID_W, 0))
        columns.append(jnp.where(is_patch, patch_id % GRID_W, 0))
    heights = jnp.concatenate(heights, axis=0).astype(wide_type)
    columns = jnp.concatenate(columns, axis=0).astype(wide_type)
    swap_table, rate_table = rotary_tables(HEAD, heads)
    swap_heads = jnp.asarray(swap_table)
    swap_one = jnp.asarray(swap_table[:HEAD, :HEAD])
    rates = rate_table[:, :HEAD]
    place_angles = heights * rates[1] + columns * rates[2]
    angles = jnp.concatenate(
        [
            own_frames[step].astype(wide_type) * rates[0][None, :] + place_angles
            for step in range(4)
        ],
        axis=0,
    )
    cosine_four, sine_four = jnp.cos(angles), jnp.sin(angles)
    cosine_rows = jnp.tile(cosine_four[:rows], (1, heads))
    sine_rows = jnp.tile(sine_four[:rows], (1, heads))
    head_from = jnp.arange(width)
    head_to = ((head_from // HEAD + ring_at) % 4) * HEAD + head_from % HEAD
    head_place = (head_to[:, None] == head_from[None, :]).astype(low_type)
    proj_turned = [
        lax.dynamic_slice_in_dim(
            jnp.concatenate([proj_weight[layer], proj_weight[layer]], axis=0),
            ring_at * HEAD,
            width,
            0,
        )
        for layer in range(level_count)
    ]
    ring_scalar = ring_at.astype(jnp.int32)
    clip_scalar = clip_at.astype(jnp.int32)

    live_all = cond_live[0].astype(wide_type)
    own_slots = lax.dynamic_index_in_dim(live_all, frame_at, 0, False)

    def live_rows(slots, chunk_id):
        picked = jnp.where(
            chunk_id < slot_count,
            lax.dynamic_index_in_dim(slots, jnp.minimum(chunk_id, slot_count - 1), 1, False),
            0.0,
        )
        return jnp.where(is_patch, 1.0, jnp.where(within == patches, picked[None, :], 0.0))

    sources = jnp.concatenate([own_frames, cross_frames])
    source_live = jnp.take(live_all, sources, axis=0)
    key_live = jnp.concatenate([live_rows(source_live, c) for c in chunk_ids], axis=0)
    reached = jnp.concatenate([jnp.ones((4,), jnp.bool_), jnp.full((4,), half_at == 1)])
    key_bias = jnp.where((key_live > 0.5) & reached[None, :], 0.0, masked_score).astype(wide_type)
    seen = own_frames[:, None] <= own_frames[None, :]
    causal = jnp.where(seen, 0.0, masked_score).astype(wide_type)
    causal = jnp.pad(jnp.repeat(causal, rows, axis=1), ((0, 4), (0, 0)))
    own_live = live_rows(own_slots[None, :], own_chunk)

    def extra_rows(slot_rows):
        picked = lax.dynamic_slice_in_dim(
            slot_rows, jnp.minimum(own_chunk, slot_count - 1), 1, 0
        )
        picked = jnp.where(own_chunk < slot_count, picked, jnp.zeros_like(picked))
        return jnp.pad(picked, ((0, EXTRA - 1), (0, 0)))

    cond_here = cond_values[0, 0]
    act_rows = jnp.dot(cond_here, act_weight, precision=highest_precision) + act_bias
    state_rows = jnp.dot(cond_here, state_weight, precision=highest_precision) + state_bias
    even_slot = (jnp.arange(slot_count) % 2 == 0)[:, None]
    cond_x = jnp.where(even_slot, act_rows, state_rows) * own_slots[:, None]

    flat_feat = jnp.concatenate(
        [
            lax.dynamic_slice_in_dim(features[0, 0], c * patches, patches, 0)
            for c in chunk_ids
        ],
        axis=0,
    )
    kept, got = halves_tensor(dot_wide(flat_feat, in_weight))
    stream = jnp.concatenate([kept + got + in_bias, extra_rows(cond_x)], axis=0)

    feat_wide = -(-feat_width // 128) * 128
    feat_low = jnp.pad(flat_feat, ((0, 0), (0, feat_wide - feat_width)))
    feats = [feat_low] + [
        lax.ppermute(feat_low, "clip", clip_shift(step)) for step in range(1, 4)
    ]
    pair_work = 2 * 32 * rows * rows * HEAD
    pair_exps = 32 * rows * rows
    weight_parts = [
        [qkv_weight[layer, :, at] for at in (1, 2, 0)] for layer in range(level_count)
    ]

    def norm(terms, gain, shift, after_far=()):
        chunk = jax.ShapeDtypeStruct((chunk_rows, model_width), wide_type)
        return call_kernel(
            norm_kernel,
            (gain[None], shift[None], *terms),
            (),
            (
                chunk,
                chunk,
                jax.ShapeDtypeStruct((chunk_rows, 128), wide_type),
                jax.ShapeDtypeStruct((chunk_rows, model_width), low_type),
            ),
            [],
            12 * chunk_rows * model_width,
            0,
            (),
            after_far,
        )

    def norm_back(part, gain, hat, inverse, grad, count, after=()):
        kept, got = halves_tensor(part)
        return call_kernel(
            functools.partial(norm_back_kernel, count),
            (kept, got, gain[None], hat, inverse, grad),
            (),
            (
                jax.ShapeDtypeStruct((chunk_rows, model_width), wide_type),
                jax.ShapeDtypeStruct((chunk_rows, model_width), low_type),
                jax.ShapeDtypeStruct((8, model_width), wide_type),
            ),
            [],
            16 * chunk_rows * model_width,
            0,
            after,
        )

    stored = []
    terms = (stream,)
    before = None
    for layer in range(level_count):
        stream, hat_one, inverse_one, first_chunk = norm(terms, attn_gain[layer], attn_shift[layer])
        first_in = join_rows_tensor(first_chunk)
        bias = jnp.pad(qkv_bias[layer], ((0, 5), (0, 0)))
        heads_out = call_kernel(
            functools.partial(project_kernel, heads),
            (
                ring_scalar[None],
                first_in,
                *weight_parts[layer],
                bias,
                cosine_rows,
                sine_rows,
                swap_heads,
            ),
            (0,),
            tuple(
                jax.ShapeDtypeStruct((rows, count * HEAD), low_type)
                for count in (3, 3, 3, 3, 2, 2, 2, 2)
            ),
            [],
            6 * rows * model_width * width,
            0,
            (),
            () if before is None else (before[0][0],),
        )
        blocks = to_heads(heads_out[:4])
        cross = pairs_to_later_half(heads_out[4:])
        attn_wide, attn_turned, log_total = call_kernel(
            attend_kernel,
            (key_bias, causal, *blocks, *cross),
            (),
            (
                jax.ShapeDtypeStruct((4 * rows, HEAD), wide_type),
                jax.ShapeDtypeStruct((4 * rows, HEAD), low_type),
                jax.ShapeDtypeStruct((8, 4 * rows), wide_type),
            ),
            [
                pltpu.VMEM((4 * rows, HEAD), low_type),
                pltpu.VMEM((8 * rows, lane_tiles(4 * rows)[0].stop), wide_type),
            ],
            2 * pair_work,
            pair_exps,
        )
        attn_relative = jnp.concatenate(
            to_frames([attn_turned[at * rows : (at + 1) * rows] for at in range(4)]), axis=1
        )
        attn_low = dot_wide(attn_relative, head_place).astype(low_type)
        if layer < level_count - 1:
            first_all = gather_clips(first_in, attn_low, ())
        kept, got = halves_tensor(dot_wide(attn_relative, proj_turned[layer]))
        middle, hat_two, inverse_two, second_chunk = norm(
            (stream, kept, got, proj_bias[layer][None]), mlp_gain[layer], mlp_shift[layer],
            () if before is None else (before[1][0],),
        )
        second_in = join_rows_tensor(second_chunk)
        hidden = dot_wide(second_in, up_weight[layer]) + up_bias[layer]
        active_low = exact_gelu(hidden).astype(low_type)
        second_all = gather_clips(second_in, active_low, ())
        if layer == level_count - 1:
            first_all = gather_clips(first_in, attn_low, (second_all[0],))
        before = (first_all, second_all)
        kept, got = halves_tensor(dot_wide(active_low, down_weight[layer]))
        terms = (middle, kept, got, down_bias[layer][None])
        stored.append(
            (
                hat_one,
                inverse_one,
                blocks,
                cross,
                log_total,
                attn_wide,
                hat_two,
                inverse_two,
                hidden,
                first_all,
                second_all,
            )
        )
    stream = terms[0] + (terms[1] + terms[2] + terms[3])

    def in_order(full, count):
        out = jnp.zeros((4 * count,) + full.shape[1:], full.dtype)
        size = full.shape[0] // 4
        for at, chunk_id in enumerate(chunk_ids):
            out = lax.dynamic_update_slice_in_dim(
                out, full[at * size : at * size + count], chunk_id * count, 0
            )
        return out

    block_full = join_rows_tensor((stream * own_live).astype(low_type))
    slot_full = jnp.concatenate(
        [
            block_full[at * chunk_rows + patches : at * chunk_rows + patches + 1]
            for at in range(4)
        ],
        axis=0,
    )
    block_out = jnp.concatenate(
        [in_order(block_full, patches), in_order(slot_full, 1)[:slot_count]], axis=0
    )[None, None]

    own_out = lax.dynamic_slice_in_dim(out_grad[0, 0], own_chunk * patches, patches, 0)
    grad_stream = (
        jnp.concatenate(
            [
                own_out.astype(wide_type),
                extra_rows(out_grad[0, 0, patch_rows:].astype(wide_type)),
            ],
            axis=0,
        )
        * own_live
    )

    small = {}
    branch_chunk = grad_stream.astype(low_type)
    small["down", level_count - 1] = jnp.sum(branch_chunk.astype(wide_type), axis=0)
    sums_list = []
    wide_part = model_width // 4
    later = None
    for layer in reversed(range(level_count)):
        (
            hat_one,
            inverse_one,
            blocks,
            cross,
            log_total,
            attn_wide,
            hat_two,
            inverse_two,
            hidden,
            first_all,
            second_all,
        ) = stored[layer]
        branch = join_rows_tensor(branch_chunk)
        _, gelu_pull = jax.vjp(exact_gelu, hidden)
        grad_hidden = gelu_pull(dot_dims(branch, down_weight[layer], 1, 1))[0].astype(low_type)
        small["up", layer] = jnp.sum(grad_hidden.astype(wide_type), axis=0)
        parts = [branch, grad_hidden] + ([] if later is None else [later["proj_out"]])
        packs = pack_parts(clip_scalar, parts, False, ())
        grad_middle, proj_chunk, sums = norm_back(
            dot_dims(grad_hidden, up_weight[layer], 1, 1),
            mlp_gain[layer],
            hat_two,
            inverse_two,
            grad_stream,
            chunk_rows,
            (packs[0],) if later is None else (packs[0], later["tall_total"], later["heads_sum"]),
        )
        sums_list.append(sums)
        packs = swap_clips(packs)
        proj_out = join_rows_tensor(proj_chunk)
        grad_attn = dot_dims(proj_out, proj_turned[layer], 1, 1).astype(low_type)
        grads = to_heads([grad_attn[:, head_cols(at)] for at in range(4)])

        if later is not None:
            later["heads_ring"] = ring_sum(
                ring_scalar, later["heads_sum"], later["heads_got"], (proj_chunk,)
            )

            later["tall_join"] = join_frames(ring_scalar, later["tall_total"], (proj_chunk,))

        def attend_back(own, after):
            return call_kernel(
                functools.partial(attend_back_kernel, own),
                (key_bias, causal, log_total, attn_wide, *blocks, *grads)
                + (() if own else tuple(cross)),
                (),
                (
                    jax.ShapeDtypeStruct((4 * rows, 2 * HEAD), wide_type),
                    jax.ShapeDtypeStruct((4 * rows, HEAD), wide_type),
                ),
                [
                    pltpu.VMEM((4 * rows, HEAD), low_type),
                    pltpu.VMEM((4 * rows, HEAD), low_type),
                ],
                5 * pair_work // 2,
                pair_exps // 2,
                after,
            )

        cross_pair, cross_query = attend_back(
            False, () if later is None else (later["heads_ring"],)
        )
        got_pair = lax.ppermute(cross_pair, "frame", DOWN_HALF)
        tall_sum = layer_grad(
            clip_scalar,
            second_all,
            packs,
            None if later is None else later["first_all"],
            (cross_pair,),
        )
        own_pair, own_query = attend_back(True, (tall_sum,))
        tall_got = ring_sends(tall_sum, ring_at)
        if later is not None:
            later["heads_total"] = half_sum(later["heads_ring"], (own_pair,))
        turned = call_kernel(
            turn_back_kernel,
            (own_pair, got_pair, own_query, cross_query, cosine_four, sine_four, swap_one),
            (),
            tuple(jax.ShapeDtypeStruct((rows, 3 * HEAD), low_type) for _ in range(4)),
            [],
            24 * rows * HEAD * HEAD,
            0,
            () if later is None else (later["heads_total"],),
        )
        mixed = to_frames(list(turned))
        tall_ring = ring_sum(ring_scalar, tall_sum, tall_got, (turned[0],))
        if later is not None:
            later["heads_join"] = join_frames(ring_scalar, later["heads_total"], (turned[0],))
        normed_part, mixed_stack, bias_sums = call_kernel(
            mix_back_kernel,
            (
                jnp.stack([ring_scalar, clip_scalar]),
                head_place,
                *weight_parts[layer],
                *mixed,
            ),
            (0,),
            (
                jax.ShapeDtypeStruct((rows, model_width), wide_type),
                jax.ShapeDtypeStruct((4, rows, 3 * HEAD), low_type),
                jax.ShapeDtypeStruct((8, width), wide_type),
            ),
            [],
            6 * rows * model_width * width,
            0,
            (tall_ring,) if later is None else (tall_ring, later["heads_join"]),
            (block_full,) if later is None else (),
        )
        small["qkv", layer] = jnp.concatenate([bias_sums[2:3], bias_sums[:2]], axis=0)
        grad_stream, branch_chunk, sums = norm_back(
            normed_part,
            attn_gain[layer],
            hat_one,
            inverse_one,
            grad_middle,
            patches if layer == 0 else chunk_rows,
        )
        sums_list.append(sums)
        tall_total = half_sum(tall_ring, (branch_chunk,))

        packs = swap_clips([mixed_stack[step] for step in range(4)])
        heads_sum = plain_grad(clip_scalar, first_all, packs, (branch_chunk,))
        heads_got = ring_sends(heads_sum, ring_at)
        if layer > 0:
            later = {
                "proj_out": proj_out,
                "first_all": first_all,
                "tall_total": tall_total,
                "heads_sum": heads_sum,
                "heads_got": heads_got,
            }

    patch_chunk = branch_chunk[:patches]
    grad_patch = join_rows_tensor(patch_chunk)
    grad_features = in_order(dot_dims(grad_patch, in_weight, 1, 1), patches)[None, None]
    slot_row = grad_stream[patches : patches + 1] * own_live[patches : patches + 1]
    own_cond = lax.dynamic_slice_in_dim(
        cond_here, jnp.minimum(own_chunk, slot_count - 1), 1, 0
    )
    slot_part = jnp.concatenate([own_cond.T * slot_row, slot_row], axis=0)
    here = own_chunk < slot_count
    is_act = here & (own_chunk % 2 == 0)
    is_state = here & (own_chunk % 2 == 1)
    act_part = jnp.where(is_act, slot_part, 0.0)
    state_part = jnp.where(is_state, slot_part, 0.0)

    def at_tensor(value, total):
        return lax.dynamic_update_slice(
            jnp.zeros((value.shape[0], total), wide_type),
            value,
            (0, tensor_at * value.shape[1]),
        )

    layers = range(level_count)
    qkv_rows = at_tensor(
        jnp.concatenate([small["qkv", layer] for layer in layers], axis=0), 4 * width
    )
    mixed_rows = jnp.concatenate(
        [qkv_rows, small["down", level_count - 1][None], jnp.zeros_like(qkv_rows[:1])], axis=0
    )
    ups = at_tensor(jnp.stack([small["up", layer] for layer in layers]), 4 * hidden_width)
    parts = [*sums_list, act_part, state_part, mixed_rows, ups.reshape(-1, model_width)]
    vector = call_kernel(
        stack_kernel,
        tuple(parts),
        (),
        jax.ShapeDtypeStruct((8 * len(parts), model_width), wide_type),
        [],
        0,
        0,
    )
    vector = vector + core_swap(vector)
    tall_join = join_frames(ring_scalar, tall_total, ())
    head_rows, patch_count, small_rows = proj_out.shape[0], grad_patch.shape[0], vector.shape[0]
    packs = call_kernel(
        last_pack_kernel,
        (clip_scalar[None], proj_out, grad_patch, vector, chip_swap(vector)),
        (0,),
        tuple(
            jax.ShapeDtypeStruct((head_rows + patch_count + 2 * small_rows, wide_part), low_type)
            for _ in range(4)
        ),
        [],
        0,
        0,
    )
    packs = swap_clips(packs)
    heads_ring = ring_sum(ring_scalar, heads_sum, heads_got, (packs[0],))
    last_sum = last_grad(clip_scalar, first_all, feats, packs, (tall_join, heads_ring))
    last_ring = ring_sum(ring_scalar, last_sum, ring_sends(last_sum, ring_at), ())
    heads_total = half_sum(heads_ring, (last_sum,))
    heads_join = join_frames(ring_scalar, heads_total, ())
    last_join = join_frames(ring_scalar, half_sum(last_ring, ()), ())
    last_pieces = clip_pieces(last_join)
    placed = place_layer(
        clip_scalar, level_count - 1, level_count, later["tall_join"], (), 0, (packs[0],)
    )
    grad_down, grad_up, grad_proj = place_layer(
        clip_scalar, 0, level_count, tall_join, placed, level_count - 1, ()
    )
    grad_in, vector, grad_proj = place_last(
        clip_scalar, feat_width, feat_wide, level_count, last_pieces, grad_proj
    )
    grad_heads = place_heads(
        clip_scalar, level_count - 1, level_count, later["heads_join"], (), (last_sum,)
    )
    grad_heads = (place_heads(clip_scalar, 0, level_count, heads_join, (grad_heads,), ()),)


    def norm_sums(layer, first, row):
        return vector[8 * (2 * (level_count - 1 - layer) + first) + row]

    grad_mlp_gain = jnp.stack([norm_sums(layer, 0, 0) for layer in layers])
    grad_mlp_shift = jnp.stack([norm_sums(layer, 0, 1) for layer in layers])
    grad_proj_bias = jnp.stack([norm_sums(layer, 0, 2) for layer in layers])
    grad_attn_gain = jnp.stack([norm_sums(layer, 1, 0) for layer in layers])
    grad_attn_shift = jnp.stack([norm_sums(layer, 1, 1) for layer in layers])
    rest = vector[16 * level_count :]
    grad_down_bias = jnp.stack(
        [norm_sums(layer + 1, 1, 2) for layer in range(level_count - 1)]
        + [rest[16 + 3 * level_count]]
    )
    grad_qkv_bias = lax.dynamic_slice_in_dim(
        rest[16 : 16 + 3 * level_count], tensor_at * width, width, 1
    )
    grad_qkv_bias = grad_qkv_bias.reshape(level_count, 3, width)
    grad_up_bias = lax.dynamic_slice_in_dim(
        rest[24:].reshape(level_count, 4 * hidden_width), tensor_at * hidden_width, hidden_width, 1
    )
    act_count = cond_here.shape[1]
    return (
        block_out,
        grad_features,
        grad_in,
        norm_sums(0, 1, 2),
        rest[:act_count],
        rest[act_count],
        rest[8 : 8 + act_count],
        rest[8 + act_count],
        grad_attn_gain,
        grad_attn_shift,
        jnp.swapaxes(grad_heads[0], 1, 2),
        grad_qkv_bias,
        grad_proj,
        grad_proj_bias,
        grad_mlp_gain,
        grad_mlp_shift,
        grad_up,
        grad_up_bias,
        grad_down,
        grad_down_bias,
    )


def solution(mesh):
    return jax.shard_map(
        on_device,
        mesh=mesh,
        in_specs=(
            P("clip", "frame", None, "tensor"),
            P("clip", "frame", None, None),
            P("clip", None, None),
            P("tensor", None),
            P(),
            P(),
            P(),
            P(),
            P(),
            P(),
            P(),
            P(None, None, None, "tensor"),
            P(None, None, "tensor"),
            P(None, "tensor", None),
            P(),
            P(),
            P(),
            P(None, None, "tensor"),
            P(None, "tensor"),
            P(None, "tensor", None),
            P(),
            P("clip", "frame", None, None),
        ),
        out_specs=(
            P("clip", "frame", None, None),
            P("clip", "frame", None, "tensor"),
            P("tensor", None),
            P(),
            P(),
            P(),
            P(),
            P(),
            P(),
            P(),
            P(None, None, None, "tensor"),
            P(None, None, "tensor"),
            P(None, "tensor", None),
            P(),
            P(),
            P(),
            P(None, None, "tensor"),
            P(None, "tensor"),
            P(None, "tensor", None),
            P(),
        ),
        check_vma=False,
    )
```

```python
import functools

import jax
import jax.numpy as jnp
import numpy as np
from jax import lax
from jax.experimental import pallas as pl
from jax.experimental.pallas import tpu as pltpu
from jax.sharding import PartitionSpec as P

HEAD = 64
GRID_W = 16
EXTRA = 8

highest_precision = lax.Precision.HIGHEST
norm_epsilon = 1e-06
masked_score = -1000000000.0
low_type = jnp.bfloat16
wide_type = jnp.float32

CORE_SWAP = [(0, 1), (1, 0), (2, 3), (3, 2)]
CHIP_SWAP = [(0, 2), (2, 0), (1, 3), (3, 1)]
HALF_SWAP = [(i, (i + 4) % 8) for i in range(8)]


def clip_shift(step):
    return [(i, (i + step) % 4) for i in range(4)]


def frame_shift(halves, step):
    return [
        (4 * half + i, 4 * ((half + halves) % 2) + (i + step) % 4)
        for half in range(2)
        for i in range(4)
    ]


def core_swap(value):
    return lax.ppermute(value, "tensor", CORE_SWAP)


def chip_swap(value):
    return lax.ppermute(value, "tensor", CHIP_SWAP)


def halves_tensor(part):
    half = part.shape[0] // 2
    pair = part[:half] + core_swap(part[half:])
    quarter = half // 2
    return pair[:quarter], chip_swap(pair[quarter:])


def join_rows_tensor(chunk):
    pair = jnp.concatenate([chunk, chip_swap(chunk)], axis=0)
    return jnp.concatenate([pair, core_swap(pair)], axis=0)


def to_heads(blocks):
    return [blocks[0]] + [
        lax.ppermute(blocks[step], "frame", frame_shift(0, step)) for step in range(1, 4)
    ]


def to_frames(blocks):
    return [blocks[0]] + [
        lax.ppermute(blocks[step], "frame", frame_shift(0, -step)) for step in range(1, 4)
    ]


def pairs_to_later_half(blocks):
    return [
        lax.ppermute(
            blocks[step],
            "frame",
            [(src, dst) for src, dst in frame_shift(1, step) if src < dst],
        )
        for step in range(4)
    ]


DOWN_HALF = [(i + 4, i) for i in range(4)]


def swap_clips(packs):
    return [packs[0]] + [
        lax.ppermute(packs[step], "clip", clip_shift(step)) for step in range(1, 4)
    ]


def ring_pieces(value):
    return [value] + [
        lax.ppermute(value, "frame", frame_shift(0, step)) for step in range(1, 4)
    ]


def ring_sends(part, ring):
    block = part.shape[0] // 4
    got = []
    for step in range(1, 4):
        sent = lax.dynamic_slice_in_dim(part, ((ring + step) % 4) * block, block, 0)
        got.append(lax.ppermute(sent.astype(low_type), "frame", frame_shift(0, step)))
    return got


def clip_pieces(joined):
    return [joined] + [
        lax.ppermute(joined, "clip", clip_shift(step)) for step in range(1, 4)
    ]


def rotary_tables(head_size, head_count):
    group_size = 2 * (head_size // 3 // 2)
    half_size = group_size // 2
    total_width = head_size * head_count
    swap_table = np.zeros((total_width, total_width), np.float32)
    rate_table = np.zeros((3, total_width), np.float32)
    for head_at in range(head_count):
        for axis_at in range(3):
            for pair_at in range(half_size):
                lower_at = head_at * head_size + axis_at * group_size + pair_at
                upper_at = lower_at + half_size
                swap_table[upper_at, lower_at] = -1.0
                swap_table[lower_at, upper_at] = 1.0
                rate_value = 10000.0 ** (-2.0 * pair_at / group_size)
                rate_table[axis_at, lower_at] = rate_value
                rate_table[axis_at, upper_at] = rate_value
    return swap_table, rate_table


def norm_rows(values):
    row_mean = jnp.mean(values, axis=-1, keepdims=True)
    centred = values - row_mean
    spread = jnp.mean(centred * centred, axis=-1, keepdims=True)
    inverse = lax.rsqrt(spread + norm_epsilon)
    return centred * inverse, inverse


def norm_kernel(gain_ref, shift_ref, *refs):
    terms, (stream_ref, hat_ref, inverse_ref, low_ref) = refs[:-4], refs[-4:]
    values = terms[0][...]
    if len(terms) > 1:
        values = values + (terms[1][...] + terms[2][...] + terms[3][...])
    hat, inverse = norm_rows(values)
    stream_ref[...] = values
    hat_ref[...] = hat
    inverse_ref[...] = jnp.broadcast_to(inverse, inverse_ref.shape)
    low_ref[...] = (hat * gain_ref[...] + shift_ref[...]).astype(low_type)


def norm_back_kernel(count, kept_ref, got_ref, gain_ref, hat_ref, inverse_ref, grad_ref, out_ref, low_ref, sums_ref):
    grad = kept_ref[...] + got_ref[...]
    hat = hat_ref[...]
    scaled = grad * gain_ref[...]
    first = jnp.mean(scaled, axis=-1, keepdims=True)
    second = jnp.mean(scaled * hat, axis=-1, keepdims=True)
    out = grad_ref[...] + (scaled - first - hat * second) * inverse_ref[:, 0:1]
    low = out.astype(low_type)
    out_ref[...] = out
    low_ref[...] = low
    sums_ref[...] = jnp.zeros_like(sums_ref)
    sums_ref[0:1, :] = jnp.sum(grad * hat, axis=0, keepdims=True)
    sums_ref[1:2, :] = jnp.sum(grad, axis=0, keepdims=True)
    sums_ref[2:3, :] = jnp.sum(low[:count].astype(wide_type), axis=0, keepdims=True)


def exact_gelu(values):
    return jax.nn.gelu(values, approximate=False)


def dot_wide(left, right):
    return jnp.dot(left, right, preferred_element_type=wide_type)


def dot_dims(left, right, left_dim, right_dim):
    return lax.dot_general(
        left, right, (((left_dim,), (right_dim,)), ((), ())), preferred_element_type=wide_type
    )


def head_cols(at):
    return slice(at * HEAD, (at + 1) * HEAD)


def ring_back(place, step):
    return lax.rem(place - step + 4, 4)


def ring_ahead(place, step):
    return lax.rem(place + step, 4)


def project_kernel(heads, at_ref, rows_ref, key_w, value_w, query_w, bias_ref, cos_ref, sin_ref, swap_ref, *out_refs):
    rows = rows_ref[...]
    swap = swap_ref[...]
    cosine = jnp.concatenate([cos_ref[: rows.shape[0], :]] * heads, axis=1)
    sine = jnp.concatenate([sin_ref[: rows.shape[0], :]] * heads, axis=1)

    def turned(weight, bias):
        value = dot_wide(rows, weight[...]) + bias
        crossed = jnp.dot(value, swap, precision=highest_precision, preferred_element_type=wide_type)
        return value * cosine + crossed * sine

    key = turned(key_w, bias_ref[1:2, :]).astype(low_type)
    value = (dot_wide(rows, value_w[...]) + bias_ref[2:3, :]).astype(low_type)
    query = (turned(query_w, bias_ref[0:1, :]).astype(low_type).astype(wide_type) * HEAD ** (-0.5)).astype(low_type)

    def write(head, step):
        for at, part in enumerate((key, value, query)):
            out_refs[step][:, head_cols(at)] = part[:, head_cols(head)]
            if at < 2:
                out_refs[4 + step][:, head_cols(at)] = part[:, head_cols(head)]

    for ring in range(4):

        @pl.when(at_ref[0] == ring)
        def _(ring=ring):
            for step in range(4):
                write((ring + step) % 4, step)


def lane_tiles(total):
    size = 384 if total % 384 == 0 else total
    return [slice(at * size, (at + 1) * size) for at in range(total // size)]


def attend_kernel(bias_ref, mask_ref, *refs):
    own_refs, cross_refs = refs[:4], refs[4:8]
    out_ref, low_ref, total_ref, own_out, cross_out, query_ref, score_ref = refs[8:]
    rows = own_refs[0].shape[0]
    total_rows = 4 * rows
    for at in range(4):
        block = slice(at * rows, (at + 1) * rows)
        query_ref[block, :] = own_refs[at][:, head_cols(2)]
        own_out[block, :] = own_refs[at][...]
        cross_out[block, :] = cross_refs[at][...]
    total_ref[...] = jnp.zeros_like(total_ref)

    def pair(at, part):
        if at < 4:
            return own_refs[at][:, head_cols(part)]
        return cross_refs[at - 4][:, head_cols(part)]

    for tile in lane_tiles(total_rows):
        query = query_ref[tile, :]
        wide = tile.stop - tile.start
        top = jnp.full((1, wide), 2.0 * masked_score, wide_type)
        for at in range(8):
            scores = dot_dims(pair(at, 0), query, 1, 1) + bias_ref[:, at : at + 1]
            if at < 4:
                scores = scores + mask_ref[at : at + 1, tile]
            score_ref[at * rows : (at + 1) * rows, :] = scores
            top = jnp.maximum(top, jnp.max(scores, axis=0, keepdims=True))
        mass = jnp.zeros((1, wide), wide_type)
        out = jnp.zeros((HEAD, wide), wide_type)
        for at in range(8):
            weights = jnp.exp(score_ref[at * rows : (at + 1) * rows, :] - top)
            mass = mass + jnp.sum(weights, axis=0, keepdims=True)
            out = out + dot_dims(pair(at, 1), weights.astype(low_type), 0, 0)
        total_ref[0:1, tile] = top + jnp.log(mass)
        rows_out = (out / mass).T
        out_ref[tile, :] = rows_out
        low_ref[tile, :] = rows_out.astype(low_type)


def attend_back_kernel(own, bias_ref, mask_ref, total_ref, out_ref, own_ref, *refs):
    grad_refs, cross_refs = refs[:4], refs[4:-4]
    pair_sum, query_sum, query_ref, grad_ref = refs[-4:]
    rows = grad_refs[0].shape[0]
    query_ref[...] = own_ref[:, head_cols(2)]
    for at in range(4):
        grad_ref[at * rows : (at + 1) * rows, :] = grad_refs[at][...]
    ones = jnp.ones((8, HEAD), wide_type)
    pair_sum[...] = jnp.zeros_like(pair_sum)
    for tile in lane_tiles(4 * rows):
        query = query_ref[tile, :]
        grad = grad_ref[tile, :]
        centre = lax.dot_general(
            ones,
            grad.astype(wide_type) * out_ref[tile, :],
            (((1,), (1,)), ((), ())),
            precision=highest_precision,
            preferred_element_type=wide_type,
        )[0:1, :]
        total = total_ref[0:1, tile]
        query_part = jnp.zeros((HEAD, tile.stop - tile.start), wide_type)
        for at in range(4):
            block = slice(at * rows, (at + 1) * rows)
            if own:
                key, value = own_ref[block, head_cols(0)], own_ref[block, head_cols(1)]
                scores = dot_dims(key, query, 1, 1) + bias_ref[:, at : at + 1] + mask_ref[at : at + 1, tile]
            else:
                key, value = cross_refs[0][block, head_cols(0)], cross_refs[0][block, head_cols(1)]
                scores = dot_dims(key, query, 1, 1) + bias_ref[:, at + 4 : at + 5]
            weights = jnp.exp(scores - total)
            pair_sum[block, head_cols(1)] += dot_wide(weights.astype(low_type), grad)
            soft = dot_dims(value, grad, 1, 1)
            back = (weights * (soft - centre)).astype(low_type)
            pair_sum[block, head_cols(0)] += dot_wide(back, query)
            query_part = query_part + dot_dims(key, back, 0, 0)
        query_sum[tile, :] = query_part.T * HEAD ** (-0.5)


def turn_back_kernel(own_pair, other_pair, own_query, other_query, cos_ref, sin_ref, swap_ref, *out_refs):
    rows = out_refs[0].shape[0]
    swap = swap_ref[...]
    for at in range(4):
        block = slice(at * rows, (at + 1) * rows)
        cosine, sine = cos_ref[block, :], sin_ref[block, :]

        def turned(value):
            crossed = jnp.dot(value, swap, precision=highest_precision, preferred_element_type=wide_type)
            return (value * cosine - crossed * sine).astype(low_type)

        pair = own_pair[block, :] + other_pair[block, :]
        out_refs[at][:, head_cols(0)] = turned(pair[:, head_cols(0)])
        out_refs[at][:, head_cols(1)] = pair[:, head_cols(1)].astype(low_type)
        out_refs[at][:, head_cols(2)] = turned(own_query[block, :] + other_query[block, :])


def mix_back_kernel(at_ref, place_ref, key_w, value_w, query_w, *refs):
    mixed_refs = refs[:4]
    out_ref, stack_ref, bias_ref = refs[4:]
    ring, clip = at_ref[0], at_ref[1]
    place = place_ref[...]
    total = None
    bias_ref[...] = jnp.zeros_like(bias_ref)
    for part, weight in ((0, key_w), (1, value_w), (2, query_w)):
        relative = jnp.concatenate([ref[:, head_cols(part)] for ref in mixed_refs], axis=1)
        ordered = dot_wide(relative, place)
        bias_ref[part : part + 1, :] = jnp.sum(ordered, axis=0, keepdims=True)
        term = dot_dims(ordered.astype(low_type), weight[...], 1, 1)
        total = term if total is None else total + term
    out_ref[...] = total
    for at in range(4):
        stack_ref[lax.rem(ring + at - clip + 4, 4)] = mixed_refs[at][...]


def clip_products(at_ref, first_ref, second_ref, pack_refs, columns):
    out = None
    half = first_ref.shape[1]
    for step in range(4):
        place = ring_back(at_ref[0], step)
        pack = pack_refs[step]
        term = dot_dims(first_ref[place], pack[:half, columns], 0, 0)
        term = term + dot_dims(second_ref[place], pack[half : 2 * half, columns], 0, 0)
        out = term if out is None else out + term
    return out


def layer_grad_kernel(at_ref, act_a, act_b, norm_a, norm_b, *refs):
    head_refs, pack_refs, out_ref = refs[:-5], refs[-5:-1], refs[-1]
    part = out_ref.shape[1] // 2
    tiles = pl.num_programs(0) - (1 if head_refs else 0)

    @pl.when(pl.program_id(0) < tiles)
    def _():
        out_ref[:, :part] = clip_products(at_ref, act_a, act_b, pack_refs, slice(0, part))
        out_ref[:, part:] = clip_products(at_ref, norm_a, norm_b, pack_refs, slice(part, 2 * part))

    if head_refs:

        @pl.when(pl.program_id(0) == tiles)
        def _():
            columns = slice(2 * part, 3 * part)
            out_ref[:, :part] = clip_products(at_ref, head_refs[0], head_refs[2], pack_refs, columns)
            out_ref[:, part:] = clip_products(at_ref, head_refs[1], head_refs[3], pack_refs, columns)


def plain_grad_kernel(at_ref, rows_a, rows_b, *refs):
    pack_refs, out_ref = refs[:4], refs[4]
    out_ref[...] = clip_products(at_ref, rows_a, rows_b, pack_refs, slice(None))


def last_grad_kernel(tiles, at_ref, head_a, head_b, *refs):
    feat_refs, pack_refs, out_ref = refs[:4], refs[4:8], refs[8]
    head_rows = 2 * head_a.shape[1]
    feat_rows = head_rows + feat_refs[0].shape[0]

    @pl.when(pl.program_id(0) < tiles)
    def _():
        out = None
        for step in range(4):
            term = dot_dims(feat_refs[step][...], pack_refs[step][head_rows:feat_rows, :], 0, 0)
            out = term if out is None else out + term
        out_ref[...] = out

    @pl.when(pl.program_id(0) == tiles + 2)
    def _():
        out = None
        small = (pack_refs[0].shape[0] - feat_rows) // 2
        for step in range(4):
            high = pack_refs[step][feat_rows : feat_rows + small, :].astype(wide_type)
            term = high + pack_refs[step][feat_rows + small :, :].astype(wide_type)
            out = term if out is None else out + term
        high = out.astype(low_type).astype(wide_type)
        out_ref[:small, :] = high
        out_ref[small:, :] = out - high

    @pl.when((pl.program_id(0) >= tiles) & (pl.program_id(0) < tiles + 2))
    def _():
        out_ref[...] = clip_products(at_ref, head_a, head_b, pack_refs, slice(None))


def ring_sum_kernel(at_ref, part_ref, *refs):
    got_refs, out_ref = refs[:3], refs[3]
    block = out_ref.shape[0]
    out = part_ref[pl.ds(pl.multiple_of(at_ref[0] * block, 8), block), :]
    for got in got_refs:
        out = out + got[...].astype(wide_type)
    out_ref[...] = out


def ring_sum(ring_at, part, got, after):
    shape = (part.shape[0] // 4, part.shape[1])
    return call_kernel(
        ring_sum_kernel,
        (ring_at[None], part, *got),
        (0,),
        jax.ShapeDtypeStruct(shape, wide_type),
        [],
        4 * shape[0] * shape[1],
        0,
        after,
    )


def half_sum_kernel(own_ref, got_ref, out_ref):
    out_ref[...] = (own_ref[...] + got_ref[...]).astype(low_type)


def half_sum(own, after):
    got = lax.ppermute(own, "frame", HALF_SWAP)
    return call_kernel(
        half_sum_kernel,
        (own, got),
        (),
        jax.ShapeDtypeStruct(own.shape, low_type),
        [],
        own.size,
        0,
        after,
    )


def join_kernel(at_ref, *refs):
    out_ref = refs[4]
    block = refs[0].shape[0]
    for step in range(4):
        start = pl.multiple_of(ring_back(at_ref[0], step) * block, 16)
        out_ref[pl.ds(start, block), :] = refs[step][...]


def join_frames(ring_at, total, after, after_far=()):
    pieces = ring_pieces(total)
    return call_kernel(
        join_kernel,
        (ring_at[None], *pieces),
        (0,),
        jax.ShapeDtypeStruct((4 * total.shape[0], total.shape[1]), low_type),
        [],
        0,
        0,
        after,
        after_far,
    )


def beside_kernel(first_ref, second_ref, out_ref):
    half, wide, other = first_ref.shape[0] // 2, first_ref.shape[1], second_ref.shape[1]
    out_ref[:, :wide] = first_ref[:half, :]
    out_ref[:, wide : wide + other] = second_ref[:half, :]
    out_ref[:, wide + other :] = second_ref[half:, :]


def gather_clips(first, second, after):
    half, wide = first.shape[0] // 2, first.shape[1]
    beside = call_kernel(
        beside_kernel,
        (first, second),
        (),
        jax.ShapeDtypeStruct((half, wide + 2 * second.shape[1]), low_type),
        [],
        0,
        0,
        after,
    )
    whole = lax.all_gather(beside, "clip")
    return whole, core_swap(whole[:, :, :wide])


def smem_spec():
    return pl.BlockSpec(memory_space=pltpu.SMEM)


def kernel_params():
    return pltpu.CompilerParams(vmem_limit_bytes=48 * 1024 * 1024)


def held_spec():
    return pl.BlockSpec(memory_space=pltpu.VMEM)


def any_specs(arrays):
    return [pl.BlockSpec(memory_space=pl.ANY)] * len(arrays)


def without(kernel, count, after):
    return lambda *refs: kernel(*refs[:count], *refs[count + len(after) :])


def layer_grad(clip_at, second_all, packs, first_all, after):
    whole, other = second_all
    half, wide = other.shape[1:]
    tiles = wide // 128
    part = 256
    block = (4, half, 128)
    heads = () if first_all is None else (first_all[0],) * 4
    held = [
        pl.BlockSpec(block, lambda i, at=at: (0, 0, tiles + at)) for at in range(len(heads))
    ]

    def moving(start):
        return pl.BlockSpec(block, lambda i: (0, 0, start + jnp.minimum(i, tiles - 1)))

    return pl.pallas_call(
        without(layer_grad_kernel, 9 + len(heads), after),
        grid=(tiles + (1 if heads else 0),),
        out_shape=jax.ShapeDtypeStruct((wide + (128 if heads else 0), 2 * part), wide_type),
        in_specs=[smem_spec(), moving(tiles), moving(2 * tiles), moving(0), moving(0)]
        + held
        + [held_spec()] * 4
        + any_specs(after),
        out_specs=pl.BlockSpec((128, 2 * part), lambda i: (i, 0)),
        compiler_params=kernel_params(),
        cost_estimate=pl.CostEstimate(
            flops=32 * half * wide * part,
            bytes_accessed=2 * whole.size + 8 * wide * part,
            transcendentals=0,
        ),
    )(clip_at[None], whole, whole, whole, other, *heads, *packs, *after)


def plain_grad(clip_at, rows_all, packs, after):
    whole, other = rows_all
    half, count = other.shape[1:]
    part = packs[0].shape[1]
    block = pl.BlockSpec((4, half, 128), lambda i: (0, 0, i))
    return pl.pallas_call(
        without(plain_grad_kernel, 7, after),
        grid=(count // 128,),
        out_shape=jax.ShapeDtypeStruct((count, part), wide_type),
        in_specs=[smem_spec(), block, block] + [held_spec()] * 4 + any_specs(after),
        out_specs=pl.BlockSpec((128, part), lambda i: (i, 0)),
        compiler_params=kernel_params(),
        cost_estimate=pl.CostEstimate(
            flops=16 * half * count * part,
            bytes_accessed=16 * half * count + 4 * count * part,
            transcendentals=0,
        ),
    )(clip_at[None], whole, other, *packs, *after)


def last_grad(clip_at, first_all, feats, packs, after):
    whole, other = first_all
    half, part = other.shape[1], packs[0].shape[1]
    first_block = other.shape[2] // 128
    tiles = feats[0].shape[1] // 128
    kernel = functools.partial(last_grad_kernel, tiles)

    def moving(start):
        return pl.BlockSpec(
            (4, half, 128), lambda i: (0, 0, start + jnp.clip(i - tiles, 0, 1))
        )

    return pl.pallas_call(
        without(kernel, 11, after),
        grid=(tiles + 3,),
        out_shape=jax.ShapeDtypeStruct(((tiles + 3) * 128, part), wide_type),
        in_specs=[smem_spec(), moving(first_block), moving(first_block + 2)]
        + [pl.BlockSpec((feats[0].shape[0], 128), lambda i: (0, jnp.minimum(i, tiles - 1)))] * 4
        + [held_spec()] * 4
        + any_specs(after),
        out_specs=pl.BlockSpec((128, part), lambda i: (i, 0)),
        compiler_params=kernel_params(),
    )(clip_at[None], whole, whole, *feats, *packs, *after)


def by_clip(clip_at, write):
    for place in range(4):

        @pl.when(clip_at == place)
        def _(place=place):
            for step in range(4):
                write((place - step) % 4, step)


def place_layer_kernel(tiles, at_ref, all_ref, *outs):
    part = all_ref.shape[2] // 2
    is_last = pl.program_id(0) == tiles

    for place in range(4):
        columns = slice(place * part, (place + 1) * part)
        left = all_ref[place, :, :part].astype(wide_type)
        right = all_ref[place, :, part:].astype(wide_type)

        @pl.when(jnp.logical_not(is_last))
        def _(columns=columns, left=left, right=right):
            outs[0][0, :, columns] = left
            outs[1][0, :, columns] = right

        if len(outs) > 2:

            @pl.when(is_last)
            def _(columns=columns, left=left, right=right):
                outs[2][0, : outs[2].shape[1] // 2, columns] = left
                outs[2][0, outs[2].shape[1] // 2 :, columns] = right


def place_layer(clip_at, layer, levels, joined, earlier, heads_layer, after):
    part = joined.shape[2] // 2
    rows = 4 * part
    tiles = rows // 128
    heads = joined.shape[1] > rows
    out = [(levels, rows, 4 * part)] * 2 + [(levels, 256, 4 * part)] * heads
    tall = pl.BlockSpec((1, 128, 4 * part), lambda i: (layer, jnp.minimum(i, tiles - 1), 0))
    wide = pl.BlockSpec((1, 256, 4 * part), lambda i: (heads_layer, 0, 0))
    return pl.pallas_call(
        without(functools.partial(place_layer_kernel, tiles), 2, (*earlier, *after)),
        grid=(tiles + (1 if heads else 0),),
        out_shape=tuple(jax.ShapeDtypeStruct(shape, wide_type) for shape in out),
        in_specs=[smem_spec(), pl.BlockSpec((4, 128, 2 * part), lambda i: (0, i, 0))]
        + any_specs(earlier)
        + any_specs(after),
        out_specs=(tall, tall) + ((wide,) if heads else ()),
        input_output_aliases={2 + at: at for at in range(len(earlier))},
        compiler_params=kernel_params(),
    )(clip_at[None], joined, *earlier, *after)


def place_last_kernel(skip, at_ref, *refs):
    pieces = refs[:4]
    in_ref, small_ref, proj_ref = refs[-3:]
    part = pieces[0].shape[1]
    heads = skip + proj_ref.shape[1]
    small = small_ref.shape[0]

    def write(place, step):
        columns = slice(place * part, (place + 1) * part)
        piece = pieces[step]
        in_ref[:, columns] = piece[: in_ref.shape[0], :].astype(wide_type)
        proj_ref[0, :, columns] = piece[skip:heads, :].astype(wide_type)
        small_ref[:, columns] = piece[heads : heads + small, :].astype(wide_type) + piece[
            heads + small :, :
        ].astype(wide_type)

    by_clip(at_ref[0], write)


def place_last(clip_at, feat_rows, skip, levels, pieces, earlier):
    part = pieces[0].shape[1]
    return pl.pallas_call(
        functools.partial(place_last_kernel, skip),
        grid=(1,),
        out_shape=(
            jax.ShapeDtypeStruct((feat_rows, 4 * part), wide_type),
            jax.ShapeDtypeStruct((64, 4 * part), wide_type),
            jax.ShapeDtypeStruct((levels, 256, 4 * part), wide_type),
        ),
        in_specs=[smem_spec()]
        + [pl.BlockSpec(pieces[0].shape, lambda i: (0, 0))] * 4
        + [pl.BlockSpec(memory_space=pl.ANY)],
        out_specs=(
            pl.BlockSpec((feat_rows, 4 * part), lambda i: (0, 0)),
            pl.BlockSpec((64, 4 * part), lambda i: (0, 0)),
            pl.BlockSpec((1, 256, 4 * part), lambda i: (0, 0, 0)),
        ),
        input_output_aliases={5: 2},
        compiler_params=kernel_params(),
    )(clip_at[None], *pieces, earlier)


def pack_kernel(by_rows, count, at_ref, *refs):
    parts, outs = refs[:count], refs[count:]
    for clip in range(4):

        @pl.when(at_ref[0] == clip)
        def _(clip=clip):
            for step in range(4):
                place, start = (clip + step) % 4, 0
                for part in parts:
                    size = part.shape[1] // 4
                    value = part[:, place * size : (place + 1) * size]
                    if by_rows:
                        outs[step][start : start + part.shape[0], :] = value
                        start += part.shape[0]
                    else:
                        outs[step][:, start : start + size] = value
                        start += size


def pack_parts(clip_at, parts, by_rows, after):
    sizes = [part.shape[1] // 4 for part in parts]
    if by_rows:
        shape = (sum(part.shape[0] for part in parts), sizes[0])
    else:
        shape = (parts[0].shape[0], sum(sizes))
    return call_kernel(
        functools.partial(pack_kernel, by_rows, len(parts)),
        (clip_at[None], *parts),
        (0,),
        tuple(jax.ShapeDtypeStruct(shape, low_type) for _ in range(4)),
        [],
        0,
        0,
        after,
    )


def place_heads_kernel(at_ref, all_ref, *refs):
    out_ref = refs[-1]
    for place in range(4):
        piece = all_ref[place].astype(wide_type)
        for at, part in ((1, 0), (2, 1), (0, 2)):
            out_ref[0, at, :, head_cols(place)] = piece[:, head_cols(part)]


def place_heads(clip_at, layer, levels, joined, earlier, after):
    rows = joined.shape[1]
    tile = 256
    count = 2
    return pl.pallas_call(
        without(place_heads_kernel, count, (*earlier, *after)),
        grid=(rows // tile,),
        out_shape=jax.ShapeDtypeStruct((levels, 3, rows, 4 * HEAD), wide_type),
        in_specs=[smem_spec(), pl.BlockSpec((4, tile, 3 * HEAD), lambda i: (0, i, 0))]
        + any_specs(earlier)
        + any_specs(after),
        out_specs=pl.BlockSpec((1, 3, tile, 4 * HEAD), lambda i: (layer, 0, i, 0)),
        input_output_aliases={count + at: at for at in range(len(earlier))},
        compiler_params=kernel_params(),
    )(clip_at[None], joined, *earlier, *after)


def stack_kernel(*refs):
    out_ref = refs[-1]
    for at, ref in enumerate(refs[:-1]):
        out_ref[8 * at : 8 * (at + 1), :] = ref[...]


def last_pack_kernel(at_ref, head_ref, patch_ref, small_a, small_b, *outs):
    heads, patches, small = head_ref.shape[0], patch_ref.shape[0], small_a.shape[0]
    values = small_a[...] + small_b[...]
    high = values.astype(low_type)
    rest = (values - high.astype(wide_type)).astype(low_type)
    for clip in range(4):

        @pl.when(at_ref[0] == clip)
        def _(clip=clip):
            for step in range(4):
                size = outs[step].shape[1]
                place = (clip + step) % 4
                columns = slice(place * size, (place + 1) * size)
                outs[step][:heads, :] = head_ref[:, columns]
                outs[step][heads : heads + patches, :] = patch_ref[:, columns]
                outs[step][heads + patches : heads + patches + small, :] = high[:, columns]
                outs[step][heads + patches + small :, :] = rest[:, columns]


def call_kernel(kernel, args, in_smem, outs, scratch, flops, exps, after=(), after_far=()):
    count = len(args)
    specs = [
        pl.BlockSpec(memory_space=pltpu.SMEM if at in in_smem else pltpu.VMEM)
        for at in range(count)
    ]
    specs += any_specs(after) + [pl.BlockSpec(memory_space=pltpu.HBM)] * len(after_far)
    after = (*after, *after_far)
    moved = sum(a.size * a.dtype.itemsize for a in args)
    return pl.pallas_call(
        without(kernel, count, after),
        out_shape=outs,
        in_specs=specs,
        out_specs=jax.tree.map(lambda _: pl.BlockSpec(memory_space=pltpu.VMEM), outs),
        scratch_shapes=scratch,
        compiler_params=kernel_params(),
        cost_estimate=pl.CostEstimate(flops=flops, bytes_accessed=moved, transcendentals=exps),
    )(*args, *after)


def on_device(
    features,
    cond_values,
    cond_live,
    in_weight,
    in_bias,
    act_weight,
    act_bias,
    state_weight,
    state_bias,
    attn_gain,
    attn_shift,
    qkv_weight,
    qkv_bias,
    proj_weight,
    proj_bias,
    mlp_gain,
    mlp_shift,
    up_weight,
    up_bias,
    down_weight,
    down_bias,
    out_grad,
):
    patch_rows = features.shape[2]
    feat_width = features.shape[3]
    slot_count = cond_values.shape[2]
    all_frames = cond_live.shape[1]
    model_width = in_weight.shape[1]
    width = qkv_weight.shape[3]
    heads = width // HEAD
    level_count = attn_gain.shape[0]
    patches = patch_rows // 4
    chunk_rows = patches + EXTRA
    rows = 4 * chunk_rows
    hidden_width = up_weight.shape[2]

    tensor_at = lax.axis_index("tensor")
    chip_at, core_at = tensor_at // 2, tensor_at % 2
    frame_at = lax.axis_index("frame")
    half_at, ring_at = frame_at // 4, frame_at % 4
    clip_at = lax.axis_index("clip")

    chunk_ids = [
        2 * jnp.bitwise_xor(core_at, core_step) + jnp.bitwise_xor(chip_at, chip_step)
        for core_step in range(2)
        for chip_step in range(2)
    ]
    own_chunk = chunk_ids[0]
    own_frames = jnp.stack([4 * half_at + (ring_at - step) % 4 for step in range(4)])
    cross_frames = jnp.stack([4 * (1 - half_at) + (ring_at - step) % 4 for step in range(4)])

    within = lax.broadcasted_iota(jnp.int32, (chunk_rows, 1), 0)
    is_patch = within < patches
    heights, columns = [], []
    for chunk_id in chunk_ids:
        patch_id = chunk_id * patches + within
        heights.append(jnp.where(is_patch, patch_id // GRID_W, 0))
        columns.append(jnp.where(is_patch, patch_id % GRID_W, 0))
    heights = jnp.concatenate(heights, axis=0).astype(wide_type)
    columns = jnp.concatenate(columns, axis=0).astype(wide_type)
    swap_table, rate_table = rotary_tables(HEAD, heads)
    swap_heads = jnp.asarray(swap_table)
    swap_one = jnp.asarray(swap_table[:HEAD, :HEAD])
    rates = rate_table[:, :HEAD]
    place_angles = heights * rates[1] + columns * rates[2]
    angles = jnp.concatenate(
        [
            own_frames[step].astype(wide_type) * rates[0][None, :] + place_angles
            for step in range(4)
        ],
        axis=0,
    )
    cosine_four, sine_four = jnp.cos(angles), jnp.sin(angles)
    head_from = jnp.arange(width)
    head_to = ((head_from // HEAD + ring_at) % 4) * HEAD + head_from % HEAD
    head_place = (head_to[:, None] == head_from[None, :]).astype(low_type)
    proj_turned = [
        lax.dynamic_slice_in_dim(
            jnp.concatenate([proj_weight[layer], proj_weight[layer]], axis=0),
            ring_at * HEAD,
            width,
            0,
        )
        for layer in range(level_count)
    ]
    ring_scalar = ring_at.astype(jnp.int32)
    clip_scalar = clip_at.astype(jnp.int32)

    live_all = cond_live[0].astype(wide_type)
    own_slots = lax.dynamic_index_in_dim(live_all, frame_at, 0, False)

    def live_rows(slots, chunk_id):
        picked = jnp.where(
            chunk_id < slot_count,
            lax.dynamic_index_in_dim(slots, jnp.minimum(chunk_id, slot_count - 1), 1, False),
            0.0,
        )
        return jnp.where(is_patch, 1.0, jnp.where(within == patches, picked[None, :], 0.0))

    sources = jnp.concatenate([own_frames, cross_frames])
    source_live = jnp.take(live_all, sources, axis=0)
    key_live = jnp.concatenate([live_rows(source_live, c) for c in chunk_ids], axis=0)
    reached = jnp.concatenate([jnp.ones((4,), jnp.bool_), jnp.full((4,), half_at == 1)])
    key_bias = jnp.where((key_live > 0.5) & reached[None, :], 0.0, masked_score).astype(wide_type)
    seen = own_frames[:, None] <= own_frames[None, :]
    causal = jnp.where(seen, 0.0, masked_score).astype(wide_type)
    causal = jnp.pad(jnp.repeat(causal, rows, axis=1), ((0, 4), (0, 0)))
    own_live = live_rows(own_slots[None, :], own_chunk)

    def extra_rows(slot_rows):
        picked = lax.dynamic_slice_in_dim(
            slot_rows, jnp.minimum(own_chunk, slot_count - 1), 1, 0
        )
        picked = jnp.where(own_chunk < slot_count, picked, jnp.zeros_like(picked))
        return jnp.pad(picked, ((0, EXTRA - 1), (0, 0)))

    cond_here = cond_values[0, 0]
    act_rows = jnp.dot(cond_here, act_weight, precision=highest_precision) + act_bias
    state_rows = jnp.dot(cond_here, state_weight, precision=highest_precision) + state_bias
    even_slot = (jnp.arange(slot_count) % 2 == 0)[:, None]
    cond_x = jnp.where(even_slot, act_rows, state_rows) * own_slots[:, None]

    flat_feat = jnp.concatenate(
        [
            lax.dynamic_slice_in_dim(features[0, 0], c * patches, patches, 0)
            for c in chunk_ids
        ],
        axis=0,
    )
    kept, got = halves_tensor(dot_wide(flat_feat, in_weight))
    stream = jnp.concatenate([kept + got + in_bias, extra_rows(cond_x)], axis=0)

    feat_wide = -(-feat_width // 128) * 128
    feat_low = jnp.pad(flat_feat, ((0, 0), (0, feat_wide - feat_width)))
    feats = [feat_low] + [
        lax.ppermute(feat_low, "clip", clip_shift(step)) for step in range(1, 4)
    ]
    pair_work = 2 * 32 * rows * rows * HEAD
    pair_exps = 32 * rows * rows
    weight_parts = [
        [qkv_weight[layer, :, at] for at in (1, 2, 0)] for layer in range(level_count)
    ]

    def norm(terms, gain, shift, after_far=()):
        chunk = jax.ShapeDtypeStruct((chunk_rows, model_width), wide_type)
        return call_kernel(
            norm_kernel,
            (gain[None], shift[None], *terms),
            (),
            (
                chunk,
                chunk,
                jax.ShapeDtypeStruct((chunk_rows, 128), wide_type),
                jax.ShapeDtypeStruct((chunk_rows, model_width), low_type),
            ),
            [],
            12 * chunk_rows * model_width,
            0,
            (),
            after_far,
        )

    def norm_back(part, gain, hat, inverse, grad, count, after=(), after_far=()):
        kept, got = halves_tensor(part)
        return call_kernel(
            functools.partial(norm_back_kernel, count),
            (kept, got, gain[None], hat, inverse, grad),
            (),
            (
                jax.ShapeDtypeStruct((chunk_rows, model_width), wide_type),
                jax.ShapeDtypeStruct((chunk_rows, model_width), low_type),
                jax.ShapeDtypeStruct((8, model_width), wide_type),
            ),
            [],
            16 * chunk_rows * model_width,
            0,
            after,
            after_far,
        )

    stored = []
    terms = (stream,)
    before = None
    for layer in range(level_count):
        stream, hat_one, inverse_one, first_chunk = norm(terms, attn_gain[layer], attn_shift[layer])
        first_in = join_rows_tensor(first_chunk)
        bias = jnp.pad(qkv_bias[layer], ((0, 5), (0, 0)))
        heads_out = call_kernel(
            functools.partial(project_kernel, heads),
            (
                ring_scalar[None],
                first_in,
                *weight_parts[layer],
                bias,
                cosine_four,
                sine_four,
                swap_heads,
            ),
            (0,),
            tuple(
                jax.ShapeDtypeStruct((rows, count * HEAD), low_type)
                for count in (3, 3, 3, 3, 2, 2, 2, 2)
            ),
            [],
            6 * rows * model_width * width,
            0,
            (),
            () if before is None else (before[0][0],),
        )
        blocks = to_heads(heads_out[:4])
        cross = pairs_to_later_half(heads_out[4:])
        attn_wide, attn_turned, log_total, own_all, cross_all = call_kernel(
            attend_kernel,
            (key_bias, causal, *blocks, *cross),
            (),
            (
                jax.ShapeDtypeStruct((4 * rows, HEAD), wide_type),
                jax.ShapeDtypeStruct((4 * rows, HEAD), low_type),
                jax.ShapeDtypeStruct((8, 4 * rows), wide_type),
                jax.ShapeDtypeStruct((4 * rows, 3 * HEAD), low_type),
                jax.ShapeDtypeStruct((4 * rows, 2 * HEAD), low_type),
            ),
            [
                pltpu.VMEM((4 * rows, HEAD), low_type),
                pltpu.VMEM((8 * rows, lane_tiles(4 * rows)[0].stop), wide_type),
            ],
            2 * pair_work,
            pair_exps,
            tuple(feats[1:]) if layer == 0 else (),
        )
        attn_relative = jnp.concatenate(
            to_frames([attn_turned[at * rows : (at + 1) * rows] for at in range(4)]), axis=1
        )
        attn_low = dot_wide(attn_relative, head_place).astype(low_type)
        if layer < level_count - 1:
            first_all = gather_clips(first_in, attn_low, ())
        kept, got = halves_tensor(dot_wide(attn_relative, proj_turned[layer]))
        middle, hat_two, inverse_two, second_chunk = norm(
            (stream, kept, got, proj_bias[layer][None]), mlp_gain[layer], mlp_shift[layer],
            () if before is None else (before[1][0],),
        )
        second_in = join_rows_tensor(second_chunk)
        hidden = dot_wide(second_in, up_weight[layer]) + up_bias[layer]
        active_low = exact_gelu(hidden).astype(low_type)
        second_all = gather_clips(second_in, active_low, ())
        if layer == level_count - 1:
            first_all = gather_clips(first_in, attn_low, (second_all[0],))
        before = (first_all, second_all)
        kept, got = halves_tensor(dot_wide(active_low, down_weight[layer]))
        terms = (middle, kept, got, down_bias[layer][None])
        stored.append(
            (
                hat_one,
                inverse_one,
                own_all,
                cross_all,
                log_total,
                attn_wide,
                hat_two,
                inverse_two,
                hidden,
                first_all,
                second_all,
            )
        )
    stream = terms[0] + (terms[1] + terms[2] + terms[3])

    def in_order(full, count):
        out = jnp.zeros((4 * count,) + full.shape[1:], full.dtype)
        size = full.shape[0] // 4
        for at, chunk_id in enumerate(chunk_ids):
            out = lax.dynamic_update_slice_in_dim(
                out, full[at * size : at * size + count], chunk_id * count, 0
            )
        return out

    block_full = join_rows_tensor((stream * own_live).astype(low_type))
    slot_full = jnp.concatenate(
        [
            block_full[at * chunk_rows + patches : at * chunk_rows + patches + 1]
            for at in range(4)
        ],
        axis=0,
    )
    block_out = jnp.concatenate(
        [in_order(block_full, patches), in_order(slot_full, 1)[:slot_count]], axis=0
    )[None, None]

    own_out = lax.dynamic_slice_in_dim(out_grad[0, 0], own_chunk * patches, patches, 0)
    grad_stream = (
        jnp.concatenate(
            [
                own_out.astype(wide_type),
                extra_rows(out_grad[0, 0, patch_rows:].astype(wide_type)),
            ],
            axis=0,
        )
        * own_live
    )

    small = {}
    branch_chunk = grad_stream.astype(low_type)
    small["down", level_count - 1] = jnp.sum(branch_chunk.astype(wide_type), axis=0)
    sums_list = []
    wide_part = model_width // 4
    later = None
    for layer in reversed(range(level_count)):
        (
            hat_one,
            inverse_one,
            own_all,
            cross_all,
            log_total,
            attn_wide,
            hat_two,
            inverse_two,
            hidden,
            first_all,
            second_all,
        ) = stored[layer]
        branch = join_rows_tensor(branch_chunk)
        _, gelu_pull = jax.vjp(exact_gelu, hidden)
        grad_hidden = gelu_pull(dot_dims(branch, down_weight[layer], 1, 1))[0].astype(low_type)
        small["up", layer] = jnp.sum(grad_hidden.astype(wide_type), axis=0)
        parts = [branch, grad_hidden] + ([] if later is None else [later["proj_out"]])
        packs = pack_parts(clip_scalar, parts, False, ())
        grad_middle, proj_chunk, sums = norm_back(
            dot_dims(grad_hidden, up_weight[layer], 1, 1),
            mlp_gain[layer],
            hat_two,
            inverse_two,
            grad_stream,
            chunk_rows,
            (packs[0],) if later is None else (packs[0], later["tall_total"], later["heads_sum"]),
        )
        sums_list.append(sums)
        packs = swap_clips(packs)
        proj_out = join_rows_tensor(proj_chunk)
        grad_attn = dot_dims(proj_out, proj_turned[layer], 1, 1).astype(low_type)
        grads = to_heads([grad_attn[:, head_cols(at)] for at in range(4)])

        if later is not None:
            later["heads_ring"] = ring_sum(
                ring_scalar, later["heads_sum"], later["heads_got"], (proj_chunk,)
            )

            later["tall_join"] = join_frames(ring_scalar, later["tall_total"], (proj_chunk,))

        def attend_back(own, after):
            return call_kernel(
                functools.partial(attend_back_kernel, own),
                (key_bias, causal, log_total, attn_wide, own_all, *grads)
                + (() if own else (cross_all,)),
                (),
                (
                    jax.ShapeDtypeStruct((4 * rows, 2 * HEAD), wide_type),
                    jax.ShapeDtypeStruct((4 * rows, HEAD), wide_type),
                ),
                [
                    pltpu.VMEM((4 * rows, HEAD), low_type),
                    pltpu.VMEM((4 * rows, HEAD), low_type),
                ],
                5 * pair_work // 2,
                pair_exps // 2,
                after,
            )

        cross_pair, cross_query = attend_back(
            False, () if later is None else (later["heads_ring"],)
        )
        got_pair = lax.ppermute(cross_pair, "frame", DOWN_HALF)
        tall_sum = layer_grad(
            clip_scalar,
            second_all,
            packs,
            None if later is None else later["first_all"],
            (cross_pair,),
        )
        own_pair, own_query = attend_back(True, (tall_sum,))
        tall_got = ring_sends(tall_sum, ring_at)
        if later is not None:
            later["heads_total"] = half_sum(later["heads_ring"], (own_pair,))
        turned = call_kernel(
            turn_back_kernel,
            (own_pair, got_pair, own_query, cross_query, cosine_four, sine_four, swap_one),
            (),
            tuple(jax.ShapeDtypeStruct((rows, 3 * HEAD), low_type) for _ in range(4)),
            [],
            24 * rows * HEAD * HEAD,
            0,
            () if later is None else (later["heads_total"], later["tall_join"]),
        )
        mixed = to_frames(list(turned))
        tall_ring = ring_sum(ring_scalar, tall_sum, tall_got, (turned[0],))
        if later is not None:
            later["tall_all"] = lax.all_gather(later["tall_join"], "clip")
            later["heads_join"] = join_frames(ring_scalar, later["heads_total"], (turned[0],))
        normed_part, mixed_stack, bias_sums = call_kernel(
            mix_back_kernel,
            (
                jnp.stack([ring_scalar, clip_scalar]),
                head_place,
                *weight_parts[layer],
                *mixed,
            ),
            (0,),
            (
                jax.ShapeDtypeStruct((rows, model_width), wide_type),
                jax.ShapeDtypeStruct((4, rows, 3 * HEAD), low_type),
                jax.ShapeDtypeStruct((8, width), wide_type),
            ),
            [],
            6 * rows * model_width * width,
            0,
            (tall_ring,) if later is None else (tall_ring, later["heads_join"]),
            (block_full,) if later is None else (),
        )
        small["qkv", layer] = jnp.concatenate([bias_sums[2:3], bias_sums[:2]], axis=0)
        packs = swap_clips([mixed_stack[step] for step in range(4)])
        grad_stream, branch_chunk, sums = norm_back(
            normed_part,
            attn_gain[layer],
            hat_one,
            inverse_one,
            grad_middle,
            patches if layer == 0 else chunk_rows,
            tuple(packs[1:]),
            () if later is None else (later["tall_all"],),
        )
        sums_list.append(sums)
        tall_total = half_sum(tall_ring, (branch_chunk,))

        heads_sum = plain_grad(clip_scalar, first_all, packs, (branch_chunk,))
        heads_got = ring_sends(heads_sum, ring_at)
        if layer > 0:
            later = {
                "proj_out": proj_out,
                "first_all": first_all,
                "tall_total": tall_total,
                "heads_sum": heads_sum,
                "heads_got": heads_got,
            }

    patch_chunk = branch_chunk[:patches]
    grad_patch = join_rows_tensor(patch_chunk)
    grad_features = in_order(dot_dims(grad_patch, in_weight, 1, 1), patches)[None, None]
    slot_row = grad_stream[patches : patches + 1] * own_live[patches : patches + 1]
    own_cond = lax.dynamic_slice_in_dim(
        cond_here, jnp.minimum(own_chunk, slot_count - 1), 1, 0
    )
    slot_part = jnp.concatenate([own_cond.T * slot_row, slot_row], axis=0)
    here = own_chunk < slot_count
    is_act = here & (own_chunk % 2 == 0)
    is_state = here & (own_chunk % 2 == 1)
    act_part = jnp.where(is_act, slot_part, 0.0)
    state_part = jnp.where(is_state, slot_part, 0.0)

    def at_tensor(value, total):
        return lax.dynamic_update_slice(
            jnp.zeros((value.shape[0], total), wide_type),
            value,
            (0, tensor_at * value.shape[1]),
        )

    layers = range(level_count)
    qkv_rows = at_tensor(
        jnp.concatenate([small["qkv", layer] for layer in layers], axis=0), 4 * width
    )
    mixed_rows = jnp.concatenate(
        [qkv_rows, small["down", level_count - 1][None], jnp.zeros_like(qkv_rows[:1])], axis=0
    )
    ups = at_tensor(jnp.stack([small["up", layer] for layer in layers]), 4 * hidden_width)
    parts = [*sums_list, act_part, state_part, mixed_rows, ups.reshape(-1, model_width)]
    vector = call_kernel(
        stack_kernel,
        tuple(parts),
        (),
        jax.ShapeDtypeStruct((8 * len(parts), model_width), wide_type),
        [],
        0,
        0,
    )
    vector = vector + core_swap(vector)
    tall_join = join_frames(ring_scalar, tall_total, ())
    head_rows, patch_count, small_rows = proj_out.shape[0], grad_patch.shape[0], vector.shape[0]
    packs = call_kernel(
        last_pack_kernel,
        (clip_scalar[None], proj_out, grad_patch, vector, chip_swap(vector)),
        (0,),
        tuple(
            jax.ShapeDtypeStruct((head_rows + patch_count + 2 * small_rows, wide_part), low_type)
            for _ in range(4)
        ),
        [],
        0,
        0,
    )
    packs = swap_clips(packs)
    heads_ring = ring_sum(ring_scalar, heads_sum, heads_got, (packs[0],))
    later["heads_all"] = lax.all_gather(later["heads_join"], "clip")
    last_sum = last_grad(clip_scalar, first_all, feats, packs, (tall_join, heads_ring))
    last_ring = ring_sum(ring_scalar, last_sum, ring_sends(last_sum, ring_at), ())
    heads_total = half_sum(heads_ring, (last_sum,))
    heads_join = join_frames(ring_scalar, heads_total, ())
    tall_all = lax.all_gather(tall_join, "clip")
    heads_all = lax.all_gather(heads_join, "clip")
    last_join = join_frames(ring_scalar, half_sum(last_ring, ()), (), (tall_all,))
    last_pieces = clip_pieces(last_join)
    placed = place_layer(
        clip_scalar, level_count - 1, level_count, later["tall_all"], (), 0, (packs[0],)
    )
    grad_down, grad_up, grad_proj = place_layer(
        clip_scalar, 0, level_count, tall_all, placed, level_count - 1, ()
    )
    grad_in, vector, grad_proj = place_last(
        clip_scalar, feat_width, feat_wide, level_count, last_pieces, grad_proj
    )
    grad_heads = place_heads(
        clip_scalar, level_count - 1, level_count, later["heads_all"], (), (last_sum,)
    )
    grad_heads = (place_heads(clip_scalar, 0, level_count, heads_all, (grad_heads,), ()),)


    def norm_sums(layer, first, row):
        return vector[8 * (2 * (level_count - 1 - layer) + first) + row]

    grad_mlp_gain = jnp.stack([norm_sums(layer, 0, 0) for layer in layers])
    grad_mlp_shift = jnp.stack([norm_sums(layer, 0, 1) for layer in layers])
    grad_proj_bias = jnp.stack([norm_sums(layer, 0, 2) for layer in layers])
    grad_attn_gain = jnp.stack([norm_sums(layer, 1, 0) for layer in layers])
    grad_attn_shift = jnp.stack([norm_sums(layer, 1, 1) for layer in layers])
    rest = vector[16 * level_count :]
    grad_down_bias = jnp.stack(
        [norm_sums(layer + 1, 1, 2) for layer in range(level_count - 1)]
        + [rest[16 + 3 * level_count]]
    )
    grad_qkv_bias = lax.dynamic_slice_in_dim(
        rest[16 : 16 + 3 * level_count], tensor_at * width, width, 1
    )
    grad_qkv_bias = grad_qkv_bias.reshape(level_count, 3, width)
    grad_up_bias = lax.dynamic_slice_in_dim(
        rest[24:].reshape(level_count, 4 * hidden_width), tensor_at * hidden_width, hidden_width, 1
    )
    act_count = cond_here.shape[1]
    return (
        block_out,
        grad_features,
        grad_in,
        norm_sums(0, 1, 2),
        rest[:act_count],
        rest[act_count],
        rest[8 : 8 + act_count],
        rest[8 + act_count],
        grad_attn_gain,
        grad_attn_shift,
        jnp.swapaxes(grad_heads[0], 1, 2),
        grad_qkv_bias,
        grad_proj,
        grad_proj_bias,
        grad_mlp_gain,
        grad_mlp_shift,
        grad_up,
        grad_up_bias,
        grad_down,
        grad_down_bias,
    )


def solution(mesh):
    return jax.shard_map(
        on_device,
        mesh=mesh,
        in_specs=(
            P("clip", "frame", None, "tensor"),
            P("clip", "frame", None, None),
            P("clip", None, None),
            P("tensor", None),
            P(),
            P(),
            P(),
            P(),
            P(),
            P(),
            P(),
            P(None, None, None, "tensor"),
            P(None, None, "tensor"),
            P(None, "tensor", None),
            P(),
            P(),
            P(),
            P(None, None, "tensor"),
            P(None, "tensor"),
            P(None, "tensor", None),
            P(),
            P("clip", "frame", None, None),
        ),
        out_specs=(
            P("clip", "frame", None, None),
            P("clip", "frame", None, "tensor"),
            P("tensor", None),
            P(),
            P(),
            P(),
            P(),
            P(),
            P(),
            P(),
            P(None, None, None, "tensor"),
            P(None, None, "tensor"),
            P(None, "tensor", None),
            P(),
            P(),
            P(),
            P(None, None, "tensor"),
            P(None, "tensor"),
            P(None, "tensor", None),
            P(),
        ),
        check_vma=False,
    )
```

```python
import functools

import jax
import jax.numpy as jnp
import numpy as np
from jax import lax
from jax.experimental import pallas as pl
from jax.experimental.pallas import tpu as pltpu
from jax.sharding import PartitionSpec as P

HEAD = 64
GRID_W = 16
EXTRA = 8

highest_precision = lax.Precision.HIGHEST
norm_epsilon = 1e-06
masked_score = -1000000000.0
low_type = jnp.bfloat16
wide_type = jnp.float32

CORE_SWAP = [(0, 1), (1, 0), (2, 3), (3, 2)]
CHIP_SWAP = [(0, 2), (2, 0), (1, 3), (3, 1)]
HALF_SWAP = [(i, (i + 4) % 8) for i in range(8)]


def clip_shift(step):
    return [(i, (i + step) % 4) for i in range(4)]


def frame_shift(halves, step):
    return [
        (4 * half + i, 4 * ((half + halves) % 2) + (i + step) % 4)
        for half in range(2)
        for i in range(4)
    ]


def core_swap(value):
    return lax.ppermute(value, "tensor", CORE_SWAP)


def chip_swap(value):
    return lax.ppermute(value, "tensor", CHIP_SWAP)


def halves_tensor(part):
    half = part.shape[0] // 2
    pair = part[:half] + core_swap(part[half:])
    quarter = half // 2
    return pair[:quarter], chip_swap(pair[quarter:])


def join_rows_tensor(chunk):
    pair = jnp.concatenate([chunk, chip_swap(chunk)], axis=0)
    return jnp.concatenate([pair, core_swap(pair)], axis=0)


def to_heads(blocks):
    return [blocks[0]] + [
        lax.ppermute(blocks[step], "frame", frame_shift(0, step)) for step in range(1, 4)
    ]


def to_frames(blocks):
    return [blocks[0]] + [
        lax.ppermute(blocks[step], "frame", frame_shift(0, -step)) for step in range(1, 4)
    ]


def pairs_to_later_half(blocks):
    return [
        lax.ppermute(
            blocks[step],
            "frame",
            [(src, dst) for src, dst in frame_shift(1, step) if src < dst],
        )
        for step in range(4)
    ]


DOWN_HALF = [(i + 4, i) for i in range(4)]


def swap_clips(packs):
    return [packs[0]] + [
        lax.ppermute(packs[step], "clip", clip_shift(step)) for step in range(1, 4)
    ]


def ring_pieces(value):
    return [value] + [
        lax.ppermute(value, "frame", frame_shift(0, step)) for step in range(1, 4)
    ]


def ring_sends(part, ring):
    block = part.shape[0] // 4
    got = []
    for step in range(1, 4):
        sent = lax.dynamic_slice_in_dim(part, ((ring + step) % 4) * block, block, 0)
        got.append(lax.ppermute(sent.astype(low_type), "frame", frame_shift(0, step)))
    return got


def clip_pieces(joined):
    return [joined] + [
        lax.ppermute(joined, "clip", clip_shift(step)) for step in range(1, 4)
    ]


def rotary_tables(head_size, head_count):
    group_size = 2 * (head_size // 3 // 2)
    half_size = group_size // 2
    total_width = head_size * head_count
    swap_table = np.zeros((total_width, total_width), np.float32)
    rate_table = np.zeros((3, total_width), np.float32)
    for head_at in range(head_count):
        for axis_at in range(3):
            for pair_at in range(half_size):
                lower_at = head_at * head_size + axis_at * group_size + pair_at
                upper_at = lower_at + half_size
                swap_table[upper_at, lower_at] = -1.0
                swap_table[lower_at, upper_at] = 1.0
                rate_value = 10000.0 ** (-2.0 * pair_at / group_size)
                rate_table[axis_at, lower_at] = rate_value
                rate_table[axis_at, upper_at] = rate_value
    return swap_table, rate_table


def norm_rows(values):
    row_mean = jnp.mean(values, axis=-1, keepdims=True)
    centred = values - row_mean
    spread = jnp.mean(centred * centred, axis=-1, keepdims=True)
    inverse = lax.rsqrt(spread + norm_epsilon)
    return centred * inverse, inverse


def norm_kernel(gain_ref, shift_ref, *refs):
    terms, (stream_ref, hat_ref, inverse_ref, low_ref) = refs[:-4], refs[-4:]
    values = terms[0][...]
    if len(terms) > 1:
        values = values + (terms[1][...] + terms[2][...] + terms[3][...])
    hat, inverse = norm_rows(values)
    stream_ref[...] = values
    hat_ref[...] = hat
    inverse_ref[...] = jnp.broadcast_to(inverse, inverse_ref.shape)
    low_ref[...] = (hat * gain_ref[...] + shift_ref[...]).astype(low_type)


def block_kernel(stream_ref, kept_ref, got_ref, bias_ref, live_ref, out_ref):
    values = stream_ref[...] + (kept_ref[...] + got_ref[...] + bias_ref[...])
    out_ref[...] = (values * live_ref[:, 0:1]).astype(low_type)


def norm_back_kernel(count, kept_ref, got_ref, gain_ref, hat_ref, inverse_ref, grad_ref, out_ref, low_ref, sums_ref):
    grad = kept_ref[...] + got_ref[...]
    hat = hat_ref[...]
    scaled = grad * gain_ref[...]
    first = jnp.mean(scaled, axis=-1, keepdims=True)
    second = jnp.mean(scaled * hat, axis=-1, keepdims=True)
    out = grad_ref[...] + (scaled - first - hat * second) * inverse_ref[:, 0:1]
    low = out.astype(low_type)
    out_ref[...] = out
    low_ref[...] = low
    sums_ref[...] = jnp.zeros_like(sums_ref)
    sums_ref[0:1, :] = jnp.sum(grad * hat, axis=0, keepdims=True)
    sums_ref[1:2, :] = jnp.sum(grad, axis=0, keepdims=True)
    sums_ref[2:3, :] = jnp.sum(low[:count].astype(wide_type), axis=0, keepdims=True)


def exact_gelu(values):
    return jax.nn.gelu(values, approximate=False)


def dot_wide(left, right):
    return jnp.dot(left, right, preferred_element_type=wide_type)


def dot_dims(left, right, left_dim, right_dim):
    return lax.dot_general(
        left, right, (((left_dim,), (right_dim,)), ((), ())), preferred_element_type=wide_type
    )


def head_cols(at):
    return slice(at * HEAD, (at + 1) * HEAD)


def ring_back(place, step):
    return lax.rem(place - step + 4, 4)


def ring_ahead(place, step):
    return lax.rem(place + step, 4)


def project_kernel(heads, at_ref, rows_ref, key_w, value_w, query_w, bias_ref, cos_ref, sin_ref, swap_ref, *out_refs):
    rows = rows_ref[...]
    swap = swap_ref[...]
    cosine = jnp.concatenate([cos_ref[: rows.shape[0], :]] * heads, axis=1)
    sine = jnp.concatenate([sin_ref[: rows.shape[0], :]] * heads, axis=1)

    def turned(weight, bias):
        value = dot_wide(rows, weight[...]) + bias
        crossed = jnp.dot(value, swap, precision=highest_precision, preferred_element_type=wide_type)
        return value * cosine + crossed * sine

    key = turned(key_w, bias_ref[1:2, :]).astype(low_type)
    value = (dot_wide(rows, value_w[...]) + bias_ref[2:3, :]).astype(low_type)
    query = (turned(query_w, bias_ref[0:1, :]).astype(low_type).astype(wide_type) * HEAD ** (-0.5)).astype(low_type)

    def write(head, step):
        for at, part in enumerate((key, value, query)):
            out_refs[step][:, head_cols(at)] = part[:, head_cols(head)]
            if at < 2:
                out_refs[4 + step][:, head_cols(at)] = part[:, head_cols(head)]

    for ring in range(4):

        @pl.when(at_ref[0] == ring)
        def _(ring=ring):
            for step in range(4):
                write((ring + step) % 4, step)


def lane_tiles(total):
    size = 384 if total % 384 == 0 else total
    return [slice(at * size, (at + 1) * size) for at in range(total // size)]


def attend_kernel(bias_ref, mask_ref, *refs):
    own_refs, cross_refs = refs[:4], refs[4:8]
    out_ref, low_ref, total_ref, own_out, cross_out, query_ref, score_ref = refs[8:]
    rows = own_refs[0].shape[0]
    total_rows = 4 * rows
    for at in range(4):
        block = slice(at * rows, (at + 1) * rows)
        query_ref[block, :] = own_refs[at][:, head_cols(2)]
        own_out[block, :] = own_refs[at][...]
        cross_out[block, :] = cross_refs[at][...]
    total_ref[...] = jnp.zeros_like(total_ref)

    def pair(at, part):
        if at < 4:
            return own_refs[at][:, head_cols(part)]
        return cross_refs[at - 4][:, head_cols(part)]

    for tile in lane_tiles(total_rows):
        query = query_ref[tile, :]
        wide = tile.stop - tile.start
        top = jnp.full((1, wide), 2.0 * masked_score, wide_type)
        for at in range(8):
            scores = dot_dims(pair(at, 0), query, 1, 1) + bias_ref[:, at : at + 1]
            if at < 4:
                scores = scores + mask_ref[at : at + 1, tile]
            score_ref[at * rows : (at + 1) * rows, :] = scores
            top = jnp.maximum(top, jnp.max(scores, axis=0, keepdims=True))
        mass = jnp.zeros((1, wide), wide_type)
        out = jnp.zeros((HEAD, wide), wide_type)
        for at in range(8):
            weights = jnp.exp(score_ref[at * rows : (at + 1) * rows, :] - top)
            mass = mass + jnp.sum(weights, axis=0, keepdims=True)
            out = out + dot_dims(pair(at, 1), weights.astype(low_type), 0, 0)
        total_ref[0:1, tile] = top + jnp.log(mass)
        rows_out = (out / mass).T
        out_ref[tile, :] = rows_out
        low_ref[tile, :] = rows_out.astype(low_type)


def attend_back_kernel(own, bias_ref, mask_ref, total_ref, out_ref, own_ref, *refs):
    grad_refs, cross_refs = refs[:4], refs[4:-4]
    pair_sum, query_sum, query_ref, grad_ref = refs[-4:]
    rows = grad_refs[0].shape[0]
    query_ref[...] = own_ref[:, head_cols(2)]
    for at in range(4):
        grad_ref[at * rows : (at + 1) * rows, :] = grad_refs[at][...]
    ones = jnp.ones((8, HEAD), wide_type)
    pair_sum[...] = jnp.zeros_like(pair_sum)
    for tile in lane_tiles(4 * rows):
        query = query_ref[tile, :]
        grad = grad_ref[tile, :]
        centre = lax.dot_general(
            ones,
            grad.astype(wide_type) * out_ref[tile, :],
            (((1,), (1,)), ((), ())),
            precision=highest_precision,
            preferred_element_type=wide_type,
        )[0:1, :]
        total = total_ref[0:1, tile]
        query_part = jnp.zeros((HEAD, tile.stop - tile.start), wide_type)
        for at in range(4):
            block = slice(at * rows, (at + 1) * rows)
            if own:
                key, value = own_ref[block, head_cols(0)], own_ref[block, head_cols(1)]
                scores = dot_dims(key, query, 1, 1) + bias_ref[:, at : at + 1] + mask_ref[at : at + 1, tile]
            else:
                key, value = cross_refs[0][block, head_cols(0)], cross_refs[0][block, head_cols(1)]
                scores = dot_dims(key, query, 1, 1) + bias_ref[:, at + 4 : at + 5]
            weights = jnp.exp(scores - total)
            pair_sum[block, head_cols(1)] += dot_wide(weights.astype(low_type), grad)
            soft = dot_dims(value, grad, 1, 1)
            back = (weights * (soft - centre)).astype(low_type)
            pair_sum[block, head_cols(0)] += dot_wide(back, query)
            query_part = query_part + dot_dims(key, back, 0, 0)
        query_sum[tile, :] = query_part.T * HEAD ** (-0.5)


def turn_back_kernel(own_pair, other_pair, own_query, other_query, cos_ref, sin_ref, swap_ref, *out_refs):
    rows = out_refs[0].shape[0]
    swap = swap_ref[...]
    for at in range(4):
        block = slice(at * rows, (at + 1) * rows)
        cosine, sine = cos_ref[block, :], sin_ref[block, :]

        def turned(value):
            crossed = jnp.dot(value, swap, precision=highest_precision, preferred_element_type=wide_type)
            return (value * cosine - crossed * sine).astype(low_type)

        pair = own_pair[block, :] + other_pair[block, :]
        out_refs[at][:, head_cols(0)] = turned(pair[:, head_cols(0)])
        out_refs[at][:, head_cols(1)] = pair[:, head_cols(1)].astype(low_type)
        out_refs[at][:, head_cols(2)] = turned(own_query[block, :] + other_query[block, :])


def mix_back_kernel(at_ref, place_ref, key_w, value_w, query_w, *refs):
    mixed_refs = refs[:4]
    out_ref, stack_ref, bias_ref = refs[4:]
    ring, clip = at_ref[0], at_ref[1]
    place = place_ref[...]
    total = None
    bias_ref[...] = jnp.zeros_like(bias_ref)
    for part, weight in ((0, key_w), (1, value_w), (2, query_w)):
        relative = jnp.concatenate([ref[:, head_cols(part)] for ref in mixed_refs], axis=1)
        ordered = dot_wide(relative, place)
        bias_ref[part : part + 1, :] = jnp.sum(ordered, axis=0, keepdims=True)
        term = dot_dims(ordered.astype(low_type), weight[...], 1, 1)
        total = term if total is None else total + term
    out_ref[...] = total
    for at in range(4):
        stack_ref[lax.rem(ring + at - clip + 4, 4)] = mixed_refs[at][...]


def clip_products(at_ref, first_ref, second_ref, pack_refs, columns):
    out = None
    half = first_ref.shape[1]
    for step in range(4):
        place = ring_back(at_ref[0], step)
        pack = pack_refs[step]
        term = dot_dims(first_ref[place], pack[:half, columns], 0, 0)
        term = term + dot_dims(second_ref[place], pack[half : 2 * half, columns], 0, 0)
        out = term if out is None else out + term
    return out


def layer_grad_kernel(at_ref, act_a, act_b, norm_a, norm_b, *refs):
    head_refs, pack_refs, out_ref = refs[:-5], refs[-5:-1], refs[-1]
    part = out_ref.shape[1] // 2
    tiles = pl.num_programs(0) - (1 if head_refs else 0)

    @pl.when(pl.program_id(0) < tiles)
    def _():
        out_ref[:, :part] = clip_products(at_ref, act_a, act_b, pack_refs, slice(0, part))
        out_ref[:, part:] = clip_products(at_ref, norm_a, norm_b, pack_refs, slice(part, 2 * part))

    if head_refs:

        @pl.when(pl.program_id(0) == tiles)
        def _():
            columns = slice(2 * part, 3 * part)
            out_ref[:, :part] = clip_products(at_ref, head_refs[0], head_refs[2], pack_refs, columns)
            out_ref[:, part:] = clip_products(at_ref, head_refs[1], head_refs[3], pack_refs, columns)


def plain_grad_kernel(at_ref, rows_a, rows_b, *refs):
    pack_refs, out_ref = refs[:4], refs[4]
    out_ref[...] = clip_products(at_ref, rows_a, rows_b, pack_refs, slice(None))


def last_grad_kernel(tiles, at_ref, head_a, head_b, *refs):
    feat_refs, pack_refs, out_ref = refs[:4], refs[4:8], refs[8]
    head_rows = 2 * head_a.shape[1]
    feat_rows = head_rows + feat_refs[0].shape[0]

    @pl.when(pl.program_id(0) < tiles)
    def _():
        out = None
        for step in range(4):
            term = dot_dims(feat_refs[step][...], pack_refs[step][head_rows:feat_rows, :], 0, 0)
            out = term if out is None else out + term
        out_ref[...] = out

    @pl.when(pl.program_id(0) == tiles + 2)
    def _():
        out = None
        small = (pack_refs[0].shape[0] - feat_rows) // 2
        for step in range(4):
            high = pack_refs[step][feat_rows : feat_rows + small, :].astype(wide_type)
            term = high + pack_refs[step][feat_rows + small :, :].astype(wide_type)
            out = term if out is None else out + term
        high = out.astype(low_type).astype(wide_type)
        out_ref[:small, :] = high
        out_ref[small:, :] = out - high

    @pl.when((pl.program_id(0) >= tiles) & (pl.program_id(0) < tiles + 2))
    def _():
        out_ref[...] = clip_products(at_ref, head_a, head_b, pack_refs, slice(None))


def ring_sum_kernel(at_ref, part_ref, *refs):
    got_refs, out_ref = refs[:3], refs[3]
    block = out_ref.shape[0]
    out = part_ref[pl.ds(pl.multiple_of(at_ref[0] * block, 8), block), :]
    for got in got_refs:
        out = out + got[...].astype(wide_type)
    out_ref[...] = out


def ring_sum(ring_at, part, got, after):
    shape = (part.shape[0] // 4, part.shape[1])
    return call_kernel(
        ring_sum_kernel,
        (ring_at[None], part, *got),
        (0,),
        jax.ShapeDtypeStruct(shape, wide_type),
        [],
        4 * shape[0] * shape[1],
        0,
        after,
    )


def half_sum_kernel(own_ref, got_ref, out_ref):
    out_ref[...] = (own_ref[...] + got_ref[...]).astype(low_type)


def half_sum(own, after):
    got = lax.ppermute(own, "frame", HALF_SWAP)
    return call_kernel(
        half_sum_kernel,
        (own, got),
        (),
        jax.ShapeDtypeStruct(own.shape, low_type),
        [],
        own.size,
        0,
        after,
    )


def join_kernel(at_ref, *refs):
    out_ref = refs[4]
    block = refs[0].shape[0]
    for step in range(4):
        start = pl.multiple_of(ring_back(at_ref[0], step) * block, 16)
        out_ref[pl.ds(start, block), :] = refs[step][...]


def join_frames(ring_at, total, after, after_far=()):
    pieces = ring_pieces(total)
    return call_kernel(
        join_kernel,
        (ring_at[None], *pieces),
        (0,),
        jax.ShapeDtypeStruct((4 * total.shape[0], total.shape[1]), low_type),
        [],
        0,
        0,
        after,
        after_far,
    )


def beside_kernel(first_ref, second_ref, out_ref):
    half, wide, other = first_ref.shape[0] // 2, first_ref.shape[1], second_ref.shape[1]
    out_ref[:, :wide] = first_ref[:half, :]
    out_ref[:, wide : wide + other] = second_ref[:half, :]
    out_ref[:, wide + other :] = second_ref[half:, :]


def gather_clips(first, second, after):
    half, wide = first.shape[0] // 2, first.shape[1]
    beside = call_kernel(
        beside_kernel,
        (first, second),
        (),
        jax.ShapeDtypeStruct((half, wide + 2 * second.shape[1]), low_type),
        [],
        0,
        0,
        after,
    )
    whole = lax.all_gather(beside, "clip")
    return whole, core_swap(whole[:, :, :wide])


def smem_spec():
    return pl.BlockSpec(memory_space=pltpu.SMEM)


def kernel_params():
    return pltpu.CompilerParams(vmem_limit_bytes=48 * 1024 * 1024)


def held_spec():
    return pl.BlockSpec(memory_space=pltpu.VMEM)


def any_specs(arrays):
    return [pl.BlockSpec(memory_space=pl.ANY)] * len(arrays)


def without(kernel, count, after):
    return lambda *refs: kernel(*refs[:count], *refs[count + len(after) :])


def layer_grad(clip_at, second_all, packs, first_all, after):
    whole, other = second_all
    half, wide = other.shape[1:]
    tiles = wide // 128
    part = 256
    block = (4, half, 128)
    heads = () if first_all is None else (first_all[0],) * 4
    held = [
        pl.BlockSpec(block, lambda i, at=at: (0, 0, tiles + at)) for at in range(len(heads))
    ]

    def moving(start):
        return pl.BlockSpec(block, lambda i: (0, 0, start + jnp.minimum(i, tiles - 1)))

    return pl.pallas_call(
        without(layer_grad_kernel, 9 + len(heads), after),
        grid=(tiles + (1 if heads else 0),),
        out_shape=jax.ShapeDtypeStruct((wide + (128 if heads else 0), 2 * part), wide_type),
        in_specs=[smem_spec(), moving(tiles), moving(2 * tiles), moving(0), moving(0)]
        + held
        + [held_spec()] * 4
        + any_specs(after),
        out_specs=pl.BlockSpec((128, 2 * part), lambda i: (i, 0)),
        compiler_params=kernel_params(),
        cost_estimate=pl.CostEstimate(
            flops=32 * half * wide * part,
            bytes_accessed=2 * whole.size + 8 * wide * part,
            transcendentals=0,
        ),
    )(clip_at[None], whole, whole, whole, other, *heads, *packs, *after)


def plain_grad(clip_at, rows_all, packs, after):
    whole, other = rows_all
    half, count = other.shape[1:]
    part = packs[0].shape[1]
    block = pl.BlockSpec((4, half, 128), lambda i: (0, 0, i))
    return pl.pallas_call(
        without(plain_grad_kernel, 7, after),
        grid=(count // 128,),
        out_shape=jax.ShapeDtypeStruct((count, part), wide_type),
        in_specs=[smem_spec(), block, block] + [held_spec()] * 4 + any_specs(after),
        out_specs=pl.BlockSpec((128, part), lambda i: (i, 0)),
        compiler_params=kernel_params(),
        cost_estimate=pl.CostEstimate(
            flops=16 * half * count * part,
            bytes_accessed=16 * half * count + 4 * count * part,
            transcendentals=0,
        ),
    )(clip_at[None], whole, other, *packs, *after)


def last_grad(clip_at, first_all, feats, packs, after, after_far):
    whole, other = first_all
    half, part = other.shape[1], packs[0].shape[1]
    first_block = other.shape[2] // 128
    tiles = feats[0].shape[1] // 128
    kernel = functools.partial(last_grad_kernel, tiles)

    def moving(start):
        return pl.BlockSpec(
            (4, half, 128), lambda i: (0, 0, start + jnp.clip(i - tiles, 0, 1))
        )

    return pl.pallas_call(
        without(kernel, 11, (*after, *after_far)),
        grid=(tiles + 3,),
        out_shape=jax.ShapeDtypeStruct(((tiles + 3) * 128, part), wide_type),
        in_specs=[smem_spec(), moving(first_block), moving(first_block + 2)]
        + [pl.BlockSpec((feats[0].shape[0], 128), lambda i: (0, jnp.minimum(i, tiles - 1)))] * 4
        + [held_spec()] * 4
        + any_specs(after)
        + [pl.BlockSpec(memory_space=pltpu.HBM)] * len(after_far),
        out_specs=pl.BlockSpec((128, part), lambda i: (i, 0)),
        compiler_params=kernel_params(),
    )(clip_at[None], whole, whole, *feats, *packs, *after, *after_far)


def by_clip(clip_at, write):
    for place in range(4):

        @pl.when(clip_at == place)
        def _(place=place):
            for step in range(4):
                write((place - step) % 4, step)


def place_layer_kernel(tiles, at_ref, all_ref, *outs):
    part = all_ref.shape[2] // 2
    is_last = pl.program_id(0) == tiles

    for place in range(4):
        columns = slice(place * part, (place + 1) * part)
        left = all_ref[place, :, :part].astype(wide_type)
        right = all_ref[place, :, part:].astype(wide_type)

        @pl.when(jnp.logical_not(is_last))
        def _(columns=columns, left=left, right=right):
            outs[0][0, :, columns] = left
            outs[1][0, :, columns] = right

        if len(outs) > 2:

            @pl.when(is_last)
            def _(columns=columns, left=left, right=right):
                outs[2][0, : outs[2].shape[1] // 2, columns] = left
                outs[2][0, outs[2].shape[1] // 2 :, columns] = right


def place_layer(clip_at, layer, levels, joined, earlier, heads_layer, after):
    part = joined.shape[2] // 2
    rows = 4 * part
    tiles = rows // 128
    heads = joined.shape[1] > rows
    out = [(levels, rows, 4 * part)] * 2 + [(levels, 256, 4 * part)] * heads
    tall = pl.BlockSpec((1, 128, 4 * part), lambda i: (layer, jnp.minimum(i, tiles - 1), 0))
    wide = pl.BlockSpec((1, 256, 4 * part), lambda i: (heads_layer, 0, 0))
    return pl.pallas_call(
        without(functools.partial(place_layer_kernel, tiles), 2, (*earlier, *after)),
        grid=(tiles + (1 if heads else 0),),
        out_shape=tuple(jax.ShapeDtypeStruct(shape, wide_type) for shape in out),
        in_specs=[smem_spec(), pl.BlockSpec((4, 128, 2 * part), lambda i: (0, i, 0))]
        + any_specs(earlier)
        + any_specs(after),
        out_specs=(tall, tall) + ((wide,) if heads else ()),
        input_output_aliases={2 + at: at for at in range(len(earlier))},
        compiler_params=kernel_params(),
    )(clip_at[None], joined, *earlier, *after)


def place_last_kernel(skip, at_ref, *refs):
    pieces = refs[:4]
    in_ref, small_ref, proj_ref = refs[-3:]
    part = pieces[0].shape[1]
    heads = skip + proj_ref.shape[1]
    small = small_ref.shape[0]

    def write(place, step):
        columns = slice(place * part, (place + 1) * part)
        piece = pieces[step]
        in_ref[:, columns] = piece[: in_ref.shape[0], :].astype(wide_type)
        proj_ref[0, :, columns] = piece[skip:heads, :].astype(wide_type)
        small_ref[:, columns] = piece[heads : heads + small, :].astype(wide_type) + piece[
            heads + small :, :
        ].astype(wide_type)

    by_clip(at_ref[0], write)


def place_last(clip_at, feat_rows, skip, levels, pieces, earlier):
    part = pieces[0].shape[1]
    return pl.pallas_call(
        functools.partial(place_last_kernel, skip),
        grid=(1,),
        out_shape=(
            jax.ShapeDtypeStruct((feat_rows, 4 * part), wide_type),
            jax.ShapeDtypeStruct((64, 4 * part), wide_type),
            jax.ShapeDtypeStruct((levels, 256, 4 * part), wide_type),
        ),
        in_specs=[smem_spec()]
        + [pl.BlockSpec(pieces[0].shape, lambda i: (0, 0))] * 4
        + [pl.BlockSpec(memory_space=pl.ANY)],
        out_specs=(
            pl.BlockSpec((feat_rows, 4 * part), lambda i: (0, 0)),
            pl.BlockSpec((64, 4 * part), lambda i: (0, 0)),
            pl.BlockSpec((1, 256, 4 * part), lambda i: (0, 0, 0)),
        ),
        input_output_aliases={5: 2},
        compiler_params=kernel_params(),
    )(clip_at[None], *pieces, earlier)


def pack_kernel(by_rows, count, at_ref, *refs):
    parts, outs = refs[:count], refs[count:]
    for clip in range(4):

        @pl.when(at_ref[0] == clip)
        def _(clip=clip):
            for step in range(4):
                place, start = (clip + step) % 4, 0
                for part in parts:
                    size = part.shape[1] // 4
                    value = part[:, place * size : (place + 1) * size]
                    if by_rows:
                        outs[step][start : start + part.shape[0], :] = value
                        start += part.shape[0]
                    else:
                        outs[step][:, start : start + size] = value
                        start += size


def pack_parts(clip_at, parts, by_rows, after):
    sizes = [part.shape[1] // 4 for part in parts]
    if by_rows:
        shape = (sum(part.shape[0] for part in parts), sizes[0])
    else:
        shape = (parts[0].shape[0], sum(sizes))
    return call_kernel(
        functools.partial(pack_kernel, by_rows, len(parts)),
        (clip_at[None], *parts),
        (0,),
        tuple(jax.ShapeDtypeStruct(shape, low_type) for _ in range(4)),
        [],
        0,
        0,
        after,
    )


def place_heads_kernel(at_ref, all_ref, *refs):
    out_ref = refs[-1]
    for place in range(4):
        piece = all_ref[place].astype(wide_type)
        for at, part in ((1, 0), (2, 1), (0, 2)):
            out_ref[0, at, :, head_cols(place)] = piece[:, head_cols(part)]


def place_heads(clip_at, layer, levels, joined, earlier, after):
    rows = joined.shape[1]
    tile = 256
    count = 2
    return pl.pallas_call(
        without(place_heads_kernel, count, (*earlier, *after)),
        grid=(rows // tile,),
        out_shape=jax.ShapeDtypeStruct((levels, 3, rows, 4 * HEAD), wide_type),
        in_specs=[smem_spec(), pl.BlockSpec((4, tile, 3 * HEAD), lambda i: (0, i, 0))]
        + any_specs(earlier)
        + any_specs(after),
        out_specs=pl.BlockSpec((1, 3, tile, 4 * HEAD), lambda i: (layer, 0, i, 0)),
        input_output_aliases={count + at: at for at in range(len(earlier))},
        compiler_params=kernel_params(),
    )(clip_at[None], joined, *earlier, *after)


def stack_kernel(*refs):
    out_ref = refs[-1]
    for at, ref in enumerate(refs[:-1]):
        out_ref[8 * at : 8 * (at + 1), :] = ref[...]


def last_pack_kernel(at_ref, head_ref, patch_ref, small_a, small_b, *outs):
    heads, patches, small = head_ref.shape[0], patch_ref.shape[0], small_a.shape[0]
    values = small_a[...] + small_b[...]
    high = values.astype(low_type)
    rest = (values - high.astype(wide_type)).astype(low_type)
    for clip in range(4):

        @pl.when(at_ref[0] == clip)
        def _(clip=clip):
            for step in range(4):
                size = outs[step].shape[1]
                place = (clip + step) % 4
                columns = slice(place * size, (place + 1) * size)
                outs[step][:heads, :] = head_ref[:, columns]
                outs[step][heads : heads + patches, :] = patch_ref[:, columns]
                outs[step][heads + patches : heads + patches + small, :] = high[:, columns]
                outs[step][heads + patches + small :, :] = rest[:, columns]


def call_kernel(kernel, args, in_smem, outs, scratch, flops, exps, after=(), after_far=()):
    count = len(args)
    specs = [
        pl.BlockSpec(memory_space=pltpu.SMEM if at in in_smem else pltpu.VMEM)
        for at in range(count)
    ]
    specs += any_specs(after) + [pl.BlockSpec(memory_space=pltpu.HBM)] * len(after_far)
    after = (*after, *after_far)
    moved = sum(a.size * a.dtype.itemsize for a in args)
    return pl.pallas_call(
        without(kernel, count, after),
        out_shape=outs,
        in_specs=specs,
        out_specs=jax.tree.map(lambda _: pl.BlockSpec(memory_space=pltpu.VMEM), outs),
        scratch_shapes=scratch,
        compiler_params=kernel_params(),
        cost_estimate=pl.CostEstimate(flops=flops, bytes_accessed=moved, transcendentals=exps),
    )(*args, *after)


def on_device(
    features,
    cond_values,
    cond_live,
    in_weight,
    in_bias,
    act_weight,
    act_bias,
    state_weight,
    state_bias,
    attn_gain,
    attn_shift,
    qkv_weight,
    qkv_bias,
    proj_weight,
    proj_bias,
    mlp_gain,
    mlp_shift,
    up_weight,
    up_bias,
    down_weight,
    down_bias,
    out_grad,
):
    patch_rows = features.shape[2]
    feat_width = features.shape[3]
    slot_count = cond_values.shape[2]
    all_frames = cond_live.shape[1]
    model_width = in_weight.shape[1]
    width = qkv_weight.shape[3]
    heads = width // HEAD
    level_count = attn_gain.shape[0]
    patches = patch_rows // 4
    chunk_rows = patches + EXTRA
    rows = 4 * chunk_rows
    hidden_width = up_weight.shape[2]

    tensor_at = lax.axis_index("tensor")
    chip_at, core_at = tensor_at // 2, tensor_at % 2
    frame_at = lax.axis_index("frame")
    half_at, ring_at = frame_at // 4, frame_at % 4
    clip_at = lax.axis_index("clip")

    chunk_ids = [
        2 * jnp.bitwise_xor(core_at, core_step) + jnp.bitwise_xor(chip_at, chip_step)
        for core_step in range(2)
        for chip_step in range(2)
    ]
    own_chunk = chunk_ids[0]
    own_frames = jnp.stack([4 * half_at + (ring_at - step) % 4 for step in range(4)])
    cross_frames = jnp.stack([4 * (1 - half_at) + (ring_at - step) % 4 for step in range(4)])

    within = lax.broadcasted_iota(jnp.int32, (chunk_rows, 1), 0)
    is_patch = within < patches
    heights, columns = [], []
    for chunk_id in chunk_ids:
        patch_id = chunk_id * patches + within
        heights.append(jnp.where(is_patch, patch_id // GRID_W, 0))
        columns.append(jnp.where(is_patch, patch_id % GRID_W, 0))
    heights = jnp.concatenate(heights, axis=0).astype(wide_type)
    columns = jnp.concatenate(columns, axis=0).astype(wide_type)
    swap_table, rate_table = rotary_tables(HEAD, heads)
    swap_heads = jnp.asarray(swap_table)
    swap_one = jnp.asarray(swap_table[:HEAD, :HEAD])
    rates = rate_table[:, :HEAD]
    place_angles = heights * rates[1] + columns * rates[2]
    angles = jnp.concatenate(
        [
            own_frames[step].astype(wide_type) * rates[0][None, :] + place_angles
            for step in range(4)
        ],
        axis=0,
    )
    cosine_four, sine_four = jnp.cos(angles), jnp.sin(angles)
    head_from = jnp.arange(width)
    head_to = ((head_from // HEAD + ring_at) % 4) * HEAD + head_from % HEAD
    head_place = (head_to[:, None] == head_from[None, :]).astype(low_type)
    proj_turned = [
        lax.dynamic_slice_in_dim(
            jnp.concatenate([proj_weight[layer], proj_weight[layer]], axis=0),
            ring_at * HEAD,
            width,
            0,
        )
        for layer in range(level_count)
    ]
    ring_scalar = ring_at.astype(jnp.int32)
    clip_scalar = clip_at.astype(jnp.int32)

    live_all = cond_live[0].astype(wide_type)
    own_slots = lax.dynamic_index_in_dim(live_all, frame_at, 0, False)

    def live_rows(slots, chunk_id):
        picked = jnp.where(
            chunk_id < slot_count,
            lax.dynamic_index_in_dim(slots, jnp.minimum(chunk_id, slot_count - 1), 1, False),
            0.0,
        )
        return jnp.where(is_patch, 1.0, jnp.where(within == patches, picked[None, :], 0.0))

    sources = jnp.concatenate([own_frames, cross_frames])
    source_live = jnp.take(live_all, sources, axis=0)
    key_live = jnp.concatenate([live_rows(source_live, c) for c in chunk_ids], axis=0)
    reached = jnp.concatenate([jnp.ones((4,), jnp.bool_), jnp.full((4,), half_at == 1)])
    key_bias = jnp.where((key_live > 0.5) & reached[None, :], 0.0, masked_score).astype(wide_type)
    seen = own_frames[:, None] <= own_frames[None, :]
    causal = jnp.where(seen, 0.0, masked_score).astype(wide_type)
    causal = jnp.pad(jnp.repeat(causal, rows, axis=1), ((0, 4), (0, 0)))
    own_live = live_rows(own_slots[None, :], own_chunk)

    def extra_rows(slot_rows):
        picked = lax.dynamic_slice_in_dim(
            slot_rows, jnp.minimum(own_chunk, slot_count - 1), 1, 0
        )
        picked = jnp.where(own_chunk < slot_count, picked, jnp.zeros_like(picked))
        return jnp.pad(picked, ((0, EXTRA - 1), (0, 0)))

    cond_here = cond_values[0, 0]
    act_rows = jnp.dot(cond_here, act_weight, precision=highest_precision) + act_bias
    state_rows = jnp.dot(cond_here, state_weight, precision=highest_precision) + state_bias
    even_slot = (jnp.arange(slot_count) % 2 == 0)[:, None]
    cond_x = jnp.where(even_slot, act_rows, state_rows) * own_slots[:, None]

    flat_feat = jnp.concatenate(
        [
            lax.dynamic_slice_in_dim(features[0, 0], c * patches, patches, 0)
            for c in chunk_ids
        ],
        axis=0,
    )
    kept, got = halves_tensor(dot_wide(flat_feat, in_weight))
    stream = jnp.concatenate([kept + got + in_bias, extra_rows(cond_x)], axis=0)

    feat_wide = -(-feat_width // 128) * 128
    feat_low = jnp.pad(flat_feat, ((0, 0), (0, feat_wide - feat_width)))
    feats = [feat_low] + [
        lax.ppermute(feat_low, "clip", clip_shift(step)) for step in range(1, 4)
    ]
    pair_work = 2 * 32 * rows * rows * HEAD
    pair_exps = 32 * rows * rows
    weight_parts = [
        [qkv_weight[layer, :, at] for at in (1, 2, 0)] for layer in range(level_count)
    ]

    def norm(terms, gain, shift, after_far=()):
        chunk = jax.ShapeDtypeStruct((chunk_rows, model_width), wide_type)
        return call_kernel(
            norm_kernel,
            (gain[None], shift[None], *terms),
            (),
            (
                chunk,
                chunk,
                jax.ShapeDtypeStruct((chunk_rows, 128), wide_type),
                jax.ShapeDtypeStruct((chunk_rows, model_width), low_type),
            ),
            [],
            12 * chunk_rows * model_width,
            0,
            (),
            after_far,
        )

    def norm_back(part, gain, hat, inverse, grad, count, after=(), after_far=()):
        kept, got = halves_tensor(part)
        return call_kernel(
            functools.partial(norm_back_kernel, count),
            (kept, got, gain[None], hat, inverse, grad),
            (),
            (
                jax.ShapeDtypeStruct((chunk_rows, model_width), wide_type),
                jax.ShapeDtypeStruct((chunk_rows, model_width), low_type),
                jax.ShapeDtypeStruct((8, model_width), wide_type),
            ),
            [],
            16 * chunk_rows * model_width,
            0,
            after,
            after_far,
        )

    stored = []
    terms = (stream,)
    before = None
    for layer in range(level_count):
        stream, hat_one, inverse_one, first_chunk = norm(terms, attn_gain[layer], attn_shift[layer])
        first_in = join_rows_tensor(first_chunk)
        bias = jnp.pad(qkv_bias[layer], ((0, 5), (0, 0)))
        heads_out = call_kernel(
            functools.partial(project_kernel, heads),
            (
                ring_scalar[None],
                first_in,
                *weight_parts[layer],
                bias,
                cosine_four,
                sine_four,
                swap_heads,
            ),
            (0,),
            tuple(
                jax.ShapeDtypeStruct((rows, count * HEAD), low_type)
                for count in (3, 3, 3, 3, 2, 2, 2, 2)
            ),
            [],
            6 * rows * model_width * width,
            0,
            (),
            () if before is None else (before[0][0],),
        )
        blocks = to_heads(heads_out[:4])
        cross = pairs_to_later_half(heads_out[4:])
        attn_wide, attn_turned, log_total, own_all, cross_all = call_kernel(
            attend_kernel,
            (key_bias, causal, *blocks, *cross),
            (),
            (
                jax.ShapeDtypeStruct((4 * rows, HEAD), wide_type),
                jax.ShapeDtypeStruct((4 * rows, HEAD), low_type),
                jax.ShapeDtypeStruct((8, 4 * rows), wide_type),
                jax.ShapeDtypeStruct((4 * rows, 3 * HEAD), low_type),
                jax.ShapeDtypeStruct((4 * rows, 2 * HEAD), low_type),
            ),
            [
                pltpu.VMEM((4 * rows, HEAD), low_type),
                pltpu.VMEM((8 * rows, lane_tiles(4 * rows)[0].stop), wide_type),
            ],
            2 * pair_work,
            pair_exps,
            tuple(feats[1:]) if layer == 0 else (),
        )
        attn_relative = jnp.concatenate(
            to_frames([attn_turned[at * rows : (at + 1) * rows] for at in range(4)]), axis=1
        )
        attn_low = dot_wide(attn_relative, head_place).astype(low_type)
        if layer < level_count - 1:
            first_all = gather_clips(first_in, attn_low, ())
        kept, got = halves_tensor(dot_wide(attn_relative, proj_turned[layer]))
        middle, hat_two, inverse_two, second_chunk = norm(
            (stream, kept, got, proj_bias[layer][None]), mlp_gain[layer], mlp_shift[layer],
            () if before is None else (before[1][0],),
        )
        second_in = join_rows_tensor(second_chunk)
        hidden = dot_wide(second_in, up_weight[layer]) + up_bias[layer]
        active_low = exact_gelu(hidden).astype(low_type)
        second_all = gather_clips(second_in, active_low, ())
        if layer == level_count - 1:
            first_all = gather_clips(first_in, attn_low, (second_all[0],))
        before = (first_all, second_all)
        kept, got = halves_tensor(dot_wide(active_low, down_weight[layer]))
        terms = (middle, kept, got, down_bias[layer][None])
        stored.append(
            (
                hat_one,
                inverse_one,
                own_all,
                cross_all,
                log_total,
                attn_wide,
                hat_two,
                inverse_two,
                hidden,
                first_all,
                second_all,
            )
        )
    def in_order(full, count):
        out = jnp.zeros((4 * count,) + full.shape[1:], full.dtype)
        size = full.shape[0] // 4
        for at, chunk_id in enumerate(chunk_ids):
            out = lax.dynamic_update_slice_in_dim(
                out, full[at * size : at * size + count], chunk_id * count, 0
            )
        return out

    def block_rows(after):
        low = call_kernel(
            block_kernel,
            (*terms, jnp.broadcast_to(own_live, (chunk_rows, 128))),
            (),
            jax.ShapeDtypeStruct((chunk_rows, model_width), low_type),
            [],
            4 * chunk_rows * model_width,
            0,
            after,
        )
        return join_rows_tensor(low)

    def block_in_order(block_full):
        slot_full = jnp.concatenate(
            [
                block_full[at * chunk_rows + patches : at * chunk_rows + patches + 1]
                for at in range(4)
            ],
            axis=0,
        )
        return jnp.concatenate(
            [in_order(block_full, patches), in_order(slot_full, 1)[:slot_count]], axis=0
        )[None, None]

    own_out = lax.dynamic_slice_in_dim(out_grad[0, 0], own_chunk * patches, patches, 0)
    grad_stream = (
        jnp.concatenate(
            [
                own_out.astype(wide_type),
                extra_rows(out_grad[0, 0, patch_rows:].astype(wide_type)),
            ],
            axis=0,
        )
        * own_live
    )

    small = {}
    small["down", level_count - 1] = jnp.sum(grad_stream, axis=0)
    slot_grads = out_grad[0, 0, patch_rows:] * own_slots[:, None].astype(low_type)
    slot_blocks = jnp.concatenate(
        [
            jnp.pad(slot_grads[:, None], ((0, 0), (0, EXTRA - 1), (0, 0))),
            jnp.zeros((4 - slot_count, EXTRA, model_width), low_type),
        ],
        axis=0,
    )
    branch_parts = []
    for chunk_id in chunk_ids:
        branch_parts.append(
            lax.dynamic_slice_in_dim(out_grad[0, 0], chunk_id * patches, patches, 0)
        )
        branch_parts.append(lax.dynamic_index_in_dim(slot_blocks, chunk_id, 0, False))
    first_branch = jnp.concatenate(branch_parts, axis=0)
    sums_list = []
    wide_part = model_width // 4
    later = None
    for layer in reversed(range(level_count)):
        (
            hat_one,
            inverse_one,
            own_all,
            cross_all,
            log_total,
            attn_wide,
            hat_two,
            inverse_two,
            hidden,
            first_all,
            second_all,
        ) = stored[layer]
        branch = first_branch if later is None else join_rows_tensor(branch_chunk)
        _, gelu_pull = jax.vjp(exact_gelu, hidden)
        grad_hidden = gelu_pull(dot_dims(branch, down_weight[layer], 1, 1))[0].astype(low_type)
        small["up", layer] = jnp.sum(grad_hidden.astype(wide_type), axis=0)
        parts = [branch, grad_hidden] + ([] if later is None else [later["proj_out"]])
        packs = pack_parts(clip_scalar, parts, False, ())
        grad_middle, proj_chunk, sums = norm_back(
            dot_dims(grad_hidden, up_weight[layer], 1, 1),
            mlp_gain[layer],
            hat_two,
            inverse_two,
            grad_stream,
            chunk_rows,
            (packs[0],) if later is None else (packs[0], later["tall_join"], later["heads_sum"]),
        )
        sums_list.append(sums)
        packs = swap_clips(packs)
        if later is None:
            block_full = block_rows((proj_chunk,))
            block_out = block_in_order(block_full)
        proj_out = join_rows_tensor(proj_chunk)
        grad_attn = dot_dims(proj_out, proj_turned[layer], 1, 1).astype(low_type)
        grads = to_heads([grad_attn[:, head_cols(at)] for at in range(4)])

        if later is not None:
            later["heads_ring"] = ring_sum(
                ring_scalar, later["heads_sum"], later["heads_got"], (proj_chunk,)
            )

            later["tall_all"] = lax.all_gather(later["tall_join"], "clip")

        def attend_back(own, after, after_far=()):
            return call_kernel(
                functools.partial(attend_back_kernel, own),
                (key_bias, causal, log_total, attn_wide, own_all, *grads)
                + (() if own else (cross_all,)),
                (),
                (
                    jax.ShapeDtypeStruct((4 * rows, 2 * HEAD), wide_type),
                    jax.ShapeDtypeStruct((4 * rows, HEAD), wide_type),
                ),
                [
                    pltpu.VMEM((4 * rows, HEAD), low_type),
                    pltpu.VMEM((4 * rows, HEAD), low_type),
                ],
                5 * pair_work // 2,
                pair_exps // 2,
                after,
                after_far,
            )

        cross_pair, cross_query = attend_back(
            False, () if later is None else (later["heads_ring"],)
        )
        got_pair = lax.ppermute(cross_pair, "frame", DOWN_HALF)
        tall_sum = layer_grad(
            clip_scalar,
            second_all,
            packs,
            None if later is None else later["first_all"],
            (cross_pair,),
        )
        own_pair, own_query = attend_back(
            True, (tall_sum,), () if later is None else (later["tall_all"],)
        )
        tall_got = ring_sends(tall_sum, ring_at)
        if later is not None:
            later["heads_total"] = half_sum(later["heads_ring"], (own_pair,))
        turned = call_kernel(
            turn_back_kernel,
            (own_pair, got_pair, own_query, cross_query, cosine_four, sine_four, swap_one),
            (),
            tuple(jax.ShapeDtypeStruct((rows, 3 * HEAD), low_type) for _ in range(4)),
            [],
            24 * rows * HEAD * HEAD,
            0,
            () if later is None else (later["heads_total"],),
        )
        mixed = to_frames(list(turned))
        tall_ring = ring_sum(ring_scalar, tall_sum, tall_got, (turned[0],))
        tall_total = half_sum(tall_ring, ())
        if later is not None:
            later["heads_join"] = join_frames(ring_scalar, later["heads_total"], (turned[0],))
        normed_part, mixed_stack, bias_sums = call_kernel(
            mix_back_kernel,
            (
                jnp.stack([ring_scalar, clip_scalar]),
                head_place,
                *weight_parts[layer],
                *mixed,
            ),
            (0,),
            (
                jax.ShapeDtypeStruct((rows, model_width), wide_type),
                jax.ShapeDtypeStruct((4, rows, 3 * HEAD), low_type),
                jax.ShapeDtypeStruct((8, width), wide_type),
            ),
            [],
            6 * rows * model_width * width,
            0,
            (tall_total,) if later is None else (tall_total, later["heads_join"]),
            (block_full,) if later is None else (),
        )
        small["qkv", layer] = jnp.concatenate([bias_sums[2:3], bias_sums[:2]], axis=0)
        packs = swap_clips([mixed_stack[step] for step in range(4)])
        grad_stream, branch_chunk, sums = norm_back(
            normed_part,
            attn_gain[layer],
            hat_one,
            inverse_one,
            grad_middle,
            patches if layer == 0 else chunk_rows,
            tuple(packs[1:]),
        )
        sums_list.append(sums)
        tall_join = join_frames(ring_scalar, tall_total, ())

        if layer > 0:
            heads_sum = plain_grad(clip_scalar, first_all, packs, (branch_chunk,))
            heads_got = ring_sends(heads_sum, ring_at)
        else:
            heads_packs = packs
        if layer > 0:
            later = {
                "proj_out": proj_out,
                "first_all": first_all,
                "tall_join": tall_join,
                "heads_sum": heads_sum,
                "heads_got": heads_got,
            }

    patch_chunk = branch_chunk[:patches]
    grad_patch = join_rows_tensor(patch_chunk)
    grad_features = in_order(dot_dims(grad_patch, in_weight, 1, 1), patches)[None, None]
    slot_row = grad_stream[patches : patches + 1] * own_live[patches : patches + 1]
    own_cond = lax.dynamic_slice_in_dim(
        cond_here, jnp.minimum(own_chunk, slot_count - 1), 1, 0
    )
    slot_part = jnp.concatenate([own_cond.T * slot_row, slot_row], axis=0)
    here = own_chunk < slot_count
    is_act = here & (own_chunk % 2 == 0)
    is_state = here & (own_chunk % 2 == 1)
    act_part = jnp.where(is_act, slot_part, 0.0)
    state_part = jnp.where(is_state, slot_part, 0.0)

    def at_tensor(value, total):
        return lax.dynamic_update_slice(
            jnp.zeros((value.shape[0], total), wide_type),
            value,
            (0, tensor_at * value.shape[1]),
        )

    layers = range(level_count)
    qkv_rows = at_tensor(
        jnp.concatenate([small["qkv", layer] for layer in layers], axis=0), 4 * width
    )
    mixed_rows = jnp.concatenate(
        [qkv_rows, small["down", level_count - 1][None], jnp.zeros_like(qkv_rows[:1])], axis=0
    )
    ups = at_tensor(jnp.stack([small["up", layer] for layer in layers]), 4 * hidden_width)
    parts = [*sums_list, act_part, state_part, mixed_rows, ups.reshape(-1, model_width)]
    vector = call_kernel(
        stack_kernel,
        tuple(parts),
        (),
        jax.ShapeDtypeStruct((8 * len(parts), model_width), wide_type),
        [],
        0,
        0,
    )
    vector = vector + core_swap(vector)
    later["heads_all"] = lax.all_gather(later["heads_join"], "clip")
    tall_all = lax.all_gather(tall_join, "clip")
    head_rows, patch_count, small_rows = proj_out.shape[0], grad_patch.shape[0], vector.shape[0]
    packs = call_kernel(
        last_pack_kernel,
        (clip_scalar[None], proj_out, grad_patch, vector, chip_swap(vector)),
        (0,),
        tuple(
            jax.ShapeDtypeStruct((head_rows + patch_count + 2 * small_rows, wide_part), low_type)
            for _ in range(4)
        ),
        [],
        0,
        0,
        (tall_join,),
        (later["heads_all"],),
    )
    heads_sum = plain_grad(clip_scalar, first_all, heads_packs, (packs[0],))
    heads_got = ring_sends(heads_sum, ring_at)
    placed = place_layer(
        clip_scalar, level_count - 1, level_count, later["tall_all"], (), 0, (packs[0],)
    )
    packs = swap_clips(packs)
    last_sum = last_grad(
        clip_scalar, first_all, feats, packs, (heads_sum,), (placed[0],)
    )
    heads_ring = ring_sum(ring_scalar, heads_sum, heads_got, (last_sum,))
    last_ring = ring_sum(ring_scalar, last_sum, ring_sends(last_sum, ring_at), ())
    heads_total = half_sum(heads_ring, ())
    heads_join = join_frames(ring_scalar, heads_total, ())
    heads_all = lax.all_gather(heads_join, "clip")
    last_join = join_frames(ring_scalar, half_sum(last_ring, ()), (), (tall_all,))
    last_pieces = clip_pieces(last_join)
    grad_down, grad_up, grad_proj = place_layer(
        clip_scalar, 0, level_count, tall_all, placed, level_count - 1, ()
    )
    grad_in, vector, grad_proj = place_last(
        clip_scalar, feat_width, feat_wide, level_count, last_pieces, grad_proj
    )
    grad_heads = place_heads(
        clip_scalar, level_count - 1, level_count, later["heads_all"], (), (last_sum,)
    )
    grad_heads = (place_heads(clip_scalar, 0, level_count, heads_all, (grad_heads,), ()),)


    def norm_sums(layer, first, row):
        return vector[8 * (2 * (level_count - 1 - layer) + first) + row]

    grad_mlp_gain = jnp.stack([norm_sums(layer, 0, 0) for layer in layers])
    grad_mlp_shift = jnp.stack([norm_sums(layer, 0, 1) for layer in layers])
    grad_proj_bias = jnp.stack([norm_sums(layer, 0, 2) for layer in layers])
    grad_attn_gain = jnp.stack([norm_sums(layer, 1, 0) for layer in layers])
    grad_attn_shift = jnp.stack([norm_sums(layer, 1, 1) for layer in layers])
    rest = vector[16 * level_count :]
    grad_down_bias = jnp.stack(
        [norm_sums(layer + 1, 1, 2) for layer in range(level_count - 1)]
        + [rest[16 + 3 * level_count]]
    )
    grad_qkv_bias = lax.dynamic_slice_in_dim(
        rest[16 : 16 + 3 * level_count], tensor_at * width, width, 1
    )
    grad_qkv_bias = grad_qkv_bias.reshape(level_count, 3, width)
    grad_up_bias = lax.dynamic_slice_in_dim(
        rest[24:].reshape(level_count, 4 * hidden_width), tensor_at * hidden_width, hidden_width, 1
    )
    act_count = cond_here.shape[1]
    return (
        block_out,
        grad_features,
        grad_in,
        norm_sums(0, 1, 2),
        rest[:act_count],
        rest[act_count],
        rest[8 : 8 + act_count],
        rest[8 + act_count],
        grad_attn_gain,
        grad_attn_shift,
        jnp.swapaxes(grad_heads[0], 1, 2),
        grad_qkv_bias,
        grad_proj,
        grad_proj_bias,
        grad_mlp_gain,
        grad_mlp_shift,
        grad_up,
        grad_up_bias,
        grad_down,
        grad_down_bias,
    )


def solution(mesh):
    return jax.shard_map(
        on_device,
        mesh=mesh,
        in_specs=(
            P("clip", "frame", None, "tensor"),
            P("clip", "frame", None, None),
            P("clip", None, None),
            P("tensor", None),
            P(),
            P(),
            P(),
            P(),
            P(),
            P(),
            P(),
            P(None, None, None, "tensor"),
            P(None, None, "tensor"),
            P(None, "tensor", None),
            P(),
            P(),
            P(),
            P(None, None, "tensor"),
            P(None, "tensor"),
            P(None, "tensor", None),
            P(),
            P("clip", "frame", None, None),
        ),
        out_specs=(
            P("clip", "frame", None, None),
            P("clip", "frame", None, "tensor"),
            P("tensor", None),
            P(),
            P(),
            P(),
            P(),
            P(),
            P(),
            P(),
            P(None, None, None, "tensor"),
            P(None, None, "tensor"),
            P(None, "tensor", None),
            P(),
            P(),
            P(),
            P(None, None, "tensor"),
            P(None, "tensor"),
            P(None, "tensor", None),
            P(),
        ),
        check_vma=False,
    )
```

```python
import functools

import jax
import jax.numpy as jnp
import numpy as np
from jax import lax
from jax.experimental import pallas as pl
from jax.experimental.pallas import tpu as pltpu
from jax.sharding import PartitionSpec as P

HEAD = 64
GRID_W = 16
EXTRA = 8

highest_precision = lax.Precision.HIGHEST
norm_epsilon = 1e-06
masked_score = -1000000000.0
low_type = jnp.bfloat16
wide_type = jnp.float32

CORE_SWAP = [(0, 1), (1, 0), (2, 3), (3, 2)]
CHIP_SWAP = [(0, 2), (2, 0), (1, 3), (3, 1)]
HALF_SWAP = [(i, (i + 4) % 8) for i in range(8)]


def clip_shift(step):
    return [(i, (i + step) % 4) for i in range(4)]


def frame_shift(halves, step):
    return [
        (4 * half + i, 4 * ((half + halves) % 2) + (i + step) % 4)
        for half in range(2)
        for i in range(4)
    ]


def core_swap(value):
    return lax.ppermute(value, "tensor", CORE_SWAP)


def chip_swap(value):
    return lax.ppermute(value, "tensor", CHIP_SWAP)


def halves_tensor(part):
    half = part.shape[0] // 2
    pair = part[:half] + core_swap(part[half:])
    quarter = half // 2
    return pair[:quarter], chip_swap(pair[quarter:])


def join_rows_tensor(chunk):
    pair = jnp.concatenate([chunk, chip_swap(chunk)], axis=0)
    return jnp.concatenate([pair, core_swap(pair)], axis=0)


def to_heads(blocks):
    return [blocks[0]] + [
        lax.ppermute(blocks[step], "frame", frame_shift(0, step)) for step in range(1, 4)
    ]


def to_frames(blocks):
    return [blocks[0]] + [
        lax.ppermute(blocks[step], "frame", frame_shift(0, -step)) for step in range(1, 4)
    ]


def pairs_to_later_half(blocks):
    return [
        lax.ppermute(
            blocks[step],
            "frame",
            [(src, dst) for src, dst in frame_shift(1, step) if src < dst],
        )
        for step in range(4)
    ]


DOWN_HALF = [(i + 4, i) for i in range(4)]


def swap_clips(packs):
    return [packs[0]] + [
        lax.ppermute(packs[step], "clip", clip_shift(step)) for step in range(1, 4)
    ]


def ring_pieces(value):
    return [value] + [
        lax.ppermute(value, "frame", frame_shift(0, step)) for step in range(1, 4)
    ]


def ring_sends(part, ring):
    block = part.shape[0] // 4
    got = []
    for step in range(1, 4):
        sent = lax.dynamic_slice_in_dim(part, ((ring + step) % 4) * block, block, 0)
        got.append(lax.ppermute(sent.astype(low_type), "frame", frame_shift(0, step)))
    return got


def clip_pieces(joined):
    return [joined] + [
        lax.ppermute(joined, "clip", clip_shift(step)) for step in range(1, 4)
    ]


def rotary_tables(head_size, head_count):
    group_size = 2 * (head_size // 3 // 2)
    half_size = group_size // 2
    total_width = head_size * head_count
    swap_table = np.zeros((total_width, total_width), np.float32)
    rate_table = np.zeros((3, total_width), np.float32)
    for head_at in range(head_count):
        for axis_at in range(3):
            for pair_at in range(half_size):
                lower_at = head_at * head_size + axis_at * group_size + pair_at
                upper_at = lower_at + half_size
                swap_table[upper_at, lower_at] = -1.0
                swap_table[lower_at, upper_at] = 1.0
                rate_value = 10000.0 ** (-2.0 * pair_at / group_size)
                rate_table[axis_at, lower_at] = rate_value
                rate_table[axis_at, upper_at] = rate_value
    return swap_table, rate_table


def norm_rows(values):
    row_mean = jnp.mean(values, axis=-1, keepdims=True)
    centred = values - row_mean
    spread = jnp.mean(centred * centred, axis=-1, keepdims=True)
    inverse = lax.rsqrt(spread + norm_epsilon)
    return centred * inverse, inverse


def norm_kernel(gain_ref, shift_ref, *refs):
    terms, (stream_ref, hat_ref, inverse_ref, low_ref) = refs[:-4], refs[-4:]
    values = terms[0][...]
    if len(terms) > 1:
        values = values + (terms[1][...] + terms[2][...] + terms[3][...])
    hat, inverse = norm_rows(values)
    stream_ref[...] = values
    hat_ref[...] = hat
    inverse_ref[...] = jnp.broadcast_to(inverse, inverse_ref.shape)
    low_ref[...] = (hat * gain_ref[...] + shift_ref[...]).astype(low_type)


def block_kernel(stream_ref, kept_ref, got_ref, bias_ref, live_ref, out_ref):
    values = stream_ref[...] + (kept_ref[...] + got_ref[...] + bias_ref[...])
    out_ref[...] = (values * live_ref[:, 0:1]).astype(low_type)


def norm_back_kernel(count, kept_ref, got_ref, gain_ref, hat_ref, inverse_ref, grad_ref, out_ref, low_ref, sums_ref):
    grad = kept_ref[...] + got_ref[...]
    hat = hat_ref[...]
    scaled = grad * gain_ref[...]
    first = jnp.mean(scaled, axis=-1, keepdims=True)
    second = jnp.mean(scaled * hat, axis=-1, keepdims=True)
    out = grad_ref[...] + (scaled - first - hat * second) * inverse_ref[:, 0:1]
    low = out.astype(low_type)
    out_ref[...] = out
    low_ref[...] = low
    sums_ref[...] = jnp.zeros_like(sums_ref)
    sums_ref[0:1, :] = jnp.sum(grad * hat, axis=0, keepdims=True)
    sums_ref[1:2, :] = jnp.sum(grad, axis=0, keepdims=True)
    sums_ref[2:3, :] = jnp.sum(low[:count].astype(wide_type), axis=0, keepdims=True)


def exact_gelu(values):
    return jax.nn.gelu(values, approximate=False)


def dot_wide(left, right):
    return jnp.dot(left, right, preferred_element_type=wide_type)


def dot_dims(left, right, left_dim, right_dim):
    return lax.dot_general(
        left, right, (((left_dim,), (right_dim,)), ((), ())), preferred_element_type=wide_type
    )


def head_cols(at):
    return slice(at * HEAD, (at + 1) * HEAD)


def ring_back(place, step):
    return lax.rem(place - step + 4, 4)


def ring_ahead(place, step):
    return lax.rem(place + step, 4)


def project_kernel(heads, at_ref, rows_ref, key_w, value_w, query_w, bias_ref, cos_ref, sin_ref, swap_ref, *out_refs):
    rows = rows_ref[...]
    swap = swap_ref[...]
    cosine = jnp.concatenate([cos_ref[: rows.shape[0], :]] * heads, axis=1)
    sine = jnp.concatenate([sin_ref[: rows.shape[0], :]] * heads, axis=1)

    def turned(weight, bias):
        value = dot_wide(rows, weight[...]) + bias
        crossed = jnp.dot(value, swap, precision=highest_precision, preferred_element_type=wide_type)
        return value * cosine + crossed * sine

    key = turned(key_w, bias_ref[1:2, :]).astype(low_type)
    value = (dot_wide(rows, value_w[...]) + bias_ref[2:3, :]).astype(low_type)
    query = (turned(query_w, bias_ref[0:1, :]).astype(low_type).astype(wide_type) * HEAD ** (-0.5)).astype(low_type)

    def write(head, step):
        for at, part in enumerate((key, value, query)):
            out_refs[step][:, head_cols(at)] = part[:, head_cols(head)]
            if at < 2:
                out_refs[4 + step][:, head_cols(at)] = part[:, head_cols(head)]

    for ring in range(4):

        @pl.when(at_ref[0] == ring)
        def _(ring=ring):
            for step in range(4):
                write((ring + step) % 4, step)


def lane_tiles(total):
    size = 384 if total % 384 == 0 else total
    return [slice(at * size, (at + 1) * size) for at in range(total // size)]


def attend_kernel(bias_ref, mask_ref, *refs):
    own_refs, cross_refs = refs[:4], refs[4:8]
    out_ref, low_ref, total_ref, own_out, cross_out, query_ref, score_ref = refs[8:]
    rows = own_refs[0].shape[0]
    total_rows = 4 * rows
    for at in range(4):
        block = slice(at * rows, (at + 1) * rows)
        query_ref[block, :] = own_refs[at][:, head_cols(2)]
        own_out[block, :] = own_refs[at][...]
        cross_out[block, :] = cross_refs[at][...]
    total_ref[...] = jnp.zeros_like(total_ref)

    def pair(at, part):
        if at < 4:
            return own_refs[at][:, head_cols(part)]
        return cross_refs[at - 4][:, head_cols(part)]

    for tile in lane_tiles(total_rows):
        query = query_ref[tile, :]
        wide = tile.stop - tile.start
        top = jnp.full((1, wide), 2.0 * masked_score, wide_type)
        for at in range(8):
            scores = dot_dims(pair(at, 0), query, 1, 1) + bias_ref[:, at : at + 1]
            if at < 4:
                scores = scores + mask_ref[at : at + 1, tile]
            score_ref[at * rows : (at + 1) * rows, :] = scores
            top = jnp.maximum(top, jnp.max(scores, axis=0, keepdims=True))
        mass = jnp.zeros((1, wide), wide_type)
        out = jnp.zeros((HEAD, wide), wide_type)
        for at in range(8):
            weights = jnp.exp(score_ref[at * rows : (at + 1) * rows, :] - top)
            mass = mass + jnp.sum(weights, axis=0, keepdims=True)
            out = out + dot_dims(pair(at, 1), weights.astype(low_type), 0, 0)
        total_ref[0:1, tile] = top + jnp.log(mass)
        rows_out = (out / mass).T
        out_ref[tile, :] = rows_out
        low_ref[tile, :] = rows_out.astype(low_type)


def attend_back_kernel(own, bias_ref, mask_ref, total_ref, out_ref, own_ref, *refs):
    grad_refs, cross_refs = refs[:4], refs[4:-4]
    pair_sum, query_sum, query_ref, grad_ref = refs[-4:]
    rows = grad_refs[0].shape[0]
    query_ref[...] = own_ref[:, head_cols(2)]
    for at in range(4):
        grad_ref[at * rows : (at + 1) * rows, :] = grad_refs[at][...]
    ones = jnp.ones((8, HEAD), wide_type)
    pair_sum[...] = jnp.zeros_like(pair_sum)
    for tile in lane_tiles(4 * rows):
        query = query_ref[tile, :]
        grad = grad_ref[tile, :]
        centre = lax.dot_general(
            ones,
            grad.astype(wide_type) * out_ref[tile, :],
            (((1,), (1,)), ((), ())),
            precision=highest_precision,
            preferred_element_type=wide_type,
        )[0:1, :]
        total = total_ref[0:1, tile]
        query_part = jnp.zeros((HEAD, tile.stop - tile.start), wide_type)
        for at in range(4):
            block = slice(at * rows, (at + 1) * rows)
            if own:
                key, value = own_ref[block, head_cols(0)], own_ref[block, head_cols(1)]
                scores = dot_dims(key, query, 1, 1) + bias_ref[:, at : at + 1] + mask_ref[at : at + 1, tile]
            else:
                key, value = cross_refs[0][block, head_cols(0)], cross_refs[0][block, head_cols(1)]
                scores = dot_dims(key, query, 1, 1) + bias_ref[:, at + 4 : at + 5]
            weights = jnp.exp(scores - total)
            pair_sum[block, head_cols(1)] += dot_wide(weights.astype(low_type), grad)
            soft = dot_dims(value, grad, 1, 1)
            back = (weights * (soft - centre)).astype(low_type)
            pair_sum[block, head_cols(0)] += dot_wide(back, query)
            query_part = query_part + dot_dims(key, back, 0, 0)
        query_sum[tile, :] = query_part.T * HEAD ** (-0.5)


def turn_back_kernel(own_pair, other_pair, own_query, other_query, cos_ref, sin_ref, swap_ref, *out_refs):
    rows = out_refs[0].shape[0]
    swap = swap_ref[...]
    for at in range(4):
        block = slice(at * rows, (at + 1) * rows)
        cosine, sine = cos_ref[block, :], sin_ref[block, :]

        def turned(value):
            crossed = jnp.dot(value, swap, precision=highest_precision, preferred_element_type=wide_type)
            return (value * cosine - crossed * sine).astype(low_type)

        pair = own_pair[block, :] + other_pair[block, :]
        out_refs[at][:, head_cols(0)] = turned(pair[:, head_cols(0)])
        out_refs[at][:, head_cols(1)] = pair[:, head_cols(1)].astype(low_type)
        out_refs[at][:, head_cols(2)] = turned(own_query[block, :] + other_query[block, :])


def mix_back_kernel(at_ref, place_ref, key_w, value_w, query_w, *refs):
    mixed_refs = refs[:4]
    out_ref, stack_ref, bias_ref = refs[4:]
    ring, clip = at_ref[0], at_ref[1]
    place = place_ref[...]
    total = None
    bias_ref[...] = jnp.zeros_like(bias_ref)
    for part, weight in ((0, key_w), (1, value_w), (2, query_w)):
        relative = jnp.concatenate([ref[:, head_cols(part)] for ref in mixed_refs], axis=1)
        ordered = dot_wide(relative, place)
        bias_ref[part : part + 1, :] = jnp.sum(ordered, axis=0, keepdims=True)
        term = dot_dims(ordered.astype(low_type), weight[...], 1, 1)
        total = term if total is None else total + term
    out_ref[...] = total
    for at in range(4):
        stack_ref[lax.rem(ring + at - clip + 4, 4)] = mixed_refs[at][...]


def clip_products(at_ref, first_ref, second_ref, pack_refs, columns):
    out = None
    half = first_ref.shape[1]
    for step in range(4):
        place = ring_back(at_ref[0], step)
        pack = pack_refs[step]
        term = dot_dims(first_ref[place], pack[:half, columns], 0, 0)
        term = term + dot_dims(second_ref[place], pack[half : 2 * half, columns], 0, 0)
        out = term if out is None else out + term
    return out


def layer_grad_kernel(at_ref, act_a, act_b, norm_a, norm_b, *refs):
    head_refs, pack_refs, out_ref = refs[:-5], refs[-5:-1], refs[-1]
    part = out_ref.shape[1] // 2
    tiles = pl.num_programs(0) - (1 if head_refs else 0)

    @pl.when(pl.program_id(0) < tiles)
    def _():
        out_ref[:, :part] = clip_products(at_ref, act_a, act_b, pack_refs, slice(0, part))
        out_ref[:, part:] = clip_products(at_ref, norm_a, norm_b, pack_refs, slice(part, 2 * part))

    if head_refs:

        @pl.when(pl.program_id(0) == tiles)
        def _():
            columns = slice(2 * part, 3 * part)
            out_ref[:, :part] = clip_products(at_ref, head_refs[0], head_refs[2], pack_refs, columns)
            out_ref[:, part:] = clip_products(at_ref, head_refs[1], head_refs[3], pack_refs, columns)


def plain_grad_kernel(at_ref, rows_a, rows_b, *refs):
    pack_refs, out_ref = refs[:4], refs[4]
    out_ref[...] = clip_products(at_ref, rows_a, rows_b, pack_refs, slice(None))


def last_grad_kernel(tiles, at_ref, head_a, head_b, *refs):
    feat_refs, pack_refs, out_ref = refs[:4], refs[4:8], refs[8]
    head_rows = 2 * head_a.shape[1]
    feat_rows = head_rows + feat_refs[0].shape[0]

    @pl.when(pl.program_id(0) < tiles)
    def _():
        out = None
        for step in range(4):
            term = dot_dims(feat_refs[step][...], pack_refs[step][head_rows:feat_rows, :], 0, 0)
            out = term if out is None else out + term
        out_ref[...] = out

    @pl.when(pl.program_id(0) == tiles + 2)
    def _():
        out = None
        small = (pack_refs[0].shape[0] - feat_rows) // 2
        for step in range(4):
            high = pack_refs[step][feat_rows : feat_rows + small, :].astype(wide_type)
            term = high + pack_refs[step][feat_rows + small :, :].astype(wide_type)
            out = term if out is None else out + term
        high = out.astype(low_type).astype(wide_type)
        out_ref[:small, :] = high
        out_ref[small:, :] = out - high

    @pl.when((pl.program_id(0) >= tiles) & (pl.program_id(0) < tiles + 2))
    def _():
        out_ref[...] = clip_products(at_ref, head_a, head_b, pack_refs, slice(None))


def ring_sum_kernel(at_ref, part_ref, *refs):
    got_refs, out_ref = refs[:3], refs[3]
    block = out_ref.shape[0]
    out = part_ref[pl.ds(pl.multiple_of(at_ref[0] * block, 8), block), :]
    for got in got_refs:
        out = out + got[...].astype(wide_type)
    out_ref[...] = out


def ring_sum(ring_at, part, got, after):
    shape = (part.shape[0] // 4, part.shape[1])
    return call_kernel(
        ring_sum_kernel,
        (ring_at[None], part, *got),
        (0,),
        jax.ShapeDtypeStruct(shape, wide_type),
        [],
        4 * shape[0] * shape[1],
        0,
        after,
    )


def half_sum_kernel(own_ref, got_ref, out_ref):
    out_ref[...] = (own_ref[...] + got_ref[...]).astype(low_type)


def half_sum(own, after):
    got = lax.ppermute(own, "frame", HALF_SWAP)
    return call_kernel(
        half_sum_kernel,
        (own, got),
        (),
        jax.ShapeDtypeStruct(own.shape, low_type),
        [],
        own.size,
        0,
        after,
    )


def join_kernel(at_ref, *refs):
    out_ref = refs[4]
    block = refs[0].shape[0]
    for step in range(4):
        start = pl.multiple_of(ring_back(at_ref[0], step) * block, 16)
        out_ref[pl.ds(start, block), :] = refs[step][...]


def join_frames(ring_at, total, after, after_far=()):
    pieces = ring_pieces(total)
    return call_kernel(
        join_kernel,
        (ring_at[None], *pieces),
        (0,),
        jax.ShapeDtypeStruct((4 * total.shape[0], total.shape[1]), low_type),
        [],
        0,
        0,
        after,
        after_far,
    )


def beside_kernel(first_ref, second_ref, out_ref):
    half, wide, other = first_ref.shape[0] // 2, first_ref.shape[1], second_ref.shape[1]
    out_ref[:, :wide] = first_ref[:half, :]
    out_ref[:, wide : wide + other] = second_ref[:half, :]
    out_ref[:, wide + other :] = second_ref[half:, :]


def gather_clips(first, second, after):
    half, wide = first.shape[0] // 2, first.shape[1]
    beside = call_kernel(
        beside_kernel,
        (first, second),
        (),
        jax.ShapeDtypeStruct((half, wide + 2 * second.shape[1]), low_type),
        [],
        0,
        0,
        after,
    )
    whole = lax.all_gather(beside, "clip")
    return whole, core_swap(whole[:, :, :wide])


def smem_spec():
    return pl.BlockSpec(memory_space=pltpu.SMEM)


def kernel_params():
    return pltpu.CompilerParams(vmem_limit_bytes=48 * 1024 * 1024)


def held_spec():
    return pl.BlockSpec(memory_space=pltpu.VMEM)


def any_specs(arrays):
    return [pl.BlockSpec(memory_space=pl.ANY)] * len(arrays)


def without(kernel, count, after):
    return lambda *refs: kernel(*refs[:count], *refs[count + len(after) :])


def layer_grad(clip_at, second_all, packs, first_all, after):
    whole, other = second_all
    half, wide = other.shape[1:]
    tiles = wide // 128
    part = 256
    block = (4, half, 128)
    heads = () if first_all is None else (first_all[0],) * 4
    held = [
        pl.BlockSpec(block, lambda i, at=at: (0, 0, tiles + at)) for at in range(len(heads))
    ]

    def moving(start):
        return pl.BlockSpec(block, lambda i: (0, 0, start + jnp.minimum(i, tiles - 1)))

    return pl.pallas_call(
        without(layer_grad_kernel, 9 + len(heads), after),
        grid=(tiles + (1 if heads else 0),),
        out_shape=jax.ShapeDtypeStruct((wide + (128 if heads else 0), 2 * part), wide_type),
        in_specs=[smem_spec(), moving(tiles), moving(2 * tiles), moving(0), moving(0)]
        + held
        + [held_spec()] * 4
        + any_specs(after),
        out_specs=pl.BlockSpec((128, 2 * part), lambda i: (i, 0)),
        compiler_params=kernel_params(),
        cost_estimate=pl.CostEstimate(
            flops=32 * half * wide * part,
            bytes_accessed=2 * whole.size + 8 * wide * part,
            transcendentals=0,
        ),
    )(clip_at[None], whole, whole, whole, other, *heads, *packs, *after)


def plain_grad(clip_at, rows_all, packs, after):
    whole, other = rows_all
    half, count = other.shape[1:]
    part = packs[0].shape[1]
    block = pl.BlockSpec((4, half, 128), lambda i: (0, 0, i))
    return pl.pallas_call(
        without(plain_grad_kernel, 7, after),
        grid=(count // 128,),
        out_shape=jax.ShapeDtypeStruct((count, part), wide_type),
        in_specs=[smem_spec(), block, block] + [held_spec()] * 4 + any_specs(after),
        out_specs=pl.BlockSpec((128, part), lambda i: (i, 0)),
        compiler_params=kernel_params(),
        cost_estimate=pl.CostEstimate(
            flops=16 * half * count * part,
            bytes_accessed=16 * half * count + 4 * count * part,
            transcendentals=0,
        ),
    )(clip_at[None], whole, other, *packs, *after)


def last_grad(clip_at, first_all, feats, packs, after, after_far):
    whole, other = first_all
    half, part = other.shape[1], packs[0].shape[1]
    first_block = other.shape[2] // 128
    tiles = feats[0].shape[1] // 128
    kernel = functools.partial(last_grad_kernel, tiles)

    def moving(start):
        return pl.BlockSpec(
            (4, half, 128), lambda i: (0, 0, start + jnp.clip(i - tiles, 0, 1))
        )

    return pl.pallas_call(
        without(kernel, 11, (*after, *after_far)),
        grid=(tiles + 3,),
        out_shape=jax.ShapeDtypeStruct(((tiles + 3) * 128, part), wide_type),
        in_specs=[smem_spec(), moving(first_block), moving(first_block + 2)]
        + [pl.BlockSpec((feats[0].shape[0], 128), lambda i: (0, jnp.minimum(i, tiles - 1)))] * 4
        + [held_spec()] * 4
        + any_specs(after)
        + [pl.BlockSpec(memory_space=pltpu.HBM)] * len(after_far),
        out_specs=pl.BlockSpec((128, part), lambda i: (i, 0)),
        compiler_params=kernel_params(),
    )(clip_at[None], whole, whole, *feats, *packs, *after, *after_far)


def by_clip(clip_at, write):
    for place in range(4):

        @pl.when(clip_at == place)
        def _(place=place):
            for step in range(4):
                write((place - step) % 4, step)


def place_layer_kernel(tiles, at_ref, all_ref, *outs):
    part = all_ref.shape[2] // 2
    is_last = pl.program_id(0) == tiles

    for place in range(4):
        columns = slice(place * part, (place + 1) * part)
        left = all_ref[place, :, :part].astype(wide_type)
        right = all_ref[place, :, part:].astype(wide_type)

        @pl.when(jnp.logical_not(is_last))
        def _(columns=columns, left=left, right=right):
            outs[0][0, :, columns] = left
            outs[1][0, :, columns] = right

        if len(outs) > 2:

            @pl.when(is_last)
            def _(columns=columns, left=left, right=right):
                outs[2][0, : outs[2].shape[1] // 2, columns] = left
                outs[2][0, outs[2].shape[1] // 2 :, columns] = right


def place_layer(clip_at, layer, levels, joined, earlier, heads_layer, after):
    part = joined.shape[2] // 2
    rows = 4 * part
    tiles = rows // 128
    heads = joined.shape[1] > rows
    out = [(levels, rows, 4 * part)] * 2 + [(levels, 256, 4 * part)] * heads
    tall = pl.BlockSpec((1, 128, 4 * part), lambda i: (layer, jnp.minimum(i, tiles - 1), 0))
    wide = pl.BlockSpec((1, 256, 4 * part), lambda i: (heads_layer, 0, 0))
    return pl.pallas_call(
        without(functools.partial(place_layer_kernel, tiles), 2, (*earlier, *after)),
        grid=(tiles + (1 if heads else 0),),
        out_shape=tuple(jax.ShapeDtypeStruct(shape, wide_type) for shape in out),
        in_specs=[smem_spec(), pl.BlockSpec((4, 128, 2 * part), lambda i: (0, i, 0))]
        + any_specs(earlier)
        + any_specs(after),
        out_specs=(tall, tall) + ((wide,) if heads else ()),
        input_output_aliases={2 + at: at for at in range(len(earlier))},
        compiler_params=kernel_params(),
    )(clip_at[None], joined, *earlier, *after)


def place_last_kernel(skip, at_ref, *refs):
    pieces = refs[:4]
    in_ref, small_ref, proj_ref = refs[-3:]
    part = pieces[0].shape[1]
    heads = skip + proj_ref.shape[1]
    small = small_ref.shape[0]

    def write(place, step):
        columns = slice(place * part, (place + 1) * part)
        piece = pieces[step]
        in_ref[:, columns] = piece[: in_ref.shape[0], :].astype(wide_type)
        proj_ref[0, :, columns] = piece[skip:heads, :].astype(wide_type)
        small_ref[:, columns] = piece[heads : heads + small, :].astype(wide_type) + piece[
            heads + small :, :
        ].astype(wide_type)

    by_clip(at_ref[0], write)


def place_last(clip_at, feat_rows, skip, levels, pieces, earlier):
    part = pieces[0].shape[1]
    return pl.pallas_call(
        functools.partial(place_last_kernel, skip),
        grid=(1,),
        out_shape=(
            jax.ShapeDtypeStruct((feat_rows, 4 * part), wide_type),
            jax.ShapeDtypeStruct((64, 4 * part), wide_type),
            jax.ShapeDtypeStruct((levels, 256, 4 * part), wide_type),
        ),
        in_specs=[smem_spec()]
        + [pl.BlockSpec(pieces[0].shape, lambda i: (0, 0))] * 4
        + [pl.BlockSpec(memory_space=pl.ANY)],
        out_specs=(
            pl.BlockSpec((feat_rows, 4 * part), lambda i: (0, 0)),
            pl.BlockSpec((64, 4 * part), lambda i: (0, 0)),
            pl.BlockSpec((1, 256, 4 * part), lambda i: (0, 0, 0)),
        ),
        input_output_aliases={5: 2},
        compiler_params=kernel_params(),
    )(clip_at[None], *pieces, earlier)


def pack_kernel(by_rows, count, at_ref, *refs):
    parts, outs = refs[:count], refs[count:]
    for clip in range(4):

        @pl.when(at_ref[0] == clip)
        def _(clip=clip):
            for step in range(4):
                place, start = (clip + step) % 4, 0
                for part in parts:
                    size = part.shape[1] // 4
                    value = part[:, place * size : (place + 1) * size]
                    if by_rows:
                        outs[step][start : start + part.shape[0], :] = value
                        start += part.shape[0]
                    else:
                        outs[step][:, start : start + size] = value
                        start += size


def pack_parts(clip_at, parts, by_rows, after):
    sizes = [part.shape[1] // 4 for part in parts]
    if by_rows:
        shape = (sum(part.shape[0] for part in parts), sizes[0])
    else:
        shape = (parts[0].shape[0], sum(sizes))
    return call_kernel(
        functools.partial(pack_kernel, by_rows, len(parts)),
        (clip_at[None], *parts),
        (0,),
        tuple(jax.ShapeDtypeStruct(shape, low_type) for _ in range(4)),
        [],
        0,
        0,
        after,
    )


def place_heads_kernel(at_ref, all_ref, *refs):
    out_ref = refs[-1]
    for place in range(4):
        piece = all_ref[place].astype(wide_type)
        for at, part in ((1, 0), (2, 1), (0, 2)):
            out_ref[0, at, :, head_cols(place)] = piece[:, head_cols(part)]


def place_heads(clip_at, layer, levels, joined, earlier, after):
    rows = joined.shape[1]
    tile = 256
    count = 2
    return pl.pallas_call(
        without(place_heads_kernel, count, (*earlier, *after)),
        grid=(rows // tile,),
        out_shape=jax.ShapeDtypeStruct((levels, 3, rows, 4 * HEAD), wide_type),
        in_specs=[smem_spec(), pl.BlockSpec((4, tile, 3 * HEAD), lambda i: (0, i, 0))]
        + any_specs(earlier)
        + any_specs(after),
        out_specs=pl.BlockSpec((1, 3, tile, 4 * HEAD), lambda i: (layer, 0, i, 0)),
        input_output_aliases={count + at: at for at in range(len(earlier))},
        compiler_params=kernel_params(),
    )(clip_at[None], joined, *earlier, *after)


def stack_kernel(*refs):
    out_ref = refs[-1]
    for at, ref in enumerate(refs[:-1]):
        out_ref[8 * at : 8 * (at + 1), :] = ref[...]


def feature_grad_kernel(ids_ref, rows_ref, weight_ref, out_ref):
    size = rows_ref.shape[0] // 4
    for at in range(4):
        start = pl.multiple_of(ids_ref[at] * size, 8)
        out_ref[pl.ds(start, size), :] = dot_dims(
            rows_ref[at * size : (at + 1) * size, :], weight_ref[...], 1, 1
        )


def last_pack_kernel(at_ref, head_ref, patch_ref, small_a, small_b, *outs):
    heads, patches, small = head_ref.shape[0], patch_ref.shape[0], small_a.shape[0]
    values = small_a[...] + small_b[...]
    high = values.astype(low_type)
    rest = (values - high.astype(wide_type)).astype(low_type)
    for clip in range(4):

        @pl.when(at_ref[0] == clip)
        def _(clip=clip):
            for step in range(4):
                size = outs[step].shape[1]
                place = (clip + step) % 4
                columns = slice(place * size, (place + 1) * size)
                outs[step][:heads, :] = head_ref[:, columns]
                outs[step][heads : heads + patches, :] = patch_ref[:, columns]
                outs[step][heads + patches : heads + patches + small, :] = high[:, columns]
                outs[step][heads + patches + small :, :] = rest[:, columns]


def call_kernel(kernel, args, in_smem, outs, scratch, flops, exps, after=(), after_far=(), piped=()):
    count = len(args)

    def spec(at):
        if at in piped:
            return pl.BlockSpec(args[at].shape, lambda i, rank=args[at].ndim: (0,) * rank)
        return pl.BlockSpec(memory_space=pltpu.SMEM if at in in_smem else pltpu.VMEM)

    specs = [spec(at) for at in range(count)]
    specs += any_specs(after) + [pl.BlockSpec(memory_space=pltpu.HBM)] * len(after_far)
    after = (*after, *after_far)
    moved = sum(a.size * a.dtype.itemsize for a in args)
    return pl.pallas_call(
        without(kernel, count, after),
        grid=(1,),
        out_shape=outs,
        in_specs=specs,
        out_specs=jax.tree.map(lambda _: pl.BlockSpec(memory_space=pltpu.VMEM), outs),
        scratch_shapes=scratch,
        compiler_params=kernel_params(),
        cost_estimate=pl.CostEstimate(flops=flops, bytes_accessed=moved, transcendentals=exps),
    )(*args, *after)


def on_device(
    features,
    cond_values,
    cond_live,
    in_weight,
    in_bias,
    act_weight,
    act_bias,
    state_weight,
    state_bias,
    attn_gain,
    attn_shift,
    qkv_weight,
    qkv_bias,
    proj_weight,
    proj_bias,
    mlp_gain,
    mlp_shift,
    up_weight,
    up_bias,
    down_weight,
    down_bias,
    out_grad,
):
    patch_rows = features.shape[2]
    feat_width = features.shape[3]
    slot_count = cond_values.shape[2]
    all_frames = cond_live.shape[1]
    model_width = in_weight.shape[1]
    width = qkv_weight.shape[3]
    heads = width // HEAD
    level_count = attn_gain.shape[0]
    patches = patch_rows // 4
    chunk_rows = patches + EXTRA
    rows = 4 * chunk_rows
    hidden_width = up_weight.shape[2]

    tensor_at = lax.axis_index("tensor")
    chip_at, core_at = tensor_at // 2, tensor_at % 2
    frame_at = lax.axis_index("frame")
    half_at, ring_at = frame_at // 4, frame_at % 4
    clip_at = lax.axis_index("clip")

    chunk_ids = [
        2 * jnp.bitwise_xor(core_at, core_step) + jnp.bitwise_xor(chip_at, chip_step)
        for core_step in range(2)
        for chip_step in range(2)
    ]
    own_chunk = chunk_ids[0]
    own_frames = jnp.stack([4 * half_at + (ring_at - step) % 4 for step in range(4)])
    cross_frames = jnp.stack([4 * (1 - half_at) + (ring_at - step) % 4 for step in range(4)])

    within = lax.broadcasted_iota(jnp.int32, (chunk_rows, 1), 0)
    is_patch = within < patches
    heights, columns = [], []
    for chunk_id in chunk_ids:
        patch_id = chunk_id * patches + within
        heights.append(jnp.where(is_patch, patch_id // GRID_W, 0))
        columns.append(jnp.where(is_patch, patch_id % GRID_W, 0))
    heights = jnp.concatenate(heights, axis=0).astype(wide_type)
    columns = jnp.concatenate(columns, axis=0).astype(wide_type)
    swap_table, rate_table = rotary_tables(HEAD, heads)
    swap_heads = jnp.asarray(swap_table)
    swap_one = jnp.asarray(swap_table[:HEAD, :HEAD])
    rates = rate_table[:, :HEAD]
    place_angles = heights * rates[1] + columns * rates[2]
    angles = jnp.concatenate(
        [
            own_frames[step].astype(wide_type) * rates[0][None, :] + place_angles
            for step in range(4)
        ],
        axis=0,
    )
    cosine_four, sine_four = jnp.cos(angles), jnp.sin(angles)
    head_from = jnp.arange(width)
    head_to = ((head_from // HEAD + ring_at) % 4) * HEAD + head_from % HEAD
    head_place = (head_to[:, None] == head_from[None, :]).astype(low_type)
    proj_turned = [
        lax.dynamic_slice_in_dim(
            jnp.concatenate([proj_weight[layer], proj_weight[layer]], axis=0),
            ring_at * HEAD,
            width,
            0,
        )
        for layer in range(level_count)
    ]
    ring_scalar = ring_at.astype(jnp.int32)
    clip_scalar = clip_at.astype(jnp.int32)

    live_all = cond_live[0].astype(wide_type)
    own_slots = lax.dynamic_index_in_dim(live_all, frame_at, 0, False)

    def live_rows(slots, chunk_id):
        picked = jnp.where(
            chunk_id < slot_count,
            lax.dynamic_index_in_dim(slots, jnp.minimum(chunk_id, slot_count - 1), 1, False),
            0.0,
        )
        return jnp.where(is_patch, 1.0, jnp.where(within == patches, picked[None, :], 0.0))

    sources = jnp.concatenate([own_frames, cross_frames])
    source_live = jnp.take(live_all, sources, axis=0)
    key_live = jnp.concatenate([live_rows(source_live, c) for c in chunk_ids], axis=0)
    reached = jnp.concatenate([jnp.ones((4,), jnp.bool_), jnp.full((4,), half_at == 1)])
    key_bias = jnp.where((key_live > 0.5) & reached[None, :], 0.0, masked_score).astype(wide_type)
    seen = own_frames[:, None] <= own_frames[None, :]
    causal = jnp.where(seen, 0.0, masked_score).astype(wide_type)
    causal = jnp.pad(jnp.repeat(causal, rows, axis=1), ((0, 4), (0, 0)))
    own_live = live_rows(own_slots[None, :], own_chunk)

    def extra_rows(slot_rows):
        picked = lax.dynamic_slice_in_dim(
            slot_rows, jnp.minimum(own_chunk, slot_count - 1), 1, 0
        )
        picked = jnp.where(own_chunk < slot_count, picked, jnp.zeros_like(picked))
        return jnp.pad(picked, ((0, EXTRA - 1), (0, 0)))

    cond_here = cond_values[0, 0]
    act_rows = jnp.dot(cond_here, act_weight, precision=highest_precision) + act_bias
    state_rows = jnp.dot(cond_here, state_weight, precision=highest_precision) + state_bias
    even_slot = (jnp.arange(slot_count) % 2 == 0)[:, None]
    cond_x = jnp.where(even_slot, act_rows, state_rows) * own_slots[:, None]

    flat_feat = jnp.concatenate(
        [
            lax.dynamic_slice_in_dim(features[0, 0], c * patches, patches, 0)
            for c in chunk_ids
        ],
        axis=0,
    )
    kept, got = halves_tensor(dot_wide(flat_feat, in_weight))
    stream = jnp.concatenate([kept + got + in_bias, extra_rows(cond_x)], axis=0)

    feat_wide = -(-feat_width // 128) * 128
    feat_low = jnp.pad(flat_feat, ((0, 0), (0, feat_wide - feat_width)))
    feats = [feat_low] + [
        lax.ppermute(feat_low, "clip", clip_shift(step)) for step in range(1, 4)
    ]
    pair_work = 2 * 32 * rows * rows * HEAD
    pair_exps = 32 * rows * rows
    weight_parts = [
        [qkv_weight[layer, :, at] for at in (1, 2, 0)] for layer in range(level_count)
    ]

    def norm(terms, gain, shift, after_far=()):
        chunk = jax.ShapeDtypeStruct((chunk_rows, model_width), wide_type)
        return call_kernel(
            norm_kernel,
            (gain[None], shift[None], *terms),
            (),
            (
                chunk,
                chunk,
                jax.ShapeDtypeStruct((chunk_rows, 128), wide_type),
                jax.ShapeDtypeStruct((chunk_rows, model_width), low_type),
            ),
            [],
            12 * chunk_rows * model_width,
            0,
            (),
            after_far,
        )

    def norm_back(part, gain, hat, inverse, grad, count, after=(), after_far=()):
        kept, got = halves_tensor(part)
        return call_kernel(
            functools.partial(norm_back_kernel, count),
            (kept, got, gain[None], hat, inverse, grad),
            (),
            (
                jax.ShapeDtypeStruct((chunk_rows, model_width), wide_type),
                jax.ShapeDtypeStruct((chunk_rows, model_width), low_type),
                jax.ShapeDtypeStruct((8, model_width), wide_type),
            ),
            [],
            16 * chunk_rows * model_width,
            0,
            after,
            after_far,
            (2, 3, 4, 5),
        )

    stored = []
    terms = (stream,)
    before = None
    for layer in range(level_count):
        stream, hat_one, inverse_one, first_chunk = norm(terms, attn_gain[layer], attn_shift[layer])
        first_in = join_rows_tensor(first_chunk)
        bias = jnp.pad(qkv_bias[layer], ((0, 5), (0, 0)))
        heads_out = call_kernel(
            functools.partial(project_kernel, heads),
            (
                ring_scalar[None],
                first_in,
                *weight_parts[layer],
                bias,
                cosine_four,
                sine_four,
                swap_heads,
            ),
            (0,),
            tuple(
                jax.ShapeDtypeStruct((rows, count * HEAD), low_type)
                for count in (3, 3, 3, 3, 2, 2, 2, 2)
            ),
            [],
            6 * rows * model_width * width,
            0,
            (),
            () if before is None else (before[0][0],),
            (2, 3, 4, 5, 6, 7, 8),
        )
        blocks = to_heads(heads_out[:4])
        cross = pairs_to_later_half(heads_out[4:])
        attn_wide, attn_turned, log_total, own_all, cross_all = call_kernel(
            attend_kernel,
            (key_bias, causal, *blocks, *cross),
            (),
            (
                jax.ShapeDtypeStruct((4 * rows, HEAD), wide_type),
                jax.ShapeDtypeStruct((4 * rows, HEAD), low_type),
                jax.ShapeDtypeStruct((8, 4 * rows), wide_type),
                jax.ShapeDtypeStruct((4 * rows, 3 * HEAD), low_type),
                jax.ShapeDtypeStruct((4 * rows, 2 * HEAD), low_type),
            ),
            [
                pltpu.VMEM((4 * rows, HEAD), low_type),
                pltpu.VMEM((8 * rows, lane_tiles(4 * rows)[0].stop), wide_type),
            ],
            2 * pair_work,
            pair_exps,
            tuple(feats[1:]) if layer == 0 else (),
        )
        attn_relative = jnp.concatenate(
            to_frames([attn_turned[at * rows : (at + 1) * rows] for at in range(4)]), axis=1
        )
        attn_low = dot_wide(attn_relative, head_place).astype(low_type)
        if layer < level_count - 1:
            first_all = gather_clips(first_in, attn_low, ())
        kept, got = halves_tensor(dot_wide(attn_relative, proj_turned[layer]))
        middle, hat_two, inverse_two, second_chunk = norm(
            (stream, kept, got, proj_bias[layer][None]), mlp_gain[layer], mlp_shift[layer],
            () if before is None else (before[1][0],),
        )
        second_in = join_rows_tensor(second_chunk)
        hidden = dot_wide(second_in, up_weight[layer]) + up_bias[layer]
        active_low = exact_gelu(hidden).astype(low_type)
        second_all = gather_clips(second_in, active_low, ())
        if layer == level_count - 1:
            first_all = gather_clips(first_in, attn_low, (second_all[0],))
        before = (first_all, second_all)
        kept, got = halves_tensor(dot_wide(active_low, down_weight[layer]))
        terms = (middle, kept, got, down_bias[layer][None])
        stored.append(
            (
                hat_one,
                inverse_one,
                own_all,
                cross_all,
                log_total,
                attn_wide,
                hat_two,
                inverse_two,
                hidden,
                first_all,
                second_all,
            )
        )
    def in_order(full, count):
        out = jnp.zeros((4 * count,) + full.shape[1:], full.dtype)
        size = full.shape[0] // 4
        for at, chunk_id in enumerate(chunk_ids):
            out = lax.dynamic_update_slice_in_dim(
                out, full[at * size : at * size + count], chunk_id * count, 0
            )
        return out

    def block_rows(after):
        low = call_kernel(
            block_kernel,
            (*terms, jnp.broadcast_to(own_live, (chunk_rows, 128))),
            (),
            jax.ShapeDtypeStruct((chunk_rows, model_width), low_type),
            [],
            4 * chunk_rows * model_width,
            0,
            after,
        )
        return join_rows_tensor(low)

    def block_in_order(block_full):
        slot_full = jnp.concatenate(
            [
                block_full[at * chunk_rows + patches : at * chunk_rows + patches + 1]
                for at in range(4)
            ],
            axis=0,
        )
        return jnp.concatenate(
            [in_order(block_full, patches), in_order(slot_full, 1)[:slot_count]], axis=0
        )[None, None]

    own_out = lax.dynamic_slice_in_dim(out_grad[0, 0], own_chunk * patches, patches, 0)
    grad_stream = (
        jnp.concatenate(
            [
                own_out.astype(wide_type),
                extra_rows(out_grad[0, 0, patch_rows:].astype(wide_type)),
            ],
            axis=0,
        )
        * own_live
    )

    small = {}
    small["down", level_count - 1] = jnp.sum(grad_stream, axis=0)
    slot_grads = out_grad[0, 0, patch_rows:] * own_slots[:, None].astype(low_type)
    slot_blocks = jnp.concatenate(
        [
            jnp.pad(slot_grads[:, None], ((0, 0), (0, EXTRA - 1), (0, 0))),
            jnp.zeros((4 - slot_count, EXTRA, model_width), low_type),
        ],
        axis=0,
    )
    branch_parts = []
    for chunk_id in chunk_ids:
        branch_parts.append(
            lax.dynamic_slice_in_dim(out_grad[0, 0], chunk_id * patches, patches, 0)
        )
        branch_parts.append(lax.dynamic_index_in_dim(slot_blocks, chunk_id, 0, False))
    first_branch = jnp.concatenate(branch_parts, axis=0)
    sums_list = []
    wide_part = model_width // 4
    later = None
    for layer in reversed(range(level_count)):
        (
            hat_one,
            inverse_one,
            own_all,
            cross_all,
            log_total,
            attn_wide,
            hat_two,
            inverse_two,
            hidden,
            first_all,
            second_all,
        ) = stored[layer]
        branch = first_branch if later is None else join_rows_tensor(branch_chunk)
        _, gelu_pull = jax.vjp(exact_gelu, hidden)
        grad_hidden = gelu_pull(dot_dims(branch, down_weight[layer], 1, 1))[0].astype(low_type)
        small["up", layer] = jnp.sum(grad_hidden.astype(wide_type), axis=0)
        parts = [branch, grad_hidden] + ([] if later is None else [later["proj_out"]])
        packs = pack_parts(clip_scalar, parts, False, ())
        grad_middle, proj_chunk, sums = norm_back(
            dot_dims(grad_hidden, up_weight[layer], 1, 1),
            mlp_gain[layer],
            hat_two,
            inverse_two,
            grad_stream,
            chunk_rows,
            (packs[0],) if later is None else (packs[0], later["tall_join"], later["heads_sum"]),
        )
        sums_list.append(sums)
        packs = swap_clips(packs)
        if later is None:
            block_full = block_rows((proj_chunk,))
            block_out = block_in_order(block_full)
        proj_out = join_rows_tensor(proj_chunk)
        grad_attn = dot_dims(proj_out, proj_turned[layer], 1, 1).astype(low_type)
        grads = to_heads([grad_attn[:, head_cols(at)] for at in range(4)])

        if later is not None:
            later["heads_ring"] = ring_sum(
                ring_scalar, later["heads_sum"], later["heads_got"], (proj_chunk,)
            )

            later["tall_all"] = lax.all_gather(later["tall_join"], "clip")

        def attend_back(own, after, after_far=()):
            return call_kernel(
                functools.partial(attend_back_kernel, own),
                (key_bias, causal, log_total, attn_wide, own_all, *grads)
                + (() if own else (cross_all,)),
                (),
                (
                    jax.ShapeDtypeStruct((4 * rows, 2 * HEAD), wide_type),
                    jax.ShapeDtypeStruct((4 * rows, HEAD), wide_type),
                ),
                [
                    pltpu.VMEM((4 * rows, HEAD), low_type),
                    pltpu.VMEM((4 * rows, HEAD), low_type),
                ],
                5 * pair_work // 2,
                pair_exps // 2,
                after,
                after_far,
                (0, 1, 2, 3, 4) if own else (0, 1, 2, 3, 4, 9),
            )

        cross_pair, cross_query = attend_back(
            False, () if later is None else (later["heads_ring"],)
        )
        got_pair = lax.ppermute(cross_pair, "frame", DOWN_HALF)
        tall_sum = layer_grad(
            clip_scalar,
            second_all,
            packs,
            None if later is None else later["first_all"],
            (cross_pair,),
        )
        own_pair, own_query = attend_back(
            True, (tall_sum,), () if later is None else (later["tall_all"], block_full)
        )
        tall_got = ring_sends(tall_sum, ring_at)
        if later is not None:
            later["heads_total"] = half_sum(later["heads_ring"], (own_pair,))
        turned = call_kernel(
            turn_back_kernel,
            (own_pair, got_pair, own_query, cross_query, cosine_four, sine_four, swap_one),
            (),
            tuple(jax.ShapeDtypeStruct((rows, 3 * HEAD), low_type) for _ in range(4)),
            [],
            24 * rows * HEAD * HEAD,
            0,
            () if later is None else (later["heads_total"],),
            (),
            (4, 5, 6),
        )
        mixed = to_frames(list(turned))
        tall_ring = ring_sum(ring_scalar, tall_sum, tall_got, (turned[0],))
        tall_total = half_sum(tall_ring, ()) if later is None else None
        if later is not None:
            later["heads_join"] = join_frames(ring_scalar, later["heads_total"], (turned[0],))
        normed_part, mixed_stack, bias_sums = call_kernel(
            mix_back_kernel,
            (
                jnp.stack([ring_scalar, clip_scalar]),
                head_place,
                *weight_parts[layer],
                *mixed,
            ),
            (0,),
            (
                jax.ShapeDtypeStruct((rows, model_width), wide_type),
                jax.ShapeDtypeStruct((4, rows, 3 * HEAD), low_type),
                jax.ShapeDtypeStruct((8, width), wide_type),
            ),
            [],
            6 * rows * model_width * width,
            0,
            (tall_total,) if later is None else (later["heads_join"],),
            (),
            (1, 2, 3, 4),
        )
        small["qkv", layer] = jnp.concatenate([bias_sums[2:3], bias_sums[:2]], axis=0)
        packs = swap_clips([mixed_stack[step] for step in range(4)])
        if layer == 0:
            heads_sum = plain_grad(clip_scalar, first_all, packs, ())
            heads_got = ring_sends(heads_sum, ring_at)
        grad_stream, branch_chunk, sums = norm_back(
            normed_part,
            attn_gain[layer],
            hat_one,
            inverse_one,
            grad_middle,
            patches if layer == 0 else chunk_rows,
            tuple(packs[1:]) if layer > 0 else (heads_sum,),
        )
        sums_list.append(sums)
        if layer > 0:
            tall_join = join_frames(ring_scalar, tall_total, (normed_part,))
        else:
            tall_total = half_sum(tall_ring, (branch_chunk,))

        if layer > 0:
            heads_sum = plain_grad(clip_scalar, first_all, packs, (branch_chunk,))
            heads_got = ring_sends(heads_sum, ring_at)
        if layer > 0:
            later = {
                "proj_out": proj_out,
                "first_all": first_all,
                "tall_join": tall_join,
                "heads_sum": heads_sum,
                "heads_got": heads_got,
            }

    patch_chunk = branch_chunk[:patches]
    grad_patch = join_rows_tensor(patch_chunk)
    grad_features = call_kernel(
        feature_grad_kernel,
        (jnp.stack(chunk_ids).astype(jnp.int32), grad_patch, in_weight),
        (0,),
        jax.ShapeDtypeStruct((patch_rows, feat_width), wide_type),
        [],
        2 * patch_rows * feat_width * model_width,
        0,
        piped=(2,),
    )
    slot_row = grad_stream[patches : patches + 1] * own_live[patches : patches + 1]
    own_cond = lax.dynamic_slice_in_dim(
        cond_here, jnp.minimum(own_chunk, slot_count - 1), 1, 0
    )
    slot_part = jnp.concatenate([own_cond.T * slot_row, slot_row], axis=0)
    here = own_chunk < slot_count
    is_act = here & (own_chunk % 2 == 0)
    is_state = here & (own_chunk % 2 == 1)
    act_part = jnp.where(is_act, slot_part, 0.0)
    state_part = jnp.where(is_state, slot_part, 0.0)

    def at_tensor(value, total):
        return lax.dynamic_update_slice(
            jnp.zeros((value.shape[0], total), wide_type),
            value,
            (0, tensor_at * value.shape[1]),
        )

    layers = range(level_count)
    qkv_rows = at_tensor(
        jnp.concatenate([small["qkv", layer] for layer in layers], axis=0), 4 * width
    )
    mixed_rows = jnp.concatenate(
        [qkv_rows, small["down", level_count - 1][None], jnp.zeros_like(qkv_rows[:1])], axis=0
    )
    ups = at_tensor(jnp.stack([small["up", layer] for layer in layers]), 4 * hidden_width)
    parts = [*sums_list, act_part, state_part, mixed_rows, ups.reshape(-1, model_width)]
    vector = call_kernel(
        stack_kernel,
        tuple(parts),
        (),
        jax.ShapeDtypeStruct((8 * len(parts), model_width), wide_type),
        [],
        0,
        0,
    )
    vector = vector + core_swap(vector)
    later["heads_all"] = lax.all_gather(later["heads_join"], "clip")
    head_rows, patch_count, small_rows = proj_out.shape[0], grad_patch.shape[0], vector.shape[0]
    packs = call_kernel(
        last_pack_kernel,
        (clip_scalar[None], proj_out, grad_patch, vector, chip_swap(vector)),
        (0,),
        tuple(
            jax.ShapeDtypeStruct((head_rows + patch_count + 2 * small_rows, wide_part), low_type)
            for _ in range(4)
        ),
        [],
        0,
        0,
        (),
        (later["heads_all"],),
    )
    tall_join = join_frames(ring_scalar, tall_total, (packs[0],))
    tall_all = lax.all_gather(tall_join, "clip")
    heads_ring = ring_sum(ring_scalar, heads_sum, heads_got, (packs[0],))
    placed = place_layer(
        clip_scalar, level_count - 1, level_count, later["tall_all"], (), 0, (packs[0],)
    )
    packs = swap_clips(packs)
    last_sum = last_grad(
        clip_scalar, first_all, feats, packs, (heads_ring, tall_join), (placed[0], grad_features)
    )
    last_ring = ring_sum(ring_scalar, last_sum, ring_sends(last_sum, ring_at), ())
    heads_total = half_sum(heads_ring, ())
    heads_join = join_frames(ring_scalar, heads_total, ())
    heads_all = lax.all_gather(heads_join, "clip")
    heads_placed = place_heads(
        clip_scalar, level_count - 1, level_count, later["heads_all"], (), (packs[0],)
    )
    last_join = join_frames(
        ring_scalar, half_sum(last_ring, ()), (), (tall_all, heads_placed)
    )
    last_pieces = clip_pieces(last_join)
    grad_down, grad_up, grad_proj = place_layer(
        clip_scalar, 0, level_count, tall_all, placed, level_count - 1, ()
    )
    grad_in, vector, grad_proj = place_last(
        clip_scalar, feat_width, feat_wide, level_count, last_pieces, grad_proj
    )
    grad_heads = (place_heads(clip_scalar, 0, level_count, heads_all, (heads_placed,), ()),)


    def norm_sums(layer, first, row):
        return vector[8 * (2 * (level_count - 1 - layer) + first) + row]

    grad_mlp_gain = jnp.stack([norm_sums(layer, 0, 0) for layer in layers])
    grad_mlp_shift = jnp.stack([norm_sums(layer, 0, 1) for layer in layers])
    grad_proj_bias = jnp.stack([norm_sums(layer, 0, 2) for layer in layers])
    grad_attn_gain = jnp.stack([norm_sums(layer, 1, 0) for layer in layers])
    grad_attn_shift = jnp.stack([norm_sums(layer, 1, 1) for layer in layers])
    rest = vector[16 * level_count :]
    grad_down_bias = jnp.stack(
        [norm_sums(layer + 1, 1, 2) for layer in range(level_count - 1)]
        + [rest[16 + 3 * level_count]]
    )
    grad_qkv_bias = lax.dynamic_slice_in_dim(
        rest[16 : 16 + 3 * level_count], tensor_at * width, width, 1
    )
    grad_qkv_bias = grad_qkv_bias.reshape(level_count, 3, width)
    grad_up_bias = lax.dynamic_slice_in_dim(
        rest[24:].reshape(level_count, 4 * hidden_width), tensor_at * hidden_width, hidden_width, 1
    )
    act_count = cond_here.shape[1]
    return (
        block_out,
        grad_features[None, None],
        grad_in,
        norm_sums(0, 1, 2),
        rest[:act_count],
        rest[act_count],
        rest[8 : 8 + act_count],
        rest[8 + act_count],
        grad_attn_gain,
        grad_attn_shift,
        jnp.swapaxes(grad_heads[0], 1, 2),
        grad_qkv_bias,
        grad_proj,
        grad_proj_bias,
        grad_mlp_gain,
        grad_mlp_shift,
        grad_up,
        grad_up_bias,
        grad_down,
        grad_down_bias,
    )


def solution(mesh):
    return jax.shard_map(
        on_device,
        mesh=mesh,
        in_specs=(
            P("clip", "frame", None, "tensor"),
            P("clip", "frame", None, None),
            P("clip", None, None),
            P("tensor", None),
            P(),
            P(),
            P(),
            P(),
            P(),
            P(),
            P(),
            P(None, None, None, "tensor"),
            P(None, None, "tensor"),
            P(None, "tensor", None),
            P(),
            P(),
            P(),
            P(None, None, "tensor"),
            P(None, "tensor"),
            P(None, "tensor", None),
            P(),
            P("clip", "frame", None, None),
        ),
        out_specs=(
            P("clip", "frame", None, None),
            P("clip", "frame", None, "tensor"),
            P("tensor", None),
            P(),
            P(),
            P(),
            P(),
            P(),
            P(),
            P(),
            P(None, None, None, "tensor"),
            P(None, None, "tensor"),
            P(None, "tensor", None),
            P(),
            P(),
            P(),
            P(None, None, "tensor"),
            P(None, "tensor"),
            P(None, "tensor", None),
            P(),
        ),
        check_vma=False,
    )
```

```python
import functools

import jax
import jax.numpy as jnp
import numpy as np
from jax import lax
from jax.experimental import pallas as pl
from jax.experimental.pallas import tpu as pltpu
from jax.sharding import PartitionSpec as P

HEAD = 64
GRID_W = 16
EXTRA = 8

highest_precision = lax.Precision.HIGHEST
norm_epsilon = 1e-06
masked_score = -1000000000.0
low_type = jnp.bfloat16
wide_type = jnp.float32

CORE_SWAP = [(0, 1), (1, 0), (2, 3), (3, 2)]
CHIP_SWAP = [(0, 2), (2, 0), (1, 3), (3, 1)]
HALF_SWAP = [(i, (i + 4) % 8) for i in range(8)]


def clip_shift(step):
    return [(i, (i + step) % 4) for i in range(4)]


def frame_shift(halves, step):
    return [
        (4 * half + i, 4 * ((half + halves) % 2) + (i + step) % 4)
        for half in range(2)
        for i in range(4)
    ]


def core_swap(value):
    return lax.ppermute(value, "tensor", CORE_SWAP)


def chip_swap(value):
    return lax.ppermute(value, "tensor", CHIP_SWAP)


def halves_tensor(part):
    half = part.shape[0] // 2
    pair = part[:half] + core_swap(part[half:])
    quarter = half // 2
    return pair[:quarter], chip_swap(pair[quarter:])


def join_rows_tensor(chunk):
    pair = jnp.concatenate([chunk, chip_swap(chunk)], axis=0)
    return jnp.concatenate([pair, core_swap(pair)], axis=0)


def to_heads(blocks):
    return [blocks[0]] + [
        lax.ppermute(blocks[step], "frame", frame_shift(0, step)) for step in range(1, 4)
    ]


def to_frames(blocks):
    return [blocks[0]] + [
        lax.ppermute(blocks[step], "frame", frame_shift(0, -step)) for step in range(1, 4)
    ]


def pairs_to_later_half(blocks):
    return [
        lax.ppermute(
            blocks[step],
            "frame",
            [(src, dst) for src, dst in frame_shift(1, step) if src < dst],
        )
        for step in range(4)
    ]


DOWN_HALF = [(i + 4, i) for i in range(4)]


def swap_clips(packs):
    return [packs[0]] + [
        lax.ppermute(packs[step], "clip", clip_shift(step)) for step in range(1, 4)
    ]


def ring_pieces(value):
    return [value] + [
        lax.ppermute(value, "frame", frame_shift(0, step)) for step in range(1, 4)
    ]


def ring_sends(part, ring):
    block = part.shape[0] // 4
    got = []
    for step in range(1, 4):
        sent = lax.dynamic_slice_in_dim(part, ((ring + step) % 4) * block, block, 0)
        got.append(lax.ppermute(sent.astype(low_type), "frame", frame_shift(0, step)))
    return got


def clip_pieces(joined):
    return [joined] + [
        lax.ppermute(joined, "clip", clip_shift(step)) for step in range(1, 4)
    ]


def rotary_tables(head_size, head_count):
    group_size = 2 * (head_size // 3 // 2)
    half_size = group_size // 2
    total_width = head_size * head_count
    swap_table = np.zeros((total_width, total_width), np.float32)
    rate_table = np.zeros((3, total_width), np.float32)
    for head_at in range(head_count):
        for axis_at in range(3):
            for pair_at in range(half_size):
                lower_at = head_at * head_size + axis_at * group_size + pair_at
                upper_at = lower_at + half_size
                swap_table[upper_at, lower_at] = -1.0
                swap_table[lower_at, upper_at] = 1.0
                rate_value = 10000.0 ** (-2.0 * pair_at / group_size)
                rate_table[axis_at, lower_at] = rate_value
                rate_table[axis_at, upper_at] = rate_value
    return swap_table, rate_table


def norm_rows(values):
    row_mean = jnp.mean(values, axis=-1, keepdims=True)
    centred = values - row_mean
    spread = jnp.mean(centred * centred, axis=-1, keepdims=True)
    inverse = lax.rsqrt(spread + norm_epsilon)
    return centred * inverse, inverse


def norm_kernel(gain_ref, shift_ref, *refs):
    terms, (stream_ref, hat_ref, inverse_ref, low_ref) = refs[:-4], refs[-4:]
    values = terms[0][...]
    if len(terms) > 1:
        values = values + (terms[1][...] + terms[2][...] + terms[3][...])
    hat, inverse = norm_rows(values)
    stream_ref[...] = values
    hat_ref[...] = hat
    inverse_ref[...] = jnp.broadcast_to(inverse, inverse_ref.shape)
    low_ref[...] = (hat * gain_ref[...] + shift_ref[...]).astype(low_type)


def block_kernel(stream_ref, kept_ref, got_ref, bias_ref, live_ref, out_ref):
    values = stream_ref[...] + (kept_ref[...] + got_ref[...] + bias_ref[...])
    out_ref[...] = (values * live_ref[:, 0:1]).astype(low_type)


def norm_back_kernel(count, kept_ref, got_ref, gain_ref, hat_ref, inverse_ref, grad_ref, out_ref, low_ref, sums_ref):
    grad = kept_ref[...] + got_ref[...]
    hat = hat_ref[...]
    scaled = grad * gain_ref[...]
    first = jnp.mean(scaled, axis=-1, keepdims=True)
    second = jnp.mean(scaled * hat, axis=-1, keepdims=True)
    out = grad_ref[...] + (scaled - first - hat * second) * inverse_ref[:, 0:1]
    low = out.astype(low_type)
    out_ref[...] = out
    low_ref[...] = low
    sums_ref[...] = jnp.zeros_like(sums_ref)
    sums_ref[0:1, :] = jnp.sum(grad * hat, axis=0, keepdims=True)
    sums_ref[1:2, :] = jnp.sum(grad, axis=0, keepdims=True)
    sums_ref[2:3, :] = jnp.sum(low[:count].astype(wide_type), axis=0, keepdims=True)


def exact_gelu(values):
    return jax.nn.gelu(values, approximate=False)


def dot_wide(left, right):
    return jnp.dot(left, right, preferred_element_type=wide_type)


def dot_dims(left, right, left_dim, right_dim):
    return lax.dot_general(
        left, right, (((left_dim,), (right_dim,)), ((), ())), preferred_element_type=wide_type
    )


def head_cols(at):
    return slice(at * HEAD, (at + 1) * HEAD)


def ring_back(place, step):
    return lax.rem(place - step + 4, 4)


def ring_ahead(place, step):
    return lax.rem(place + step, 4)


def project_kernel(heads, at_ref, rows_ref, key_w, value_w, query_w, bias_ref, cos_ref, sin_ref, swap_ref, *out_refs):
    rows = rows_ref[...]
    swap = swap_ref[...]
    cosine = jnp.concatenate([cos_ref[: rows.shape[0], :]] * heads, axis=1)
    sine = jnp.concatenate([sin_ref[: rows.shape[0], :]] * heads, axis=1)

    def turned(weight, bias):
        value = dot_wide(rows, weight[...]) + bias
        crossed = jnp.dot(value, swap, precision=highest_precision, preferred_element_type=wide_type)
        return value * cosine + crossed * sine

    key = turned(key_w, bias_ref[1:2, :]).astype(low_type)
    value = (dot_wide(rows, value_w[...]) + bias_ref[2:3, :]).astype(low_type)
    query = (turned(query_w, bias_ref[0:1, :]).astype(low_type).astype(wide_type) * HEAD ** (-0.5)).astype(low_type)

    def write(head, step):
        for at, part in enumerate((key, value, query)):
            out_refs[step][:, head_cols(at)] = part[:, head_cols(head)]
            if at < 2:
                out_refs[4 + step][:, head_cols(at)] = part[:, head_cols(head)]

    for ring in range(4):

        @pl.when(at_ref[0] == ring)
        def _(ring=ring):
            for step in range(4):
                write((ring + step) % 4, step)


def lane_tiles(total):
    size = 384 if total % 384 == 0 else total
    return [slice(at * size, (at + 1) * size) for at in range(total // size)]


def attend_kernel(bias_ref, mask_ref, *refs):
    own_refs, cross_refs = refs[:4], refs[4:8]
    out_ref, low_ref, total_ref, own_out, cross_out, query_ref, score_ref = refs[8:]
    rows = own_refs[0].shape[0]
    total_rows = 4 * rows
    for at in range(4):
        block = slice(at * rows, (at + 1) * rows)
        query_ref[block, :] = own_refs[at][:, head_cols(2)]
        own_out[block, :] = own_refs[at][...]
        cross_out[block, :] = cross_refs[at][...]
    total_ref[...] = jnp.zeros_like(total_ref)

    def pair(at, part):
        if at < 4:
            return own_refs[at][:, head_cols(part)]
        return cross_refs[at - 4][:, head_cols(part)]

    for tile in lane_tiles(total_rows):
        query = query_ref[tile, :]
        wide = tile.stop - tile.start
        top = jnp.full((1, wide), 2.0 * masked_score, wide_type)
        for at in range(8):
            scores = dot_dims(pair(at, 0), query, 1, 1) + bias_ref[:, at : at + 1]
            if at < 4:
                scores = scores + mask_ref[at : at + 1, tile]
            score_ref[at * rows : (at + 1) * rows, :] = scores
            top = jnp.maximum(top, jnp.max(scores, axis=0, keepdims=True))
        mass = jnp.zeros((1, wide), wide_type)
        out = jnp.zeros((HEAD, wide), wide_type)
        for at in range(8):
            weights = jnp.exp(score_ref[at * rows : (at + 1) * rows, :] - top)
            mass = mass + jnp.sum(weights, axis=0, keepdims=True)
            out = out + dot_dims(pair(at, 1), weights.astype(low_type), 0, 0)
        total_ref[0:1, tile] = top + jnp.log(mass)
        rows_out = (out / mass).T
        out_ref[tile, :] = rows_out
        low_ref[tile, :] = rows_out.astype(low_type)


def attend_back_kernel(own, bias_ref, mask_ref, total_ref, out_ref, own_ref, *refs):
    grad_refs, cross_refs = refs[:4], refs[4:-4]
    pair_sum, query_sum, query_ref, grad_ref = refs[-4:]
    rows = grad_refs[0].shape[0]
    query_ref[...] = own_ref[:, head_cols(2)]
    for at in range(4):
        grad_ref[at * rows : (at + 1) * rows, :] = grad_refs[at][...]
    ones = jnp.ones((8, HEAD), wide_type)
    pair_sum[...] = jnp.zeros_like(pair_sum)
    for tile in lane_tiles(4 * rows):
        query = query_ref[tile, :]
        grad = grad_ref[tile, :]
        centre = lax.dot_general(
            ones,
            grad.astype(wide_type) * out_ref[tile, :],
            (((1,), (1,)), ((), ())),
            precision=highest_precision,
            preferred_element_type=wide_type,
        )[0:1, :]
        total = total_ref[0:1, tile]
        query_part = jnp.zeros((HEAD, tile.stop - tile.start), wide_type)
        for at in range(4):
            block = slice(at * rows, (at + 1) * rows)
            if own:
                key, value = own_ref[block, head_cols(0)], own_ref[block, head_cols(1)]
                scores = dot_dims(key, query, 1, 1) + bias_ref[:, at : at + 1] + mask_ref[at : at + 1, tile]
            else:
                key, value = cross_refs[0][block, head_cols(0)], cross_refs[0][block, head_cols(1)]
                scores = dot_dims(key, query, 1, 1) + bias_ref[:, at + 4 : at + 5]
            weights = jnp.exp(scores - total)
            pair_sum[block, head_cols(1)] += dot_wide(weights.astype(low_type), grad)
            soft = dot_dims(value, grad, 1, 1)
            back = (weights * (soft - centre)).astype(low_type)
            pair_sum[block, head_cols(0)] += dot_wide(back, query)
            query_part = query_part + dot_dims(key, back, 0, 0)
        query_sum[tile, :] = query_part.T * HEAD ** (-0.5)


def turn_back_kernel(own_pair, other_pair, own_query, other_query, cos_ref, sin_ref, swap_ref, *out_refs):
    rows = out_refs[0].shape[0]
    swap = swap_ref[...]
    for at in range(4):
        block = slice(at * rows, (at + 1) * rows)
        cosine, sine = cos_ref[block, :], sin_ref[block, :]

        def turned(value):
            crossed = jnp.dot(value, swap, precision=highest_precision, preferred_element_type=wide_type)
            return (value * cosine - crossed * sine).astype(low_type)

        pair = own_pair[block, :] + other_pair[block, :]
        out_refs[at][:, head_cols(0)] = turned(pair[:, head_cols(0)])
        out_refs[at][:, head_cols(1)] = pair[:, head_cols(1)].astype(low_type)
        out_refs[at][:, head_cols(2)] = turned(own_query[block, :] + other_query[block, :])


def mix_back_kernel(at_ref, place_ref, key_w, value_w, query_w, *refs):
    mixed_refs = refs[:4]
    out_ref, stack_ref, bias_ref = refs[4:]
    ring, clip = at_ref[0], at_ref[1]
    place = place_ref[...]
    total = None
    bias_ref[...] = jnp.zeros_like(bias_ref)
    for part, weight in ((0, key_w), (1, value_w), (2, query_w)):
        relative = jnp.concatenate([ref[:, head_cols(part)] for ref in mixed_refs], axis=1)
        ordered = dot_wide(relative, place)
        bias_ref[part : part + 1, :] = jnp.sum(ordered, axis=0, keepdims=True)
        term = dot_dims(ordered.astype(low_type), weight[...], 1, 1)
        total = term if total is None else total + term
    out_ref[...] = total
    for at in range(4):
        stack_ref[lax.rem(ring + at - clip + 4, 4)] = mixed_refs[at][...]


def clip_products(at_ref, first_ref, second_ref, pack_refs, columns):
    out = None
    half = first_ref.shape[1]
    for step in range(4):
        place = ring_back(at_ref[0], step)
        pack = pack_refs[step]
        term = dot_dims(first_ref[place], pack[:half, columns], 0, 0)
        term = term + dot_dims(second_ref[place], pack[half : 2 * half, columns], 0, 0)
        out = term if out is None else out + term
    return out


def layer_grad_kernel(at_ref, act_a, act_b, norm_a, norm_b, *refs):
    head_refs, pack_refs, out_ref = refs[:-5], refs[-5:-1], refs[-1]
    part = out_ref.shape[1] // 2
    tiles = pl.num_programs(0) - (1 if head_refs else 0)

    @pl.when(pl.program_id(0) < tiles)
    def _():
        out_ref[:, :part] = clip_products(at_ref, act_a, act_b, pack_refs, slice(0, part))
        out_ref[:, part:] = clip_products(at_ref, norm_a, norm_b, pack_refs, slice(part, 2 * part))

    if head_refs:

        @pl.when(pl.program_id(0) == tiles)
        def _():
            columns = slice(2 * part, 3 * part)
            out_ref[:, :part] = clip_products(at_ref, head_refs[0], head_refs[2], pack_refs, columns)
            out_ref[:, part:] = clip_products(at_ref, head_refs[1], head_refs[3], pack_refs, columns)


def plain_grad_kernel(at_ref, rows_a, rows_b, *refs):
    pack_refs, out_ref = refs[:4], refs[4]
    out_ref[...] = clip_products(at_ref, rows_a, rows_b, pack_refs, slice(None))


def last_grad_kernel(tiles, at_ref, head_a, head_b, *refs):
    feat_refs, pack_refs, out_ref = refs[:4], refs[4:8], refs[8]
    head_rows = 2 * head_a.shape[1]
    feat_rows = head_rows + feat_refs[0].shape[0]

    @pl.when(pl.program_id(0) < tiles)
    def _():
        out = None
        for step in range(4):
            term = dot_dims(feat_refs[step][...], pack_refs[step][head_rows:feat_rows, :], 0, 0)
            out = term if out is None else out + term
        out_ref[...] = out

    @pl.when(pl.program_id(0) == tiles + 2)
    def _():
        out = None
        small = (pack_refs[0].shape[0] - feat_rows) // 2
        for step in range(4):
            high = pack_refs[step][feat_rows : feat_rows + small, :].astype(wide_type)
            term = high + pack_refs[step][feat_rows + small :, :].astype(wide_type)
            out = term if out is None else out + term
        high = out.astype(low_type).astype(wide_type)
        out_ref[:small, :] = high
        out_ref[small:, :] = out - high

    @pl.when((pl.program_id(0) >= tiles) & (pl.program_id(0) < tiles + 2))
    def _():
        out_ref[...] = clip_products(at_ref, head_a, head_b, pack_refs, slice(None))


def ring_sum_kernel(at_ref, part_ref, *refs):
    got_refs, out_ref = refs[:3], refs[3]
    block = out_ref.shape[0]
    out = part_ref[pl.ds(pl.multiple_of(at_ref[0] * block, 8), block), :]
    for got in got_refs:
        out = out + got[...].astype(wide_type)
    out_ref[...] = out


def ring_sum(ring_at, part, got, after):
    shape = (part.shape[0] // 4, part.shape[1])
    return call_kernel(
        ring_sum_kernel,
        (ring_at[None], part, *got),
        (0,),
        jax.ShapeDtypeStruct(shape, wide_type),
        [],
        4 * shape[0] * shape[1],
        0,
        after,
    )


def half_sum_kernel(own_ref, got_ref, out_ref):
    out_ref[...] = (own_ref[...] + got_ref[...]).astype(low_type)


def half_sum(own, after):
    got = lax.ppermute(own, "frame", HALF_SWAP)
    return call_kernel(
        half_sum_kernel,
        (own, got),
        (),
        jax.ShapeDtypeStruct(own.shape, low_type),
        [],
        own.size,
        0,
        after,
    )


def join_kernel(at_ref, *refs):
    out_ref = refs[4]
    block = refs[0].shape[0]
    for step in range(4):
        start = pl.multiple_of(ring_back(at_ref[0], step) * block, 16)
        out_ref[pl.ds(start, block), :] = refs[step][...]


def join_frames(ring_at, total, after, after_far=()):
    pieces = ring_pieces(total)
    return call_kernel(
        join_kernel,
        (ring_at[None], *pieces),
        (0,),
        jax.ShapeDtypeStruct((4 * total.shape[0], total.shape[1]), low_type),
        [],
        0,
        0,
        after,
        after_far,
    )


def beside_kernel(first_ref, second_ref, out_ref):
    half, wide, other = first_ref.shape[0] // 2, first_ref.shape[1], second_ref.shape[1]
    out_ref[:, :wide] = first_ref[:half, :]
    out_ref[:, wide : wide + other] = second_ref[:half, :]
    out_ref[:, wide + other :] = second_ref[half:, :]


def gather_clips(first, second, after):
    half, wide = first.shape[0] // 2, first.shape[1]
    beside = call_kernel(
        beside_kernel,
        (first, second),
        (),
        jax.ShapeDtypeStruct((half, wide + 2 * second.shape[1]), low_type),
        [],
        0,
        0,
        after,
    )
    whole = lax.all_gather(beside, "clip")
    return whole, core_swap(whole[:, :, :wide])


def smem_spec():
    return pl.BlockSpec(memory_space=pltpu.SMEM)


def kernel_params():
    return pltpu.CompilerParams(vmem_limit_bytes=20 * 1024 * 1024)


def held_spec():
    return pl.BlockSpec(memory_space=pltpu.VMEM)


def any_specs(arrays):
    return [pl.BlockSpec(memory_space=pl.ANY)] * len(arrays)


def without(kernel, count, after):
    return lambda *refs: kernel(*refs[:count], *refs[count + len(after) :])


def layer_grad(clip_at, second_all, packs, first_all, after):
    whole, other = second_all
    half, wide = other.shape[1:]
    tiles = wide // 128
    part = 256
    block = (4, half, 128)
    heads = () if first_all is None else (first_all[0],) * 4
    held = [
        pl.BlockSpec(block, lambda i, at=at: (0, 0, tiles + at)) for at in range(len(heads))
    ]

    def moving(start):
        return pl.BlockSpec(block, lambda i: (0, 0, start + jnp.minimum(i, tiles - 1)))

    return pl.pallas_call(
        without(layer_grad_kernel, 9 + len(heads), after),
        grid=(tiles + (1 if heads else 0),),
        out_shape=jax.ShapeDtypeStruct((wide + (128 if heads else 0), 2 * part), wide_type),
        in_specs=[smem_spec(), moving(tiles), moving(2 * tiles), moving(0), moving(0)]
        + held
        + [held_spec()] * 4
        + any_specs(after),
        out_specs=pl.BlockSpec((128, 2 * part), lambda i: (i, 0)),
        compiler_params=kernel_params(),
        cost_estimate=pl.CostEstimate(
            flops=32 * half * wide * part,
            bytes_accessed=2 * whole.size + 8 * wide * part,
            transcendentals=0,
        ),
    )(clip_at[None], whole, whole, whole, other, *heads, *packs, *after)


def plain_grad(clip_at, rows_all, packs, after):
    whole, other = rows_all
    half, count = other.shape[1:]
    part = packs[0].shape[1]
    block = pl.BlockSpec((4, half, 128), lambda i: (0, 0, i))
    return pl.pallas_call(
        without(plain_grad_kernel, 7, after),
        grid=(count // 128,),
        out_shape=jax.ShapeDtypeStruct((count, part), wide_type),
        in_specs=[smem_spec(), block, block] + [held_spec()] * 4 + any_specs(after),
        out_specs=pl.BlockSpec((128, part), lambda i: (i, 0)),
        compiler_params=kernel_params(),
        cost_estimate=pl.CostEstimate(
            flops=16 * half * count * part,
            bytes_accessed=16 * half * count + 4 * count * part,
            transcendentals=0,
        ),
    )(clip_at[None], whole, other, *packs, *after)


def last_grad(clip_at, first_all, feats, packs, after, after_far):
    whole, other = first_all
    half, part = other.shape[1], packs[0].shape[1]
    first_block = other.shape[2] // 128
    tiles = feats[0].shape[1] // 128
    kernel = functools.partial(last_grad_kernel, tiles)

    def moving(start):
        return pl.BlockSpec(
            (4, half, 128), lambda i: (0, 0, start + jnp.clip(i - tiles, 0, 1))
        )

    return pl.pallas_call(
        without(kernel, 11, (*after, *after_far)),
        grid=(tiles + 3,),
        out_shape=jax.ShapeDtypeStruct(((tiles + 3) * 128, part), wide_type),
        in_specs=[smem_spec(), moving(first_block), moving(first_block + 2)]
        + [pl.BlockSpec((feats[0].shape[0], 128), lambda i: (0, jnp.minimum(i, tiles - 1)))] * 4
        + [held_spec()] * 4
        + any_specs(after)
        + [pl.BlockSpec(memory_space=pltpu.HBM)] * len(after_far),
        out_specs=pl.BlockSpec((128, part), lambda i: (i, 0)),
        compiler_params=kernel_params(),
    )(clip_at[None], whole, whole, *feats, *packs, *after, *after_far)


def by_clip(clip_at, write):
    for place in range(4):

        @pl.when(clip_at == place)
        def _(place=place):
            for step in range(4):
                write((place - step) % 4, step)


def place_layer_kernel(tiles, at_ref, all_ref, *outs):
    part = all_ref.shape[2] // 2
    is_last = pl.program_id(0) == tiles

    for place in range(4):
        columns = slice(place * part, (place + 1) * part)
        left = all_ref[place, :, :part].astype(wide_type)
        right = all_ref[place, :, part:].astype(wide_type)

        @pl.when(jnp.logical_not(is_last))
        def _(columns=columns, left=left, right=right):
            outs[0][0, :, columns] = left
            outs[1][0, :, columns] = right

        if len(outs) > 2:

            @pl.when(is_last)
            def _(columns=columns, left=left, right=right):
                outs[2][0, : outs[2].shape[1] // 2, columns] = left
                outs[2][0, outs[2].shape[1] // 2 :, columns] = right


def place_layer(clip_at, layer, levels, joined, earlier, heads_layer, after):
    part = joined.shape[2] // 2
    rows = 4 * part
    tiles = rows // 128
    heads = joined.shape[1] > rows
    out = [(levels, rows, 4 * part)] * 2 + [(levels, 256, 4 * part)] * heads
    tall = pl.BlockSpec((1, 128, 4 * part), lambda i: (layer, jnp.minimum(i, tiles - 1), 0))
    wide = pl.BlockSpec((1, 256, 4 * part), lambda i: (heads_layer, 0, 0))
    return pl.pallas_call(
        without(functools.partial(place_layer_kernel, tiles), 2, (*earlier, *after)),
        grid=(tiles + (1 if heads else 0),),
        out_shape=tuple(jax.ShapeDtypeStruct(shape, wide_type) for shape in out),
        in_specs=[smem_spec(), pl.BlockSpec((4, 128, 2 * part), lambda i: (0, i, 0))]
        + any_specs(earlier)
        + any_specs(after),
        out_specs=(tall, tall) + ((wide,) if heads else ()),
        input_output_aliases={2 + at: at for at in range(len(earlier))},
        compiler_params=kernel_params(),
    )(clip_at[None], joined, *earlier, *after)


def place_last_kernel(skip, at_ref, *refs):
    pieces = refs[:4]
    in_ref, small_ref, proj_ref = refs[-3:]
    part = pieces[0].shape[1]
    heads = skip + proj_ref.shape[1]
    small = small_ref.shape[0]

    def write(place, step):
        columns = slice(place * part, (place + 1) * part)
        piece = pieces[step]
        in_ref[:, columns] = piece[: in_ref.shape[0], :].astype(wide_type)
        proj_ref[0, :, columns] = piece[skip:heads, :].astype(wide_type)
        small_ref[:, columns] = piece[heads : heads + small, :].astype(wide_type) + piece[
            heads + small :, :
        ].astype(wide_type)

    by_clip(at_ref[0], write)


def place_last(clip_at, feat_rows, skip, levels, pieces, earlier):
    part = pieces[0].shape[1]
    return pl.pallas_call(
        functools.partial(place_last_kernel, skip),
        grid=(1,),
        out_shape=(
            jax.ShapeDtypeStruct((feat_rows, 4 * part), wide_type),
            jax.ShapeDtypeStruct((64, 4 * part), wide_type),
            jax.ShapeDtypeStruct((levels, 256, 4 * part), wide_type),
        ),
        in_specs=[smem_spec()]
        + [pl.BlockSpec(pieces[0].shape, lambda i: (0, 0))] * 4
        + [pl.BlockSpec(memory_space=pl.ANY)],
        out_specs=(
            pl.BlockSpec((feat_rows, 4 * part), lambda i: (0, 0)),
            pl.BlockSpec((64, 4 * part), lambda i: (0, 0)),
            pl.BlockSpec((1, 256, 4 * part), lambda i: (0, 0, 0)),
        ),
        input_output_aliases={5: 2},
        compiler_params=kernel_params(),
    )(clip_at[None], *pieces, earlier)


def pack_kernel(by_rows, count, at_ref, *refs):
    parts, outs = refs[:count], refs[count:]
    for clip in range(4):

        @pl.when(at_ref[0] == clip)
        def _(clip=clip):
            for step in range(4):
                place, start = (clip + step) % 4, 0
                for part in parts:
                    size = part.shape[1] // 4
                    value = part[:, place * size : (place + 1) * size]
                    if by_rows:
                        outs[step][start : start + part.shape[0], :] = value
                        start += part.shape[0]
                    else:
                        outs[step][:, start : start + size] = value
                        start += size


def pack_parts(clip_at, parts, by_rows, after):
    sizes = [part.shape[1] // 4 for part in parts]
    if by_rows:
        shape = (sum(part.shape[0] for part in parts), sizes[0])
    else:
        shape = (parts[0].shape[0], sum(sizes))
    return call_kernel(
        functools.partial(pack_kernel, by_rows, len(parts)),
        (clip_at[None], *parts),
        (0,),
        tuple(jax.ShapeDtypeStruct(shape, low_type) for _ in range(4)),
        [],
        0,
        0,
        after,
    )


def place_heads_kernel(at_ref, all_ref, *refs):
    out_ref = refs[-1]
    for place in range(4):
        piece = all_ref[place].astype(wide_type)
        for at, part in ((1, 0), (2, 1), (0, 2)):
            out_ref[0, at, :, head_cols(place)] = piece[:, head_cols(part)]


def place_heads(clip_at, layer, levels, joined, earlier, after):
    rows = joined.shape[1]
    tile = 256
    count = 2
    return pl.pallas_call(
        without(place_heads_kernel, count, (*earlier, *after)),
        grid=(rows // tile,),
        out_shape=jax.ShapeDtypeStruct((levels, 3, rows, 4 * HEAD), wide_type),
        in_specs=[smem_spec(), pl.BlockSpec((4, tile, 3 * HEAD), lambda i: (0, i, 0))]
        + any_specs(earlier)
        + any_specs(after),
        out_specs=pl.BlockSpec((1, 3, tile, 4 * HEAD), lambda i: (layer, 0, i, 0)),
        input_output_aliases={count + at: at for at in range(len(earlier))},
        compiler_params=kernel_params(),
    )(clip_at[None], joined, *earlier, *after)


def stack_kernel(*refs):
    out_ref = refs[-1]
    for at, ref in enumerate(refs[:-1]):
        out_ref[8 * at : 8 * (at + 1), :] = ref[...]


def feature_grad_kernel(ids_ref, rows_ref, weight_ref, out_ref):
    size = rows_ref.shape[0] // 4
    for at in range(4):
        start = pl.multiple_of(ids_ref[at] * size, 8)
        out_ref[pl.ds(start, size), :] = dot_dims(
            rows_ref[at * size : (at + 1) * size, :], weight_ref[...], 1, 1
        )


def last_pack_kernel(at_ref, head_ref, patch_ref, small_a, small_b, *outs):
    heads, patches, small = head_ref.shape[0], patch_ref.shape[0], small_a.shape[0]
    values = small_a[...] + small_b[...]
    high = values.astype(low_type)
    rest = (values - high.astype(wide_type)).astype(low_type)
    for clip in range(4):

        @pl.when(at_ref[0] == clip)
        def _(clip=clip):
            for step in range(4):
                size = outs[step].shape[1]
                place = (clip + step) % 4
                columns = slice(place * size, (place + 1) * size)
                outs[step][:heads, :] = head_ref[:, columns]
                outs[step][heads : heads + patches, :] = patch_ref[:, columns]
                outs[step][heads + patches : heads + patches + small, :] = high[:, columns]
                outs[step][heads + patches + small :, :] = rest[:, columns]


def call_kernel(kernel, args, in_smem, outs, scratch, flops, exps, after=(), after_far=(), piped=()):
    count = len(args)

    def spec(at):
        if at in piped:
            return pl.BlockSpec(args[at].shape, lambda i, rank=args[at].ndim: (0,) * rank)
        return pl.BlockSpec(memory_space=pltpu.SMEM if at in in_smem else pltpu.VMEM)

    specs = [spec(at) for at in range(count)]
    specs += any_specs(after) + [pl.BlockSpec(memory_space=pltpu.HBM)] * len(after_far)
    after = (*after, *after_far)
    moved = sum(a.size * a.dtype.itemsize for a in args)
    return pl.pallas_call(
        without(kernel, count, after),
        grid=(1,),
        out_shape=outs,
        in_specs=specs,
        out_specs=jax.tree.map(lambda _: pl.BlockSpec(memory_space=pltpu.VMEM), outs),
        scratch_shapes=scratch,
        compiler_params=kernel_params(),
        cost_estimate=pl.CostEstimate(flops=flops, bytes_accessed=moved, transcendentals=exps),
    )(*args, *after)


def on_device(
    features,
    cond_values,
    cond_live,
    in_weight,
    in_bias,
    act_weight,
    act_bias,
    state_weight,
    state_bias,
    attn_gain,
    attn_shift,
    qkv_weight,
    qkv_bias,
    proj_weight,
    proj_bias,
    mlp_gain,
    mlp_shift,
    up_weight,
    up_bias,
    down_weight,
    down_bias,
    out_grad,
):
    patch_rows = features.shape[2]
    feat_width = features.shape[3]
    slot_count = cond_values.shape[2]
    all_frames = cond_live.shape[1]
    model_width = in_weight.shape[1]
    width = qkv_weight.shape[3]
    heads = width // HEAD
    level_count = attn_gain.shape[0]
    patches = patch_rows // 4
    chunk_rows = patches + EXTRA
    rows = 4 * chunk_rows
    hidden_width = up_weight.shape[2]

    tensor_at = lax.axis_index("tensor")
    chip_at, core_at = tensor_at // 2, tensor_at % 2
    frame_at = lax.axis_index("frame")
    half_at, ring_at = frame_at // 4, frame_at % 4
    clip_at = lax.axis_index("clip")

    chunk_ids = [
        2 * jnp.bitwise_xor(core_at, core_step) + jnp.bitwise_xor(chip_at, chip_step)
        for core_step in range(2)
        for chip_step in range(2)
    ]
    own_chunk = chunk_ids[0]
    own_frames = jnp.stack([4 * half_at + (ring_at - step) % 4 for step in range(4)])
    cross_frames = jnp.stack([4 * (1 - half_at) + (ring_at - step) % 4 for step in range(4)])

    within = lax.broadcasted_iota(jnp.int32, (chunk_rows, 1), 0)
    is_patch = within < patches
    heights, columns = [], []
    for chunk_id in chunk_ids:
        patch_id = chunk_id * patches + within
        heights.append(jnp.where(is_patch, patch_id // GRID_W, 0))
        columns.append(jnp.where(is_patch, patch_id % GRID_W, 0))
    heights = jnp.concatenate(heights, axis=0).astype(wide_type)
    columns = jnp.concatenate(columns, axis=0).astype(wide_type)
    swap_table, rate_table = rotary_tables(HEAD, heads)
    swap_heads = jnp.asarray(swap_table)
    swap_one = jnp.asarray(swap_table[:HEAD, :HEAD])
    rates = rate_table[:, :HEAD]
    place_angles = heights * rates[1] + columns * rates[2]
    angles = jnp.concatenate(
        [
            own_frames[step].astype(wide_type) * rates[0][None, :] + place_angles
            for step in range(4)
        ],
        axis=0,
    )
    cosine_four, sine_four = jnp.cos(angles), jnp.sin(angles)
    head_from = jnp.arange(width)
    head_to = ((head_from // HEAD + ring_at) % 4) * HEAD + head_from % HEAD
    head_place = (head_to[:, None] == head_from[None, :]).astype(low_type)
    proj_turned = [
        lax.dynamic_slice_in_dim(
            jnp.concatenate([proj_weight[layer], proj_weight[layer]], axis=0),
            ring_at * HEAD,
            width,
            0,
        )
        for layer in range(level_count)
    ]
    ring_scalar = ring_at.astype(jnp.int32)
    clip_scalar = clip_at.astype(jnp.int32)

    live_all = cond_live[0].astype(wide_type)
    own_slots = lax.dynamic_index_in_dim(live_all, frame_at, 0, False)

    def live_rows(slots, chunk_id):
        picked = jnp.where(
            chunk_id < slot_count,
            lax.dynamic_index_in_dim(slots, jnp.minimum(chunk_id, slot_count - 1), 1, False),
            0.0,
        )
        return jnp.where(is_patch, 1.0, jnp.where(within == patches, picked[None, :], 0.0))

    sources = jnp.concatenate([own_frames, cross_frames])
    source_live = jnp.take(live_all, sources, axis=0)
    key_live = jnp.concatenate([live_rows(source_live, c) for c in chunk_ids], axis=0)
    reached = jnp.concatenate([jnp.ones((4,), jnp.bool_), jnp.full((4,), half_at == 1)])
    key_bias = jnp.where((key_live > 0.5) & reached[None, :], 0.0, masked_score).astype(wide_type)
    seen = own_frames[:, None] <= own_frames[None, :]
    causal = jnp.where(seen, 0.0, masked_score).astype(wide_type)
    causal = jnp.pad(jnp.repeat(causal, rows, axis=1), ((0, 4), (0, 0)))
    own_live = live_rows(own_slots[None, :], own_chunk)

    def extra_rows(slot_rows):
        picked = lax.dynamic_slice_in_dim(
            slot_rows, jnp.minimum(own_chunk, slot_count - 1), 1, 0
        )
        picked = jnp.where(own_chunk < slot_count, picked, jnp.zeros_like(picked))
        return jnp.pad(picked, ((0, EXTRA - 1), (0, 0)))

    cond_here = cond_values[0, 0]
    act_rows = jnp.dot(cond_here, act_weight, precision=highest_precision) + act_bias
    state_rows = jnp.dot(cond_here, state_weight, precision=highest_precision) + state_bias
    even_slot = (jnp.arange(slot_count) % 2 == 0)[:, None]
    cond_x = jnp.where(even_slot, act_rows, state_rows) * own_slots[:, None]

    flat_feat = jnp.concatenate(
        [
            lax.dynamic_slice_in_dim(features[0, 0], c * patches, patches, 0)
            for c in chunk_ids
        ],
        axis=0,
    )
    kept, got = halves_tensor(dot_wide(flat_feat, in_weight))
    stream = jnp.concatenate([kept + got + in_bias, extra_rows(cond_x)], axis=0)

    feat_wide = -(-feat_width // 128) * 128
    feat_low = jnp.pad(flat_feat, ((0, 0), (0, feat_wide - feat_width)))
    feats = [feat_low] + [
        lax.ppermute(feat_low, "clip", clip_shift(step)) for step in range(1, 4)
    ]
    pair_work = 2 * 32 * rows * rows * HEAD
    pair_exps = 32 * rows * rows
    weight_parts = [
        [qkv_weight[layer, :, at] for at in (1, 2, 0)] for layer in range(level_count)
    ]

    def norm(terms, gain, shift, after_far=()):
        chunk = jax.ShapeDtypeStruct((chunk_rows, model_width), wide_type)
        return call_kernel(
            norm_kernel,
            (gain[None], shift[None], *terms),
            (),
            (
                chunk,
                chunk,
                jax.ShapeDtypeStruct((chunk_rows, 128), wide_type),
                jax.ShapeDtypeStruct((chunk_rows, model_width), low_type),
            ),
            [],
            12 * chunk_rows * model_width,
            0,
            (),
            after_far,
        )

    def norm_back(part, gain, hat, inverse, grad, count, after=(), after_far=()):
        kept, got = halves_tensor(part)
        return call_kernel(
            functools.partial(norm_back_kernel, count),
            (kept, got, gain[None], hat, inverse, grad),
            (),
            (
                jax.ShapeDtypeStruct((chunk_rows, model_width), wide_type),
                jax.ShapeDtypeStruct((chunk_rows, model_width), low_type),
                jax.ShapeDtypeStruct((8, model_width), wide_type),
            ),
            [],
            16 * chunk_rows * model_width,
            0,
            after,
            after_far,
            (2, 3, 4, 5),
        )

    slot_grads = out_grad[0, 0, patch_rows:] * own_slots[:, None].astype(low_type)
    slot_blocks = jnp.concatenate(
        [
            jnp.pad(slot_grads[:, None], ((0, 0), (0, EXTRA - 1), (0, 0))),
            jnp.zeros((4 - slot_count, EXTRA, model_width), low_type),
        ],
        axis=0,
    )
    branch_parts = []
    for chunk_id in chunk_ids:
        branch_parts.append(
            lax.dynamic_slice_in_dim(out_grad[0, 0], chunk_id * patches, patches, 0)
        )
        branch_parts.append(lax.dynamic_index_in_dim(slot_blocks, chunk_id, 0, False))
    first_branch = jnp.concatenate(branch_parts, axis=0)
    stored = []
    terms = (stream,)
    before = None
    for layer in range(level_count):
        stream, hat_one, inverse_one, first_chunk = norm(terms, attn_gain[layer], attn_shift[layer])
        first_in = join_rows_tensor(first_chunk)
        bias = jnp.pad(qkv_bias[layer], ((0, 5), (0, 0)))
        heads_out = call_kernel(
            functools.partial(project_kernel, heads),
            (
                ring_scalar[None],
                first_in,
                *weight_parts[layer],
                bias,
                cosine_four,
                sine_four,
                swap_heads,
            ),
            (0,),
            tuple(
                jax.ShapeDtypeStruct((rows, count * HEAD), low_type)
                for count in (3, 3, 3, 3, 2, 2, 2, 2)
            ),
            [],
            6 * rows * model_width * width,
            0,
            (),
            () if before is None else (before[0][0],),
            (2, 3, 4, 5, 6, 7, 8),
        )
        blocks = to_heads(heads_out[:4])
        cross = pairs_to_later_half(heads_out[4:])
        attn_wide, attn_turned, log_total, own_all, cross_all = call_kernel(
            attend_kernel,
            (key_bias, causal, *blocks, *cross),
            (),
            (
                jax.ShapeDtypeStruct((4 * rows, HEAD), wide_type),
                jax.ShapeDtypeStruct((4 * rows, HEAD), low_type),
                jax.ShapeDtypeStruct((8, 4 * rows), wide_type),
                jax.ShapeDtypeStruct((4 * rows, 3 * HEAD), low_type),
                jax.ShapeDtypeStruct((4 * rows, 2 * HEAD), low_type),
            ),
            [
                pltpu.VMEM((4 * rows, HEAD), low_type),
                pltpu.VMEM((8 * rows, lane_tiles(4 * rows)[0].stop), wide_type),
            ],
            2 * pair_work,
            pair_exps,
            tuple(feats[1:]) if layer == 0 else (),
        )
        attn_relative = jnp.concatenate(
            to_frames([attn_turned[at * rows : (at + 1) * rows] for at in range(4)]), axis=1
        )
        attn_low = dot_wide(attn_relative, head_place).astype(low_type)
        if layer < level_count - 1:
            first_all = gather_clips(first_in, attn_low, ())
        kept, got = halves_tensor(dot_wide(attn_relative, proj_turned[layer]))
        middle, hat_two, inverse_two, second_chunk = norm(
            (stream, kept, got, proj_bias[layer][None]), mlp_gain[layer], mlp_shift[layer],
            () if before is None else (before[1][0], first_branch),
        )
        second_in = join_rows_tensor(second_chunk)
        hidden = dot_wide(second_in, up_weight[layer]) + up_bias[layer]
        active_low = exact_gelu(hidden).astype(low_type)
        second_all = gather_clips(second_in, active_low, ())
        if layer == level_count - 1:
            first_all = (first_in, attn_low)
        before = (first_all, second_all)
        kept, got = halves_tensor(dot_wide(active_low, down_weight[layer]))
        terms = (middle, kept, got, down_bias[layer][None])
        stored.append(
            (
                hat_one,
                inverse_one,
                own_all,
                cross_all,
                log_total,
                attn_wide,
                hat_two,
                inverse_two,
                hidden,
                first_all,
                second_all,
            )
        )
    def in_order(full, count):
        out = jnp.zeros((4 * count,) + full.shape[1:], full.dtype)
        size = full.shape[0] // 4
        for at, chunk_id in enumerate(chunk_ids):
            out = lax.dynamic_update_slice_in_dim(
                out, full[at * size : at * size + count], chunk_id * count, 0
            )
        return out

    def block_rows(after):
        low = call_kernel(
            block_kernel,
            (*terms, jnp.broadcast_to(own_live, (chunk_rows, 128))),
            (),
            jax.ShapeDtypeStruct((chunk_rows, model_width), low_type),
            [],
            4 * chunk_rows * model_width,
            0,
            after,
        )
        return join_rows_tensor(low)

    def block_in_order(block_full):
        slot_full = jnp.concatenate(
            [
                block_full[at * chunk_rows + patches : at * chunk_rows + patches + 1]
                for at in range(4)
            ],
            axis=0,
        )
        return jnp.concatenate(
            [in_order(block_full, patches), in_order(slot_full, 1)[:slot_count]], axis=0
        )[None, None]

    own_out = lax.dynamic_slice_in_dim(out_grad[0, 0], own_chunk * patches, patches, 0)
    grad_stream = (
        jnp.concatenate(
            [
                own_out.astype(wide_type),
                extra_rows(out_grad[0, 0, patch_rows:].astype(wide_type)),
            ],
            axis=0,
        )
        * own_live
    )

    small = {}
    small["down", level_count - 1] = jnp.sum(grad_stream, axis=0)
    sums_list = []
    wide_part = model_width // 4
    later = None
    for layer in reversed(range(level_count)):
        (
            hat_one,
            inverse_one,
            own_all,
            cross_all,
            log_total,
            attn_wide,
            hat_two,
            inverse_two,
            hidden,
            first_all,
            second_all,
        ) = stored[layer]
        branch = first_branch if later is None else join_rows_tensor(branch_chunk)
        _, gelu_pull = jax.vjp(exact_gelu, hidden)
        grad_hidden = gelu_pull(dot_dims(branch, down_weight[layer], 1, 1))[0].astype(low_type)
        small["up", layer] = jnp.sum(grad_hidden.astype(wide_type), axis=0)
        parts = [branch, grad_hidden] + ([] if later is None else [later["proj_out"]])
        packs = pack_parts(clip_scalar, parts, False, ())
        grad_middle, proj_chunk, sums = norm_back(
            dot_dims(grad_hidden, up_weight[layer], 1, 1),
            mlp_gain[layer],
            hat_two,
            inverse_two,
            grad_stream,
            chunk_rows,
            (packs[0],) if later is None else (packs[0], later["tall_join"], later["heads_sum"]),
        )
        sums_list.append(sums)
        packs = swap_clips(packs)
        if later is None:
            block_full = block_rows((proj_chunk,))
            block_out = block_in_order(block_full)
        proj_out = join_rows_tensor(proj_chunk)
        grad_attn = dot_dims(proj_out, proj_turned[layer], 1, 1).astype(low_type)
        grads = to_heads([grad_attn[:, head_cols(at)] for at in range(4)])

        if later is not None:
            later["heads_ring"] = ring_sum(
                ring_scalar, later["heads_sum"], later["heads_got"], (proj_chunk,)
            )

            later["tall_all"] = lax.all_gather(later["tall_join"], "clip")

        def attend_back(own, after, after_far=()):
            return call_kernel(
                functools.partial(attend_back_kernel, own),
                (key_bias, causal, log_total, attn_wide, own_all, *grads)
                + (() if own else (cross_all,)),
                (),
                (
                    jax.ShapeDtypeStruct((4 * rows, 2 * HEAD), wide_type),
                    jax.ShapeDtypeStruct((4 * rows, HEAD), wide_type),
                ),
                [
                    pltpu.VMEM((4 * rows, HEAD), low_type),
                    pltpu.VMEM((4 * rows, HEAD), low_type),
                ],
                5 * pair_work // 2,
                pair_exps // 2,
                after,
                after_far,
                (0, 1, 2, 3, 4) if own else (0, 1, 2, 3, 4, 9),
            )

        cross_pair, cross_query = attend_back(
            False, () if later is None else (later["heads_ring"],)
        )
        got_pair = lax.ppermute(cross_pair, "frame", DOWN_HALF)
        if later is None:
            first_all = gather_clips(*first_all, (cross_pair,))
        tall_sum = layer_grad(
            clip_scalar,
            second_all,
            packs,
            None if later is None else later["first_all"],
            (cross_pair,),
        )
        own_pair, own_query = attend_back(
            True, (), (tall_sum,) if later is None else (tall_sum, later["tall_all"], block_full)
        )
        tall_got = ring_sends(tall_sum, ring_at)
        if later is not None:
            later["heads_total"] = half_sum(later["heads_ring"], (own_pair,))
        tall_ring = ring_sum(ring_scalar, tall_sum, tall_got, ())
        tall_total = half_sum(tall_ring, ())
        turned = call_kernel(
            turn_back_kernel,
            (own_pair, got_pair, own_query, cross_query, cosine_four, sine_four, swap_one),
            (),
            tuple(jax.ShapeDtypeStruct((rows, 3 * HEAD), low_type) for _ in range(4)),
            [],
            24 * rows * HEAD * HEAD,
            0,
            (tall_ring,) if later is None else (tall_ring, later["heads_total"]),
            (),
            (4, 5, 6),
        )
        mixed = to_frames(list(turned))
        if later is not None:
            later["heads_join"] = join_frames(ring_scalar, later["heads_total"], (turned[0],))
        normed_part, mixed_stack, bias_sums = call_kernel(
            mix_back_kernel,
            (
                jnp.stack([ring_scalar, clip_scalar]),
                head_place,
                *weight_parts[layer],
                *mixed,
            ),
            (0,),
            (
                jax.ShapeDtypeStruct((rows, model_width), wide_type),
                jax.ShapeDtypeStruct((4, rows, 3 * HEAD), low_type),
                jax.ShapeDtypeStruct((8, width), wide_type),
            ),
            [],
            6 * rows * model_width * width,
            0,
            (tall_total,) if later is None else (tall_total, later["heads_join"]),
            (),
            (1, 2, 3, 4),
        )
        small["qkv", layer] = jnp.concatenate([bias_sums[2:3], bias_sums[:2]], axis=0)
        packs = swap_clips([mixed_stack[step] for step in range(4)])
        if layer == 0:
            heads_sum = plain_grad(clip_scalar, first_all, packs, ())
            heads_got = ring_sends(heads_sum, ring_at)
        grad_stream, branch_chunk, sums = norm_back(
            normed_part,
            attn_gain[layer],
            hat_one,
            inverse_one,
            grad_middle,
            patches if layer == 0 else chunk_rows,
            tuple(packs[1:]) if layer > 0 else (heads_sum,),
        )
        sums_list.append(sums)
        tall_join = join_frames(ring_scalar, tall_total, (branch_chunk,))

        if layer > 0:
            heads_sum = plain_grad(clip_scalar, first_all, packs, (branch_chunk,))
            heads_got = ring_sends(heads_sum, ring_at)
        if layer > 0:
            later = {
                "proj_out": proj_out,
                "first_all": first_all,
                "tall_join": tall_join,
                "heads_sum": heads_sum,
                "heads_got": heads_got,
            }

    patch_chunk = branch_chunk[:patches]
    grad_patch = join_rows_tensor(patch_chunk)
    grad_features = call_kernel(
        feature_grad_kernel,
        (jnp.stack(chunk_ids).astype(jnp.int32), grad_patch, in_weight),
        (0,),
        jax.ShapeDtypeStruct((patch_rows, feat_width), wide_type),
        [],
        2 * patch_rows * feat_width * model_width,
        0,
        piped=(2,),
    )
    slot_row = grad_stream[patches : patches + 1] * own_live[patches : patches + 1]
    own_cond = lax.dynamic_slice_in_dim(
        cond_here, jnp.minimum(own_chunk, slot_count - 1), 1, 0
    )
    slot_part = jnp.concatenate([own_cond.T * slot_row, slot_row], axis=0)
    here = own_chunk < slot_count
    is_act = here & (own_chunk % 2 == 0)
    is_state = here & (own_chunk % 2 == 1)
    act_part = jnp.where(is_act, slot_part, 0.0)
    state_part = jnp.where(is_state, slot_part, 0.0)

    def at_tensor(value, total):
        return lax.dynamic_update_slice(
            jnp.zeros((value.shape[0], total), wide_type),
            value,
            (0, tensor_at * value.shape[1]),
        )

    layers = range(level_count)
    qkv_rows = at_tensor(
        jnp.concatenate([small["qkv", layer] for layer in layers], axis=0), 4 * width
    )
    mixed_rows = jnp.concatenate(
        [qkv_rows, small["down", level_count - 1][None], jnp.zeros_like(qkv_rows[:1])], axis=0
    )
    ups = at_tensor(jnp.stack([small["up", layer] for layer in layers]), 4 * hidden_width)
    parts = [*sums_list, act_part, state_part, mixed_rows, ups.reshape(-1, model_width)]
    vector = call_kernel(
        stack_kernel,
        tuple(parts),
        (),
        jax.ShapeDtypeStruct((8 * len(parts), model_width), wide_type),
        [],
        0,
        0,
    )
    vector = vector + core_swap(vector)
    later["heads_all"] = lax.all_gather(later["heads_join"], "clip")
    head_rows, patch_count, small_rows = proj_out.shape[0], grad_patch.shape[0], vector.shape[0]
    packs = call_kernel(
        last_pack_kernel,
        (clip_scalar[None], proj_out, grad_patch, vector, chip_swap(vector)),
        (0,),
        tuple(
            jax.ShapeDtypeStruct((head_rows + patch_count + 2 * small_rows, wide_part), low_type)
            for _ in range(4)
        ),
        [],
        0,
        0,
    )
    tall_all = lax.all_gather(tall_join, "clip")
    placed = place_layer(
        clip_scalar, level_count - 1, level_count, later["tall_all"], (), 0, (packs[0],)
    )
    packs = swap_clips(packs)
    heads_ring = ring_sum(ring_scalar, heads_sum, heads_got, (packs[1],))
    last_sum = last_grad(
        clip_scalar, first_all, feats, packs, (heads_ring,), (placed[0], grad_features)
    )
    last_ring = ring_sum(ring_scalar, last_sum, ring_sends(last_sum, ring_at), ())
    heads_total = half_sum(heads_ring, ())
    heads_join = join_frames(ring_scalar, heads_total, ())
    heads_all = lax.all_gather(heads_join, "clip")
    heads_placed = place_heads(
        clip_scalar, level_count - 1, level_count, later["heads_all"], (), (packs[0],)
    )
    last_join = join_frames(
        ring_scalar, half_sum(last_ring, ()), (), (tall_all, heads_placed)
    )
    last_pieces = clip_pieces(last_join)
    grad_down, grad_up, grad_proj = place_layer(
        clip_scalar, 0, level_count, tall_all, placed, level_count - 1, ()
    )
    grad_in, vector, grad_proj = place_last(
        clip_scalar, feat_width, feat_wide, level_count, last_pieces, grad_proj
    )
    grad_heads = (place_heads(clip_scalar, 0, level_count, heads_all, (heads_placed,), ()),)


    def norm_sums(layer, first, row):
        return vector[8 * (2 * (level_count - 1 - layer) + first) + row]

    grad_mlp_gain = jnp.stack([norm_sums(layer, 0, 0) for layer in layers])
    grad_mlp_shift = jnp.stack([norm_sums(layer, 0, 1) for layer in layers])
    grad_proj_bias = jnp.stack([norm_sums(layer, 0, 2) for layer in layers])
    grad_attn_gain = jnp.stack([norm_sums(layer, 1, 0) for layer in layers])
    grad_attn_shift = jnp.stack([norm_sums(layer, 1, 1) for layer in layers])
    rest = vector[16 * level_count :]
    grad_down_bias = jnp.stack(
        [norm_sums(layer + 1, 1, 2) for layer in range(level_count - 1)]
        + [rest[16 + 3 * level_count]]
    )
    grad_qkv_bias = lax.dynamic_slice_in_dim(
        rest[16 : 16 + 3 * level_count], tensor_at * width, width, 1
    )
    grad_qkv_bias = grad_qkv_bias.reshape(level_count, 3, width)
    grad_up_bias = lax.dynamic_slice_in_dim(
        rest[24:].reshape(level_count, 4 * hidden_width), tensor_at * hidden_width, hidden_width, 1
    )
    act_count = cond_here.shape[1]
    return (
        block_out,
        grad_features[None, None],
        grad_in,
        norm_sums(0, 1, 2),
        rest[:act_count],
        rest[act_count],
        rest[8 : 8 + act_count],
        rest[8 + act_count],
        grad_attn_gain,
        grad_attn_shift,
        jnp.swapaxes(grad_heads[0], 1, 2),
        grad_qkv_bias,
        grad_proj,
        grad_proj_bias,
        grad_mlp_gain,
        grad_mlp_shift,
        grad_up,
        grad_up_bias,
        grad_down,
        grad_down_bias,
    )


def solution(mesh):
    return jax.shard_map(
        on_device,
        mesh=mesh,
        in_specs=(
            P("clip", "frame", None, "tensor"),
            P("clip", "frame", None, None),
            P("clip", None, None),
            P("tensor", None),
            P(),
            P(),
            P(),
            P(),
            P(),
            P(),
            P(),
            P(None, None, None, "tensor"),
            P(None, None, "tensor"),
            P(None, "tensor", None),
            P(),
            P(),
            P(),
            P(None, None, "tensor"),
            P(None, "tensor"),
            P(None, "tensor", None),
            P(),
            P("clip", "frame", None, None),
        ),
        out_specs=(
            P("clip", "frame", None, None),
            P("clip", "frame", None, "tensor"),
            P("tensor", None),
            P(),
            P(),
            P(),
            P(),
            P(),
            P(),
            P(),
            P(None, None, None, "tensor"),
            P(None, None, "tensor"),
            P(None, "tensor", None),
            P(),
            P(),
            P(),
            P(None, None, "tensor"),
            P(None, "tensor"),
            P(None, "tensor", None),
            P(),
        ),
        check_vma=False,
    )
```

```python
import functools

import jax
import jax.numpy as jnp
import numpy as np
from jax import lax
from jax.experimental import pallas as pl
from jax.experimental.pallas import tpu as pltpu
from jax.sharding import PartitionSpec as P

HEAD = 64
GRID_W = 16
EXTRA = 8

highest_precision = lax.Precision.HIGHEST
norm_epsilon = 1e-06
masked_score = -1000000000.0
low_type = jnp.bfloat16
wide_type = jnp.float32

CORE_SWAP = [(0, 1), (1, 0), (2, 3), (3, 2)]
CHIP_SWAP = [(0, 2), (2, 0), (1, 3), (3, 1)]
HALF_SWAP = [(i, (i + 4) % 8) for i in range(8)]


def clip_shift(step):
    return [(i, (i + step) % 4) for i in range(4)]


def frame_shift(halves, step):
    return [
        (4 * half + i, 4 * ((half + halves) % 2) + (i + step) % 4)
        for half in range(2)
        for i in range(4)
    ]


def core_swap(value):
    return lax.ppermute(value, "tensor", CORE_SWAP)


def chip_swap(value):
    return lax.ppermute(value, "tensor", CHIP_SWAP)


def halves_tensor(part):
    half = part.shape[0] // 2
    pair = part[:half] + core_swap(part[half:])
    quarter = half // 2
    return pair[:quarter], chip_swap(pair[quarter:])


def join_rows_tensor(chunk):
    pair = jnp.concatenate([chunk, chip_swap(chunk)], axis=0)
    return jnp.concatenate([pair, core_swap(pair)], axis=0)


def to_heads(blocks):
    return [blocks[0]] + [
        lax.ppermute(blocks[step], "frame", frame_shift(0, step)) for step in range(1, 4)
    ]


def to_frames(blocks):
    return [blocks[0]] + [
        lax.ppermute(blocks[step], "frame", frame_shift(0, -step)) for step in range(1, 4)
    ]


def pairs_to_later_half(blocks):
    return [
        lax.ppermute(
            blocks[step],
            "frame",
            [(src, dst) for src, dst in frame_shift(1, step) if src < dst],
        )
        for step in range(4)
    ]


DOWN_HALF = [(i + 4, i) for i in range(4)]


def swap_clips(packs):
    return [packs[0]] + [
        lax.ppermute(packs[step], "clip", clip_shift(step)) for step in range(1, 4)
    ]


def ring_pieces(value):
    return [value] + [
        lax.ppermute(value, "frame", frame_shift(0, step)) for step in range(1, 4)
    ]


def ring_sends(part, ring):
    block = part.shape[0] // 4
    got = []
    for step in range(1, 4):
        sent = lax.dynamic_slice_in_dim(part, ((ring + step) % 4) * block, block, 0)
        got.append(lax.ppermute(sent.astype(low_type), "frame", frame_shift(0, step)))
    return got


def clip_pieces(joined):
    return [joined] + [
        lax.ppermute(joined, "clip", clip_shift(step)) for step in range(1, 4)
    ]


def rotary_tables(head_size, head_count):
    group_size = 2 * (head_size // 3 // 2)
    half_size = group_size // 2
    total_width = head_size * head_count
    swap_table = np.zeros((total_width, total_width), np.float32)
    rate_table = np.zeros((3, total_width), np.float32)
    for head_at in range(head_count):
        for axis_at in range(3):
            for pair_at in range(half_size):
                lower_at = head_at * head_size + axis_at * group_size + pair_at
                upper_at = lower_at + half_size
                swap_table[upper_at, lower_at] = -1.0
                swap_table[lower_at, upper_at] = 1.0
                rate_value = 10000.0 ** (-2.0 * pair_at / group_size)
                rate_table[axis_at, lower_at] = rate_value
                rate_table[axis_at, upper_at] = rate_value
    return swap_table, rate_table


def norm_rows(values):
    row_mean = jnp.mean(values, axis=-1, keepdims=True)
    centred = values - row_mean
    spread = jnp.mean(centred * centred, axis=-1, keepdims=True)
    inverse = lax.rsqrt(spread + norm_epsilon)
    return centred * inverse, inverse


def norm_kernel(gain_ref, shift_ref, *refs):
    terms, (stream_ref, hat_ref, inverse_ref, low_ref) = refs[:-4], refs[-4:]
    values = terms[0][...]
    if len(terms) > 1:
        values = values + (terms[1][...] + terms[2][...] + terms[3][...])
    hat, inverse = norm_rows(values)
    stream_ref[...] = values
    hat_ref[...] = hat
    inverse_ref[...] = jnp.broadcast_to(inverse, inverse_ref.shape)
    low_ref[...] = (hat * gain_ref[...] + shift_ref[...]).astype(low_type)


def block_kernel(stream_ref, kept_ref, got_ref, bias_ref, live_ref, out_ref):
    values = stream_ref[...] + (kept_ref[...] + got_ref[...] + bias_ref[...])
    out_ref[...] = (values * live_ref[:, 0:1]).astype(low_type)


def norm_back_kernel(count, kept_ref, got_ref, gain_ref, hat_ref, inverse_ref, grad_ref, out_ref, low_ref, sums_ref):
    grad = kept_ref[...] + got_ref[...]
    hat = hat_ref[...]
    scaled = grad * gain_ref[...]
    first = jnp.mean(scaled, axis=-1, keepdims=True)
    second = jnp.mean(scaled * hat, axis=-1, keepdims=True)
    out = grad_ref[...] + (scaled - first - hat * second) * inverse_ref[:, 0:1]
    low = out.astype(low_type)
    out_ref[...] = out
    low_ref[...] = low
    sums_ref[...] = jnp.zeros_like(sums_ref)
    sums_ref[0:1, :] = jnp.sum(grad * hat, axis=0, keepdims=True)
    sums_ref[1:2, :] = jnp.sum(grad, axis=0, keepdims=True)
    sums_ref[2:3, :] = jnp.sum(low[:count].astype(wide_type), axis=0, keepdims=True)


def exact_gelu(values):
    return jax.nn.gelu(values, approximate=False)


def dot_wide(left, right):
    return jnp.dot(left, right, preferred_element_type=wide_type)


def dot_dims(left, right, left_dim, right_dim):
    return lax.dot_general(
        left, right, (((left_dim,), (right_dim,)), ((), ())), preferred_element_type=wide_type
    )


def head_cols(at):
    return slice(at * HEAD, (at + 1) * HEAD)


def ring_back(place, step):
    return lax.rem(place - step + 4, 4)


def ring_ahead(place, step):
    return lax.rem(place + step, 4)


def project_kernel(heads, at_ref, rows_ref, key_w, value_w, query_w, bias_ref, cos_ref, sin_ref, swap_ref, *out_refs):
    rows = rows_ref[...]
    swap = swap_ref[...]
    cosine = jnp.concatenate([cos_ref[: rows.shape[0], :]] * heads, axis=1)
    sine = jnp.concatenate([sin_ref[: rows.shape[0], :]] * heads, axis=1)

    def turned(weight, bias):
        value = dot_wide(rows, weight[...]) + bias
        crossed = jnp.dot(value, swap, precision=highest_precision, preferred_element_type=wide_type)
        return value * cosine + crossed * sine

    key = turned(key_w, bias_ref[1:2, :]).astype(low_type)
    value = (dot_wide(rows, value_w[...]) + bias_ref[2:3, :]).astype(low_type)
    query = (turned(query_w, bias_ref[0:1, :]).astype(low_type).astype(wide_type) * HEAD ** (-0.5)).astype(low_type)

    def write(head, step):
        for at, part in enumerate((key, value, query)):
            out_refs[step][:, head_cols(at)] = part[:, head_cols(head)]
            if at < 2:
                out_refs[4 + step][:, head_cols(at)] = part[:, head_cols(head)]

    for ring in range(4):

        @pl.when(at_ref[0] == ring)
        def _(ring=ring):
            for step in range(4):
                write((ring + step) % 4, step)


def lane_tiles(total):
    size = 384 if total % 384 == 0 else total
    return [slice(at * size, (at + 1) * size) for at in range(total // size)]


def attend_kernel(bias_ref, mask_ref, *refs):
    own_refs, cross_refs = refs[:4], refs[4:8]
    out_ref, low_ref, total_ref, own_out, cross_out, query_ref, score_ref = refs[8:]
    rows = own_refs[0].shape[0]
    total_rows = 4 * rows
    for at in range(4):
        block = slice(at * rows, (at + 1) * rows)
        query_ref[block, :] = own_refs[at][:, head_cols(2)]
        own_out[block, :] = own_refs[at][...]
        cross_out[block, :] = cross_refs[at][...]
    total_ref[...] = jnp.zeros_like(total_ref)

    def pair(at, part):
        if at < 4:
            return own_refs[at][:, head_cols(part)]
        return cross_refs[at - 4][:, head_cols(part)]

    for tile in lane_tiles(total_rows):
        query = query_ref[tile, :]
        wide = tile.stop - tile.start
        top = jnp.full((1, wide), 2.0 * masked_score, wide_type)
        for at in range(8):
            scores = dot_dims(pair(at, 0), query, 1, 1) + bias_ref[:, at : at + 1]
            if at < 4:
                scores = scores + mask_ref[at : at + 1, tile]
            score_ref[at * rows : (at + 1) * rows, :] = scores
            top = jnp.maximum(top, jnp.max(scores, axis=0, keepdims=True))
        mass = jnp.zeros((1, wide), wide_type)
        out = jnp.zeros((HEAD, wide), wide_type)
        for at in range(8):
            weights = jnp.exp(score_ref[at * rows : (at + 1) * rows, :] - top)
            mass = mass + jnp.sum(weights, axis=0, keepdims=True)
            out = out + dot_dims(pair(at, 1), weights.astype(low_type), 0, 0)
        total_ref[0:1, tile] = top + jnp.log(mass)
        rows_out = (out / mass).T
        out_ref[tile, :] = rows_out
        low_ref[tile, :] = rows_out.astype(low_type)


def attend_back_kernel(own, bias_ref, mask_ref, total_ref, out_ref, own_ref, *refs):
    grad_refs, cross_refs = refs[:4], refs[4:-4]
    pair_sum, query_sum, query_ref, grad_ref = refs[-4:]
    rows = grad_refs[0].shape[0]
    query_ref[...] = own_ref[:, head_cols(2)]
    for at in range(4):
        grad_ref[at * rows : (at + 1) * rows, :] = grad_refs[at][...]
    ones = jnp.ones((8, HEAD), wide_type)
    pair_sum[...] = jnp.zeros_like(pair_sum)
    for tile in lane_tiles(4 * rows):
        query = query_ref[tile, :]
        grad = grad_ref[tile, :]
        centre = lax.dot_general(
            ones,
            grad.astype(wide_type) * out_ref[tile, :],
            (((1,), (1,)), ((), ())),
            precision=highest_precision,
            preferred_element_type=wide_type,
        )[0:1, :]
        total = total_ref[0:1, tile]
        query_part = jnp.zeros((HEAD, tile.stop - tile.start), wide_type)
        for at in range(4):
            block = slice(at * rows, (at + 1) * rows)
            if own:
                key, value = own_ref[block, head_cols(0)], own_ref[block, head_cols(1)]
                scores = dot_dims(key, query, 1, 1) + bias_ref[:, at : at + 1] + mask_ref[at : at + 1, tile]
            else:
                key, value = cross_refs[0][block, head_cols(0)], cross_refs[0][block, head_cols(1)]
                scores = dot_dims(key, query, 1, 1) + bias_ref[:, at + 4 : at + 5]
            weights = jnp.exp(scores - total)
            pair_sum[block, head_cols(1)] += dot_wide(weights.astype(low_type), grad)
            soft = dot_dims(value, grad, 1, 1)
            back = (weights * (soft - centre)).astype(low_type)
            pair_sum[block, head_cols(0)] += dot_wide(back, query)
            query_part = query_part + dot_dims(key, back, 0, 0)
        query_sum[tile, :] = query_part.T * HEAD ** (-0.5)


def turn_back_kernel(own_pair, other_pair, own_query, other_query, cos_ref, sin_ref, swap_ref, *out_refs):
    rows = out_refs[0].shape[0]
    swap = swap_ref[...]
    for at in range(4):
        block = slice(at * rows, (at + 1) * rows)
        cosine, sine = cos_ref[block, :], sin_ref[block, :]

        def turned(value):
            crossed = jnp.dot(value, swap, precision=highest_precision, preferred_element_type=wide_type)
            return (value * cosine - crossed * sine).astype(low_type)

        pair = own_pair[block, :] + other_pair[block, :]
        out_refs[at][:, head_cols(0)] = turned(pair[:, head_cols(0)])
        out_refs[at][:, head_cols(1)] = pair[:, head_cols(1)].astype(low_type)
        out_refs[at][:, head_cols(2)] = turned(own_query[block, :] + other_query[block, :])


def mix_back_kernel(at_ref, place_ref, key_w, value_w, query_w, *refs):
    mixed_refs = refs[:4]
    out_ref, stack_ref, bias_ref = refs[4:]
    ring, clip = at_ref[0], at_ref[1]
    place = place_ref[...]
    total = None
    bias_ref[...] = jnp.zeros_like(bias_ref)
    for part, weight in ((0, key_w), (1, value_w), (2, query_w)):
        relative = jnp.concatenate([ref[:, head_cols(part)] for ref in mixed_refs], axis=1)
        ordered = dot_wide(relative, place)
        bias_ref[part : part + 1, :] = jnp.sum(ordered, axis=0, keepdims=True)
        term = dot_dims(ordered.astype(low_type), weight[...], 1, 1)
        total = term if total is None else total + term
    out_ref[...] = total
    for at in range(4):
        stack_ref[lax.rem(ring + at - clip + 4, 4)] = mixed_refs[at][...]


def clip_products(at_ref, first_ref, second_ref, pack_refs, columns):
    out = None
    half = first_ref.shape[1]
    for step in range(4):
        place = ring_back(at_ref[0], step)
        pack = pack_refs[step]
        term = dot_dims(first_ref[place], pack[:half, columns], 0, 0)
        term = term + dot_dims(second_ref[place], pack[half : 2 * half, columns], 0, 0)
        out = term if out is None else out + term
    return out


def layer_grad_kernel(at_ref, act_a, act_b, norm_a, norm_b, *refs):
    head_refs, pack_refs, out_ref = refs[:-5], refs[-5:-1], refs[-1]
    part = out_ref.shape[1] // 2
    tiles = pl.num_programs(0) - (1 if head_refs else 0)

    @pl.when(pl.program_id(0) < tiles)
    def _():
        out_ref[:, :part] = clip_products(at_ref, act_a, act_b, pack_refs, slice(0, part))
        out_ref[:, part:] = clip_products(at_ref, norm_a, norm_b, pack_refs, slice(part, 2 * part))

    if head_refs:

        @pl.when(pl.program_id(0) == tiles)
        def _():
            columns = slice(2 * part, 3 * part)
            out_ref[:, :part] = clip_products(at_ref, head_refs[0], head_refs[2], pack_refs, columns)
            out_ref[:, part:] = clip_products(at_ref, head_refs[1], head_refs[3], pack_refs, columns)


def plain_grad_kernel(at_ref, rows_a, rows_b, *refs):
    pack_refs, out_ref = refs[:4], refs[4]
    out_ref[...] = clip_products(at_ref, rows_a, rows_b, pack_refs, slice(None))


def last_grad_kernel(tiles, at_ref, head_a, head_b, *refs):
    feat_refs, pack_refs, out_ref = refs[:4], refs[4:8], refs[8]
    head_rows = 2 * head_a.shape[1]
    feat_rows = head_rows + feat_refs[0].shape[0]

    @pl.when(pl.program_id(0) < tiles)
    def _():
        out = None
        for step in range(4):
            term = dot_dims(feat_refs[step][...], pack_refs[step][head_rows:feat_rows, :], 0, 0)
            out = term if out is None else out + term
        out_ref[...] = out

    @pl.when(pl.program_id(0) == tiles + 2)
    def _():
        out = None
        small = (pack_refs[0].shape[0] - feat_rows) // 2
        for step in range(4):
            high = pack_refs[step][feat_rows : feat_rows + small, :].astype(wide_type)
            term = high + pack_refs[step][feat_rows + small :, :].astype(wide_type)
            out = term if out is None else out + term
        high = out.astype(low_type).astype(wide_type)
        out_ref[:small, :] = high
        out_ref[small:, :] = out - high

    @pl.when((pl.program_id(0) >= tiles) & (pl.program_id(0) < tiles + 2))
    def _():
        out_ref[...] = clip_products(at_ref, head_a, head_b, pack_refs, slice(None))


def ring_sum_kernel(at_ref, part_ref, *refs):
    got_refs, out_ref = refs[:3], refs[3]
    block = out_ref.shape[0]
    out = part_ref[pl.ds(pl.multiple_of(at_ref[0] * block, 8), block), :]
    for got in got_refs:
        out = out + got[...].astype(wide_type)
    out_ref[...] = out


def ring_sum(ring_at, part, got, after):
    shape = (part.shape[0] // 4, part.shape[1])
    return call_kernel(
        ring_sum_kernel,
        (ring_at[None], part, *got),
        (0,),
        jax.ShapeDtypeStruct(shape, wide_type),
        [],
        4 * shape[0] * shape[1],
        0,
        after,
    )


def half_sum_kernel(own_ref, got_ref, out_ref):
    out_ref[...] = (own_ref[...] + got_ref[...]).astype(low_type)


def half_sum(own, after):
    got = lax.ppermute(own, "frame", HALF_SWAP)
    return call_kernel(
        half_sum_kernel,
        (own, got),
        (),
        jax.ShapeDtypeStruct(own.shape, low_type),
        [],
        own.size,
        0,
        after,
    )


def join_kernel(at_ref, *refs):
    out_ref = refs[4]
    block = refs[0].shape[0]
    for step in range(4):
        start = pl.multiple_of(ring_back(at_ref[0], step) * block, 16)
        out_ref[pl.ds(start, block), :] = refs[step][...]


def join_frames(ring_at, total, after, after_far=()):
    pieces = ring_pieces(total)
    return call_kernel(
        join_kernel,
        (ring_at[None], *pieces),
        (0,),
        jax.ShapeDtypeStruct((4 * total.shape[0], total.shape[1]), low_type),
        [],
        0,
        0,
        after,
        after_far,
    )


def beside_kernel(first_ref, second_ref, out_ref):
    half, wide, other = first_ref.shape[0] // 2, first_ref.shape[1], second_ref.shape[1]
    out_ref[:, :wide] = first_ref[:half, :]
    out_ref[:, wide : wide + other] = second_ref[:half, :]
    out_ref[:, wide + other :] = second_ref[half:, :]


def gather_clips(first, second, after):
    half, wide = first.shape[0] // 2, first.shape[1]
    beside = call_kernel(
        beside_kernel,
        (first, second),
        (),
        jax.ShapeDtypeStruct((half, wide + 2 * second.shape[1]), low_type),
        [],
        0,
        0,
        after,
    )
    return lax.all_gather(beside, "clip")


def take_kernel(whole_ref, out_ref):
    out_ref[...] = whole_ref[:, :, : out_ref.shape[2]]


def with_other_core(whole, wide, after):
    shape = (*whole.shape[:2], wide)
    columns = pl.pallas_call(
        without(take_kernel, 1, after),
        grid=(1,),
        out_shape=jax.ShapeDtypeStruct(shape, low_type),
        in_specs=[pl.BlockSpec(shape, lambda i: (0, 0, 0))] + any_specs(after),
        out_specs=pl.BlockSpec(shape, lambda i: (0, 0, 0)),
        compiler_params=kernel_params(),
    )(whole, *after)
    return whole, core_swap(columns)


def smem_spec():
    return pl.BlockSpec(memory_space=pltpu.SMEM)


def kernel_params():
    return pltpu.CompilerParams(vmem_limit_bytes=48 * 1024 * 1024)


def held_spec():
    return pl.BlockSpec(memory_space=pltpu.VMEM)


def any_specs(arrays):
    return [pl.BlockSpec(memory_space=pl.ANY)] * len(arrays)


def mark(value):
    while value.ndim > 2:
        value = value[0]
    return value[:8, :128]


def without(kernel, count, after):
    return lambda *refs: kernel(*refs[:count], *refs[count + len(after) :])


def layer_grad(clip_at, second_all, packs, first_all, after):
    whole, other = second_all
    half, wide = other.shape[1:]
    tiles = wide // 128
    part = 256
    block = (4, half, 128)
    heads = () if first_all is None else (first_all[0],) * 4
    held = [
        pl.BlockSpec(block, lambda i, at=at: (0, 0, tiles + at)) for at in range(len(heads))
    ]

    def moving(start):
        return pl.BlockSpec(block, lambda i: (0, 0, start + jnp.minimum(i, tiles - 1)))

    return pl.pallas_call(
        without(layer_grad_kernel, 9 + len(heads), after),
        grid=(tiles + (1 if heads else 0),),
        out_shape=jax.ShapeDtypeStruct((wide + (128 if heads else 0), 2 * part), wide_type),
        in_specs=[smem_spec(), moving(tiles), moving(2 * tiles), moving(0), moving(0)]
        + held
        + [held_spec()] * 4
        + any_specs(after),
        out_specs=pl.BlockSpec((128, 2 * part), lambda i: (i, 0)),
        compiler_params=kernel_params(),
        cost_estimate=pl.CostEstimate(
            flops=32 * half * wide * part,
            bytes_accessed=2 * whole.size + 8 * wide * part,
            transcendentals=0,
        ),
    )(clip_at[None], whole, whole, whole, other, *heads, *packs, *after)


def plain_grad(clip_at, rows_all, packs, after):
    whole, other = rows_all
    half, count = other.shape[1:]
    part = packs[0].shape[1]
    block = pl.BlockSpec((4, half, 128), lambda i: (0, 0, i))
    return pl.pallas_call(
        without(plain_grad_kernel, 7, after),
        grid=(count // 128,),
        out_shape=jax.ShapeDtypeStruct((count, part), wide_type),
        in_specs=[smem_spec(), block, block] + [held_spec()] * 4 + any_specs(after),
        out_specs=pl.BlockSpec((128, part), lambda i: (i, 0)),
        compiler_params=kernel_params(),
        cost_estimate=pl.CostEstimate(
            flops=16 * half * count * part,
            bytes_accessed=16 * half * count + 4 * count * part,
            transcendentals=0,
        ),
    )(clip_at[None], whole, other, *packs, *after)


def last_grad(clip_at, first_all, feats, packs, after, after_far):
    whole, other = first_all
    half, part = other.shape[1], packs[0].shape[1]
    first_block = other.shape[2] // 128
    tiles = feats[0].shape[1] // 128
    kernel = functools.partial(last_grad_kernel, tiles)
    after_far = tuple(mark(value) for value in after_far)

    def moving(start):
        return pl.BlockSpec(
            (4, half, 128), lambda i: (0, 0, start + jnp.clip(i - tiles, 0, 1))
        )

    return pl.pallas_call(
        without(kernel, 11, (*after, *after_far)),
        grid=(tiles + 3,),
        out_shape=jax.ShapeDtypeStruct(((tiles + 3) * 128, part), wide_type),
        in_specs=[smem_spec(), moving(first_block), moving(first_block + 2)]
        + [pl.BlockSpec((feats[0].shape[0], 128), lambda i: (0, jnp.minimum(i, tiles - 1)))] * 4
        + [held_spec()] * 4
        + any_specs(after)
        + any_specs(after_far),
        out_specs=pl.BlockSpec((128, part), lambda i: (i, 0)),
        compiler_params=kernel_params(),
    )(clip_at[None], whole, whole, *feats, *packs, *after, *after_far)


def by_clip(clip_at, write):
    for place in range(4):

        @pl.when(clip_at == place)
        def _(place=place):
            for step in range(4):
                write((place - step) % 4, step)


def place_layer_kernel(tiles, at_ref, all_ref, *outs):
    part = all_ref.shape[2] // 2
    is_last = pl.program_id(0) == tiles

    for place in range(4):
        columns = slice(place * part, (place + 1) * part)
        left = all_ref[place, :, :part].astype(wide_type)
        right = all_ref[place, :, part:].astype(wide_type)

        @pl.when(jnp.logical_not(is_last))
        def _(columns=columns, left=left, right=right):
            outs[0][0, :, columns] = left
            outs[1][0, :, columns] = right

        if len(outs) > 2:

            @pl.when(is_last)
            def _(columns=columns, left=left, right=right):
                outs[2][0, : outs[2].shape[1] // 2, columns] = left
                outs[2][0, outs[2].shape[1] // 2 :, columns] = right


def place_layer(clip_at, layer, levels, joined, earlier, heads_layer, after):
    part = joined.shape[2] // 2
    rows = 4 * part
    tiles = rows // 128
    heads = joined.shape[1] > rows
    out = [(levels, rows, 4 * part)] * 2 + [(levels, 256, 4 * part)] * heads
    tall = pl.BlockSpec((1, 128, 4 * part), lambda i: (layer, jnp.minimum(i, tiles - 1), 0))
    wide = pl.BlockSpec((1, 256, 4 * part), lambda i: (heads_layer, 0, 0))
    return pl.pallas_call(
        without(functools.partial(place_layer_kernel, tiles), 2, (*earlier, *after)),
        grid=(tiles + (1 if heads else 0),),
        out_shape=tuple(jax.ShapeDtypeStruct(shape, wide_type) for shape in out),
        in_specs=[smem_spec(), pl.BlockSpec((4, 128, 2 * part), lambda i: (0, i, 0))]
        + any_specs(earlier)
        + any_specs(after),
        out_specs=(tall, tall) + ((wide,) if heads else ()),
        input_output_aliases={2 + at: at for at in range(len(earlier))},
        compiler_params=kernel_params(),
    )(clip_at[None], joined, *earlier, *after)


def place_last_kernel(skip, at_ref, *refs):
    pieces = refs[:4]
    in_ref, small_ref, proj_ref = refs[-3:]
    part = pieces[0].shape[1]
    heads = skip + proj_ref.shape[1]
    small = small_ref.shape[0]

    def write(place, step):
        columns = slice(place * part, (place + 1) * part)
        piece = pieces[step]
        in_ref[:, columns] = piece[: in_ref.shape[0], :].astype(wide_type)
        proj_ref[0, :, columns] = piece[skip:heads, :].astype(wide_type)
        small_ref[:, columns] = piece[heads : heads + small, :].astype(wide_type) + piece[
            heads + small :, :
        ].astype(wide_type)

    by_clip(at_ref[0], write)


def place_last(clip_at, feat_rows, skip, levels, pieces, earlier):
    part = pieces[0].shape[1]
    return pl.pallas_call(
        functools.partial(place_last_kernel, skip),
        grid=(1,),
        out_shape=(
            jax.ShapeDtypeStruct((feat_rows, 4 * part), wide_type),
            jax.ShapeDtypeStruct((64, 4 * part), wide_type),
            jax.ShapeDtypeStruct((levels, 256, 4 * part), wide_type),
        ),
        in_specs=[smem_spec()]
        + [pl.BlockSpec(pieces[0].shape, lambda i: (0, 0))] * 4
        + [pl.BlockSpec(memory_space=pl.ANY)],
        out_specs=(
            pl.BlockSpec((feat_rows, 4 * part), lambda i: (0, 0)),
            pl.BlockSpec((64, 4 * part), lambda i: (0, 0)),
            pl.BlockSpec((1, 256, 4 * part), lambda i: (0, 0, 0)),
        ),
        input_output_aliases={5: 2},
        compiler_params=kernel_params(),
    )(clip_at[None], *pieces, earlier)


def pack_kernel(by_rows, count, at_ref, *refs):
    parts, outs = refs[:count], refs[count:]
    for clip in range(4):

        @pl.when(at_ref[0] == clip)
        def _(clip=clip):
            for step in range(4):
                place, start = (clip + step) % 4, 0
                for part in parts:
                    size = part.shape[1] // 4
                    value = part[:, place * size : (place + 1) * size]
                    if by_rows:
                        outs[step][start : start + part.shape[0], :] = value
                        start += part.shape[0]
                    else:
                        outs[step][:, start : start + size] = value
                        start += size


def pack_parts(clip_at, parts, by_rows, after):
    sizes = [part.shape[1] // 4 for part in parts]
    if by_rows:
        shape = (sum(part.shape[0] for part in parts), sizes[0])
    else:
        shape = (parts[0].shape[0], sum(sizes))
    return call_kernel(
        functools.partial(pack_kernel, by_rows, len(parts)),
        (clip_at[None], *parts),
        (0,),
        tuple(jax.ShapeDtypeStruct(shape, low_type) for _ in range(4)),
        [],
        0,
        0,
        after,
    )


def place_heads_kernel(at_ref, all_ref, *refs):
    out_ref = refs[-1]
    for place in range(4):
        piece = all_ref[place].astype(wide_type)
        for at, part in ((1, 0), (2, 1), (0, 2)):
            out_ref[0, at, :, head_cols(place)] = piece[:, head_cols(part)]


def place_heads(clip_at, layer, levels, joined, earlier, after):
    rows = joined.shape[1]
    tile = 256
    count = 2
    return pl.pallas_call(
        without(place_heads_kernel, count, (*earlier, *after)),
        grid=(rows // tile,),
        out_shape=jax.ShapeDtypeStruct((levels, 3, rows, 4 * HEAD), wide_type),
        in_specs=[smem_spec(), pl.BlockSpec((4, tile, 3 * HEAD), lambda i: (0, i, 0))]
        + any_specs(earlier)
        + any_specs(after),
        out_specs=pl.BlockSpec((1, 3, tile, 4 * HEAD), lambda i: (layer, 0, i, 0)),
        input_output_aliases={count + at: at for at in range(len(earlier))},
        compiler_params=kernel_params(),
    )(clip_at[None], joined, *earlier, *after)


def stack_kernel(*refs):
    out_ref = refs[-1]
    for at, ref in enumerate(refs[:-1]):
        out_ref[8 * at : 8 * (at + 1), :] = ref[...]


def feature_grad_kernel(ids_ref, rows_ref, weight_ref, out_ref):
    size = rows_ref.shape[0] // 4
    for at in range(4):
        start = pl.multiple_of(ids_ref[at] * size, 8)
        out_ref[pl.ds(start, size), :] = dot_dims(
            rows_ref[at * size : (at + 1) * size, :], weight_ref[...], 1, 1
        )


def last_pack_kernel(at_ref, head_ref, patch_ref, small_a, small_b, *outs):
    heads, patches, small = head_ref.shape[0], patch_ref.shape[0], small_a.shape[0]
    values = small_a[...] + small_b[...]
    high = values.astype(low_type)
    rest = (values - high.astype(wide_type)).astype(low_type)
    for clip in range(4):

        @pl.when(at_ref[0] == clip)
        def _(clip=clip):
            for step in range(4):
                size = outs[step].shape[1]
                place = (clip + step) % 4
                columns = slice(place * size, (place + 1) * size)
                outs[step][:heads, :] = head_ref[:, columns]
                outs[step][heads : heads + patches, :] = patch_ref[:, columns]
                outs[step][heads + patches : heads + patches + small, :] = high[:, columns]
                outs[step][heads + patches + small :, :] = rest[:, columns]


def call_kernel(kernel, args, in_smem, outs, scratch, flops, exps, after=(), after_far=(), piped=()):
    count = len(args)

    def spec(at):
        if at in piped:
            return pl.BlockSpec(args[at].shape, lambda i, rank=args[at].ndim: (0,) * rank)
        return pl.BlockSpec(memory_space=pltpu.SMEM if at in in_smem else pltpu.VMEM)

    specs = [spec(at) for at in range(count)]
    after = (*after, *(mark(value) for value in after_far))
    specs += any_specs(after)
    moved = sum(a.size * a.dtype.itemsize for a in args)
    return pl.pallas_call(
        without(kernel, count, after),
        grid=(1,),
        out_shape=outs,
        in_specs=specs,
        out_specs=jax.tree.map(lambda _: pl.BlockSpec(memory_space=pltpu.VMEM), outs),
        scratch_shapes=scratch,
        compiler_params=kernel_params(),
        cost_estimate=pl.CostEstimate(flops=flops, bytes_accessed=moved, transcendentals=exps),
    )(*args, *after)


def on_device(
    features,
    cond_values,
    cond_live,
    in_weight,
    in_bias,
    act_weight,
    act_bias,
    state_weight,
    state_bias,
    attn_gain,
    attn_shift,
    qkv_weight,
    qkv_bias,
    proj_weight,
    proj_bias,
    mlp_gain,
    mlp_shift,
    up_weight,
    up_bias,
    down_weight,
    down_bias,
    out_grad,
):
    patch_rows = features.shape[2]
    feat_width = features.shape[3]
    slot_count = cond_values.shape[2]
    all_frames = cond_live.shape[1]
    model_width = in_weight.shape[1]
    width = qkv_weight.shape[3]
    heads = width // HEAD
    level_count = attn_gain.shape[0]
    patches = patch_rows // 4
    chunk_rows = patches + EXTRA
    rows = 4 * chunk_rows
    hidden_width = up_weight.shape[2]

    tensor_at = lax.axis_index("tensor")
    chip_at, core_at = tensor_at // 2, tensor_at % 2
    frame_at = lax.axis_index("frame")
    half_at, ring_at = frame_at // 4, frame_at % 4
    clip_at = lax.axis_index("clip")

    chunk_ids = [
        2 * jnp.bitwise_xor(core_at, core_step) + jnp.bitwise_xor(chip_at, chip_step)
        for core_step in range(2)
        for chip_step in range(2)
    ]
    own_chunk = chunk_ids[0]
    own_frames = jnp.stack([4 * half_at + (ring_at - step) % 4 for step in range(4)])
    cross_frames = jnp.stack([4 * (1 - half_at) + (ring_at - step) % 4 for step in range(4)])

    within = lax.broadcasted_iota(jnp.int32, (chunk_rows, 1), 0)
    is_patch = within < patches
    heights, columns = [], []
    for chunk_id in chunk_ids:
        patch_id = chunk_id * patches + within
        heights.append(jnp.where(is_patch, patch_id // GRID_W, 0))
        columns.append(jnp.where(is_patch, patch_id % GRID_W, 0))
    heights = jnp.concatenate(heights, axis=0).astype(wide_type)
    columns = jnp.concatenate(columns, axis=0).astype(wide_type)
    swap_table, rate_table = rotary_tables(HEAD, heads)
    swap_heads = jnp.asarray(swap_table)
    swap_one = jnp.asarray(swap_table[:HEAD, :HEAD])
    rates = rate_table[:, :HEAD]
    place_angles = heights * rates[1] + columns * rates[2]
    angles = jnp.concatenate(
        [
            own_frames[step].astype(wide_type) * rates[0][None, :] + place_angles
            for step in range(4)
        ],
        axis=0,
    )
    cosine_four, sine_four = jnp.cos(angles), jnp.sin(angles)
    head_from = jnp.arange(width)
    head_to = ((head_from // HEAD + ring_at) % 4) * HEAD + head_from % HEAD
    head_place = (head_to[:, None] == head_from[None, :]).astype(low_type)
    proj_turned = [
        lax.dynamic_slice_in_dim(
            jnp.concatenate([proj_weight[layer], proj_weight[layer]], axis=0),
            ring_at * HEAD,
            width,
            0,
        )
        for layer in range(level_count)
    ]
    ring_scalar = ring_at.astype(jnp.int32)
    clip_scalar = clip_at.astype(jnp.int32)

    live_all = cond_live[0].astype(wide_type)
    own_slots = lax.dynamic_index_in_dim(live_all, frame_at, 0, False)

    def live_rows(slots, chunk_id):
        picked = jnp.where(
            chunk_id < slot_count,
            lax.dynamic_index_in_dim(slots, jnp.minimum(chunk_id, slot_count - 1), 1, False),
            0.0,
        )
        return jnp.where(is_patch, 1.0, jnp.where(within == patches, picked[None, :], 0.0))

    sources = jnp.concatenate([own_frames, cross_frames])
    source_live = jnp.take(live_all, sources, axis=0)
    key_live = jnp.concatenate([live_rows(source_live, c) for c in chunk_ids], axis=0)
    reached = jnp.concatenate([jnp.ones((4,), jnp.bool_), jnp.full((4,), half_at == 1)])
    key_bias = jnp.where((key_live > 0.5) & reached[None, :], 0.0, masked_score).astype(wide_type)
    seen = own_frames[:, None] <= own_frames[None, :]
    causal = jnp.where(seen, 0.0, masked_score).astype(wide_type)
    causal = jnp.pad(jnp.repeat(causal, rows, axis=1), ((0, 4), (0, 0)))
    own_live = live_rows(own_slots[None, :], own_chunk)

    def extra_rows(slot_rows):
        picked = lax.dynamic_slice_in_dim(
            slot_rows, jnp.minimum(own_chunk, slot_count - 1), 1, 0
        )
        picked = jnp.where(own_chunk < slot_count, picked, jnp.zeros_like(picked))
        return jnp.pad(picked, ((0, EXTRA - 1), (0, 0)))

    cond_here = cond_values[0, 0]
    act_rows = jnp.dot(cond_here, act_weight, precision=highest_precision) + act_bias
    state_rows = jnp.dot(cond_here, state_weight, precision=highest_precision) + state_bias
    even_slot = (jnp.arange(slot_count) % 2 == 0)[:, None]
    cond_x = jnp.where(even_slot, act_rows, state_rows) * own_slots[:, None]

    flat_feat = jnp.concatenate(
        [
            lax.dynamic_slice_in_dim(features[0, 0], c * patches, patches, 0)
            for c in chunk_ids
        ],
        axis=0,
    )
    kept, got = halves_tensor(dot_wide(flat_feat, in_weight))
    stream = jnp.concatenate([kept + got + in_bias, extra_rows(cond_x)], axis=0)

    feat_wide = -(-feat_width // 128) * 128
    feat_low = jnp.pad(flat_feat, ((0, 0), (0, feat_wide - feat_width)))
    feats = [feat_low] + [
        lax.ppermute(feat_low, "clip", clip_shift(step)) for step in range(1, 4)
    ]
    pair_work = 2 * 32 * rows * rows * HEAD
    pair_exps = 32 * rows * rows
    weight_parts = [
        [qkv_weight[layer, :, at] for at in (1, 2, 0)] for layer in range(level_count)
    ]

    def norm(terms, gain, shift, after_far=()):
        chunk = jax.ShapeDtypeStruct((chunk_rows, model_width), wide_type)
        return call_kernel(
            norm_kernel,
            (gain[None], shift[None], *terms),
            (),
            (
                chunk,
                chunk,
                jax.ShapeDtypeStruct((chunk_rows, 128), wide_type),
                jax.ShapeDtypeStruct((chunk_rows, model_width), low_type),
            ),
            [],
            12 * chunk_rows * model_width,
            0,
            (),
            after_far,
        )

    def norm_back(part, gain, hat, inverse, grad, count, after=(), after_far=()):
        kept, got = halves_tensor(part)
        return call_kernel(
            functools.partial(norm_back_kernel, count),
            (kept, got, gain[None], hat, inverse, grad),
            (),
            (
                jax.ShapeDtypeStruct((chunk_rows, model_width), wide_type),
                jax.ShapeDtypeStruct((chunk_rows, model_width), low_type),
                jax.ShapeDtypeStruct((8, model_width), wide_type),
            ),
            [],
            16 * chunk_rows * model_width,
            0,
            after,
            after_far,
            (2, 3, 4, 5),
        )

    slot_grads = out_grad[0, 0, patch_rows:] * own_slots[:, None].astype(low_type)
    slot_blocks = jnp.concatenate(
        [
            jnp.pad(slot_grads[:, None], ((0, 0), (0, EXTRA - 1), (0, 0))),
            jnp.zeros((4 - slot_count, EXTRA, model_width), low_type),
        ],
        axis=0,
    )
    branch_parts = []
    for chunk_id in chunk_ids:
        branch_parts.append(
            lax.dynamic_slice_in_dim(out_grad[0, 0], chunk_id * patches, patches, 0)
        )
        branch_parts.append(lax.dynamic_index_in_dim(slot_blocks, chunk_id, 0, False))
    first_branch = jnp.concatenate(branch_parts, axis=0)
    stored = []
    terms = (stream,)
    before = None
    for layer in range(level_count):
        stream, hat_one, inverse_one, first_chunk = norm(terms, attn_gain[layer], attn_shift[layer])
        first_in = join_rows_tensor(first_chunk)
        bias = jnp.pad(qkv_bias[layer], ((0, 5), (0, 0)))
        heads_out = call_kernel(
            functools.partial(project_kernel, heads),
            (
                ring_scalar[None],
                first_in,
                *weight_parts[layer],
                bias,
                cosine_four,
                sine_four,
                swap_heads,
            ),
            (0,),
            tuple(
                jax.ShapeDtypeStruct((rows, count * HEAD), low_type)
                for count in (3, 3, 3, 3, 2, 2, 2, 2)
            ),
            [],
            6 * rows * model_width * width,
            0,
            (),
            () if before is None else (before[0],),
            (2, 3, 4, 5, 6, 7, 8),
        )
        blocks = to_heads(heads_out[:4])
        cross = pairs_to_later_half(heads_out[4:])
        attn_wide, attn_turned, log_total, own_all, cross_all = call_kernel(
            attend_kernel,
            (key_bias, causal, *blocks, *cross),
            (),
            (
                jax.ShapeDtypeStruct((4 * rows, HEAD), wide_type),
                jax.ShapeDtypeStruct((4 * rows, HEAD), low_type),
                jax.ShapeDtypeStruct((8, 4 * rows), wide_type),
                jax.ShapeDtypeStruct((4 * rows, 3 * HEAD), low_type),
                jax.ShapeDtypeStruct((4 * rows, 2 * HEAD), low_type),
            ),
            [
                pltpu.VMEM((4 * rows, HEAD), low_type),
                pltpu.VMEM((8 * rows, lane_tiles(4 * rows)[0].stop), wide_type),
            ],
            2 * pair_work,
            pair_exps,
            tuple(feats[1:]) if layer == 0 else (),
        )
        attn_relative = jnp.concatenate(
            to_frames([attn_turned[at * rows : (at + 1) * rows] for at in range(4)]), axis=1
        )
        attn_low = dot_wide(attn_relative, head_place).astype(low_type)
        if layer < level_count - 1:
            first_all = gather_clips(first_in, attn_low, ())
        kept, got = halves_tensor(dot_wide(attn_relative, proj_turned[layer]))
        middle, hat_two, inverse_two, second_chunk = norm(
            (stream, kept, got, proj_bias[layer][None]), mlp_gain[layer], mlp_shift[layer],
            () if before is None else (before[1], first_branch),
        )
        second_in = join_rows_tensor(second_chunk)
        hidden = dot_wide(second_in, up_weight[layer]) + up_bias[layer]
        active_low = exact_gelu(hidden).astype(low_type)
        second_all = gather_clips(second_in, active_low, ())
        if layer == level_count - 1:
            first_all = (first_in, attn_low)
        before = (first_all, second_all)
        kept, got = halves_tensor(dot_wide(active_low, down_weight[layer]))
        terms = (middle, kept, got, down_bias[layer][None])
        stored.append(
            (
                hat_one,
                inverse_one,
                own_all,
                cross_all,
                log_total,
                attn_wide,
                hat_two,
                inverse_two,
                hidden,
                first_all,
                second_all,
            )
        )
    def in_order(full, count):
        out = jnp.zeros((4 * count,) + full.shape[1:], full.dtype)
        size = full.shape[0] // 4
        for at, chunk_id in enumerate(chunk_ids):
            out = lax.dynamic_update_slice_in_dim(
                out, full[at * size : at * size + count], chunk_id * count, 0
            )
        return out

    def block_rows(after):
        low = call_kernel(
            block_kernel,
            (*terms, jnp.broadcast_to(own_live, (chunk_rows, 128))),
            (),
            jax.ShapeDtypeStruct((chunk_rows, model_width), low_type),
            [],
            4 * chunk_rows * model_width,
            0,
            after,
        )
        return join_rows_tensor(low)

    def block_in_order(block_full):
        slot_full = jnp.concatenate(
            [
                block_full[at * chunk_rows + patches : at * chunk_rows + patches + 1]
                for at in range(4)
            ],
            axis=0,
        )
        return jnp.concatenate(
            [in_order(block_full, patches), in_order(slot_full, 1)[:slot_count]], axis=0
        )[None, None]

    own_out = lax.dynamic_slice_in_dim(out_grad[0, 0], own_chunk * patches, patches, 0)
    grad_stream = (
        jnp.concatenate(
            [
                own_out.astype(wide_type),
                extra_rows(out_grad[0, 0, patch_rows:].astype(wide_type)),
            ],
            axis=0,
        )
        * own_live
    )

    small = {}
    small["down", level_count - 1] = jnp.sum(grad_stream, axis=0)
    sums_list = []
    wide_part = model_width // 4
    later = None
    for layer in reversed(range(level_count)):
        (
            hat_one,
            inverse_one,
            own_all,
            cross_all,
            log_total,
            attn_wide,
            hat_two,
            inverse_two,
            hidden,
            first_all,
            second_all,
        ) = stored[layer]
        branch = first_branch if later is None else join_rows_tensor(branch_chunk)
        if later is not None:
            first_all = with_other_core(first_all, model_width, (branch,))
            second_all = with_other_core(second_all, model_width, (branch,))
        _, gelu_pull = jax.vjp(exact_gelu, hidden)
        grad_hidden = gelu_pull(dot_dims(branch, down_weight[layer], 1, 1))[0].astype(low_type)
        small["up", layer] = jnp.sum(grad_hidden.astype(wide_type), axis=0)
        parts = [branch, grad_hidden] + ([] if later is None else [later["proj_out"]])
        packs = pack_parts(clip_scalar, parts, False, ())
        grad_middle, proj_chunk, sums = norm_back(
            dot_dims(grad_hidden, up_weight[layer], 1, 1),
            mlp_gain[layer],
            hat_two,
            inverse_two,
            grad_stream,
            chunk_rows,
            (packs[0],) if later is None else (packs[0], later["tall_join"]),
            () if later is None else (later["heads_sum"],),
        )
        sums_list.append(sums)
        packs = swap_clips(packs)
        if later is None:
            second_all = with_other_core(second_all, model_width, (proj_chunk,))
            block_full = block_rows((proj_chunk,))
            block_out = block_in_order(block_full)
        proj_out = join_rows_tensor(proj_chunk)
        grad_attn = dot_dims(proj_out, proj_turned[layer], 1, 1).astype(low_type)
        grads = to_heads([grad_attn[:, head_cols(at)] for at in range(4)])

        if later is not None:
            later["heads_ring"] = ring_sum(
                ring_scalar, later["heads_sum"], later["heads_got"], (proj_chunk,)
            )

            later["tall_all"] = lax.all_gather(later["tall_join"], "clip")

        def attend_back(own, after, after_far=()):
            return call_kernel(
                functools.partial(attend_back_kernel, own),
                (key_bias, causal, log_total, attn_wide, own_all, *grads)
                + (() if own else (cross_all,)),
                (),
                (
                    jax.ShapeDtypeStruct((4 * rows, 2 * HEAD), wide_type),
                    jax.ShapeDtypeStruct((4 * rows, HEAD), wide_type),
                ),
                [
                    pltpu.VMEM((4 * rows, HEAD), low_type),
                    pltpu.VMEM((4 * rows, HEAD), low_type),
                ],
                5 * pair_work // 2,
                pair_exps // 2,
                after,
                after_far,
                (0, 1, 2, 3, 4) if own else (0, 1, 2, 3, 4, 9),
            )

        cross_pair, cross_query = attend_back(
            False, () if later is None else (later["heads_ring"],)
        )
        got_pair = lax.ppermute(cross_pair, "frame", DOWN_HALF)
        if later is None:
            first_all = with_other_core(
                gather_clips(*first_all, (cross_pair,)), model_width, (cross_pair,)
            )
        tall_sum = layer_grad(
            clip_scalar,
            second_all,
            packs,
            None if later is None else later["first_all"],
            (cross_pair,),
        )
        own_pair, own_query = attend_back(
            True, (), (tall_sum,) if later is None else (tall_sum, later["tall_all"], block_full)
        )
        tall_got = ring_sends(tall_sum, ring_at)
        if later is not None:
            later["heads_total"] = half_sum(later["heads_ring"], (own_pair,))
        tall_ring = ring_sum(ring_scalar, tall_sum, tall_got, ())
        tall_total = half_sum(tall_ring, ())
        turned = call_kernel(
            turn_back_kernel,
            (own_pair, got_pair, own_query, cross_query, cosine_four, sine_four, swap_one),
            (),
            tuple(jax.ShapeDtypeStruct((rows, 3 * HEAD), low_type) for _ in range(4)),
            [],
            24 * rows * HEAD * HEAD,
            0,
            (tall_ring,) if later is None else (tall_ring, later["heads_total"]),
            (),
            (4, 5, 6),
        )
        mixed = to_frames(list(turned))
        if later is not None:
            later["heads_join"] = join_frames(ring_scalar, later["heads_total"], (turned[0],))
        normed_part, mixed_stack, bias_sums = call_kernel(
            mix_back_kernel,
            (
                jnp.stack([ring_scalar, clip_scalar]),
                head_place,
                *weight_parts[layer],
                *mixed,
            ),
            (0,),
            (
                jax.ShapeDtypeStruct((rows, model_width), wide_type),
                jax.ShapeDtypeStruct((4, rows, 3 * HEAD), low_type),
                jax.ShapeDtypeStruct((8, width), wide_type),
            ),
            [],
            6 * rows * model_width * width,
            0,
            (tall_total,) if later is None else (tall_total, later["heads_join"]),
            (),
            (1, 2, 3, 4),
        )
        small["qkv", layer] = jnp.concatenate([bias_sums[2:3], bias_sums[:2]], axis=0)
        packs = swap_clips([mixed_stack[step] for step in range(4)])
        grad_stream, branch_chunk, sums = norm_back(
            normed_part,
            attn_gain[layer],
            hat_one,
            inverse_one,
            grad_middle,
            patches if layer == 0 else chunk_rows,
        )
        sums_list.append(sums)
        tall_join = join_frames(ring_scalar, tall_total, (branch_chunk,))

        heads_sum = plain_grad(clip_scalar, first_all, packs, (branch_chunk,))
        heads_got = ring_sends(heads_sum, ring_at)
        if layer > 0:
            later = {
                "proj_out": proj_out,
                "first_all": first_all,
                "tall_join": tall_join,
                "heads_sum": heads_sum,
                "heads_got": heads_got,
            }

    patch_chunk = branch_chunk[:patches]
    grad_patch = join_rows_tensor(patch_chunk)
    grad_features = call_kernel(
        feature_grad_kernel,
        (jnp.stack(chunk_ids).astype(jnp.int32), grad_patch, in_weight),
        (0,),
        jax.ShapeDtypeStruct((patch_rows, feat_width), wide_type),
        [],
        2 * patch_rows * feat_width * model_width,
        0,
        piped=(2,),
    )
    slot_row = grad_stream[patches : patches + 1] * own_live[patches : patches + 1]
    own_cond = lax.dynamic_slice_in_dim(
        cond_here, jnp.minimum(own_chunk, slot_count - 1), 1, 0
    )
    slot_part = jnp.concatenate([own_cond.T * slot_row, slot_row], axis=0)
    here = own_chunk < slot_count
    is_act = here & (own_chunk % 2 == 0)
    is_state = here & (own_chunk % 2 == 1)
    act_part = jnp.where(is_act, slot_part, 0.0)
    state_part = jnp.where(is_state, slot_part, 0.0)

    def at_tensor(value, total):
        return lax.dynamic_update_slice(
            jnp.zeros((value.shape[0], total), wide_type),
            value,
            (0, tensor_at * value.shape[1]),
        )

    layers = range(level_count)
    qkv_rows = at_tensor(
        jnp.concatenate([small["qkv", layer] for layer in layers], axis=0), 4 * width
    )
    mixed_rows = jnp.concatenate(
        [qkv_rows, small["down", level_count - 1][None], jnp.zeros_like(qkv_rows[:1])], axis=0
    )
    ups = at_tensor(jnp.stack([small["up", layer] for layer in layers]), 4 * hidden_width)
    parts = [*sums_list, act_part, state_part, mixed_rows, ups.reshape(-1, model_width)]
    vector = call_kernel(
        stack_kernel,
        tuple(parts),
        (),
        jax.ShapeDtypeStruct((8 * len(parts), model_width), wide_type),
        [],
        0,
        0,
    )
    vector = vector + core_swap(vector)
    later["heads_all"] = lax.all_gather(later["heads_join"], "clip")
    head_rows, patch_count, small_rows = proj_out.shape[0], grad_patch.shape[0], vector.shape[0]
    packs = call_kernel(
        last_pack_kernel,
        (clip_scalar[None], proj_out, grad_patch, vector, chip_swap(vector)),
        (0,),
        tuple(
            jax.ShapeDtypeStruct((head_rows + patch_count + 2 * small_rows, wide_part), low_type)
            for _ in range(4)
        ),
        [],
        0,
        0,
        (),
        (heads_sum,),
    )
    tall_all = lax.all_gather(tall_join, "clip")
    placed = place_layer(
        clip_scalar, level_count - 1, level_count, later["tall_all"], (), 0, (packs[0],)
    )
    packs = swap_clips(packs)
    heads_ring = ring_sum(ring_scalar, heads_sum, heads_got, tuple(packs[1:]))
    last_sum = last_grad(
        clip_scalar, first_all, feats, packs, (heads_ring,), (placed[0], grad_features)
    )
    last_ring = ring_sum(ring_scalar, last_sum, ring_sends(last_sum, ring_at), ())
    heads_total = half_sum(heads_ring, (mark(last_sum),))
    heads_join = join_frames(ring_scalar, heads_total, (last_ring,))
    heads_all = lax.all_gather(heads_join, "clip")
    heads_placed = place_heads(
        clip_scalar, level_count - 1, level_count, later["heads_all"], (), (packs[0],)
    )
    last_join = join_frames(
        ring_scalar, half_sum(last_ring, ()), (), (tall_all, heads_placed)
    )
    last_pieces = clip_pieces(last_join)
    grad_down, grad_up, grad_proj = place_layer(
        clip_scalar, 0, level_count, tall_all, placed, level_count - 1, ()
    )
    grad_in, vector, grad_proj = place_last(
        clip_scalar, feat_width, feat_wide, level_count, last_pieces, grad_proj
    )
    grad_heads = (place_heads(clip_scalar, 0, level_count, heads_all, (heads_placed,), ()),)


    def norm_sums(layer, first, row):
        return vector[8 * (2 * (level_count - 1 - layer) + first) + row]

    grad_mlp_gain = jnp.stack([norm_sums(layer, 0, 0) for layer in layers])
    grad_mlp_shift = jnp.stack([norm_sums(layer, 0, 1) for layer in layers])
    grad_proj_bias = jnp.stack([norm_sums(layer, 0, 2) for layer in layers])
    grad_attn_gain = jnp.stack([norm_sums(layer, 1, 0) for layer in layers])
    grad_attn_shift = jnp.stack([norm_sums(layer, 1, 1) for layer in layers])
    rest = vector[16 * level_count :]
    grad_down_bias = jnp.stack(
        [norm_sums(layer + 1, 1, 2) for layer in range(level_count - 1)]
        + [rest[16 + 3 * level_count]]
    )
    grad_qkv_bias = lax.dynamic_slice_in_dim(
        rest[16 : 16 + 3 * level_count], tensor_at * width, width, 1
    )
    grad_qkv_bias = grad_qkv_bias.reshape(level_count, 3, width)
    grad_up_bias = lax.dynamic_slice_in_dim(
        rest[24:].reshape(level_count, 4 * hidden_width), tensor_at * hidden_width, hidden_width, 1
    )
    act_count = cond_here.shape[1]
    return (
        block_out,
        grad_features[None, None],
        grad_in,
        norm_sums(0, 1, 2),
        rest[:act_count],
        rest[act_count],
        rest[8 : 8 + act_count],
        rest[8 + act_count],
        grad_attn_gain,
        grad_attn_shift,
        jnp.swapaxes(grad_heads[0], 1, 2),
        grad_qkv_bias,
        grad_proj,
        grad_proj_bias,
        grad_mlp_gain,
        grad_mlp_shift,
        grad_up,
        grad_up_bias,
        grad_down,
        grad_down_bias,
    )


def solution(mesh):
    return jax.shard_map(
        on_device,
        mesh=mesh,
        in_specs=(
            P("clip", "frame", None, "tensor"),
            P("clip", "frame", None, None),
            P("clip", None, None),
            P("tensor", None),
            P(),
            P(),
            P(),
            P(),
            P(),
            P(),
            P(),
            P(None, None, None, "tensor"),
            P(None, None, "tensor"),
            P(None, "tensor", None),
            P(),
            P(),
            P(),
            P(None, None, "tensor"),
            P(None, "tensor"),
            P(None, "tensor", None),
            P(),
            P("clip", "frame", None, None),
        ),
        out_specs=(
            P("clip", "frame", None, None),
            P("clip", "frame", None, "tensor"),
            P("tensor", None),
            P(),
            P(),
            P(),
            P(),
            P(),
            P(),
            P(),
            P(None, None, None, "tensor"),
            P(None, None, "tensor"),
            P(None, "tensor", None),
            P(),
            P(),
            P(),
            P(None, None, "tensor"),
            P(None, "tensor"),
            P(None, "tensor", None),
            P(),
        ),
        check_vma=False,
    )
```

```python
import functools

import jax
import jax.numpy as jnp
import numpy as np
from jax import lax
from jax.experimental import pallas as pl
from jax.experimental.pallas import tpu as pltpu
from jax.sharding import PartitionSpec as P

HEAD = 64
GRID_W = 16
EXTRA = 8

highest_precision = lax.Precision.HIGHEST
norm_epsilon = 1e-06
masked_score = -1000000000.0
low_type = jnp.bfloat16
wide_type = jnp.float32

CORE_SWAP = [(0, 1), (1, 0), (2, 3), (3, 2)]
CHIP_SWAP = [(0, 2), (2, 0), (1, 3), (3, 1)]
HALF_SWAP = [(i, (i + 4) % 8) for i in range(8)]


def clip_shift(step):
    return [(i, (i + step) % 4) for i in range(4)]


def frame_shift(halves, step):
    return [
        (4 * half + i, 4 * ((half + halves) % 2) + (i + step) % 4)
        for half in range(2)
        for i in range(4)
    ]


def core_swap(value):
    return lax.ppermute(value, "tensor", CORE_SWAP)


def chip_swap(value):
    return lax.ppermute(value, "tensor", CHIP_SWAP)


def halves_tensor(part):
    half = part.shape[0] // 2
    pair = part[:half] + core_swap(part[half:])
    quarter = half // 2
    return pair[:quarter], chip_swap(pair[quarter:])


def join_rows_tensor(chunk):
    pair = jnp.concatenate([chunk, chip_swap(chunk)], axis=0)
    return jnp.concatenate([pair, core_swap(pair)], axis=0)


def to_heads(blocks):
    return [blocks[0]] + [
        lax.ppermute(blocks[step], "frame", frame_shift(0, step)) for step in range(1, 4)
    ]


def to_frames(blocks):
    return [blocks[0]] + [
        lax.ppermute(blocks[step], "frame", frame_shift(0, -step)) for step in range(1, 4)
    ]


def pairs_to_later_half(blocks):
    return [
        lax.ppermute(
            blocks[step],
            "frame",
            [(src, dst) for src, dst in frame_shift(1, step) if src < dst],
        )
        for step in range(4)
    ]


DOWN_HALF = [(i + 4, i) for i in range(4)]


def swap_clips(packs):
    return [packs[0]] + [
        lax.ppermute(packs[step], "clip", clip_shift(step)) for step in range(1, 4)
    ]


def ring_pieces(value):
    return [value] + [
        lax.ppermute(value, "frame", frame_shift(0, step)) for step in range(1, 4)
    ]


def ring_sends(part, ring):
    block = part.shape[0] // 4
    got = []
    for step in range(1, 4):
        sent = lax.dynamic_slice_in_dim(part, ((ring + step) % 4) * block, block, 0)
        got.append(lax.ppermute(sent.astype(low_type), "frame", frame_shift(0, step)))
    return got


def clip_pieces(joined):
    return [joined] + [
        lax.ppermute(joined, "clip", clip_shift(step)) for step in range(1, 4)
    ]


def rotary_tables(head_size, head_count):
    group_size = 2 * (head_size // 3 // 2)
    half_size = group_size // 2
    total_width = head_size * head_count
    swap_table = np.zeros((total_width, total_width), np.float32)
    rate_table = np.zeros((3, total_width), np.float32)
    for head_at in range(head_count):
        for axis_at in range(3):
            for pair_at in range(half_size):
                lower_at = head_at * head_size + axis_at * group_size + pair_at
                upper_at = lower_at + half_size
                swap_table[upper_at, lower_at] = -1.0
                swap_table[lower_at, upper_at] = 1.0
                rate_value = 10000.0 ** (-2.0 * pair_at / group_size)
                rate_table[axis_at, lower_at] = rate_value
                rate_table[axis_at, upper_at] = rate_value
    return swap_table, rate_table


def norm_rows(values):
    row_mean = jnp.mean(values, axis=-1, keepdims=True)
    centred = values - row_mean
    spread = jnp.mean(centred * centred, axis=-1, keepdims=True)
    inverse = lax.rsqrt(spread + norm_epsilon)
    return centred * inverse, inverse


def norm_kernel(gain_ref, shift_ref, *refs):
    terms, (stream_ref, hat_ref, inverse_ref, low_ref) = refs[:-4], refs[-4:]
    values = terms[0][...]
    if len(terms) > 1:
        values = values + (terms[1][...] + terms[2][...] + terms[3][...])
    hat, inverse = norm_rows(values)
    stream_ref[...] = values
    hat_ref[...] = hat
    inverse_ref[...] = jnp.broadcast_to(inverse, inverse_ref.shape)
    low_ref[...] = (hat * gain_ref[...] + shift_ref[...]).astype(low_type)


def block_kernel(stream_ref, kept_ref, got_ref, bias_ref, live_ref, out_ref):
    values = stream_ref[...] + (kept_ref[...] + got_ref[...] + bias_ref[...])
    out_ref[...] = (values * live_ref[:, 0:1]).astype(low_type)


def norm_back_kernel(count, kept_ref, got_ref, gain_ref, hat_ref, inverse_ref, grad_ref, out_ref, low_ref, sums_ref):
    grad = kept_ref[...] + got_ref[...]
    hat = hat_ref[...]
    scaled = grad * gain_ref[...]
    first = jnp.mean(scaled, axis=-1, keepdims=True)
    second = jnp.mean(scaled * hat, axis=-1, keepdims=True)
    out = grad_ref[...] + (scaled - first - hat * second) * inverse_ref[:, 0:1]
    low = out.astype(low_type)
    out_ref[...] = out
    low_ref[...] = low
    sums_ref[...] = jnp.zeros_like(sums_ref)
    sums_ref[0:1, :] = jnp.sum(grad * hat, axis=0, keepdims=True)
    sums_ref[1:2, :] = jnp.sum(grad, axis=0, keepdims=True)
    sums_ref[2:3, :] = jnp.sum(low[:count].astype(wide_type), axis=0, keepdims=True)


def exact_gelu(values):
    return jax.nn.gelu(values, approximate=False)


def dot_wide(left, right):
    return jnp.dot(left, right, preferred_element_type=wide_type)


def dot_dims(left, right, left_dim, right_dim):
    return lax.dot_general(
        left, right, (((left_dim,), (right_dim,)), ((), ())), preferred_element_type=wide_type
    )


def head_cols(at):
    return slice(at * HEAD, (at + 1) * HEAD)


def ring_back(place, step):
    return lax.rem(place - step + 4, 4)


def ring_ahead(place, step):
    return lax.rem(place + step, 4)


def project_kernel(heads, at_ref, rows_ref, key_w, value_w, query_w, bias_ref, cos_ref, sin_ref, swap_ref, *out_refs):
    rows = rows_ref[...]
    swap = swap_ref[...]
    cosine = jnp.concatenate([cos_ref[: rows.shape[0], :]] * heads, axis=1)
    sine = jnp.concatenate([sin_ref[: rows.shape[0], :]] * heads, axis=1)

    def turned(weight, bias):
        value = dot_wide(rows, weight[...]) + bias
        crossed = jnp.dot(value, swap, precision=highest_precision, preferred_element_type=wide_type)
        return value * cosine + crossed * sine

    key = turned(key_w, bias_ref[1:2, :]).astype(low_type)
    value = (dot_wide(rows, value_w[...]) + bias_ref[2:3, :]).astype(low_type)
    query = (turned(query_w, bias_ref[0:1, :]).astype(low_type).astype(wide_type) * HEAD ** (-0.5)).astype(low_type)

    def write(head, step):
        for at, part in enumerate((key, value, query)):
            out_refs[step][:, head_cols(at)] = part[:, head_cols(head)]
            if at < 2:
                out_refs[4 + step][:, head_cols(at)] = part[:, head_cols(head)]

    for ring in range(4):

        @pl.when(at_ref[0] == ring)
        def _(ring=ring):
            for step in range(4):
                write((ring + step) % 4, step)


def lane_tiles(total):
    size = 384 if total % 384 == 0 else total
    return [slice(at * size, (at + 1) * size) for at in range(total // size)]


def attend_kernel(bias_ref, mask_ref, *refs):
    own_refs, cross_refs = refs[:4], refs[4:8]
    out_ref, low_ref, total_ref, own_out, cross_out, query_ref, score_ref = refs[8:]
    rows = own_refs[0].shape[0]
    total_rows = 4 * rows
    for at in range(4):
        block = slice(at * rows, (at + 1) * rows)
        query_ref[block, :] = own_refs[at][:, head_cols(2)]
        own_out[block, :] = own_refs[at][...]
        cross_out[block, :] = cross_refs[at][...]
    total_ref[...] = jnp.zeros_like(total_ref)

    def pair(at, part):
        if at < 4:
            return own_refs[at][:, head_cols(part)]
        return cross_refs[at - 4][:, head_cols(part)]

    for tile in lane_tiles(total_rows):
        query = query_ref[tile, :]
        wide = tile.stop - tile.start
        top = jnp.full((1, wide), 2.0 * masked_score, wide_type)
        for at in range(8):
            scores = dot_dims(pair(at, 0), query, 1, 1) + bias_ref[:, at : at + 1]
            if at < 4:
                scores = scores + mask_ref[at : at + 1, tile]
            score_ref[at * rows : (at + 1) * rows, :] = scores
            top = jnp.maximum(top, jnp.max(scores, axis=0, keepdims=True))
        mass = jnp.zeros((1, wide), wide_type)
        out = jnp.zeros((HEAD, wide), wide_type)
        for at in range(8):
            weights = jnp.exp(score_ref[at * rows : (at + 1) * rows, :] - top)
            mass = mass + jnp.sum(weights, axis=0, keepdims=True)
            out = out + dot_dims(pair(at, 1), weights.astype(low_type), 0, 0)
        total_ref[0:1, tile] = top + jnp.log(mass)
        rows_out = (out / mass).T
        out_ref[tile, :] = rows_out
        low_ref[tile, :] = rows_out.astype(low_type)


def attend_back_kernel(own, bias_ref, mask_ref, total_ref, out_ref, own_ref, *refs):
    grad_refs, cross_refs = refs[:4], refs[4:-4]
    pair_sum, query_sum, query_ref, grad_ref = refs[-4:]
    rows = grad_refs[0].shape[0]
    query_ref[...] = own_ref[:, head_cols(2)]
    for at in range(4):
        grad_ref[at * rows : (at + 1) * rows, :] = grad_refs[at][...]
    ones = jnp.ones((8, HEAD), wide_type)
    pair_sum[...] = jnp.zeros_like(pair_sum)
    for tile in lane_tiles(4 * rows):
        query = query_ref[tile, :]
        grad = grad_ref[tile, :]
        centre = lax.dot_general(
            ones,
            grad.astype(wide_type) * out_ref[tile, :],
            (((1,), (1,)), ((), ())),
            precision=highest_precision,
            preferred_element_type=wide_type,
        )[0:1, :]
        total = total_ref[0:1, tile]
        query_part = jnp.zeros((HEAD, tile.stop - tile.start), wide_type)
        for at in range(4):
            block = slice(at * rows, (at + 1) * rows)
            if own:
                key, value = own_ref[block, head_cols(0)], own_ref[block, head_cols(1)]
                scores = dot_dims(key, query, 1, 1) + bias_ref[:, at : at + 1] + mask_ref[at : at + 1, tile]
            else:
                key, value = cross_refs[0][block, head_cols(0)], cross_refs[0][block, head_cols(1)]
                scores = dot_dims(key, query, 1, 1) + bias_ref[:, at + 4 : at + 5]
            weights = jnp.exp(scores - total)
            pair_sum[block, head_cols(1)] += dot_wide(weights.astype(low_type), grad)
            soft = dot_dims(value, grad, 1, 1)
            back = (weights * (soft - centre)).astype(low_type)
            pair_sum[block, head_cols(0)] += dot_wide(back, query)
            query_part = query_part + dot_dims(key, back, 0, 0)
        query_sum[tile, :] = query_part.T * HEAD ** (-0.5)


def turn_back_kernel(own_pair, other_pair, own_query, other_query, cos_ref, sin_ref, swap_ref, *out_refs):
    rows = out_refs[0].shape[0]
    swap = swap_ref[...]
    for at in range(4):
        block = slice(at * rows, (at + 1) * rows)
        cosine, sine = cos_ref[block, :], sin_ref[block, :]

        def turned(value):
            crossed = jnp.dot(value, swap, precision=highest_precision, preferred_element_type=wide_type)
            return (value * cosine - crossed * sine).astype(low_type)

        pair = own_pair[block, :] + other_pair[block, :]
        out_refs[at][:, head_cols(0)] = turned(pair[:, head_cols(0)])
        out_refs[at][:, head_cols(1)] = pair[:, head_cols(1)].astype(low_type)
        out_refs[at][:, head_cols(2)] = turned(own_query[block, :] + other_query[block, :])


def mix_back_kernel(at_ref, place_ref, key_w, value_w, query_w, *refs):
    mixed_refs = refs[:4]
    out_ref, stack_ref, bias_ref = refs[4:]
    ring, clip = at_ref[0], at_ref[1]
    place = place_ref[...]
    total = None
    bias_ref[...] = jnp.zeros_like(bias_ref)
    for part, weight in ((0, key_w), (1, value_w), (2, query_w)):
        relative = jnp.concatenate([ref[:, head_cols(part)] for ref in mixed_refs], axis=1)
        ordered = dot_wide(relative, place)
        bias_ref[part : part + 1, :] = jnp.sum(ordered, axis=0, keepdims=True)
        term = dot_dims(ordered.astype(low_type), weight[...], 1, 1)
        total = term if total is None else total + term
    out_ref[...] = total
    for at in range(4):
        stack_ref[lax.rem(ring + at - clip + 4, 4)] = mixed_refs[at][...]


def clip_products(at_ref, first_ref, second_ref, pack_refs, columns):
    out = None
    half = first_ref.shape[1]
    for step in range(4):
        place = ring_back(at_ref[0], step)
        pack = pack_refs[step]
        term = dot_dims(first_ref[place], pack[:half, columns], 0, 0)
        term = term + dot_dims(second_ref[place], pack[half : 2 * half, columns], 0, 0)
        out = term if out is None else out + term
    return out


def layer_grad_kernel(at_ref, act_a, act_b, norm_a, norm_b, *refs):
    head_refs, pack_refs, out_ref = refs[:-5], refs[-5:-1], refs[-1]
    part = out_ref.shape[1] // 2
    tiles = pl.num_programs(0) - (1 if head_refs else 0)

    @pl.when(pl.program_id(0) < tiles)
    def _():
        out_ref[:, :part] = clip_products(at_ref, act_a, act_b, pack_refs, slice(0, part))
        out_ref[:, part:] = clip_products(at_ref, norm_a, norm_b, pack_refs, slice(part, 2 * part))

    if head_refs:

        @pl.when(pl.program_id(0) == tiles)
        def _():
            columns = slice(2 * part, 3 * part)
            out_ref[:, :part] = clip_products(at_ref, head_refs[0], head_refs[2], pack_refs, columns)
            out_ref[:, part:] = clip_products(at_ref, head_refs[1], head_refs[3], pack_refs, columns)


def plain_grad_kernel(at_ref, rows_a, rows_b, *refs):
    pack_refs, out_ref = refs[:4], refs[4]
    out_ref[...] = clip_products(at_ref, rows_a, rows_b, pack_refs, slice(None))


def last_grad_kernel(tiles, at_ref, head_a, head_b, *refs):
    feat_refs, pack_refs, out_ref = refs[:4], refs[4:8], refs[8]
    head_rows = 2 * head_a.shape[1]
    feat_rows = head_rows + feat_refs[0].shape[0]

    @pl.when(pl.program_id(0) < tiles)
    def _():
        out = None
        for step in range(4):
            term = dot_dims(feat_refs[step][...], pack_refs[step][head_rows:feat_rows, :], 0, 0)
            out = term if out is None else out + term
        out_ref[...] = out

    @pl.when(pl.program_id(0) == tiles + 2)
    def _():
        out = None
        small = (pack_refs[0].shape[0] - feat_rows) // 2
        for step in range(4):
            high = pack_refs[step][feat_rows : feat_rows + small, :].astype(wide_type)
            term = high + pack_refs[step][feat_rows + small :, :].astype(wide_type)
            out = term if out is None else out + term
        high = out.astype(low_type).astype(wide_type)
        out_ref[:small, :] = high
        out_ref[small:, :] = out - high

    @pl.when((pl.program_id(0) >= tiles) & (pl.program_id(0) < tiles + 2))
    def _():
        out_ref[...] = clip_products(at_ref, head_a, head_b, pack_refs, slice(None))


def ring_sum_kernel(at_ref, part_ref, *refs):
    got_refs, out_ref = refs[:3], refs[3]
    block = out_ref.shape[0]
    out = part_ref[pl.ds(pl.multiple_of(at_ref[0] * block, 8), block), :]
    for got in got_refs:
        out = out + got[...].astype(wide_type)
    out_ref[...] = out


def ring_sum(ring_at, part, got, after):
    shape = (part.shape[0] // 4, part.shape[1])
    return call_kernel(
        ring_sum_kernel,
        (ring_at[None], part, *got),
        (0,),
        jax.ShapeDtypeStruct(shape, wide_type),
        [],
        4 * shape[0] * shape[1],
        0,
        after,
    )


def half_sum_kernel(own_ref, got_ref, out_ref):
    out_ref[...] = (own_ref[...] + got_ref[...]).astype(low_type)


def half_sum(own, after):
    got = lax.ppermute(own, "frame", HALF_SWAP)
    return call_kernel(
        half_sum_kernel,
        (own, got),
        (),
        jax.ShapeDtypeStruct(own.shape, low_type),
        [],
        own.size,
        0,
        after,
    )


def join_kernel(at_ref, *refs):
    out_ref = refs[4]
    block = refs[0].shape[0]
    for step in range(4):
        start = pl.multiple_of(ring_back(at_ref[0], step) * block, 16)
        out_ref[pl.ds(start, block), :] = refs[step][...]


def join_frames(ring_at, total, after, after_far=()):
    pieces = ring_pieces(total)
    return call_kernel(
        join_kernel,
        (ring_at[None], *pieces),
        (0,),
        jax.ShapeDtypeStruct((4 * total.shape[0], total.shape[1]), low_type),
        [],
        0,
        0,
        after,
        after_far,
    )


def beside_kernel(first_ref, second_ref, out_ref):
    half, wide, other = first_ref.shape[0] // 2, first_ref.shape[1], second_ref.shape[1]
    out_ref[:, :wide] = first_ref[:half, :]
    out_ref[:, wide : wide + other] = second_ref[:half, :]
    out_ref[:, wide + other :] = second_ref[half:, :]


def gather_clips(first, second, after):
    half, wide = first.shape[0] // 2, first.shape[1]
    beside = call_kernel(
        beside_kernel,
        (first, second),
        (),
        jax.ShapeDtypeStruct((half, wide + 2 * second.shape[1]), low_type),
        [],
        0,
        0,
        after,
    )
    return lax.all_gather(beside, "clip")


def take_kernel(whole_ref, out_ref):
    out_ref[...] = whole_ref[:, :, : out_ref.shape[2]]


def with_other_core(whole, wide, after):
    shape = (*whole.shape[:2], wide)
    columns = pl.pallas_call(
        without(take_kernel, 1, after),
        grid=(1,),
        out_shape=jax.ShapeDtypeStruct(shape, low_type),
        in_specs=[pl.BlockSpec(shape, lambda i: (0, 0, 0))] + any_specs(after),
        out_specs=pl.BlockSpec(shape, lambda i: (0, 0, 0)),
        compiler_params=kernel_params(),
    )(whole, *after)
    return whole, core_swap(columns)


def smem_spec():
    return pl.BlockSpec(memory_space=pltpu.SMEM)


def kernel_params():
    return pltpu.CompilerParams(vmem_limit_bytes=32 * 1024 * 1024)


def held_spec():
    return pl.BlockSpec(memory_space=pltpu.VMEM)


def any_specs(arrays):
    return [pl.BlockSpec(memory_space=pl.ANY)] * len(arrays)


def mark(value):
    while value.ndim > 2:
        value = value[0]
    return value[-8:, -128:]


def without(kernel, count, after):
    return lambda *refs: kernel(*refs[:count], *refs[count + len(after) :])


def layer_grad(clip_at, second_all, packs, first_all, after):
    whole, other = second_all
    half, wide = other.shape[1:]
    tiles = wide // 128
    part = 256
    block = (4, half, 128)
    heads = () if first_all is None else (first_all[0],) * 4
    held = [
        pl.BlockSpec(block, lambda i, at=at: (0, 0, tiles + at)) for at in range(len(heads))
    ]

    def moving(start):
        return pl.BlockSpec(block, lambda i: (0, 0, start + jnp.minimum(i, tiles - 1)))

    return pl.pallas_call(
        without(layer_grad_kernel, 9 + len(heads), after),
        grid=(tiles + (1 if heads else 0),),
        out_shape=jax.ShapeDtypeStruct((wide + (128 if heads else 0), 2 * part), wide_type),
        in_specs=[smem_spec(), moving(tiles), moving(2 * tiles), moving(0), moving(0)]
        + held
        + [held_spec()] * 4
        + any_specs(after),
        out_specs=pl.BlockSpec((128, 2 * part), lambda i: (i, 0)),
        compiler_params=kernel_params(),
        cost_estimate=pl.CostEstimate(
            flops=32 * half * wide * part,
            bytes_accessed=2 * whole.size + 8 * wide * part,
            transcendentals=0,
        ),
    )(clip_at[None], whole, whole, whole, other, *heads, *packs, *after)


def plain_grad(clip_at, rows_all, packs, after):
    whole, other = rows_all
    half, count = other.shape[1:]
    part = packs[0].shape[1]
    block = pl.BlockSpec((4, half, 128), lambda i: (0, 0, i))
    return pl.pallas_call(
        without(plain_grad_kernel, 7, after),
        grid=(count // 128,),
        out_shape=jax.ShapeDtypeStruct((count, part), wide_type),
        in_specs=[smem_spec(), block, block] + [held_spec()] * 4 + any_specs(after),
        out_specs=pl.BlockSpec((128, part), lambda i: (i, 0)),
        compiler_params=kernel_params(),
        cost_estimate=pl.CostEstimate(
            flops=16 * half * count * part,
            bytes_accessed=16 * half * count + 4 * count * part,
            transcendentals=0,
        ),
    )(clip_at[None], whole, other, *packs, *after)


def last_grad(clip_at, first_all, feats, packs, after, after_far):
    whole, other = first_all
    half, part = other.shape[1], packs[0].shape[1]
    first_block = other.shape[2] // 128
    tiles = feats[0].shape[1] // 128
    kernel = functools.partial(last_grad_kernel, tiles)
    after_far = tuple(mark(value) for value in after_far)

    def moving(start):
        return pl.BlockSpec(
            (4, half, 128), lambda i: (0, 0, start + jnp.clip(i - tiles, 0, 1))
        )

    return pl.pallas_call(
        without(kernel, 11, (*after, *after_far)),
        grid=(tiles + 3,),
        out_shape=jax.ShapeDtypeStruct(((tiles + 3) * 128, part), wide_type),
        in_specs=[smem_spec(), moving(first_block), moving(first_block + 2)]
        + [pl.BlockSpec((feats[0].shape[0], 128), lambda i: (0, jnp.minimum(i, tiles - 1)))] * 4
        + [held_spec()] * 4
        + any_specs(after)
        + any_specs(after_far),
        out_specs=pl.BlockSpec((128, part), lambda i: (i, 0)),
        compiler_params=kernel_params(),
    )(clip_at[None], whole, whole, *feats, *packs, *after, *after_far)


def by_clip(clip_at, write):
    for place in range(4):

        @pl.when(clip_at == place)
        def _(place=place):
            for step in range(4):
                write((place - step) % 4, step)


def place_layer_kernel(tiles, at_ref, all_ref, *outs):
    part = all_ref.shape[2] // 2
    is_last = pl.program_id(0) == tiles

    for place in range(4):
        columns = slice(place * part, (place + 1) * part)
        left = all_ref[place, :, :part].astype(wide_type)
        right = all_ref[place, :, part:].astype(wide_type)

        @pl.when(jnp.logical_not(is_last))
        def _(columns=columns, left=left, right=right):
            outs[0][0, :, columns] = left
            outs[1][0, :, columns] = right

        if len(outs) > 2:

            @pl.when(is_last)
            def _(columns=columns, left=left, right=right):
                outs[2][0, : outs[2].shape[1] // 2, columns] = left
                outs[2][0, outs[2].shape[1] // 2 :, columns] = right


def place_layer(clip_at, layer, levels, joined, earlier, heads_layer, after):
    part = joined.shape[2] // 2
    rows = 4 * part
    tiles = rows // 128
    heads = joined.shape[1] > rows
    out = [(levels, rows, 4 * part)] * 2 + [(levels, 256, 4 * part)] * heads
    tall = pl.BlockSpec((1, 128, 4 * part), lambda i: (layer, jnp.minimum(i, tiles - 1), 0))
    wide = pl.BlockSpec((1, 256, 4 * part), lambda i: (heads_layer, 0, 0))
    return pl.pallas_call(
        without(functools.partial(place_layer_kernel, tiles), 2, (*earlier, *after)),
        grid=(tiles + (1 if heads else 0),),
        out_shape=tuple(jax.ShapeDtypeStruct(shape, wide_type) for shape in out),
        in_specs=[smem_spec(), pl.BlockSpec((4, 128, 2 * part), lambda i: (0, i, 0))]
        + any_specs(earlier)
        + any_specs(after),
        out_specs=(tall, tall) + ((wide,) if heads else ()),
        input_output_aliases={2 + at: at for at in range(len(earlier))},
        compiler_params=kernel_params(),
    )(clip_at[None], joined, *earlier, *after)


def place_last_kernel(skip, at_ref, *refs):
    pieces = refs[:4]
    in_ref, small_ref, proj_ref = refs[-3:]
    part = pieces[0].shape[1]
    heads = skip + proj_ref.shape[1]
    small = small_ref.shape[0]

    def write(place, step):
        columns = slice(place * part, (place + 1) * part)
        piece = pieces[step]
        in_ref[:, columns] = piece[: in_ref.shape[0], :].astype(wide_type)
        proj_ref[0, :, columns] = piece[skip:heads, :].astype(wide_type)
        small_ref[:, columns] = piece[heads : heads + small, :].astype(wide_type) + piece[
            heads + small :, :
        ].astype(wide_type)

    by_clip(at_ref[0], write)


def place_last(clip_at, feat_rows, skip, levels, pieces, earlier):
    part = pieces[0].shape[1]
    return pl.pallas_call(
        functools.partial(place_last_kernel, skip),
        grid=(1,),
        out_shape=(
            jax.ShapeDtypeStruct((feat_rows, 4 * part), wide_type),
            jax.ShapeDtypeStruct((64, 4 * part), wide_type),
            jax.ShapeDtypeStruct((levels, 256, 4 * part), wide_type),
        ),
        in_specs=[smem_spec()]
        + [pl.BlockSpec(pieces[0].shape, lambda i: (0, 0))] * 4
        + [pl.BlockSpec(memory_space=pl.ANY)],
        out_specs=(
            pl.BlockSpec((feat_rows, 4 * part), lambda i: (0, 0)),
            pl.BlockSpec((64, 4 * part), lambda i: (0, 0)),
            pl.BlockSpec((1, 256, 4 * part), lambda i: (0, 0, 0)),
        ),
        input_output_aliases={5: 2},
        compiler_params=kernel_params(),
    )(clip_at[None], *pieces, earlier)


def pack_kernel(by_rows, count, at_ref, *refs):
    parts, outs = refs[:count], refs[count:]
    for clip in range(4):

        @pl.when(at_ref[0] == clip)
        def _(clip=clip):
            for step in range(4):
                place, start = (clip + step) % 4, 0
                for part in parts:
                    size = part.shape[1] // 4
                    value = part[:, place * size : (place + 1) * size]
                    if by_rows:
                        outs[step][start : start + part.shape[0], :] = value
                        start += part.shape[0]
                    else:
                        outs[step][:, start : start + size] = value
                        start += size


def pack_parts(clip_at, parts, by_rows, after):
    sizes = [part.shape[1] // 4 for part in parts]
    if by_rows:
        shape = (sum(part.shape[0] for part in parts), sizes[0])
    else:
        shape = (parts[0].shape[0], sum(sizes))
    return call_kernel(
        functools.partial(pack_kernel, by_rows, len(parts)),
        (clip_at[None], *parts),
        (0,),
        tuple(jax.ShapeDtypeStruct(shape, low_type) for _ in range(4)),
        [],
        0,
        0,
        after,
    )


def place_heads_kernel(at_ref, all_ref, *refs):
    out_ref = refs[-1]
    for place in range(4):
        piece = all_ref[place].astype(wide_type)
        for at, part in ((1, 0), (2, 1), (0, 2)):
            out_ref[0, at, :, head_cols(place)] = piece[:, head_cols(part)]


def place_heads(clip_at, layer, levels, joined, earlier, after):
    rows = joined.shape[1]
    tile = 256
    count = 2
    return pl.pallas_call(
        without(place_heads_kernel, count, (*earlier, *after)),
        grid=(rows // tile,),
        out_shape=jax.ShapeDtypeStruct((levels, 3, rows, 4 * HEAD), wide_type),
        in_specs=[smem_spec(), pl.BlockSpec((4, tile, 3 * HEAD), lambda i: (0, i, 0))]
        + any_specs(earlier)
        + any_specs(after),
        out_specs=pl.BlockSpec((1, 3, tile, 4 * HEAD), lambda i: (layer, 0, i, 0)),
        input_output_aliases={count + at: at for at in range(len(earlier))},
        compiler_params=kernel_params(),
    )(clip_at[None], joined, *earlier, *after)


def stack_kernel(*refs):
    out_ref = refs[-1]
    for at, ref in enumerate(refs[:-1]):
        out_ref[8 * at : 8 * (at + 1), :] = ref[...]


def feature_grad_kernel(ids_ref, rows_ref, weight_ref, out_ref):
    size = rows_ref.shape[0] // 4
    for at in range(4):
        start = pl.multiple_of(ids_ref[at] * size, 8)
        out_ref[pl.ds(start, size), :] = dot_dims(
            rows_ref[at * size : (at + 1) * size, :], weight_ref[...], 1, 1
        )


def last_pack_kernel(at_ref, head_ref, patch_ref, small_a, small_b, *outs):
    heads, patches, small = head_ref.shape[0], patch_ref.shape[0], small_a.shape[0]
    values = small_a[...] + small_b[...]
    high = values.astype(low_type)
    rest = (values - high.astype(wide_type)).astype(low_type)
    for clip in range(4):

        @pl.when(at_ref[0] == clip)
        def _(clip=clip):
            for step in range(4):
                size = outs[step].shape[1]
                place = (clip + step) % 4
                columns = slice(place * size, (place + 1) * size)
                outs[step][:heads, :] = head_ref[:, columns]
                outs[step][heads : heads + patches, :] = patch_ref[:, columns]
                outs[step][heads + patches : heads + patches + small, :] = high[:, columns]
                outs[step][heads + patches + small :, :] = rest[:, columns]


def call_kernel(kernel, args, in_smem, outs, scratch, flops, exps, after=(), after_far=(), piped=()):
    count = len(args)

    def spec(at):
        if at in piped:
            return pl.BlockSpec(args[at].shape, lambda i, rank=args[at].ndim: (0,) * rank)
        return pl.BlockSpec(memory_space=pltpu.SMEM if at in in_smem else pltpu.VMEM)

    specs = [spec(at) for at in range(count)]
    after = (*after, *(mark(value) for value in after_far))
    specs += any_specs(after)
    moved = sum(a.size * a.dtype.itemsize for a in args)
    return pl.pallas_call(
        without(kernel, count, after),
        grid=(1,),
        out_shape=outs,
        in_specs=specs,
        out_specs=jax.tree.map(lambda _: pl.BlockSpec(memory_space=pltpu.VMEM), outs),
        scratch_shapes=scratch,
        compiler_params=kernel_params(),
        cost_estimate=pl.CostEstimate(flops=flops, bytes_accessed=moved, transcendentals=exps),
    )(*args, *after)


def on_device(
    features,
    cond_values,
    cond_live,
    in_weight,
    in_bias,
    act_weight,
    act_bias,
    state_weight,
    state_bias,
    attn_gain,
    attn_shift,
    qkv_weight,
    qkv_bias,
    proj_weight,
    proj_bias,
    mlp_gain,
    mlp_shift,
    up_weight,
    up_bias,
    down_weight,
    down_bias,
    out_grad,
):
    patch_rows = features.shape[2]
    feat_width = features.shape[3]
    slot_count = cond_values.shape[2]
    all_frames = cond_live.shape[1]
    model_width = in_weight.shape[1]
    width = qkv_weight.shape[3]
    heads = width // HEAD
    level_count = attn_gain.shape[0]
    patches = patch_rows // 4
    chunk_rows = patches + EXTRA
    rows = 4 * chunk_rows
    hidden_width = up_weight.shape[2]

    tensor_at = lax.axis_index("tensor")
    chip_at, core_at = tensor_at // 2, tensor_at % 2
    frame_at = lax.axis_index("frame")
    half_at, ring_at = frame_at // 4, frame_at % 4
    clip_at = lax.axis_index("clip")

    chunk_ids = [
        2 * jnp.bitwise_xor(core_at, core_step) + jnp.bitwise_xor(chip_at, chip_step)
        for core_step in range(2)
        for chip_step in range(2)
    ]
    own_chunk = chunk_ids[0]
    own_frames = jnp.stack([4 * half_at + (ring_at - step) % 4 for step in range(4)])
    cross_frames = jnp.stack([4 * (1 - half_at) + (ring_at - step) % 4 for step in range(4)])

    within = lax.broadcasted_iota(jnp.int32, (chunk_rows, 1), 0)
    is_patch = within < patches
    heights, columns = [], []
    for chunk_id in chunk_ids:
        patch_id = chunk_id * patches + within
        heights.append(jnp.where(is_patch, patch_id // GRID_W, 0))
        columns.append(jnp.where(is_patch, patch_id % GRID_W, 0))
    heights = jnp.concatenate(heights, axis=0).astype(wide_type)
    columns = jnp.concatenate(columns, axis=0).astype(wide_type)
    swap_table, rate_table = rotary_tables(HEAD, heads)
    swap_heads = jnp.asarray(swap_table)
    swap_one = jnp.asarray(swap_table[:HEAD, :HEAD])
    rates = rate_table[:, :HEAD]
    place_angles = heights * rates[1] + columns * rates[2]
    angles = jnp.concatenate(
        [
            own_frames[step].astype(wide_type) * rates[0][None, :] + place_angles
            for step in range(4)
        ],
        axis=0,
    )
    cosine_four, sine_four = jnp.cos(angles), jnp.sin(angles)
    head_from = jnp.arange(width)
    head_to = ((head_from // HEAD + ring_at) % 4) * HEAD + head_from % HEAD
    head_place = (head_to[:, None] == head_from[None, :]).astype(low_type)
    proj_turned = [
        lax.dynamic_slice_in_dim(
            jnp.concatenate([proj_weight[layer], proj_weight[layer]], axis=0),
            ring_at * HEAD,
            width,
            0,
        )
        for layer in range(level_count)
    ]
    ring_scalar = ring_at.astype(jnp.int32)
    clip_scalar = clip_at.astype(jnp.int32)

    live_all = cond_live[0].astype(wide_type)
    own_slots = lax.dynamic_index_in_dim(live_all, frame_at, 0, False)

    def live_rows(slots, chunk_id):
        picked = jnp.where(
            chunk_id < slot_count,
            lax.dynamic_index_in_dim(slots, jnp.minimum(chunk_id, slot_count - 1), 1, False),
            0.0,
        )
        return jnp.where(is_patch, 1.0, jnp.where(within == patches, picked[None, :], 0.0))

    sources = jnp.concatenate([own_frames, cross_frames])
    source_live = jnp.take(live_all, sources, axis=0)
    key_live = jnp.concatenate([live_rows(source_live, c) for c in chunk_ids], axis=0)
    reached = jnp.concatenate([jnp.ones((4,), jnp.bool_), jnp.full((4,), half_at == 1)])
    key_bias = jnp.where((key_live > 0.5) & reached[None, :], 0.0, masked_score).astype(wide_type)
    seen = own_frames[:, None] <= own_frames[None, :]
    causal = jnp.where(seen, 0.0, masked_score).astype(wide_type)
    causal = jnp.pad(jnp.repeat(causal, rows, axis=1), ((0, 4), (0, 0)))
    own_live = live_rows(own_slots[None, :], own_chunk)

    def extra_rows(slot_rows):
        picked = lax.dynamic_slice_in_dim(
            slot_rows, jnp.minimum(own_chunk, slot_count - 1), 1, 0
        )
        picked = jnp.where(own_chunk < slot_count, picked, jnp.zeros_like(picked))
        return jnp.pad(picked, ((0, EXTRA - 1), (0, 0)))

    cond_here = cond_values[0, 0]
    act_rows = jnp.dot(cond_here, act_weight, precision=highest_precision) + act_bias
    state_rows = jnp.dot(cond_here, state_weight, precision=highest_precision) + state_bias
    even_slot = (jnp.arange(slot_count) % 2 == 0)[:, None]
    cond_x = jnp.where(even_slot, act_rows, state_rows) * own_slots[:, None]

    flat_feat = jnp.concatenate(
        [
            lax.dynamic_slice_in_dim(features[0, 0], c * patches, patches, 0)
            for c in chunk_ids
        ],
        axis=0,
    )
    kept, got = halves_tensor(dot_wide(flat_feat, in_weight))
    stream = jnp.concatenate([kept + got + in_bias, extra_rows(cond_x)], axis=0)

    feat_wide = -(-feat_width // 128) * 128
    feat_low = jnp.pad(flat_feat, ((0, 0), (0, feat_wide - feat_width)))
    feats = [feat_low] + [
        lax.ppermute(feat_low, "clip", clip_shift(step)) for step in range(1, 4)
    ]
    pair_work = 2 * 32 * rows * rows * HEAD
    pair_exps = 32 * rows * rows
    weight_parts = [
        [qkv_weight[layer, :, at] for at in (1, 2, 0)] for layer in range(level_count)
    ]

    def norm(terms, gain, shift, after=(), after_far=()):
        chunk = jax.ShapeDtypeStruct((chunk_rows, model_width), wide_type)
        return call_kernel(
            norm_kernel,
            (gain[None], shift[None], *terms),
            (),
            (
                chunk,
                chunk,
                jax.ShapeDtypeStruct((chunk_rows, 128), wide_type),
                jax.ShapeDtypeStruct((chunk_rows, model_width), low_type),
            ),
            [],
            12 * chunk_rows * model_width,
            0,
            after,
            after_far,
        )

    def norm_back(part, gain, hat, inverse, grad, count, after=(), after_far=()):
        kept, got = halves_tensor(part)
        return call_kernel(
            functools.partial(norm_back_kernel, count),
            (kept, got, gain[None], hat, inverse, grad),
            (),
            (
                jax.ShapeDtypeStruct((chunk_rows, model_width), wide_type),
                jax.ShapeDtypeStruct((chunk_rows, model_width), low_type),
                jax.ShapeDtypeStruct((8, model_width), wide_type),
            ),
            [],
            16 * chunk_rows * model_width,
            0,
            after,
            after_far,
            (2, 3, 4, 5),
        )

    slot_grads = out_grad[0, 0, patch_rows:] * own_slots[:, None].astype(low_type)
    slot_blocks = jnp.concatenate(
        [
            jnp.pad(slot_grads[:, None], ((0, 0), (0, EXTRA - 1), (0, 0))),
            jnp.zeros((4 - slot_count, EXTRA, model_width), low_type),
        ],
        axis=0,
    )
    branch_parts = []
    for chunk_id in chunk_ids:
        branch_parts.append(
            lax.dynamic_slice_in_dim(out_grad[0, 0], chunk_id * patches, patches, 0)
        )
        branch_parts.append(lax.dynamic_index_in_dim(slot_blocks, chunk_id, 0, False))
    first_branch = jnp.concatenate(branch_parts, axis=0)
    stored = []
    terms = (stream,)
    before = None
    for layer in range(level_count):
        stream, hat_one, inverse_one, first_chunk = norm(terms, attn_gain[layer], attn_shift[layer])
        first_in = join_rows_tensor(first_chunk)
        bias = jnp.pad(qkv_bias[layer], ((0, 5), (0, 0)))
        heads_out = call_kernel(
            functools.partial(project_kernel, heads),
            (
                ring_scalar[None],
                first_in,
                *weight_parts[layer],
                bias,
                cosine_four,
                sine_four,
                swap_heads,
            ),
            (0,),
            tuple(
                jax.ShapeDtypeStruct((rows, count * HEAD), low_type)
                for count in (3, 3, 3, 3, 2, 2, 2, 2)
            ),
            [],
            6 * rows * model_width * width,
            0,
            (),
            () if before is None else (before[0],),
            (2, 3, 4, 5, 6, 7, 8),
        )
        blocks = to_heads(heads_out[:4])
        cross = pairs_to_later_half(heads_out[4:])
        attn_wide, attn_turned, log_total, own_all, cross_all = call_kernel(
            attend_kernel,
            (key_bias, causal, *blocks, *cross),
            (),
            (
                jax.ShapeDtypeStruct((4 * rows, HEAD), wide_type),
                jax.ShapeDtypeStruct((4 * rows, HEAD), low_type),
                jax.ShapeDtypeStruct((8, 4 * rows), wide_type),
                jax.ShapeDtypeStruct((4 * rows, 3 * HEAD), low_type),
                jax.ShapeDtypeStruct((4 * rows, 2 * HEAD), low_type),
            ),
            [
                pltpu.VMEM((4 * rows, HEAD), low_type),
                pltpu.VMEM((8 * rows, lane_tiles(4 * rows)[0].stop), wide_type),
            ],
            2 * pair_work,
            pair_exps,
            tuple(feats[1:]) if layer == 0 else (),
        )
        attn_relative = jnp.concatenate(
            to_frames([attn_turned[at * rows : (at + 1) * rows] for at in range(4)]), axis=1
        )
        attn_low = dot_wide(attn_relative, head_place).astype(low_type)
        if layer < level_count - 1:
            first_all = gather_clips(first_in, attn_low, ())
        kept, got = halves_tensor(dot_wide(attn_relative, proj_turned[layer]))
        middle, hat_two, inverse_two, second_chunk = norm(
            (stream, kept, got, proj_bias[layer][None]), mlp_gain[layer], mlp_shift[layer],
            () if before is None else (first_branch,),
            () if before is None else (before[1],),
        )
        second_in = join_rows_tensor(second_chunk)
        hidden = dot_wide(second_in, up_weight[layer]) + up_bias[layer]
        active_low = exact_gelu(hidden).astype(low_type)
        second_all = gather_clips(second_in, active_low, ())
        if layer == level_count - 1:
            first_all = (first_in, attn_low)
        before = (first_all, second_all)
        kept, got = halves_tensor(dot_wide(active_low, down_weight[layer]))
        terms = (middle, kept, got, down_bias[layer][None])
        stored.append(
            (
                hat_one,
                inverse_one,
                own_all,
                cross_all,
                log_total,
                attn_wide,
                hat_two,
                inverse_two,
                hidden,
                first_all,
                second_all,
            )
        )
    def in_order(full, count):
        out = jnp.zeros((4 * count,) + full.shape[1:], full.dtype)
        size = full.shape[0] // 4
        for at, chunk_id in enumerate(chunk_ids):
            out = lax.dynamic_update_slice_in_dim(
                out, full[at * size : at * size + count], chunk_id * count, 0
            )
        return out

    def block_rows(after):
        low = call_kernel(
            block_kernel,
            (*terms, jnp.broadcast_to(own_live, (chunk_rows, 128))),
            (),
            jax.ShapeDtypeStruct((chunk_rows, model_width), low_type),
            [],
            4 * chunk_rows * model_width,
            0,
            after,
        )
        return join_rows_tensor(low)

    def block_in_order(block_full):
        slot_full = jnp.concatenate(
            [
                block_full[at * chunk_rows + patches : at * chunk_rows + patches + 1]
                for at in range(4)
            ],
            axis=0,
        )
        return jnp.concatenate(
            [in_order(block_full, patches), in_order(slot_full, 1)[:slot_count]], axis=0
        )[None, None]

    own_out = lax.dynamic_slice_in_dim(out_grad[0, 0], own_chunk * patches, patches, 0)
    grad_stream = (
        jnp.concatenate(
            [
                own_out.astype(wide_type),
                extra_rows(out_grad[0, 0, patch_rows:].astype(wide_type)),
            ],
            axis=0,
        )
        * own_live
    )

    small = {}
    small["down", level_count - 1] = jnp.sum(grad_stream, axis=0)
    sums_list = []
    wide_part = model_width // 4
    later = None
    for layer in reversed(range(level_count)):
        (
            hat_one,
            inverse_one,
            own_all,
            cross_all,
            log_total,
            attn_wide,
            hat_two,
            inverse_two,
            hidden,
            first_all,
            second_all,
        ) = stored[layer]
        branch = first_branch if later is None else join_rows_tensor(branch_chunk)
        if later is not None:
            first_all = with_other_core(first_all, model_width, (branch,))
            second_all = with_other_core(second_all, model_width, (branch,))
        _, gelu_pull = jax.vjp(exact_gelu, hidden)
        grad_hidden = gelu_pull(dot_dims(branch, down_weight[layer], 1, 1))[0].astype(low_type)
        small["up", layer] = jnp.sum(grad_hidden.astype(wide_type), axis=0)
        parts = [branch, grad_hidden] + ([] if later is None else [later["proj_out"]])
        packs = pack_parts(clip_scalar, parts, False, ())
        grad_middle, proj_chunk, sums = norm_back(
            dot_dims(grad_hidden, up_weight[layer], 1, 1),
            mlp_gain[layer],
            hat_two,
            inverse_two,
            grad_stream,
            chunk_rows,
            (packs[0],) if later is None else (packs[0], later["tall_join"]),
        )
        sums_list.append(sums)
        packs = swap_clips(packs)
        if later is None:
            block_full = block_rows((proj_chunk,))
            block_out = block_in_order(block_full)
        proj_out = join_rows_tensor(proj_chunk)
        grad_attn = dot_dims(proj_out, proj_turned[layer], 1, 1).astype(low_type)
        grads = to_heads([grad_attn[:, head_cols(at)] for at in range(4)])

        if later is not None:
            heads_sum = plain_grad(
                clip_scalar, later["first_all"], later["heads_packs"], (proj_chunk,)
            )
            heads_got = ring_sends(heads_sum, ring_at)

            later["tall_all"] = lax.all_gather(later["tall_join"], "clip")

        def attend_back(own, after, after_far=()):
            return call_kernel(
                functools.partial(attend_back_kernel, own),
                (key_bias, causal, log_total, attn_wide, own_all, *grads)
                + (() if own else (cross_all,)),
                (),
                (
                    jax.ShapeDtypeStruct((4 * rows, 2 * HEAD), wide_type),
                    jax.ShapeDtypeStruct((4 * rows, HEAD), wide_type),
                ),
                [
                    pltpu.VMEM((4 * rows, HEAD), low_type),
                    pltpu.VMEM((4 * rows, HEAD), low_type),
                ],
                5 * pair_work // 2,
                pair_exps // 2,
                after,
                after_far,
                (0, 1, 2, 3, 4) if own else (0, 1, 2, 3, 4, 9),
            )

        cross_pair, cross_query = attend_back(
            False, (), () if later is None else (heads_sum,)
        )
        if later is not None:
            later["heads_ring"] = ring_sum(ring_scalar, heads_sum, heads_got, (cross_pair,))
        got_pair = lax.ppermute(cross_pair, "frame", DOWN_HALF)
        if later is None:
            second_all = with_other_core(second_all, model_width, (cross_pair,))
            first_all = with_other_core(
                gather_clips(*first_all, (cross_pair,)), model_width, (cross_pair,)
            )
        tall_sum = layer_grad(
            clip_scalar,
            second_all,
            packs,
            None if later is None else later["first_all"],
            (cross_pair,),
        )
        own_pair, own_query = attend_back(
            True,
            () if later is None else (later["heads_ring"],),
            (tall_sum,) if later is None else (tall_sum, later["tall_all"], block_full),
        )
        tall_got = ring_sends(tall_sum, ring_at)
        if later is not None:
            later["heads_total"] = half_sum(later["heads_ring"], (own_pair,))
        tall_ring = ring_sum(ring_scalar, tall_sum, tall_got, ())
        tall_total = half_sum(tall_ring, ())
        turned = call_kernel(
            turn_back_kernel,
            (own_pair, got_pair, own_query, cross_query, cosine_four, sine_four, swap_one),
            (),
            tuple(jax.ShapeDtypeStruct((rows, 3 * HEAD), low_type) for _ in range(4)),
            [],
            24 * rows * HEAD * HEAD,
            0,
            (tall_ring,) if later is None else (tall_ring, later["heads_total"]),
            (),
            (4, 5, 6),
        )
        mixed = to_frames(list(turned))
        if later is not None:
            later["heads_join"] = join_frames(ring_scalar, later["heads_total"], (turned[0],))
        normed_part, mixed_stack, bias_sums = call_kernel(
            mix_back_kernel,
            (
                jnp.stack([ring_scalar, clip_scalar]),
                head_place,
                *weight_parts[layer],
                *mixed,
            ),
            (0,),
            (
                jax.ShapeDtypeStruct((rows, model_width), wide_type),
                jax.ShapeDtypeStruct((4, rows, 3 * HEAD), low_type),
                jax.ShapeDtypeStruct((8, width), wide_type),
            ),
            [],
            6 * rows * model_width * width,
            0,
            (tall_total,) if later is None else (tall_total, later["heads_join"]),
            (),
            (1, 2, 3, 4),
        )
        small["qkv", layer] = jnp.concatenate([bias_sums[2:3], bias_sums[:2]], axis=0)
        packs = swap_clips([mixed_stack[step] for step in range(4)])
        grad_stream, branch_chunk, sums = norm_back(
            normed_part,
            attn_gain[layer],
            hat_one,
            inverse_one,
            grad_middle,
            patches if layer == 0 else chunk_rows,
        )
        sums_list.append(sums)
        if layer > 0:
            tall_join = join_frames(ring_scalar, tall_total, (branch_chunk,))
            later = {
                "proj_out": proj_out,
                "first_all": first_all,
                "tall_join": tall_join,
                "heads_packs": packs,
            }

    heads_packs = packs
    patch_chunk = branch_chunk[:patches]
    grad_patch = join_rows_tensor(patch_chunk)
    grad_features = call_kernel(
        feature_grad_kernel,
        (jnp.stack(chunk_ids).astype(jnp.int32), grad_patch, in_weight),
        (0,),
        jax.ShapeDtypeStruct((patch_rows, feat_width), wide_type),
        [],
        2 * patch_rows * feat_width * model_width,
        0,
        piped=(2,),
    )
    slot_row = grad_stream[patches : patches + 1] * own_live[patches : patches + 1]
    own_cond = lax.dynamic_slice_in_dim(
        cond_here, jnp.minimum(own_chunk, slot_count - 1), 1, 0
    )
    slot_part = jnp.concatenate([own_cond.T * slot_row, slot_row], axis=0)
    here = own_chunk < slot_count
    is_act = here & (own_chunk % 2 == 0)
    is_state = here & (own_chunk % 2 == 1)
    act_part = jnp.where(is_act, slot_part, 0.0)
    state_part = jnp.where(is_state, slot_part, 0.0)

    def at_tensor(value, total):
        return lax.dynamic_update_slice(
            jnp.zeros((value.shape[0], total), wide_type),
            value,
            (0, tensor_at * value.shape[1]),
        )

    layers = range(level_count)
    qkv_rows = at_tensor(
        jnp.concatenate([small["qkv", layer] for layer in layers], axis=0), 4 * width
    )
    mixed_rows = jnp.concatenate(
        [qkv_rows, small["down", level_count - 1][None], jnp.zeros_like(qkv_rows[:1])], axis=0
    )
    ups = at_tensor(jnp.stack([small["up", layer] for layer in layers]), 4 * hidden_width)
    parts = [*sums_list, act_part, state_part, mixed_rows, ups.reshape(-1, model_width)]
    vector = call_kernel(
        stack_kernel,
        tuple(parts),
        (),
        jax.ShapeDtypeStruct((8 * len(parts), model_width), wide_type),
        [],
        0,
        0,
    )
    vector = vector + core_swap(vector)
    later["heads_all"] = lax.all_gather(later["heads_join"], "clip")
    head_rows, patch_count, small_rows = proj_out.shape[0], grad_patch.shape[0], vector.shape[0]
    packs = call_kernel(
        last_pack_kernel,
        (clip_scalar[None], proj_out, grad_patch, vector, chip_swap(vector)),
        (0,),
        tuple(
            jax.ShapeDtypeStruct((head_rows + patch_count + 2 * small_rows, wide_part), low_type)
            for _ in range(4)
        ),
        [],
        0,
        0,
    )
    heads_sum = plain_grad(clip_scalar, first_all, heads_packs, (packs[0],))
    heads_got = ring_sends(heads_sum, ring_at)
    tall_join = join_frames(ring_scalar, tall_total, (grad_patch,))
    tall_all = lax.all_gather(tall_join, "clip")
    placed = place_layer(
        clip_scalar, level_count - 1, level_count, later["tall_all"], (), 0, (packs[0],)
    )
    packs = swap_clips(packs)
    heads_ring = ring_sum(ring_scalar, heads_sum, heads_got, tuple(packs[1:]))
    last_sum = last_grad(
        clip_scalar, first_all, feats, packs, (heads_ring,), (placed[0], grad_features)
    )
    last_ring = ring_sum(ring_scalar, last_sum, ring_sends(last_sum, ring_at), ())
    heads_total = half_sum(heads_ring, (mark(last_sum),))
    heads_join = join_frames(ring_scalar, heads_total, (last_ring,))
    heads_all = lax.all_gather(heads_join, "clip")
    heads_placed = place_heads(
        clip_scalar, level_count - 1, level_count, later["heads_all"], (), (packs[0],)
    )
    last_join = join_frames(
        ring_scalar, half_sum(last_ring, ()), (), (tall_all, heads_placed)
    )
    last_pieces = clip_pieces(last_join)
    grad_down, grad_up, grad_proj = place_layer(
        clip_scalar, 0, level_count, tall_all, placed, level_count - 1, ()
    )
    grad_in, vector, grad_proj = place_last(
        clip_scalar, feat_width, feat_wide, level_count, last_pieces, grad_proj
    )
    grad_heads = (place_heads(clip_scalar, 0, level_count, heads_all, (heads_placed,), ()),)


    def norm_sums(layer, first, row):
        return vector[8 * (2 * (level_count - 1 - layer) + first) + row]

    grad_mlp_gain = jnp.stack([norm_sums(layer, 0, 0) for layer in layers])
    grad_mlp_shift = jnp.stack([norm_sums(layer, 0, 1) for layer in layers])
    grad_proj_bias = jnp.stack([norm_sums(layer, 0, 2) for layer in layers])
    grad_attn_gain = jnp.stack([norm_sums(layer, 1, 0) for layer in layers])
    grad_attn_shift = jnp.stack([norm_sums(layer, 1, 1) for layer in layers])
    rest = vector[16 * level_count :]
    grad_down_bias = jnp.stack(
        [norm_sums(layer + 1, 1, 2) for layer in range(level_count - 1)]
        + [rest[16 + 3 * level_count]]
    )
    grad_qkv_bias = lax.dynamic_slice_in_dim(
        rest[16 : 16 + 3 * level_count], tensor_at * width, width, 1
    )
    grad_qkv_bias = grad_qkv_bias.reshape(level_count, 3, width)
    grad_up_bias = lax.dynamic_slice_in_dim(
        rest[24:].reshape(level_count, 4 * hidden_width), tensor_at * hidden_width, hidden_width, 1
    )
    act_count = cond_here.shape[1]
    return (
        block_out,
        grad_features[None, None],
        grad_in,
        norm_sums(0, 1, 2),
        rest[:act_count],
        rest[act_count],
        rest[8 : 8 + act_count],
        rest[8 + act_count],
        grad_attn_gain,
        grad_attn_shift,
        jnp.swapaxes(grad_heads[0], 1, 2),
        grad_qkv_bias,
        grad_proj,
        grad_proj_bias,
        grad_mlp_gain,
        grad_mlp_shift,
        grad_up,
        grad_up_bias,
        grad_down,
        grad_down_bias,
    )


def solution(mesh):
    return jax.shard_map(
        on_device,
        mesh=mesh,
        in_specs=(
            P("clip", "frame", None, "tensor"),
            P("clip", "frame", None, None),
            P("clip", None, None),
            P("tensor", None),
            P(),
            P(),
            P(),
            P(),
            P(),
            P(),
            P(),
            P(None, None, None, "tensor"),
            P(None, None, "tensor"),
            P(None, "tensor", None),
            P(),
            P(),
            P(),
            P(None, None, "tensor"),
            P(None, "tensor"),
            P(None, "tensor", None),
            P(),
            P("clip", "frame", None, None),
        ),
        out_specs=(
            P("clip", "frame", None, None),
            P("clip", "frame", None, "tensor"),
            P("tensor", None),
            P(),
            P(),
            P(),
            P(),
            P(),
            P(),
            P(),
            P(None, None, None, "tensor"),
            P(None, None, "tensor"),
            P(None, "tensor", None),
            P(),
            P(),
            P(),
            P(None, None, "tensor"),
            P(None, "tensor"),
            P(None, "tensor", None),
            P(),
        ),
        check_vma=False,
    )
```

```python
import functools

import jax
import jax.numpy as jnp
import numpy as np
from jax import lax
from jax.experimental import pallas as pl
from jax.experimental.pallas import tpu as pltpu
from jax.sharding import PartitionSpec as P

HEAD = 64
GRID_W = 16
EXTRA = 8

highest_precision = lax.Precision.HIGHEST
norm_epsilon = 1e-06
masked_score = -1000000000.0
low_type = jnp.bfloat16
wide_type = jnp.float32

CORE_SWAP = [(0, 1), (1, 0), (2, 3), (3, 2)]
CHIP_SWAP = [(0, 2), (2, 0), (1, 3), (3, 1)]
HALF_SWAP = [(i, (i + 4) % 8) for i in range(8)]


def clip_shift(step):
    return [(i, (i + step) % 4) for i in range(4)]


def frame_shift(halves, step):
    return [
        (4 * half + i, 4 * ((half + halves) % 2) + (i + step) % 4)
        for half in range(2)
        for i in range(4)
    ]


def core_swap(value):
    return lax.ppermute(value, "tensor", CORE_SWAP)


def chip_swap(value):
    return lax.ppermute(value, "tensor", CHIP_SWAP)


def halves_tensor(part):
    half = part.shape[0] // 2
    pair = part[:half] + core_swap(part[half:])
    quarter = half // 2
    return pair[:quarter], chip_swap(pair[quarter:])


def join_rows_tensor(chunk):
    pair = jnp.concatenate([chunk, chip_swap(chunk)], axis=0)
    return jnp.concatenate([pair, core_swap(pair)], axis=0)


def to_heads(blocks):
    return [blocks[0]] + [
        lax.ppermute(blocks[step], "frame", frame_shift(0, step)) for step in range(1, 4)
    ]


def to_frames(blocks):
    return [blocks[0]] + [
        lax.ppermute(blocks[step], "frame", frame_shift(0, -step)) for step in range(1, 4)
    ]


def pairs_to_later_half(blocks):
    return [
        lax.ppermute(
            blocks[step],
            "frame",
            [(src, dst) for src, dst in frame_shift(1, step) if src < dst],
        )
        for step in range(4)
    ]


DOWN_HALF = [(i + 4, i) for i in range(4)]


def swap_clips(packs):
    return [packs[0]] + [
        lax.ppermute(packs[step], "clip", clip_shift(step)) for step in range(1, 4)
    ]


def ring_pieces(value):
    return [value] + [
        lax.ppermute(value, "frame", frame_shift(0, step)) for step in range(1, 4)
    ]


def ring_sends(part, ring):
    block = part.shape[0] // 4
    got = []
    for step in range(1, 4):
        sent = lax.dynamic_slice_in_dim(part, ((ring + step) % 4) * block, block, 0)
        got.append(lax.ppermute(sent.astype(low_type), "frame", frame_shift(0, step)))
    return got


def clip_pieces(joined):
    return [joined] + [
        lax.ppermute(joined, "clip", clip_shift(step)) for step in range(1, 4)
    ]


def rotary_tables(head_size, head_count):
    group_size = 2 * (head_size // 3 // 2)
    half_size = group_size // 2
    total_width = head_size * head_count
    swap_table = np.zeros((total_width, total_width), np.float32)
    rate_table = np.zeros((3, total_width), np.float32)
    for head_at in range(head_count):
        for axis_at in range(3):
            for pair_at in range(half_size):
                lower_at = head_at * head_size + axis_at * group_size + pair_at
                upper_at = lower_at + half_size
                swap_table[upper_at, lower_at] = -1.0
                swap_table[lower_at, upper_at] = 1.0
                rate_value = 10000.0 ** (-2.0 * pair_at / group_size)
                rate_table[axis_at, lower_at] = rate_value
                rate_table[axis_at, upper_at] = rate_value
    return swap_table, rate_table


def norm_rows(values):
    row_mean = jnp.mean(values, axis=-1, keepdims=True)
    centred = values - row_mean
    spread = jnp.mean(centred * centred, axis=-1, keepdims=True)
    inverse = lax.rsqrt(spread + norm_epsilon)
    return centred * inverse, inverse


def norm_kernel(gain_ref, shift_ref, *refs):
    terms, (stream_ref, hat_ref, inverse_ref, low_ref) = refs[:-4], refs[-4:]
    values = terms[0][...]
    if len(terms) > 1:
        values = values + (terms[1][...] + terms[2][...] + terms[3][...])
    hat, inverse = norm_rows(values)
    stream_ref[...] = values
    hat_ref[...] = hat
    inverse_ref[...] = jnp.broadcast_to(inverse, inverse_ref.shape)
    low_ref[...] = (hat * gain_ref[...] + shift_ref[...]).astype(low_type)


def block_kernel(stream_ref, kept_ref, got_ref, bias_ref, live_ref, out_ref):
    values = stream_ref[...] + (kept_ref[...] + got_ref[...] + bias_ref[...])
    out_ref[...] = (values * live_ref[:, 0:1]).astype(low_type)


def norm_back_kernel(count, kept_ref, got_ref, gain_ref, hat_ref, inverse_ref, grad_ref, out_ref, low_ref, sums_ref):
    grad = kept_ref[...] + got_ref[...]
    hat = hat_ref[...]
    scaled = grad * gain_ref[...]
    first = jnp.mean(scaled, axis=-1, keepdims=True)
    second = jnp.mean(scaled * hat, axis=-1, keepdims=True)
    out = grad_ref[...] + (scaled - first - hat * second) * inverse_ref[:, 0:1]
    low = out.astype(low_type)
    out_ref[...] = out
    low_ref[...] = low
    sums_ref[...] = jnp.zeros_like(sums_ref)
    sums_ref[0:1, :] = jnp.sum(grad * hat, axis=0, keepdims=True)
    sums_ref[1:2, :] = jnp.sum(grad, axis=0, keepdims=True)
    sums_ref[2:3, :] = jnp.sum(low[:count].astype(wide_type), axis=0, keepdims=True)


def exact_gelu(values):
    return jax.nn.gelu(values, approximate=False)


def dot_wide(left, right):
    return jnp.dot(left, right, preferred_element_type=wide_type)


def dot_dims(left, right, left_dim, right_dim):
    return lax.dot_general(
        left, right, (((left_dim,), (right_dim,)), ((), ())), preferred_element_type=wide_type
    )


def head_cols(at):
    return slice(at * HEAD, (at + 1) * HEAD)


def ring_back(place, step):
    return lax.rem(place - step + 4, 4)


def ring_ahead(place, step):
    return lax.rem(place + step, 4)


def project_kernel(heads, at_ref, rows_ref, key_w, value_w, query_w, bias_ref, cos_ref, sin_ref, swap_ref, *out_refs):
    rows = rows_ref[...]
    swap = swap_ref[...]
    cosine = jnp.concatenate([cos_ref[: rows.shape[0], :]] * heads, axis=1)
    sine = jnp.concatenate([sin_ref[: rows.shape[0], :]] * heads, axis=1)

    def turned(weight, bias):
        value = dot_wide(rows, weight[...]) + bias
        crossed = jnp.dot(value, swap, precision=highest_precision, preferred_element_type=wide_type)
        return value * cosine + crossed * sine

    key = turned(key_w, bias_ref[1:2, :]).astype(low_type)
    value = (dot_wide(rows, value_w[...]) + bias_ref[2:3, :]).astype(low_type)
    query = (turned(query_w, bias_ref[0:1, :]).astype(low_type).astype(wide_type) * HEAD ** (-0.5)).astype(low_type)

    def write(head, step):
        for at, part in enumerate((key, value, query)):
            out_refs[step][:, head_cols(at)] = part[:, head_cols(head)]
            if at < 2:
                out_refs[4 + step][:, head_cols(at)] = part[:, head_cols(head)]

    for ring in range(4):

        @pl.when(at_ref[0] == ring)
        def _(ring=ring):
            for step in range(4):
                write((ring + step) % 4, step)


def lane_tiles(total):
    size = 384 if total % 384 == 0 else total
    return [slice(at * size, (at + 1) * size) for at in range(total // size)]


def attend_kernel(bias_ref, mask_ref, *refs):
    own_refs, cross_refs = refs[:4], refs[4:8]
    out_ref, low_ref, total_ref, own_out, cross_out, query_ref, score_ref = refs[8:]
    rows = own_refs[0].shape[0]
    total_rows = 4 * rows
    for at in range(4):
        block = slice(at * rows, (at + 1) * rows)
        query_ref[block, :] = own_refs[at][:, head_cols(2)]
        own_out[block, :] = own_refs[at][...]
        cross_out[block, :] = cross_refs[at][...]
    total_ref[...] = jnp.zeros_like(total_ref)

    def pair(at, part):
        if at < 4:
            return own_refs[at][:, head_cols(part)]
        return cross_refs[at - 4][:, head_cols(part)]

    for tile in lane_tiles(total_rows):
        query = query_ref[tile, :]
        wide = tile.stop - tile.start
        top = jnp.full((1, wide), 2.0 * masked_score, wide_type)
        for at in range(8):
            scores = dot_dims(pair(at, 0), query, 1, 1) + bias_ref[:, at : at + 1]
            if at < 4:
                scores = scores + mask_ref[at : at + 1, tile]
            score_ref[at * rows : (at + 1) * rows, :] = scores
            top = jnp.maximum(top, jnp.max(scores, axis=0, keepdims=True))
        mass = jnp.zeros((1, wide), wide_type)
        out = jnp.zeros((HEAD, wide), wide_type)
        for at in range(8):
            weights = jnp.exp(score_ref[at * rows : (at + 1) * rows, :] - top)
            mass = mass + jnp.sum(weights, axis=0, keepdims=True)
            out = out + dot_dims(pair(at, 1), weights.astype(low_type), 0, 0)
        total_ref[0:1, tile] = top + jnp.log(mass)
        rows_out = (out / mass).T
        out_ref[tile, :] = rows_out
        low_ref[tile, :] = rows_out.astype(low_type)


def attend_back_kernel(own, bias_ref, mask_ref, total_ref, out_ref, own_ref, *refs):
    grad_refs, cross_refs = refs[:4], refs[4:-4]
    pair_sum, query_sum, query_ref, grad_ref = refs[-4:]
    rows = grad_refs[0].shape[0]
    query_ref[...] = own_ref[:, head_cols(2)]
    for at in range(4):
        grad_ref[at * rows : (at + 1) * rows, :] = grad_refs[at][...]
    ones = jnp.ones((8, HEAD), wide_type)
    pair_sum[...] = jnp.zeros_like(pair_sum)
    for tile in lane_tiles(4 * rows):
        query = query_ref[tile, :]
        grad = grad_ref[tile, :]
        centre = lax.dot_general(
            ones,
            grad.astype(wide_type) * out_ref[tile, :],
            (((1,), (1,)), ((), ())),
            precision=highest_precision,
            preferred_element_type=wide_type,
        )[0:1, :]
        total = total_ref[0:1, tile]
        query_part = jnp.zeros((HEAD, tile.stop - tile.start), wide_type)
        for at in range(4):
            block = slice(at * rows, (at + 1) * rows)
            if own:
                key, value = own_ref[block, head_cols(0)], own_ref[block, head_cols(1)]
                scores = dot_dims(key, query, 1, 1) + bias_ref[:, at : at + 1] + mask_ref[at : at + 1, tile]
            else:
                key, value = cross_refs[0][block, head_cols(0)], cross_refs[0][block, head_cols(1)]
                scores = dot_dims(key, query, 1, 1) + bias_ref[:, at + 4 : at + 5]
            weights = jnp.exp(scores - total)
            pair_sum[block, head_cols(1)] += dot_wide(weights.astype(low_type), grad)
            soft = dot_dims(value, grad, 1, 1)
            back = (weights * (soft - centre)).astype(low_type)
            pair_sum[block, head_cols(0)] += dot_wide(back, query)
            query_part = query_part + dot_dims(key, back, 0, 0)
        query_sum[tile, :] = query_part.T * HEAD ** (-0.5)


def turn_back_kernel(own_pair, other_pair, own_query, other_query, cos_ref, sin_ref, swap_ref, *out_refs):
    rows = out_refs[0].shape[0]
    swap = swap_ref[...]
    for at in range(4):
        block = slice(at * rows, (at + 1) * rows)
        cosine, sine = cos_ref[block, :], sin_ref[block, :]

        def turned(value):
            crossed = jnp.dot(value, swap, precision=highest_precision, preferred_element_type=wide_type)
            return (value * cosine - crossed * sine).astype(low_type)

        pair = own_pair[block, :] + other_pair[block, :]
        out_refs[at][:, head_cols(0)] = turned(pair[:, head_cols(0)])
        out_refs[at][:, head_cols(1)] = pair[:, head_cols(1)].astype(low_type)
        out_refs[at][:, head_cols(2)] = turned(own_query[block, :] + other_query[block, :])


def mix_back_kernel(at_ref, place_ref, key_w, value_w, query_w, *refs):
    mixed_refs = refs[:4]
    out_ref, stack_ref, bias_ref = refs[4:]
    ring, clip = at_ref[0], at_ref[1]
    place = place_ref[...]
    total = None
    bias_ref[...] = jnp.zeros_like(bias_ref)
    for part, weight in ((0, key_w), (1, value_w), (2, query_w)):
        relative = jnp.concatenate([ref[:, head_cols(part)] for ref in mixed_refs], axis=1)
        ordered = dot_wide(relative, place)
        bias_ref[part : part + 1, :] = jnp.sum(ordered, axis=0, keepdims=True)
        term = dot_dims(ordered.astype(low_type), weight[...], 1, 1)
        total = term if total is None else total + term
    out_ref[...] = total
    for at in range(4):
        stack_ref[lax.rem(ring + at - clip + 4, 4)] = mixed_refs[at][...]


def clip_products(at_ref, first_ref, second_ref, pack_refs, columns):
    out = None
    half = first_ref.shape[1]
    for step in range(4):
        place = ring_back(at_ref[0], step)
        pack = pack_refs[step]
        term = dot_dims(first_ref[place], pack[:half, columns], 0, 0)
        term = term + dot_dims(second_ref[place], pack[half : 2 * half, columns], 0, 0)
        out = term if out is None else out + term
    return out


def layer_grad_kernel(at_ref, act_a, act_b, norm_a, norm_b, *refs):
    head_refs, pack_refs, out_ref = refs[:-5], refs[-5:-1], refs[-1]
    part = out_ref.shape[1] // 2
    tiles = pl.num_programs(0) - (1 if head_refs else 0)

    @pl.when(pl.program_id(0) < tiles)
    def _():
        out_ref[:, :part] = clip_products(at_ref, act_a, act_b, pack_refs, slice(0, part))
        out_ref[:, part:] = clip_products(at_ref, norm_a, norm_b, pack_refs, slice(part, 2 * part))

    if head_refs:

        @pl.when(pl.program_id(0) == tiles)
        def _():
            columns = slice(2 * part, 3 * part)
            out_ref[:, :part] = clip_products(at_ref, head_refs[0], head_refs[2], pack_refs, columns)
            out_ref[:, part:] = clip_products(at_ref, head_refs[1], head_refs[3], pack_refs, columns)


def plain_grad_kernel(at_ref, rows_a, rows_b, *refs):
    pack_refs, out_ref = refs[:4], refs[4]
    out_ref[...] = clip_products(at_ref, rows_a, rows_b, pack_refs, slice(None))


def last_grad_kernel(tiles, at_ref, head_a, head_b, *refs):
    feat_refs, pack_refs, out_ref = refs[:4], refs[4:8], refs[8]
    head_rows = 2 * head_a.shape[1]
    feat_rows = head_rows + feat_refs[0].shape[0]

    @pl.when(pl.program_id(0) < tiles)
    def _():
        out = None
        for step in range(4):
            term = dot_dims(feat_refs[step][...], pack_refs[step][head_rows:feat_rows, :], 0, 0)
            out = term if out is None else out + term
        out_ref[...] = out

    @pl.when(pl.program_id(0) == tiles + 2)
    def _():
        out = None
        small = (pack_refs[0].shape[0] - feat_rows) // 2
        for step in range(4):
            high = pack_refs[step][feat_rows : feat_rows + small, :].astype(wide_type)
            term = high + pack_refs[step][feat_rows + small :, :].astype(wide_type)
            out = term if out is None else out + term
        high = out.astype(low_type).astype(wide_type)
        out_ref[:small, :] = high
        out_ref[small:, :] = out - high

    @pl.when((pl.program_id(0) >= tiles) & (pl.program_id(0) < tiles + 2))
    def _():
        out_ref[...] = clip_products(at_ref, head_a, head_b, pack_refs, slice(None))


def ring_sum_kernel(at_ref, part_ref, *refs):
    got_refs, out_ref = refs[:3], refs[3]
    block = out_ref.shape[0]
    out = part_ref[pl.ds(pl.multiple_of(at_ref[0] * block, 8), block), :]
    for got in got_refs:
        out = out + got[...].astype(wide_type)
    out_ref[...] = out


def ring_sum(ring_at, part, got, after):
    shape = (part.shape[0] // 4, part.shape[1])
    return call_kernel(
        ring_sum_kernel,
        (ring_at[None], part, *got),
        (0,),
        jax.ShapeDtypeStruct(shape, wide_type),
        [],
        4 * shape[0] * shape[1],
        0,
        after,
    )


def half_sum_kernel(own_ref, got_ref, out_ref):
    out_ref[...] = (own_ref[...] + got_ref[...]).astype(low_type)


def half_sum(own, after):
    got = lax.ppermute(own, "frame", HALF_SWAP)
    return call_kernel(
        half_sum_kernel,
        (own, got),
        (),
        jax.ShapeDtypeStruct(own.shape, low_type),
        [],
        own.size,
        0,
        after,
    )


def join_kernel(at_ref, *refs):
    out_ref = refs[4]
    block = refs[0].shape[0]
    for step in range(4):
        start = pl.multiple_of(ring_back(at_ref[0], step) * block, 16)
        out_ref[pl.ds(start, block), :] = refs[step][...]


def join_frames(ring_at, total, after, after_far=()):
    pieces = ring_pieces(total)
    return call_kernel(
        join_kernel,
        (ring_at[None], *pieces),
        (0,),
        jax.ShapeDtypeStruct((4 * total.shape[0], total.shape[1]), low_type),
        [],
        0,
        0,
        after,
        after_far,
    )


def beside_kernel(first_ref, second_ref, out_ref):
    half, wide, other = first_ref.shape[0] // 2, first_ref.shape[1], second_ref.shape[1]
    out_ref[:, :wide] = first_ref[:half, :]
    out_ref[:, wide : wide + other] = second_ref[:half, :]
    out_ref[:, wide + other :] = second_ref[half:, :]


def beside_whole_kernel(first_ref, second_ref, out_ref):
    half, wide, other = first_ref.shape[0] // 2, first_ref.shape[1], second_ref.shape[1]
    for at in range(2):
        rows = slice(at * half, (at + 1) * half)
        out_ref[:, at * wide : (at + 1) * wide] = first_ref[rows, :]
        start = 2 * wide + at * other
        out_ref[:, start : start + other] = second_ref[rows, :]


def gather_clips(first, second, after, whole=False):
    half, wide = first.shape[0] // 2, first.shape[1]
    beside = call_kernel(
        beside_whole_kernel if whole else beside_kernel,
        (first, second),
        (),
        jax.ShapeDtypeStruct(
            (half, (2 if whole else 1) * wide + 2 * second.shape[1]), low_type
        ),
        [],
        0,
        0,
        after,
    )
    return lax.all_gather(beside, "clip")


def take_kernel(whole_ref, out_ref):
    out_ref[...] = whole_ref[:, :, : out_ref.shape[2]]


def with_other_core(whole, wide, after):
    shape = (*whole.shape[:2], wide)
    columns = pl.pallas_call(
        without(take_kernel, 1, after),
        grid=(1,),
        out_shape=jax.ShapeDtypeStruct(shape, low_type),
        in_specs=[pl.BlockSpec(shape, lambda i: (0, 0, 0))] + any_specs(after),
        out_specs=pl.BlockSpec(shape, lambda i: (0, 0, 0)),
        compiler_params=kernel_params(),
    )(whole, *after)
    return whole, core_swap(columns)


def smem_spec():
    return pl.BlockSpec(memory_space=pltpu.SMEM)


def kernel_params():
    return pltpu.CompilerParams(vmem_limit_bytes=48 * 1024 * 1024)


def held_spec():
    return pl.BlockSpec(memory_space=pltpu.VMEM)


def any_specs(arrays):
    return [pl.BlockSpec(memory_space=pl.ANY)] * len(arrays)


def mark(value):
    while value.ndim > 2:
        value = value[0]
    return value[-8:, -128:]


def without(kernel, count, after):
    return lambda *refs: kernel(*refs[:count], *refs[count + len(after) :])


def layer_grad(clip_at, second_all, packs, first_all, after):
    whole, other = second_all
    half = whole.shape[1]
    wide = whole.shape[2] // 4 if other is None else other.shape[2]
    tiles = wide // 128
    part = 256
    block = (4, half, 128)
    starts = (2 * tiles, 3 * tiles, 0, tiles) if other is None else (tiles, 2 * tiles, 0, 0)
    other = whole if other is None else other
    heads = () if first_all is None else (first_all[0],) * 4
    held = [
        pl.BlockSpec(block, lambda i, at=at: (0, 0, tiles + at)) for at in range(len(heads))
    ]

    def moving(start):
        return pl.BlockSpec(block, lambda i: (0, 0, start + jnp.minimum(i, tiles - 1)))

    return pl.pallas_call(
        without(layer_grad_kernel, 9 + len(heads), after),
        grid=(tiles + (1 if heads else 0),),
        out_shape=jax.ShapeDtypeStruct((wide + (128 if heads else 0), 2 * part), wide_type),
        in_specs=[smem_spec()]
        + [moving(start) for start in starts]
        + held
        + [held_spec()] * 4
        + any_specs(after),
        out_specs=pl.BlockSpec((128, 2 * part), lambda i: (i, 0)),
        compiler_params=kernel_params(),
        cost_estimate=pl.CostEstimate(
            flops=32 * half * wide * part,
            bytes_accessed=2 * whole.size + 8 * wide * part,
            transcendentals=0,
        ),
    )(clip_at[None], whole, whole, whole, other, *heads, *packs, *after)


def plain_grad(clip_at, rows_all, packs, after):
    whole, other = rows_all
    half, count = other.shape[1:]
    part = packs[0].shape[1]
    block = pl.BlockSpec((4, half, 128), lambda i: (0, 0, i))
    return pl.pallas_call(
        without(plain_grad_kernel, 7, after),
        grid=(count // 128,),
        out_shape=jax.ShapeDtypeStruct((count, part), wide_type),
        in_specs=[smem_spec(), block, block] + [held_spec()] * 4 + any_specs(after),
        out_specs=pl.BlockSpec((128, part), lambda i: (i, 0)),
        compiler_params=kernel_params(),
        cost_estimate=pl.CostEstimate(
            flops=16 * half * count * part,
            bytes_accessed=16 * half * count + 4 * count * part,
            transcendentals=0,
        ),
    )(clip_at[None], whole, other, *packs, *after)


def last_grad(clip_at, first_all, feats, packs, after, after_far):
    whole, other = first_all
    half, part = other.shape[1], packs[0].shape[1]
    first_block = other.shape[2] // 128
    tiles = feats[0].shape[1] // 128
    kernel = functools.partial(last_grad_kernel, tiles)
    after_far = tuple(mark(value) for value in after_far)

    def moving(start):
        return pl.BlockSpec(
            (4, half, 128), lambda i: (0, 0, start + jnp.clip(i - tiles, 0, 1))
        )

    return pl.pallas_call(
        without(kernel, 11, (*after, *after_far)),
        grid=(tiles + 3,),
        out_shape=jax.ShapeDtypeStruct(((tiles + 3) * 128, part), wide_type),
        in_specs=[smem_spec(), moving(first_block), moving(first_block + 2)]
        + [pl.BlockSpec((feats[0].shape[0], 128), lambda i: (0, jnp.minimum(i, tiles - 1)))] * 4
        + [held_spec()] * 4
        + any_specs(after)
        + any_specs(after_far),
        out_specs=pl.BlockSpec((128, part), lambda i: (i, 0)),
        compiler_params=kernel_params(),
    )(clip_at[None], whole, whole, *feats, *packs, *after, *after_far)


def by_clip(clip_at, write):
    for place in range(4):

        @pl.when(clip_at == place)
        def _(place=place):
            for step in range(4):
                write((place - step) % 4, step)


def place_layer_kernel(tiles, at_ref, all_ref, *outs):
    part = all_ref.shape[2] // 2
    is_last = pl.program_id(0) == tiles

    for place in range(4):
        columns = slice(place * part, (place + 1) * part)
        left = all_ref[place, :, :part].astype(wide_type)
        right = all_ref[place, :, part:].astype(wide_type)

        @pl.when(jnp.logical_not(is_last))
        def _(columns=columns, left=left, right=right):
            outs[0][0, :, columns] = left
            outs[1][0, :, columns] = right

        if len(outs) > 2:

            @pl.when(is_last)
            def _(columns=columns, left=left, right=right):
                outs[2][0, : outs[2].shape[1] // 2, columns] = left
                outs[2][0, outs[2].shape[1] // 2 :, columns] = right


def place_layer(clip_at, layer, levels, joined, earlier, heads_layer, after):
    part = joined.shape[2] // 2
    rows = 4 * part
    tiles = rows // 128
    heads = joined.shape[1] > rows
    out = [(levels, rows, 4 * part)] * 2 + [(levels, 256, 4 * part)] * heads
    tall = pl.BlockSpec((1, 128, 4 * part), lambda i: (layer, jnp.minimum(i, tiles - 1), 0))
    wide = pl.BlockSpec((1, 256, 4 * part), lambda i: (heads_layer, 0, 0))
    return pl.pallas_call(
        without(functools.partial(place_layer_kernel, tiles), 2, (*earlier, *after)),
        grid=(tiles + (1 if heads else 0),),
        out_shape=tuple(jax.ShapeDtypeStruct(shape, wide_type) for shape in out),
        in_specs=[smem_spec(), pl.BlockSpec((4, 128, 2 * part), lambda i: (0, i, 0))]
        + any_specs(earlier)
        + any_specs(after),
        out_specs=(tall, tall) + ((wide,) if heads else ()),
        input_output_aliases={2 + at: at for at in range(len(earlier))},
        compiler_params=kernel_params(),
    )(clip_at[None], joined, *earlier, *after)


def place_last_kernel(skip, at_ref, *refs):
    pieces = refs[:4]
    in_ref, small_ref, proj_ref = refs[-3:]
    part = pieces[0].shape[1]
    heads = skip + proj_ref.shape[1]
    small = small_ref.shape[0]

    def write(place, step):
        columns = slice(place * part, (place + 1) * part)
        piece = pieces[step]
        in_ref[:, columns] = piece[: in_ref.shape[0], :].astype(wide_type)
        proj_ref[0, :, columns] = piece[skip:heads, :].astype(wide_type)
        small_ref[:, columns] = piece[heads : heads + small, :].astype(wide_type) + piece[
            heads + small :, :
        ].astype(wide_type)

    by_clip(at_ref[0], write)


def place_last(clip_at, feat_rows, skip, levels, pieces, earlier):
    part = pieces[0].shape[1]
    return pl.pallas_call(
        functools.partial(place_last_kernel, skip),
        grid=(1,),
        out_shape=(
            jax.ShapeDtypeStruct((feat_rows, 4 * part), wide_type),
            jax.ShapeDtypeStruct((64, 4 * part), wide_type),
            jax.ShapeDtypeStruct((levels, 256, 4 * part), wide_type),
        ),
        in_specs=[smem_spec()]
        + [pl.BlockSpec(pieces[0].shape, lambda i: (0, 0))] * 4
        + [pl.BlockSpec(memory_space=pl.ANY)],
        out_specs=(
            pl.BlockSpec((feat_rows, 4 * part), lambda i: (0, 0)),
            pl.BlockSpec((64, 4 * part), lambda i: (0, 0)),
            pl.BlockSpec((1, 256, 4 * part), lambda i: (0, 0, 0)),
        ),
        input_output_aliases={5: 2},
        compiler_params=kernel_params(),
    )(clip_at[None], *pieces, earlier)


def pack_kernel(by_rows, count, at_ref, *refs):
    parts, outs = refs[:count], refs[count:]
    for clip in range(4):

        @pl.when(at_ref[0] == clip)
        def _(clip=clip):
            for step in range(4):
                place, start = (clip + step) % 4, 0
                for part in parts:
                    size = part.shape[1] // 4
                    value = part[:, place * size : (place + 1) * size]
                    if by_rows:
                        outs[step][start : start + part.shape[0], :] = value
                        start += part.shape[0]
                    else:
                        outs[step][:, start : start + size] = value
                        start += size


def pack_parts(clip_at, parts, by_rows, after):
    sizes = [part.shape[1] // 4 for part in parts]
    if by_rows:
        shape = (sum(part.shape[0] for part in parts), sizes[0])
    else:
        shape = (parts[0].shape[0], sum(sizes))
    return call_kernel(
        functools.partial(pack_kernel, by_rows, len(parts)),
        (clip_at[None], *parts),
        (0,),
        tuple(jax.ShapeDtypeStruct(shape, low_type) for _ in range(4)),
        [],
        0,
        0,
        after,
    )


def place_heads_kernel(at_ref, all_ref, *refs):
    out_ref = refs[-1]
    for place in range(4):
        piece = all_ref[place].astype(wide_type)
        for at, part in ((1, 0), (2, 1), (0, 2)):
            out_ref[0, at, :, head_cols(place)] = piece[:, head_cols(part)]


def place_heads(clip_at, layer, levels, joined, earlier, after):
    rows = joined.shape[1]
    tile = 256
    count = 2
    return pl.pallas_call(
        without(place_heads_kernel, count, (*earlier, *after)),
        grid=(rows // tile,),
        out_shape=jax.ShapeDtypeStruct((levels, 3, rows, 4 * HEAD), wide_type),
        in_specs=[smem_spec(), pl.BlockSpec((4, tile, 3 * HEAD), lambda i: (0, i, 0))]
        + any_specs(earlier)
        + any_specs(after),
        out_specs=pl.BlockSpec((1, 3, tile, 4 * HEAD), lambda i: (layer, 0, i, 0)),
        input_output_aliases={count + at: at for at in range(len(earlier))},
        compiler_params=kernel_params(),
    )(clip_at[None], joined, *earlier, *after)


def stack_kernel(*refs):
    out_ref = refs[-1]
    for at, ref in enumerate(refs[:-1]):
        out_ref[8 * at : 8 * (at + 1), :] = ref[...]


def feature_grad_kernel(ids_ref, rows_ref, weight_ref, out_ref):
    size = rows_ref.shape[0] // 4
    for at in range(4):
        start = pl.multiple_of(ids_ref[at] * size, 8)
        out_ref[pl.ds(start, size), :] = dot_dims(
            rows_ref[at * size : (at + 1) * size, :], weight_ref[...], 1, 1
        )


def last_pack_kernel(at_ref, head_ref, patch_ref, small_a, small_b, *outs):
    heads, patches, small = head_ref.shape[0], patch_ref.shape[0], small_a.shape[0]
    values = small_a[...] + small_b[...]
    high = values.astype(low_type)
    rest = (values - high.astype(wide_type)).astype(low_type)
    for clip in range(4):

        @pl.when(at_ref[0] == clip)
        def _(clip=clip):
            for step in range(4):
                size = outs[step].shape[1]
                place = (clip + step) % 4
                columns = slice(place * size, (place + 1) * size)
                outs[step][:heads, :] = head_ref[:, columns]
                outs[step][heads : heads + patches, :] = patch_ref[:, columns]
                outs[step][heads + patches : heads + patches + small, :] = high[:, columns]
                outs[step][heads + patches + small :, :] = rest[:, columns]


def call_kernel(kernel, args, in_smem, outs, scratch, flops, exps, after=(), after_far=(), piped=()):
    count = len(args)

    def spec(at):
        if at in piped:
            return pl.BlockSpec(args[at].shape, lambda i, rank=args[at].ndim: (0,) * rank)
        return pl.BlockSpec(memory_space=pltpu.SMEM if at in in_smem else pltpu.VMEM)

    specs = [spec(at) for at in range(count)]
    after = (*after, *(mark(value) for value in after_far))
    specs += any_specs(after)
    moved = sum(a.size * a.dtype.itemsize for a in args)
    return pl.pallas_call(
        without(kernel, count, after),
        grid=(1,),
        out_shape=outs,
        in_specs=specs,
        out_specs=jax.tree.map(lambda _: pl.BlockSpec(memory_space=pltpu.VMEM), outs),
        scratch_shapes=scratch,
        compiler_params=kernel_params(),
        cost_estimate=pl.CostEstimate(flops=flops, bytes_accessed=moved, transcendentals=exps),
    )(*args, *after)


def on_device(
    features,
    cond_values,
    cond_live,
    in_weight,
    in_bias,
    act_weight,
    act_bias,
    state_weight,
    state_bias,
    attn_gain,
    attn_shift,
    qkv_weight,
    qkv_bias,
    proj_weight,
    proj_bias,
    mlp_gain,
    mlp_shift,
    up_weight,
    up_bias,
    down_weight,
    down_bias,
    out_grad,
):
    patch_rows = features.shape[2]
    feat_width = features.shape[3]
    slot_count = cond_values.shape[2]
    all_frames = cond_live.shape[1]
    model_width = in_weight.shape[1]
    width = qkv_weight.shape[3]
    heads = width // HEAD
    level_count = attn_gain.shape[0]
    patches = patch_rows // 4
    chunk_rows = patches + EXTRA
    rows = 4 * chunk_rows
    hidden_width = up_weight.shape[2]

    tensor_at = lax.axis_index("tensor")
    chip_at, core_at = tensor_at // 2, tensor_at % 2
    frame_at = lax.axis_index("frame")
    half_at, ring_at = frame_at // 4, frame_at % 4
    clip_at = lax.axis_index("clip")

    chunk_ids = [
        2 * jnp.bitwise_xor(core_at, core_step) + jnp.bitwise_xor(chip_at, chip_step)
        for core_step in range(2)
        for chip_step in range(2)
    ]
    own_chunk = chunk_ids[0]
    own_frames = jnp.stack([4 * half_at + (ring_at - step) % 4 for step in range(4)])
    cross_frames = jnp.stack([4 * (1 - half_at) + (ring_at - step) % 4 for step in range(4)])

    within = lax.broadcasted_iota(jnp.int32, (chunk_rows, 1), 0)
    is_patch = within < patches
    heights, columns = [], []
    for chunk_id in chunk_ids:
        patch_id = chunk_id * patches + within
        heights.append(jnp.where(is_patch, patch_id // GRID_W, 0))
        columns.append(jnp.where(is_patch, patch_id % GRID_W, 0))
    heights = jnp.concatenate(heights, axis=0).astype(wide_type)
    columns = jnp.concatenate(columns, axis=0).astype(wide_type)
    swap_table, rate_table = rotary_tables(HEAD, heads)
    swap_heads = jnp.asarray(swap_table)
    swap_one = jnp.asarray(swap_table[:HEAD, :HEAD])
    rates = rate_table[:, :HEAD]
    place_angles = heights * rates[1] + columns * rates[2]
    angles = jnp.concatenate(
        [
            own_frames[step].astype(wide_type) * rates[0][None, :] + place_angles
            for step in range(4)
        ],
        axis=0,
    )
    cosine_four, sine_four = jnp.cos(angles), jnp.sin(angles)
    head_from = jnp.arange(width)
    head_to = ((head_from // HEAD + ring_at) % 4) * HEAD + head_from % HEAD
    head_place = (head_to[:, None] == head_from[None, :]).astype(low_type)
    proj_turned = [
        lax.dynamic_slice_in_dim(
            jnp.concatenate([proj_weight[layer], proj_weight[layer]], axis=0),
            ring_at * HEAD,
            width,
            0,
        )
        for layer in range(level_count)
    ]
    ring_scalar = ring_at.astype(jnp.int32)
    clip_scalar = clip_at.astype(jnp.int32)

    live_all = cond_live[0].astype(wide_type)
    own_slots = lax.dynamic_index_in_dim(live_all, frame_at, 0, False)

    def live_rows(slots, chunk_id):
        picked = jnp.where(
            chunk_id < slot_count,
            lax.dynamic_index_in_dim(slots, jnp.minimum(chunk_id, slot_count - 1), 1, False),
            0.0,
        )
        return jnp.where(is_patch, 1.0, jnp.where(within == patches, picked[None, :], 0.0))

    sources = jnp.concatenate([own_frames, cross_frames])
    source_live = jnp.take(live_all, sources, axis=0)
    key_live = jnp.concatenate([live_rows(source_live, c) for c in chunk_ids], axis=0)
    reached = jnp.concatenate([jnp.ones((4,), jnp.bool_), jnp.full((4,), half_at == 1)])
    key_bias = jnp.where((key_live > 0.5) & reached[None, :], 0.0, masked_score).astype(wide_type)
    seen = own_frames[:, None] <= own_frames[None, :]
    causal = jnp.where(seen, 0.0, masked_score).astype(wide_type)
    causal = jnp.pad(jnp.repeat(causal, rows, axis=1), ((0, 4), (0, 0)))
    own_live = live_rows(own_slots[None, :], own_chunk)

    def extra_rows(slot_rows):
        picked = lax.dynamic_slice_in_dim(
            slot_rows, jnp.minimum(own_chunk, slot_count - 1), 1, 0
        )
        picked = jnp.where(own_chunk < slot_count, picked, jnp.zeros_like(picked))
        return jnp.pad(picked, ((0, EXTRA - 1), (0, 0)))

    cond_here = cond_values[0, 0]
    act_rows = jnp.dot(cond_here, act_weight, precision=highest_precision) + act_bias
    state_rows = jnp.dot(cond_here, state_weight, precision=highest_precision) + state_bias
    even_slot = (jnp.arange(slot_count) % 2 == 0)[:, None]
    cond_x = jnp.where(even_slot, act_rows, state_rows) * own_slots[:, None]

    flat_feat = jnp.concatenate(
        [
            lax.dynamic_slice_in_dim(features[0, 0], c * patches, patches, 0)
            for c in chunk_ids
        ],
        axis=0,
    )
    kept, got = halves_tensor(dot_wide(flat_feat, in_weight))
    stream = jnp.concatenate([kept + got + in_bias, extra_rows(cond_x)], axis=0)

    feat_wide = -(-feat_width // 128) * 128
    feat_low = jnp.pad(flat_feat, ((0, 0), (0, feat_wide - feat_width)))
    feats = [feat_low] + [
        lax.ppermute(feat_low, "clip", clip_shift(step)) for step in range(1, 4)
    ]
    pair_work = 2 * 32 * rows * rows * HEAD
    pair_exps = 32 * rows * rows
    weight_parts = [
        [qkv_weight[layer, :, at] for at in (1, 2, 0)] for layer in range(level_count)
    ]

    def norm(terms, gain, shift, after_far=()):
        chunk = jax.ShapeDtypeStruct((chunk_rows, model_width), wide_type)
        return call_kernel(
            norm_kernel,
            (gain[None], shift[None], *terms),
            (),
            (
                chunk,
                chunk,
                jax.ShapeDtypeStruct((chunk_rows, 128), wide_type),
                jax.ShapeDtypeStruct((chunk_rows, model_width), low_type),
            ),
            [],
            12 * chunk_rows * model_width,
            0,
            (),
            after_far,
        )

    def norm_back(part, gain, hat, inverse, grad, count, after=(), after_far=()):
        kept, got = halves_tensor(part)
        return call_kernel(
            functools.partial(norm_back_kernel, count),
            (kept, got, gain[None], hat, inverse, grad),
            (),
            (
                jax.ShapeDtypeStruct((chunk_rows, model_width), wide_type),
                jax.ShapeDtypeStruct((chunk_rows, model_width), low_type),
                jax.ShapeDtypeStruct((8, model_width), wide_type),
            ),
            [],
            16 * chunk_rows * model_width,
            0,
            after,
            after_far,
            (2, 3, 4, 5),
        )

    slot_grads = out_grad[0, 0, patch_rows:] * own_slots[:, None].astype(low_type)
    slot_blocks = jnp.concatenate(
        [
            jnp.pad(slot_grads[:, None], ((0, 0), (0, EXTRA - 1), (0, 0))),
            jnp.zeros((4 - slot_count, EXTRA, model_width), low_type),
        ],
        axis=0,
    )
    branch_parts = []
    for chunk_id in chunk_ids:
        branch_parts.append(
            lax.dynamic_slice_in_dim(out_grad[0, 0], chunk_id * patches, patches, 0)
        )
        branch_parts.append(lax.dynamic_index_in_dim(slot_blocks, chunk_id, 0, False))
    first_branch = jnp.concatenate(branch_parts, axis=0)
    stored = []
    terms = (stream,)
    before = None
    for layer in range(level_count):
        stream, hat_one, inverse_one, first_chunk = norm(terms, attn_gain[layer], attn_shift[layer])
        first_in = join_rows_tensor(first_chunk)
        bias = jnp.pad(qkv_bias[layer], ((0, 5), (0, 0)))
        heads_out = call_kernel(
            functools.partial(project_kernel, heads),
            (
                ring_scalar[None],
                first_in,
                *weight_parts[layer],
                bias,
                cosine_four,
                sine_four,
                swap_heads,
            ),
            (0,),
            tuple(
                jax.ShapeDtypeStruct((rows, count * HEAD), low_type)
                for count in (3, 3, 3, 3, 2, 2, 2, 2)
            ),
            [],
            6 * rows * model_width * width,
            0,
            (),
            () if before is None else (before[0],),
            (2, 3, 4, 5, 6, 7, 8),
        )
        blocks = to_heads(heads_out[:4])
        cross = pairs_to_later_half(heads_out[4:])
        attn_wide, attn_turned, log_total, own_all, cross_all = call_kernel(
            attend_kernel,
            (key_bias, causal, *blocks, *cross),
            (),
            (
                jax.ShapeDtypeStruct((4 * rows, HEAD), wide_type),
                jax.ShapeDtypeStruct((4 * rows, HEAD), low_type),
                jax.ShapeDtypeStruct((8, 4 * rows), wide_type),
                jax.ShapeDtypeStruct((4 * rows, 3 * HEAD), low_type),
                jax.ShapeDtypeStruct((4 * rows, 2 * HEAD), low_type),
            ),
            [
                pltpu.VMEM((4 * rows, HEAD), low_type),
                pltpu.VMEM((8 * rows, lane_tiles(4 * rows)[0].stop), wide_type),
            ],
            2 * pair_work,
            pair_exps,
            tuple(feats[1:]) if layer == 0 else (),
        )
        attn_relative = jnp.concatenate(
            to_frames([attn_turned[at * rows : (at + 1) * rows] for at in range(4)]), axis=1
        )
        attn_low = dot_wide(attn_relative, head_place).astype(low_type)
        if layer < level_count - 1:
            first_all = gather_clips(first_in, attn_low, ())
        kept, got = halves_tensor(dot_wide(attn_relative, proj_turned[layer]))
        middle, hat_two, inverse_two, second_chunk = norm(
            (stream, kept, got, proj_bias[layer][None]), mlp_gain[layer], mlp_shift[layer],
            () if before is None else (before[1], first_branch),
        )
        second_in = join_rows_tensor(second_chunk)
        hidden = dot_wide(second_in, up_weight[layer]) + up_bias[layer]
        active_low = exact_gelu(hidden).astype(low_type)
        second_all = gather_clips(second_in, active_low, (), layer == level_count - 1)
        if layer == level_count - 1:
            first_all = (first_in, attn_low)
        before = (first_all, second_all)
        kept, got = halves_tensor(dot_wide(active_low, down_weight[layer]))
        terms = (middle, kept, got, down_bias[layer][None])
        stored.append(
            (
                hat_one,
                inverse_one,
                own_all,
                cross_all,
                log_total,
                attn_wide,
                hat_two,
                inverse_two,
                hidden,
                first_all,
                second_all,
            )
        )
    def in_order(full, count):
        out = jnp.zeros((4 * count,) + full.shape[1:], full.dtype)
        size = full.shape[0] // 4
        for at, chunk_id in enumerate(chunk_ids):
            out = lax.dynamic_update_slice_in_dim(
                out, full[at * size : at * size + count], chunk_id * count, 0
            )
        return out

    def block_rows(after):
        low = call_kernel(
            block_kernel,
            (*terms, jnp.broadcast_to(own_live, (chunk_rows, 128))),
            (),
            jax.ShapeDtypeStruct((chunk_rows, model_width), low_type),
            [],
            4 * chunk_rows * model_width,
            0,
            after,
        )
        return join_rows_tensor(low)

    def block_in_order(block_full):
        slot_full = jnp.concatenate(
            [
                block_full[at * chunk_rows + patches : at * chunk_rows + patches + 1]
                for at in range(4)
            ],
            axis=0,
        )
        return jnp.concatenate(
            [in_order(block_full, patches), in_order(slot_full, 1)[:slot_count]], axis=0
        )[None, None]

    own_out = lax.dynamic_slice_in_dim(out_grad[0, 0], own_chunk * patches, patches, 0)
    grad_stream = (
        jnp.concatenate(
            [
                own_out.astype(wide_type),
                extra_rows(out_grad[0, 0, patch_rows:].astype(wide_type)),
            ],
            axis=0,
        )
        * own_live
    )

    small = {}
    small["down", level_count - 1] = jnp.sum(grad_stream, axis=0)
    sums_list = []
    wide_part = model_width // 4
    later = None
    for layer in reversed(range(level_count)):
        (
            hat_one,
            inverse_one,
            own_all,
            cross_all,
            log_total,
            attn_wide,
            hat_two,
            inverse_two,
            hidden,
            first_all,
            second_all,
        ) = stored[layer]
        branch = first_branch if later is None else join_rows_tensor(branch_chunk)
        if later is not None:
            first_all = with_other_core(first_all, model_width, (branch,))
            second_all = with_other_core(second_all, model_width, (branch,))
        _, gelu_pull = jax.vjp(exact_gelu, hidden)
        grad_hidden = gelu_pull(dot_dims(branch, down_weight[layer], 1, 1))[0].astype(low_type)
        small["up", layer] = jnp.sum(grad_hidden.astype(wide_type), axis=0)
        parts = [branch, grad_hidden] + ([] if later is None else [later["proj_out"]])
        packs = pack_parts(clip_scalar, parts, False, ())
        grad_middle, proj_chunk, sums = norm_back(
            dot_dims(grad_hidden, up_weight[layer], 1, 1),
            mlp_gain[layer],
            hat_two,
            inverse_two,
            grad_stream,
            chunk_rows,
            (packs[0],) if later is None else (packs[0], later["tall_join"]),
            () if later is None else (later["heads_sum"],),
        )
        sums_list.append(sums)
        packs = swap_clips(packs)
        if later is None:
            second_all = (second_all, None)
            block_full = block_rows((proj_chunk,))
            block_out = block_in_order(block_full)
        proj_out = join_rows_tensor(proj_chunk)
        grad_attn = dot_dims(proj_out, proj_turned[layer], 1, 1).astype(low_type)
        grads = to_heads([grad_attn[:, head_cols(at)] for at in range(4)])

        if later is not None:
            later["heads_ring"] = ring_sum(
                ring_scalar, later["heads_sum"], later["heads_got"], (proj_chunk,)
            )

            later["tall_all"] = lax.all_gather(later["tall_join"], "clip")

        def attend_back(own, after, after_far=()):
            return call_kernel(
                functools.partial(attend_back_kernel, own),
                (key_bias, causal, log_total, attn_wide, own_all, *grads)
                + (() if own else (cross_all,)),
                (),
                (
                    jax.ShapeDtypeStruct((4 * rows, 2 * HEAD), wide_type),
                    jax.ShapeDtypeStruct((4 * rows, HEAD), wide_type),
                ),
                [
                    pltpu.VMEM((4 * rows, HEAD), low_type),
                    pltpu.VMEM((4 * rows, HEAD), low_type),
                ],
                5 * pair_work // 2,
                pair_exps // 2,
                after,
                after_far,
                tuple(range(9 if own else 10)),
            )

        cross_pair, cross_query = attend_back(
            False, () if later is None else (later["heads_ring"],)
        )
        got_pair = lax.ppermute(cross_pair, "frame", DOWN_HALF)
        if later is None:
            first_all = with_other_core(
                gather_clips(*first_all, (cross_pair,)), model_width, (cross_pair,)
            )
        tall_sum = layer_grad(
            clip_scalar,
            second_all,
            packs,
            None if later is None else later["first_all"],
            (cross_pair,),
        )
        own_pair, own_query = attend_back(
            True, (), (tall_sum,) if later is None else (tall_sum, later["tall_all"], block_full)
        )
        tall_got = ring_sends(tall_sum, ring_at)
        if later is not None:
            later["heads_total"] = half_sum(later["heads_ring"], (own_pair,))
        tall_ring = ring_sum(ring_scalar, tall_sum, tall_got, (own_pair,))
        tall_total = half_sum(tall_ring, ())
        turned = call_kernel(
            turn_back_kernel,
            (own_pair, got_pair, own_query, cross_query, cosine_four, sine_four, swap_one),
            (),
            tuple(jax.ShapeDtypeStruct((rows, 3 * HEAD), low_type) for _ in range(4)),
            [],
            24 * rows * HEAD * HEAD,
            0,
            (tall_ring,) if later is None else (tall_ring, later["heads_total"]),
            (),
            (4, 5, 6),
        )
        mixed = to_frames(list(turned))
        if later is not None:
            later["heads_join"] = join_frames(ring_scalar, later["heads_total"], (turned[0],))
        normed_part, mixed_stack, bias_sums = call_kernel(
            mix_back_kernel,
            (
                jnp.stack([ring_scalar, clip_scalar]),
                head_place,
                *weight_parts[layer],
                *mixed,
            ),
            (0,),
            (
                jax.ShapeDtypeStruct((rows, model_width), wide_type),
                jax.ShapeDtypeStruct((4, rows, 3 * HEAD), low_type),
                jax.ShapeDtypeStruct((8, width), wide_type),
            ),
            [],
            6 * rows * model_width * width,
            0,
            (tall_total,) if later is None else (tall_total, later["heads_join"]),
            (),
            (1, 2, 3, 4),
        )
        small["qkv", layer] = jnp.concatenate([bias_sums[2:3], bias_sums[:2]], axis=0)
        packs = swap_clips([mixed_stack[step] for step in range(4)])
        grad_stream, branch_chunk, sums = norm_back(
            normed_part,
            attn_gain[layer],
            hat_one,
            inverse_one,
            grad_middle,
            patches if layer == 0 else chunk_rows,
        )
        sums_list.append(sums)
        tall_join = join_frames(ring_scalar, tall_total, (branch_chunk,))

        heads_sum = plain_grad(clip_scalar, first_all, packs, (branch_chunk,))
        heads_got = ring_sends(heads_sum, ring_at)
        if layer > 0:
            later = {
                "proj_out": proj_out,
                "first_all": first_all,
                "tall_join": tall_join,
                "heads_sum": heads_sum,
                "heads_got": heads_got,
            }

    patch_chunk = branch_chunk[:patches]
    grad_patch = join_rows_tensor(patch_chunk)
    grad_features = call_kernel(
        feature_grad_kernel,
        (jnp.stack(chunk_ids).astype(jnp.int32), grad_patch, in_weight),
        (0,),
        jax.ShapeDtypeStruct((patch_rows, feat_width), wide_type),
        [],
        2 * patch_rows * feat_width * model_width,
        0,
        piped=(2,),
    )
    slot_row = grad_stream[patches : patches + 1] * own_live[patches : patches + 1]
    own_cond = lax.dynamic_slice_in_dim(
        cond_here, jnp.minimum(own_chunk, slot_count - 1), 1, 0
    )
    slot_part = jnp.concatenate([own_cond.T * slot_row, slot_row], axis=0)
    here = own_chunk < slot_count
    is_act = here & (own_chunk % 2 == 0)
    is_state = here & (own_chunk % 2 == 1)
    act_part = jnp.where(is_act, slot_part, 0.0)
    state_part = jnp.where(is_state, slot_part, 0.0)

    def at_tensor(value, total):
        return lax.dynamic_update_slice(
            jnp.zeros((value.shape[0], total), wide_type),
            value,
            (0, tensor_at * value.shape[1]),
        )

    layers = range(level_count)
    qkv_rows = at_tensor(
        jnp.concatenate([small["qkv", layer] for layer in layers], axis=0), 4 * width
    )
    mixed_rows = jnp.concatenate(
        [qkv_rows, small["down", level_count - 1][None], jnp.zeros_like(qkv_rows[:1])], axis=0
    )
    ups = at_tensor(jnp.stack([small["up", layer] for layer in layers]), 4 * hidden_width)
    parts = [*sums_list, act_part, state_part, mixed_rows, ups.reshape(-1, model_width)]
    vector = call_kernel(
        stack_kernel,
        tuple(parts),
        (),
        jax.ShapeDtypeStruct((8 * len(parts), model_width), wide_type),
        [],
        0,
        0,
    )
    vector = vector + core_swap(vector)
    later["heads_all"] = lax.all_gather(later["heads_join"], "clip")
    head_rows, patch_count, small_rows = proj_out.shape[0], grad_patch.shape[0], vector.shape[0]
    packs = call_kernel(
        last_pack_kernel,
        (clip_scalar[None], proj_out, grad_patch, vector, chip_swap(vector)),
        (0,),
        tuple(
            jax.ShapeDtypeStruct((head_rows + patch_count + 2 * small_rows, wide_part), low_type)
            for _ in range(4)
        ),
        [],
        0,
        0,
        (),
        (heads_sum,),
    )
    tall_all = lax.all_gather(tall_join, "clip")
    placed = place_layer(
        clip_scalar, level_count - 1, level_count, later["tall_all"], (), 0, (packs[0],)
    )
    packs = swap_clips(packs)
    heads_ring = ring_sum(ring_scalar, heads_sum, heads_got, tuple(packs[1:]))
    last_sum = last_grad(
        clip_scalar, first_all, feats, packs, (heads_ring,), (placed[0], grad_features)
    )
    last_ring = ring_sum(ring_scalar, last_sum, ring_sends(last_sum, ring_at), ())
    heads_total = half_sum(heads_ring, (mark(last_sum),))
    heads_join = join_frames(ring_scalar, heads_total, (last_ring,))
    heads_all = lax.all_gather(heads_join, "clip")
    heads_placed = place_heads(
        clip_scalar, level_count - 1, level_count, later["heads_all"], (), (packs[0],)
    )
    last_join = join_frames(
        ring_scalar, half_sum(last_ring, ()), (), (tall_all, heads_placed)
    )
    last_pieces = clip_pieces(last_join)
    grad_down, grad_up, grad_proj = place_layer(
        clip_scalar, 0, level_count, tall_all, placed, level_count - 1, ()
    )
    grad_in, vector, grad_proj = place_last(
        clip_scalar, feat_width, feat_wide, level_count, last_pieces, grad_proj
    )
    grad_heads = (place_heads(clip_scalar, 0, level_count, heads_all, (heads_placed,), ()),)


    def norm_sums(layer, first, row):
        return vector[8 * (2 * (level_count - 1 - layer) + first) + row]

    grad_mlp_gain = jnp.stack([norm_sums(layer, 0, 0) for layer in layers])
    grad_mlp_shift = jnp.stack([norm_sums(layer, 0, 1) for layer in layers])
    grad_proj_bias = jnp.stack([norm_sums(layer, 0, 2) for layer in layers])
    grad_attn_gain = jnp.stack([norm_sums(layer, 1, 0) for layer in layers])
    grad_attn_shift = jnp.stack([norm_sums(layer, 1, 1) for layer in layers])
    rest = vector[16 * level_count :]
    grad_down_bias = jnp.stack(
        [norm_sums(layer + 1, 1, 2) for layer in range(level_count - 1)]
        + [rest[16 + 3 * level_count]]
    )
    grad_qkv_bias = lax.dynamic_slice_in_dim(
        rest[16 : 16 + 3 * level_count], tensor_at * width, width, 1
    )
    grad_qkv_bias = grad_qkv_bias.reshape(level_count, 3, width)
    grad_up_bias = lax.dynamic_slice_in_dim(
        rest[24:].reshape(level_count, 4 * hidden_width), tensor_at * hidden_width, hidden_width, 1
    )
    act_count = cond_here.shape[1]
    return (
        block_out,
        grad_features[None, None],
        grad_in,
        norm_sums(0, 1, 2),
        rest[:act_count],
        rest[act_count],
        rest[8 : 8 + act_count],
        rest[8 + act_count],
        grad_attn_gain,
        grad_attn_shift,
        jnp.swapaxes(grad_heads[0], 1, 2),
        grad_qkv_bias,
        grad_proj,
        grad_proj_bias,
        grad_mlp_gain,
        grad_mlp_shift,
        grad_up,
        grad_up_bias,
        grad_down,
        grad_down_bias,
    )


def solution(mesh):
    return jax.shard_map(
        on_device,
        mesh=mesh,
        in_specs=(
            P("clip", "frame", None, "tensor"),
            P("clip", "frame", None, None),
            P("clip", None, None),
            P("tensor", None),
            P(),
            P(),
            P(),
            P(),
            P(),
            P(),
            P(),
            P(None, None, None, "tensor"),
            P(None, None, "tensor"),
            P(None, "tensor", None),
            P(),
            P(),
            P(),
            P(None, None, "tensor"),
            P(None, "tensor"),
            P(None, "tensor", None),
            P(),
            P("clip", "frame", None, None),
        ),
        out_specs=(
            P("clip", "frame", None, None),
            P("clip", "frame", None, "tensor"),
            P("tensor", None),
            P(),
            P(),
            P(),
            P(),
            P(),
            P(),
            P(),
            P(None, None, None, "tensor"),
            P(None, None, "tensor"),
            P(None, "tensor", None),
            P(),
            P(),
            P(),
            P(None, None, "tensor"),
            P(None, "tensor"),
            P(None, "tensor", None),
            P(),
        ),
        check_vma=False,
    )
```

```python
import functools

import jax
import jax.numpy as jnp
import numpy as np
from jax import lax
from jax.experimental import pallas as pl
from jax.experimental.pallas import tpu as pltpu
from jax.sharding import PartitionSpec as P

HEAD = 64
GRID_W = 16
EXTRA = 8

highest_precision = lax.Precision.HIGHEST
norm_epsilon = 1e-06
masked_score = -1000000000.0
low_type = jnp.bfloat16
wide_type = jnp.float32

CORE_SWAP = [(0, 1), (1, 0), (2, 3), (3, 2)]
CHIP_SWAP = [(0, 2), (2, 0), (1, 3), (3, 1)]
HALF_SWAP = [(i, (i + 4) % 8) for i in range(8)]


def clip_shift(step):
    return [(i, (i + step) % 4) for i in range(4)]


def frame_shift(halves, step):
    return [
        (4 * half + i, 4 * ((half + halves) % 2) + (i + step) % 4)
        for half in range(2)
        for i in range(4)
    ]


def core_swap(value):
    return lax.ppermute(value, "tensor", CORE_SWAP)


def chip_swap(value):
    return lax.ppermute(value, "tensor", CHIP_SWAP)


def halves_tensor(part):
    half = part.shape[0] // 2
    pair = part[:half] + core_swap(part[half:])
    quarter = half // 2
    return pair[:quarter], chip_swap(pair[quarter:])


def join_rows_tensor(chunk):
    pair = jnp.concatenate([chunk, chip_swap(chunk)], axis=0)
    return jnp.concatenate([pair, core_swap(pair)], axis=0)


def to_heads(blocks):
    return [blocks[0]] + [
        lax.ppermute(blocks[step], "frame", frame_shift(0, step)) for step in range(1, 4)
    ]


def to_frames(blocks):
    return [blocks[0]] + [
        lax.ppermute(blocks[step], "frame", frame_shift(0, -step)) for step in range(1, 4)
    ]


def pairs_to_later_half(blocks):
    return [
        lax.ppermute(
            blocks[step],
            "frame",
            [(src, dst) for src, dst in frame_shift(1, step) if src < dst],
        )
        for step in range(4)
    ]


DOWN_HALF = [(i + 4, i) for i in range(4)]


def swap_clips(packs):
    return [packs[0]] + [
        lax.ppermute(packs[step], "clip", clip_shift(step)) for step in range(1, 4)
    ]


def ring_pieces(value):
    return [value] + [
        lax.ppermute(value, "frame", frame_shift(0, step)) for step in range(1, 4)
    ]


def ring_sends(part, ring):
    block = part.shape[0] // 4
    got = []
    for step in range(1, 4):
        sent = lax.dynamic_slice_in_dim(part, ((ring + step) % 4) * block, block, 0)
        got.append(lax.ppermute(sent.astype(low_type), "frame", frame_shift(0, step)))
    return got


def clip_pieces(joined):
    return [joined] + [
        lax.ppermute(joined, "clip", clip_shift(step)) for step in range(1, 4)
    ]


def rotary_tables(head_size, head_count):
    group_size = 2 * (head_size // 3 // 2)
    half_size = group_size // 2
    total_width = head_size * head_count
    swap_table = np.zeros((total_width, total_width), np.float32)
    rate_table = np.zeros((3, total_width), np.float32)
    for head_at in range(head_count):
        for axis_at in range(3):
            for pair_at in range(half_size):
                lower_at = head_at * head_size + axis_at * group_size + pair_at
                upper_at = lower_at + half_size
                swap_table[upper_at, lower_at] = -1.0
                swap_table[lower_at, upper_at] = 1.0
                rate_value = 10000.0 ** (-2.0 * pair_at / group_size)
                rate_table[axis_at, lower_at] = rate_value
                rate_table[axis_at, upper_at] = rate_value
    return swap_table, rate_table


def norm_rows(values):
    row_mean = jnp.mean(values, axis=-1, keepdims=True)
    centred = values - row_mean
    spread = jnp.mean(centred * centred, axis=-1, keepdims=True)
    inverse = lax.rsqrt(spread + norm_epsilon)
    return centred * inverse, inverse


def norm_kernel(gain_ref, shift_ref, *refs):
    terms, (stream_ref, hat_ref, inverse_ref, low_ref) = refs[:-4], refs[-4:]
    values = terms[0][...]
    if len(terms) > 1:
        values = values + (terms[1][...] + terms[2][...] + terms[3][...])
    hat, inverse = norm_rows(values)
    stream_ref[...] = values
    hat_ref[...] = hat
    inverse_ref[...] = jnp.broadcast_to(inverse, inverse_ref.shape)
    low_ref[...] = (hat * gain_ref[...] + shift_ref[...]).astype(low_type)


def block_kernel(stream_ref, kept_ref, got_ref, bias_ref, live_ref, out_ref):
    values = stream_ref[...] + (kept_ref[...] + got_ref[...] + bias_ref[...])
    out_ref[...] = (values * live_ref[:, 0:1]).astype(low_type)


def norm_back_kernel(count, kept_ref, got_ref, gain_ref, hat_ref, inverse_ref, grad_ref, out_ref, low_ref, sums_ref):
    grad = kept_ref[...] + got_ref[...]
    hat = hat_ref[...]
    scaled = grad * gain_ref[...]
    first = jnp.mean(scaled, axis=-1, keepdims=True)
    second = jnp.mean(scaled * hat, axis=-1, keepdims=True)
    out = grad_ref[...] + (scaled - first - hat * second) * inverse_ref[:, 0:1]
    low = out.astype(low_type)
    out_ref[...] = out
    low_ref[...] = low
    sums_ref[...] = jnp.zeros_like(sums_ref)
    sums_ref[0:1, :] = jnp.sum(grad * hat, axis=0, keepdims=True)
    sums_ref[1:2, :] = jnp.sum(grad, axis=0, keepdims=True)
    sums_ref[2:3, :] = jnp.sum(low[:count].astype(wide_type), axis=0, keepdims=True)


def exact_gelu(values):
    return jax.nn.gelu(values, approximate=False)


def dot_wide(left, right):
    return jnp.dot(left, right, preferred_element_type=wide_type)


def dot_dims(left, right, left_dim, right_dim):
    return lax.dot_general(
        left, right, (((left_dim,), (right_dim,)), ((), ())), preferred_element_type=wide_type
    )


def head_cols(at):
    return slice(at * HEAD, (at + 1) * HEAD)


def ring_back(place, step):
    return lax.rem(place - step + 4, 4)


def ring_ahead(place, step):
    return lax.rem(place + step, 4)


def project_kernel(heads, at_ref, rows_ref, key_w, value_w, query_w, bias_ref, cos_ref, sin_ref, swap_ref, *out_refs):
    rows = rows_ref[...]
    swap = swap_ref[...]
    cosine = jnp.concatenate([cos_ref[: rows.shape[0], :]] * heads, axis=1)
    sine = jnp.concatenate([sin_ref[: rows.shape[0], :]] * heads, axis=1)

    def turned(weight, bias):
        value = dot_wide(rows, weight[...]) + bias
        crossed = jnp.dot(value, swap, precision=highest_precision, preferred_element_type=wide_type)
        return value * cosine + crossed * sine

    key = turned(key_w, bias_ref[1:2, :]).astype(low_type)
    value = (dot_wide(rows, value_w[...]) + bias_ref[2:3, :]).astype(low_type)
    query = (turned(query_w, bias_ref[0:1, :]).astype(low_type).astype(wide_type) * HEAD ** (-0.5)).astype(low_type)

    def write(head, step):
        for at, part in enumerate((key, value, query)):
            out_refs[step][:, head_cols(at)] = part[:, head_cols(head)]
            if at < 2:
                out_refs[4 + step][:, head_cols(at)] = part[:, head_cols(head)]

    for ring in range(4):

        @pl.when(at_ref[0] == ring)
        def _(ring=ring):
            for step in range(4):
                write((ring + step) % 4, step)


def lane_tiles(total):
    size = 384 if total % 384 == 0 else total
    return [slice(at * size, (at + 1) * size) for at in range(total // size)]


def attend_kernel(bias_ref, mask_ref, *refs):
    own_refs, cross_refs = refs[:4], refs[4:8]
    out_ref, low_ref, total_ref, own_out, cross_out, query_ref, score_ref = refs[8:]
    rows = own_refs[0].shape[0]
    total_rows = 4 * rows
    for at in range(4):
        block = slice(at * rows, (at + 1) * rows)
        query_ref[block, :] = own_refs[at][:, head_cols(2)]
        own_out[block, :] = own_refs[at][...]
        cross_out[block, :] = cross_refs[at][...]
    total_ref[...] = jnp.zeros_like(total_ref)

    def pair(at, part):
        if at < 4:
            return own_refs[at][:, head_cols(part)]
        return cross_refs[at - 4][:, head_cols(part)]

    for tile in lane_tiles(total_rows):
        query = query_ref[tile, :]
        wide = tile.stop - tile.start
        top = jnp.full((1, wide), 2.0 * masked_score, wide_type)
        for at in range(8):
            scores = dot_dims(pair(at, 0), query, 1, 1) + bias_ref[:, at : at + 1]
            if at < 4:
                scores = scores + mask_ref[at : at + 1, tile]
            score_ref[at * rows : (at + 1) * rows, :] = scores
            top = jnp.maximum(top, jnp.max(scores, axis=0, keepdims=True))
        mass = jnp.zeros((1, wide), wide_type)
        out = jnp.zeros((HEAD, wide), wide_type)
        for at in range(8):
            weights = jnp.exp(score_ref[at * rows : (at + 1) * rows, :] - top)
            mass = mass + jnp.sum(weights, axis=0, keepdims=True)
            out = out + dot_dims(pair(at, 1), weights.astype(low_type), 0, 0)
        total_ref[0:1, tile] = top + jnp.log(mass)
        rows_out = (out / mass).T
        out_ref[tile, :] = rows_out
        low_ref[tile, :] = rows_out.astype(low_type)


def attend_back_kernel(own, bias_ref, mask_ref, total_ref, out_ref, own_ref, *refs):
    grad_refs, cross_refs = refs[:4], refs[4:-4]
    pair_sum, query_sum, query_ref, grad_ref = refs[-4:]
    rows = grad_refs[0].shape[0]
    query_ref[...] = own_ref[:, head_cols(2)]
    for at in range(4):
        grad_ref[at * rows : (at + 1) * rows, :] = grad_refs[at][...]
    ones = jnp.ones((8, HEAD), wide_type)
    pair_sum[...] = jnp.zeros_like(pair_sum)
    for tile in lane_tiles(4 * rows):
        query = query_ref[tile, :]
        grad = grad_ref[tile, :]
        centre = lax.dot_general(
            ones,
            grad.astype(wide_type) * out_ref[tile, :],
            (((1,), (1,)), ((), ())),
            precision=highest_precision,
            preferred_element_type=wide_type,
        )[0:1, :]
        total = total_ref[0:1, tile]
        query_part = jnp.zeros((HEAD, tile.stop - tile.start), wide_type)
        for at in range(4):
            block = slice(at * rows, (at + 1) * rows)
            if own:
                key, value = own_ref[block, head_cols(0)], own_ref[block, head_cols(1)]
                scores = dot_dims(key, query, 1, 1) + bias_ref[:, at : at + 1] + mask_ref[at : at + 1, tile]
            else:
                key, value = cross_refs[0][block, head_cols(0)], cross_refs[0][block, head_cols(1)]
                scores = dot_dims(key, query, 1, 1) + bias_ref[:, at + 4 : at + 5]
            weights = jnp.exp(scores - total)
            pair_sum[block, head_cols(1)] += dot_wide(weights.astype(low_type), grad)
            soft = dot_dims(value, grad, 1, 1)
            back = (weights * (soft - centre)).astype(low_type)
            pair_sum[block, head_cols(0)] += dot_wide(back, query)
            query_part = query_part + dot_dims(key, back, 0, 0)
        query_sum[tile, :] = query_part.T * HEAD ** (-0.5)


def turn_back_kernel(own_pair, other_pair, own_query, other_query, cos_ref, sin_ref, swap_ref, *out_refs):
    rows = out_refs[0].shape[0]
    swap = swap_ref[...]
    for at in range(4):
        block = slice(at * rows, (at + 1) * rows)
        cosine, sine = cos_ref[block, :], sin_ref[block, :]

        def turned(value):
            crossed = jnp.dot(value, swap, precision=highest_precision, preferred_element_type=wide_type)
            return (value * cosine - crossed * sine).astype(low_type)

        pair = own_pair[block, :] + other_pair[block, :]
        out_refs[at][:, head_cols(0)] = turned(pair[:, head_cols(0)])
        out_refs[at][:, head_cols(1)] = pair[:, head_cols(1)].astype(low_type)
        out_refs[at][:, head_cols(2)] = turned(own_query[block, :] + other_query[block, :])


def mix_back_kernel(at_ref, place_ref, key_w, value_w, query_w, *refs):
    mixed_refs = refs[:4]
    out_ref, stack_ref, bias_ref = refs[4:]
    ring, clip = at_ref[0], at_ref[1]
    place = place_ref[...]
    total = None
    bias_ref[...] = jnp.zeros_like(bias_ref)
    for part, weight in ((0, key_w), (1, value_w), (2, query_w)):
        relative = jnp.concatenate([ref[:, head_cols(part)] for ref in mixed_refs], axis=1)
        ordered = dot_wide(relative, place)
        bias_ref[part : part + 1, :] = jnp.sum(ordered, axis=0, keepdims=True)
        term = dot_dims(ordered.astype(low_type), weight[...], 1, 1)
        total = term if total is None else total + term
    out_ref[...] = total
    for at in range(4):
        stack_ref[lax.rem(ring + at - clip + 4, 4)] = mixed_refs[at][...]


def clip_products(at_ref, first_ref, second_ref, pack_refs, columns):
    out = None
    half = first_ref.shape[1]
    for step in range(4):
        place = ring_back(at_ref[0], step)
        pack = pack_refs[step]
        term = dot_dims(first_ref[place], pack[:half, columns], 0, 0)
        term = term + dot_dims(second_ref[place], pack[half : 2 * half, columns], 0, 0)
        out = term if out is None else out + term
    return out


def layer_grad_kernel(at_ref, act_a, act_b, norm_a, norm_b, *refs):
    head_refs, pack_refs, out_ref = refs[:-5], refs[-5:-1], refs[-1]
    part = out_ref.shape[1] // 2
    tiles = pl.num_programs(0) - (1 if head_refs else 0)

    @pl.when(pl.program_id(0) < tiles)
    def _():
        out_ref[:, :part] = clip_products(at_ref, act_a, act_b, pack_refs, slice(0, part))
        out_ref[:, part:] = clip_products(at_ref, norm_a, norm_b, pack_refs, slice(part, 2 * part))

    if head_refs:

        @pl.when(pl.program_id(0) == tiles)
        def _():
            columns = slice(2 * part, 3 * part)
            out_ref[:, :part] = clip_products(at_ref, head_refs[0], head_refs[2], pack_refs, columns)
            out_ref[:, part:] = clip_products(at_ref, head_refs[1], head_refs[3], pack_refs, columns)


def plain_grad_kernel(at_ref, rows_a, rows_b, *refs):
    pack_refs, out_ref = refs[:4], refs[4]
    out_ref[...] = clip_products(at_ref, rows_a, rows_b, pack_refs, slice(None))


def last_grad_kernel(tiles, at_ref, head_a, head_b, *refs):
    feat_refs, pack_refs, out_ref = refs[:4], refs[4:8], refs[8]
    head_rows = 2 * head_a.shape[1]
    feat_rows = head_rows + feat_refs[0].shape[0]

    @pl.when(pl.program_id(0) < tiles)
    def _():
        out = None
        for step in range(4):
            term = dot_dims(feat_refs[step][...], pack_refs[step][head_rows:feat_rows, :], 0, 0)
            out = term if out is None else out + term
        out_ref[...] = out

    @pl.when(pl.program_id(0) == tiles + 2)
    def _():
        out = None
        small = (pack_refs[0].shape[0] - feat_rows) // 2
        for step in range(4):
            high = pack_refs[step][feat_rows : feat_rows + small, :].astype(wide_type)
            term = high + pack_refs[step][feat_rows + small :, :].astype(wide_type)
            out = term if out is None else out + term
        high = out.astype(low_type).astype(wide_type)
        out_ref[:small, :] = high
        out_ref[small:, :] = out - high

    @pl.when((pl.program_id(0) >= tiles) & (pl.program_id(0) < tiles + 2))
    def _():
        out_ref[...] = clip_products(at_ref, head_a, head_b, pack_refs, slice(None))


def ring_sum_kernel(at_ref, part_ref, *refs):
    got_refs, out_ref = refs[:3], refs[3]
    block = out_ref.shape[0]
    out = part_ref[pl.ds(pl.multiple_of(at_ref[0] * block, 8), block), :]
    for got in got_refs:
        out = out + got[...].astype(wide_type)
    out_ref[...] = out


def ring_sum(ring_at, part, got, after):
    shape = (part.shape[0] // 4, part.shape[1])
    return call_kernel(
        ring_sum_kernel,
        (ring_at[None], part, *got),
        (0,),
        jax.ShapeDtypeStruct(shape, wide_type),
        [],
        4 * shape[0] * shape[1],
        0,
        after,
    )


def half_sum_kernel(own_ref, got_ref, out_ref):
    out_ref[...] = (own_ref[...] + got_ref[...]).astype(low_type)


def half_sum(own, after):
    got = lax.ppermute(own, "frame", HALF_SWAP)
    return call_kernel(
        half_sum_kernel,
        (own, got),
        (),
        jax.ShapeDtypeStruct(own.shape, low_type),
        [],
        own.size,
        0,
        after,
    )


def join_kernel(at_ref, *refs):
    out_ref = refs[4]
    block = refs[0].shape[0]
    for step in range(4):
        start = pl.multiple_of(ring_back(at_ref[0], step) * block, 16)
        out_ref[pl.ds(start, block), :] = refs[step][...]


def join_frames(ring_at, total, after, after_far=()):
    pieces = ring_pieces(total)
    return call_kernel(
        join_kernel,
        (ring_at[None], *pieces),
        (0,),
        jax.ShapeDtypeStruct((4 * total.shape[0], total.shape[1]), low_type),
        [],
        0,
        0,
        after,
        after_far,
    )


def beside_kernel(first_ref, second_ref, out_ref):
    half, wide, other = first_ref.shape[0] // 2, first_ref.shape[1], second_ref.shape[1]
    out_ref[:, :wide] = first_ref[:half, :]
    out_ref[:, wide : wide + other] = second_ref[:half, :]
    out_ref[:, wide + other :] = second_ref[half:, :]


def beside_whole_kernel(first_ref, second_ref, out_ref):
    half, wide, other = first_ref.shape[0] // 2, first_ref.shape[1], second_ref.shape[1]
    for at in range(2):
        rows = slice(at * half, (at + 1) * half)
        out_ref[:, at * wide : (at + 1) * wide] = first_ref[rows, :]
        start = 2 * wide + at * other
        out_ref[:, start : start + other] = second_ref[rows, :]


def gather_clips(first, second, after, whole=False):
    half, wide = first.shape[0] // 2, first.shape[1]
    beside = call_kernel(
        beside_whole_kernel if whole else beside_kernel,
        (first, second),
        (),
        jax.ShapeDtypeStruct(
            (half, (2 if whole else 1) * wide + 2 * second.shape[1]), low_type
        ),
        [],
        0,
        0,
        after,
    )
    return lax.all_gather(beside, "clip")


def take_kernel(whole_ref, out_ref):
    out_ref[...] = whole_ref[:, :, : out_ref.shape[2]]


def with_other_core(whole, wide, after):
    shape = (*whole.shape[:2], wide)
    columns = pl.pallas_call(
        without(take_kernel, 1, after),
        grid=(1,),
        out_shape=jax.ShapeDtypeStruct(shape, low_type),
        in_specs=[pl.BlockSpec(shape, lambda i: (0, 0, 0))] + any_specs(after),
        out_specs=pl.BlockSpec(shape, lambda i: (0, 0, 0)),
        compiler_params=kernel_params(),
    )(whole, *after)
    return whole, core_swap(columns)


def smem_spec():
    return pl.BlockSpec(memory_space=pltpu.SMEM)


def kernel_params():
    return pltpu.CompilerParams(vmem_limit_bytes=48 * 1024 * 1024)


def held_spec():
    return pl.BlockSpec(memory_space=pltpu.VMEM)


def any_specs(arrays):
    return [pl.BlockSpec(memory_space=pl.ANY)] * len(arrays)


def mark(value):
    while value.ndim > 2:
        value = value[0]
    return value[:8, :128]


def without(kernel, count, after):
    return lambda *refs: kernel(*refs[:count], *refs[count + len(after) :])


def layer_grad(clip_at, second_all, packs, first_all, after):
    whole, other = second_all
    half = whole.shape[1]
    wide = whole.shape[2] // 4 if other is None else other.shape[2]
    tiles = wide // 128
    part = 256
    block = (4, half, 128)
    starts = (2 * tiles, 3 * tiles, 0, tiles) if other is None else (tiles, 2 * tiles, 0, 0)
    other = whole if other is None else other
    heads = () if first_all is None else (first_all[0],) * 4
    held = [
        pl.BlockSpec(block, lambda i, at=at: (0, 0, tiles + at)) for at in range(len(heads))
    ]

    def moving(start):
        return pl.BlockSpec(block, lambda i: (0, 0, start + jnp.minimum(i, tiles - 1)))

    return pl.pallas_call(
        without(layer_grad_kernel, 9 + len(heads), after),
        grid=(tiles + (1 if heads else 0),),
        out_shape=jax.ShapeDtypeStruct((wide + (128 if heads else 0), 2 * part), wide_type),
        in_specs=[smem_spec()]
        + [moving(start) for start in starts]
        + held
        + [held_spec()] * 4
        + any_specs(after),
        out_specs=pl.BlockSpec((128, 2 * part), lambda i: (i, 0)),
        compiler_params=kernel_params(),
        cost_estimate=pl.CostEstimate(
            flops=32 * half * wide * part,
            bytes_accessed=2 * whole.size + 8 * wide * part,
            transcendentals=0,
        ),
    )(clip_at[None], whole, whole, whole, other, *heads, *packs, *after)


def plain_grad(clip_at, rows_all, packs, after):
    whole, other = rows_all
    half, count = other.shape[1:]
    part = packs[0].shape[1]
    block = pl.BlockSpec((4, half, 128), lambda i: (0, 0, i))
    return pl.pallas_call(
        without(plain_grad_kernel, 7, after),
        grid=(count // 128,),
        out_shape=jax.ShapeDtypeStruct((count, part), wide_type),
        in_specs=[smem_spec(), block, block] + [held_spec()] * 4 + any_specs(after),
        out_specs=pl.BlockSpec((128, part), lambda i: (i, 0)),
        compiler_params=kernel_params(),
        cost_estimate=pl.CostEstimate(
            flops=16 * half * count * part,
            bytes_accessed=16 * half * count + 4 * count * part,
            transcendentals=0,
        ),
    )(clip_at[None], whole, other, *packs, *after)


def last_grad(clip_at, first_all, feats, packs, after, after_far):
    whole, other = first_all
    half, part = other.shape[1], packs[0].shape[1]
    first_block = other.shape[2] // 128
    tiles = feats[0].shape[1] // 128
    kernel = functools.partial(last_grad_kernel, tiles)
    after_far = tuple(mark(value) for value in after_far)

    def moving(start):
        return pl.BlockSpec(
            (4, half, 128), lambda i: (0, 0, start + jnp.clip(i - tiles, 0, 1))
        )

    return pl.pallas_call(
        without(kernel, 11, (*after, *after_far)),
        grid=(tiles + 3,),
        out_shape=jax.ShapeDtypeStruct(((tiles + 3) * 128, part), wide_type),
        in_specs=[smem_spec(), moving(first_block), moving(first_block + 2)]
        + [pl.BlockSpec((feats[0].shape[0], 128), lambda i: (0, jnp.minimum(i, tiles - 1)))] * 4
        + [held_spec()] * 4
        + any_specs(after)
        + any_specs(after_far),
        out_specs=pl.BlockSpec((128, part), lambda i: (i, 0)),
        compiler_params=kernel_params(),
    )(clip_at[None], whole, whole, *feats, *packs, *after, *after_far)


def by_clip(clip_at, write):
    for place in range(4):

        @pl.when(clip_at == place)
        def _(place=place):
            for step in range(4):
                write((place - step) % 4, step)


def place_layer_kernel(tiles, at_ref, all_ref, *outs):
    part = all_ref.shape[2] // 2
    is_last = pl.program_id(0) == tiles

    for place in range(4):
        columns = slice(place * part, (place + 1) * part)
        left = all_ref[place, :, :part].astype(wide_type)
        right = all_ref[place, :, part:].astype(wide_type)

        @pl.when(jnp.logical_not(is_last))
        def _(columns=columns, left=left, right=right):
            outs[0][0, :, columns] = left
            outs[1][0, :, columns] = right

        if len(outs) > 2:

            @pl.when(is_last)
            def _(columns=columns, left=left, right=right):
                outs[2][0, : outs[2].shape[1] // 2, columns] = left
                outs[2][0, outs[2].shape[1] // 2 :, columns] = right


def place_layer(clip_at, layer, levels, joined, earlier, heads_layer, after):
    part = joined.shape[2] // 2
    rows = 4 * part
    tiles = rows // 128
    heads = joined.shape[1] > rows
    out = [(levels, rows, 4 * part)] * 2 + [(levels, 256, 4 * part)] * heads
    tall = pl.BlockSpec((1, 128, 4 * part), lambda i: (layer, jnp.minimum(i, tiles - 1), 0))
    wide = pl.BlockSpec((1, 256, 4 * part), lambda i: (heads_layer, 0, 0))
    return pl.pallas_call(
        without(functools.partial(place_layer_kernel, tiles), 2, (*earlier, *after)),
        grid=(tiles + (1 if heads else 0),),
        out_shape=tuple(jax.ShapeDtypeStruct(shape, wide_type) for shape in out),
        in_specs=[smem_spec(), pl.BlockSpec((4, 128, 2 * part), lambda i: (0, i, 0))]
        + any_specs(earlier)
        + any_specs(after),
        out_specs=(tall, tall) + ((wide,) if heads else ()),
        input_output_aliases={2 + at: at for at in range(len(earlier))},
        compiler_params=kernel_params(),
    )(clip_at[None], joined, *earlier, *after)


def place_last_kernel(skip, at_ref, *refs):
    pieces = refs[:4]
    in_ref, small_ref, proj_ref = refs[-3:]
    part = pieces[0].shape[1]
    heads = skip + proj_ref.shape[1]
    small = small_ref.shape[0]

    def write(place, step):
        columns = slice(place * part, (place + 1) * part)
        piece = pieces[step]
        in_ref[:, columns] = piece[: in_ref.shape[0], :].astype(wide_type)
        proj_ref[0, :, columns] = piece[skip:heads, :].astype(wide_type)
        small_ref[:, columns] = piece[heads : heads + small, :].astype(wide_type) + piece[
            heads + small :, :
        ].astype(wide_type)

    by_clip(at_ref[0], write)


def place_last(clip_at, feat_rows, skip, levels, pieces, earlier):
    part = pieces[0].shape[1]
    return pl.pallas_call(
        functools.partial(place_last_kernel, skip),
        grid=(1,),
        out_shape=(
            jax.ShapeDtypeStruct((feat_rows, 4 * part), wide_type),
            jax.ShapeDtypeStruct((64, 4 * part), wide_type),
            jax.ShapeDtypeStruct((levels, 256, 4 * part), wide_type),
        ),
        in_specs=[smem_spec()]
        + [pl.BlockSpec(pieces[0].shape, lambda i: (0, 0))] * 4
        + [pl.BlockSpec(memory_space=pl.ANY)],
        out_specs=(
            pl.BlockSpec((feat_rows, 4 * part), lambda i: (0, 0)),
            pl.BlockSpec((64, 4 * part), lambda i: (0, 0)),
            pl.BlockSpec((1, 256, 4 * part), lambda i: (0, 0, 0)),
        ),
        input_output_aliases={5: 2},
        compiler_params=kernel_params(),
    )(clip_at[None], *pieces, earlier)


def pack_kernel(by_rows, count, at_ref, *refs):
    parts, outs = refs[:count], refs[count:]
    for clip in range(4):

        @pl.when(at_ref[0] == clip)
        def _(clip=clip):
            for step in range(4):
                place, start = (clip + step) % 4, 0
                for part in parts:
                    size = part.shape[1] // 4
                    value = part[:, place * size : (place + 1) * size]
                    if by_rows:
                        outs[step][start : start + part.shape[0], :] = value
                        start += part.shape[0]
                    else:
                        outs[step][:, start : start + size] = value
                        start += size


def pack_parts(clip_at, parts, by_rows, after):
    sizes = [part.shape[1] // 4 for part in parts]
    if by_rows:
        shape = (sum(part.shape[0] for part in parts), sizes[0])
    else:
        shape = (parts[0].shape[0], sum(sizes))
    return call_kernel(
        functools.partial(pack_kernel, by_rows, len(parts)),
        (clip_at[None], *parts),
        (0,),
        tuple(jax.ShapeDtypeStruct(shape, low_type) for _ in range(4)),
        [],
        0,
        0,
        after,
    )


def place_heads_kernel(at_ref, all_ref, *refs):
    out_ref = refs[-1]
    for place in range(4):
        piece = all_ref[place].astype(wide_type)
        for at, part in ((1, 0), (2, 1), (0, 2)):
            out_ref[0, at, :, head_cols(place)] = piece[:, head_cols(part)]


def place_heads(clip_at, layer, levels, joined, earlier, after):
    rows = joined.shape[1]
    tile = 256
    count = 2
    return pl.pallas_call(
        without(place_heads_kernel, count, (*earlier, *after)),
        grid=(rows // tile,),
        out_shape=jax.ShapeDtypeStruct((levels, 3, rows, 4 * HEAD), wide_type),
        in_specs=[smem_spec(), pl.BlockSpec((4, tile, 3 * HEAD), lambda i: (0, i, 0))]
        + any_specs(earlier)
        + any_specs(after),
        out_specs=pl.BlockSpec((1, 3, tile, 4 * HEAD), lambda i: (layer, 0, i, 0)),
        input_output_aliases={count + at: at for at in range(len(earlier))},
        compiler_params=kernel_params(),
    )(clip_at[None], joined, *earlier, *after)


def stack_kernel(*refs):
    out_ref = refs[-1]
    for at, ref in enumerate(refs[:-1]):
        out_ref[8 * at : 8 * (at + 1), :] = ref[...]


def feature_grad_kernel(ids_ref, rows_ref, weight_ref, out_ref):
    size = rows_ref.shape[0] // 4
    for at in range(4):
        start = pl.multiple_of(ids_ref[at] * size, 8)
        out_ref[pl.ds(start, size), :] = dot_dims(
            rows_ref[at * size : (at + 1) * size, :], weight_ref[...], 1, 1
        )


def last_pack_kernel(at_ref, head_ref, patch_ref, small_a, small_b, *outs):
    heads, patches, small = head_ref.shape[0], patch_ref.shape[0], small_a.shape[0]
    values = small_a[...] + small_b[...]
    high = values.astype(low_type)
    rest = (values - high.astype(wide_type)).astype(low_type)
    for clip in range(4):

        @pl.when(at_ref[0] == clip)
        def _(clip=clip):
            for step in range(4):
                size = outs[step].shape[1]
                place = (clip + step) % 4
                columns = slice(place * size, (place + 1) * size)
                outs[step][:heads, :] = head_ref[:, columns]
                outs[step][heads : heads + patches, :] = patch_ref[:, columns]
                outs[step][heads + patches : heads + patches + small, :] = high[:, columns]
                outs[step][heads + patches + small :, :] = rest[:, columns]


def call_kernel(kernel, args, in_smem, outs, scratch, flops, exps, after=(), after_far=(), piped=()):
    count = len(args)

    def spec(at):
        if at in piped:
            return pl.BlockSpec(args[at].shape, lambda i, rank=args[at].ndim: (0,) * rank)
        return pl.BlockSpec(memory_space=pltpu.SMEM if at in in_smem else pltpu.VMEM)

    specs = [spec(at) for at in range(count)]
    after = (*after, *(mark(value) for value in after_far))
    specs += any_specs(after)
    moved = sum(a.size * a.dtype.itemsize for a in args)
    return pl.pallas_call(
        without(kernel, count, after),
        grid=(1,),
        out_shape=outs,
        in_specs=specs,
        out_specs=jax.tree.map(lambda _: pl.BlockSpec(memory_space=pltpu.VMEM), outs),
        scratch_shapes=scratch,
        compiler_params=kernel_params(),
        cost_estimate=pl.CostEstimate(flops=flops, bytes_accessed=moved, transcendentals=exps),
    )(*args, *after)


def on_device(
    features,
    cond_values,
    cond_live,
    in_weight,
    in_bias,
    act_weight,
    act_bias,
    state_weight,
    state_bias,
    attn_gain,
    attn_shift,
    qkv_weight,
    qkv_bias,
    proj_weight,
    proj_bias,
    mlp_gain,
    mlp_shift,
    up_weight,
    up_bias,
    down_weight,
    down_bias,
    out_grad,
):
    patch_rows = features.shape[2]
    feat_width = features.shape[3]
    slot_count = cond_values.shape[2]
    all_frames = cond_live.shape[1]
    model_width = in_weight.shape[1]
    width = qkv_weight.shape[3]
    heads = width // HEAD
    level_count = attn_gain.shape[0]
    patches = patch_rows // 4
    chunk_rows = patches + EXTRA
    rows = 4 * chunk_rows
    hidden_width = up_weight.shape[2]

    tensor_at = lax.axis_index("tensor")
    chip_at, core_at = tensor_at // 2, tensor_at % 2
    frame_at = lax.axis_index("frame")
    half_at, ring_at = frame_at // 4, frame_at % 4
    clip_at = lax.axis_index("clip")

    chunk_ids = [
        2 * jnp.bitwise_xor(core_at, core_step) + jnp.bitwise_xor(chip_at, chip_step)
        for core_step in range(2)
        for chip_step in range(2)
    ]
    own_chunk = chunk_ids[0]
    own_frames = jnp.stack([4 * half_at + (ring_at - step) % 4 for step in range(4)])
    cross_frames = jnp.stack([4 * (1 - half_at) + (ring_at - step) % 4 for step in range(4)])

    within = lax.broadcasted_iota(jnp.int32, (chunk_rows, 1), 0)
    is_patch = within < patches
    heights, columns = [], []
    for chunk_id in chunk_ids:
        patch_id = chunk_id * patches + within
        heights.append(jnp.where(is_patch, patch_id // GRID_W, 0))
        columns.append(jnp.where(is_patch, patch_id % GRID_W, 0))
    heights = jnp.concatenate(heights, axis=0).astype(wide_type)
    columns = jnp.concatenate(columns, axis=0).astype(wide_type)
    swap_table, rate_table = rotary_tables(HEAD, heads)
    swap_heads = jnp.asarray(swap_table)
    swap_one = jnp.asarray(swap_table[:HEAD, :HEAD])
    rates = rate_table[:, :HEAD]
    place_angles = heights * rates[1] + columns * rates[2]
    angles = jnp.concatenate(
        [
            own_frames[step].astype(wide_type) * rates[0][None, :] + place_angles
            for step in range(4)
        ],
        axis=0,
    )
    cosine_four, sine_four = jnp.cos(angles), jnp.sin(angles)
    head_from = jnp.arange(width)
    head_to = ((head_from // HEAD + ring_at) % 4) * HEAD + head_from % HEAD
    head_place = (head_to[:, None] == head_from[None, :]).astype(low_type)
    proj_turned = [
        lax.dynamic_slice_in_dim(
            jnp.concatenate([proj_weight[layer], proj_weight[layer]], axis=0),
            ring_at * HEAD,
            width,
            0,
        )
        for layer in range(level_count)
    ]
    ring_scalar = ring_at.astype(jnp.int32)
    clip_scalar = clip_at.astype(jnp.int32)

    live_all = cond_live[0].astype(wide_type)
    own_slots = lax.dynamic_index_in_dim(live_all, frame_at, 0, False)

    def live_rows(slots, chunk_id):
        picked = jnp.where(
            chunk_id < slot_count,
            lax.dynamic_index_in_dim(slots, jnp.minimum(chunk_id, slot_count - 1), 1, False),
            0.0,
        )
        return jnp.where(is_patch, 1.0, jnp.where(within == patches, picked[None, :], 0.0))

    sources = jnp.concatenate([own_frames, cross_frames])
    source_live = jnp.take(live_all, sources, axis=0)
    key_live = jnp.concatenate([live_rows(source_live, c) for c in chunk_ids], axis=0)
    reached = jnp.concatenate([jnp.ones((4,), jnp.bool_), jnp.full((4,), half_at == 1)])
    key_bias = jnp.where((key_live > 0.5) & reached[None, :], 0.0, masked_score).astype(wide_type)
    seen = own_frames[:, None] <= own_frames[None, :]
    causal = jnp.where(seen, 0.0, masked_score).astype(wide_type)
    causal = jnp.pad(jnp.repeat(causal, rows, axis=1), ((0, 4), (0, 0)))
    own_live = live_rows(own_slots[None, :], own_chunk)

    def extra_rows(slot_rows):
        picked = lax.dynamic_slice_in_dim(
            slot_rows, jnp.minimum(own_chunk, slot_count - 1), 1, 0
        )
        picked = jnp.where(own_chunk < slot_count, picked, jnp.zeros_like(picked))
        return jnp.pad(picked, ((0, EXTRA - 1), (0, 0)))

    cond_here = cond_values[0, 0]
    act_rows = jnp.dot(cond_here, act_weight, precision=highest_precision) + act_bias
    state_rows = jnp.dot(cond_here, state_weight, precision=highest_precision) + state_bias
    even_slot = (jnp.arange(slot_count) % 2 == 0)[:, None]
    cond_x = jnp.where(even_slot, act_rows, state_rows) * own_slots[:, None]

    flat_feat = jnp.concatenate(
        [
            lax.dynamic_slice_in_dim(features[0, 0], c * patches, patches, 0)
            for c in chunk_ids
        ],
        axis=0,
    )
    kept, got = halves_tensor(dot_wide(flat_feat, in_weight))
    stream = jnp.concatenate([kept + got + in_bias, extra_rows(cond_x)], axis=0)

    feat_wide = -(-feat_width // 128) * 128
    feat_low = jnp.pad(flat_feat, ((0, 0), (0, feat_wide - feat_width)))
    feats = [feat_low] + [
        lax.ppermute(feat_low, "clip", clip_shift(step)) for step in range(1, 4)
    ]
    pair_work = 2 * 32 * rows * rows * HEAD
    pair_exps = 32 * rows * rows
    weight_parts = [
        [qkv_weight[layer, :, at] for at in (1, 2, 0)] for layer in range(level_count)
    ]

    def norm(terms, gain, shift, after_far=()):
        chunk = jax.ShapeDtypeStruct((chunk_rows, model_width), wide_type)
        return call_kernel(
            norm_kernel,
            (gain[None], shift[None], *terms),
            (),
            (
                chunk,
                chunk,
                jax.ShapeDtypeStruct((chunk_rows, 128), wide_type),
                jax.ShapeDtypeStruct((chunk_rows, model_width), low_type),
            ),
            [],
            12 * chunk_rows * model_width,
            0,
            (),
            after_far,
        )

    def norm_back(part, gain, hat, inverse, grad, count, after=(), after_far=()):
        kept, got = halves_tensor(part)
        return call_kernel(
            functools.partial(norm_back_kernel, count),
            (kept, got, gain[None], hat, inverse, grad),
            (),
            (
                jax.ShapeDtypeStruct((chunk_rows, model_width), wide_type),
                jax.ShapeDtypeStruct((chunk_rows, model_width), low_type),
                jax.ShapeDtypeStruct((8, model_width), wide_type),
            ),
            [],
            16 * chunk_rows * model_width,
            0,
            after,
            after_far,
            (2, 3, 4, 5),
        )

    slot_grads = out_grad[0, 0, patch_rows:] * own_slots[:, None].astype(low_type)
    slot_blocks = jnp.concatenate(
        [
            jnp.pad(slot_grads[:, None], ((0, 0), (0, EXTRA - 1), (0, 0))),
            jnp.zeros((4 - slot_count, EXTRA, model_width), low_type),
        ],
        axis=0,
    )
    branch_parts = []
    for chunk_id in chunk_ids:
        branch_parts.append(
            lax.dynamic_slice_in_dim(out_grad[0, 0], chunk_id * patches, patches, 0)
        )
        branch_parts.append(lax.dynamic_index_in_dim(slot_blocks, chunk_id, 0, False))
    first_branch = jnp.concatenate(branch_parts, axis=0)
    stored = []
    terms = (stream,)
    before = None
    for layer in range(level_count):
        stream, hat_one, inverse_one, first_chunk = norm(terms, attn_gain[layer], attn_shift[layer])
        first_in = join_rows_tensor(first_chunk)
        bias = jnp.pad(qkv_bias[layer], ((0, 5), (0, 0)))
        heads_out = call_kernel(
            functools.partial(project_kernel, heads),
            (
                ring_scalar[None],
                first_in,
                *weight_parts[layer],
                bias,
                cosine_four,
                sine_four,
                swap_heads,
            ),
            (0,),
            tuple(
                jax.ShapeDtypeStruct((rows, count * HEAD), low_type)
                for count in (3, 3, 3, 3, 2, 2, 2, 2)
            ),
            [],
            6 * rows * model_width * width,
            0,
            (),
            () if before is None else (before[0],),
            (2, 3, 4, 5, 6, 7, 8),
        )
        blocks = to_heads(heads_out[:4])
        cross = pairs_to_later_half(heads_out[4:])
        attn_wide, attn_turned, log_total, own_all, cross_all = call_kernel(
            attend_kernel,
            (key_bias, causal, *blocks, *cross),
            (),
            (
                jax.ShapeDtypeStruct((4 * rows, HEAD), wide_type),
                jax.ShapeDtypeStruct((4 * rows, HEAD), low_type),
                jax.ShapeDtypeStruct((8, 4 * rows), wide_type),
                jax.ShapeDtypeStruct((4 * rows, 3 * HEAD), low_type),
                jax.ShapeDtypeStruct((4 * rows, 2 * HEAD), low_type),
            ),
            [
                pltpu.VMEM((4 * rows, HEAD), low_type),
                pltpu.VMEM((8 * rows, lane_tiles(4 * rows)[0].stop), wide_type),
            ],
            2 * pair_work,
            pair_exps,
            tuple(feats[1:]) if layer == 0 else (),
        )
        attn_relative = jnp.concatenate(
            to_frames([attn_turned[at * rows : (at + 1) * rows] for at in range(4)]), axis=1
        )
        attn_low = dot_wide(attn_relative, head_place).astype(low_type)
        if layer < level_count - 1:
            first_all = gather_clips(first_in, attn_low, ())
        kept, got = halves_tensor(dot_wide(attn_relative, proj_turned[layer]))
        middle, hat_two, inverse_two, second_chunk = norm(
            (stream, kept, got, proj_bias[layer][None]), mlp_gain[layer], mlp_shift[layer],
            () if before is None else (before[1], first_branch),
        )
        second_in = join_rows_tensor(second_chunk)
        hidden = dot_wide(second_in, up_weight[layer]) + up_bias[layer]
        active_low = exact_gelu(hidden).astype(low_type)
        second_all = gather_clips(second_in, active_low, (), layer == level_count - 1)
        if layer == level_count - 1:
            first_all = (first_in, attn_low)
        before = (first_all, second_all)
        kept, got = halves_tensor(dot_wide(active_low, down_weight[layer]))
        terms = (middle, kept, got, down_bias[layer][None])
        stored.append(
            (
                hat_one,
                inverse_one,
                own_all,
                cross_all,
                log_total,
                attn_wide,
                hat_two,
                inverse_two,
                hidden,
                first_all,
                second_all,
            )
        )
    def in_order(full, count):
        out = jnp.zeros((4 * count,) + full.shape[1:], full.dtype)
        size = full.shape[0] // 4
        for at, chunk_id in enumerate(chunk_ids):
            out = lax.dynamic_update_slice_in_dim(
                out, full[at * size : at * size + count], chunk_id * count, 0
            )
        return out

    def block_rows(after):
        low = call_kernel(
            block_kernel,
            (*terms, jnp.broadcast_to(own_live, (chunk_rows, 128))),
            (),
            jax.ShapeDtypeStruct((chunk_rows, model_width), low_type),
            [],
            4 * chunk_rows * model_width,
            0,
            after,
        )
        return join_rows_tensor(low)

    def block_in_order(block_full):
        slot_full = jnp.concatenate(
            [
                block_full[at * chunk_rows + patches : at * chunk_rows + patches + 1]
                for at in range(4)
            ],
            axis=0,
        )
        return jnp.concatenate(
            [in_order(block_full, patches), in_order(slot_full, 1)[:slot_count]], axis=0
        )[None, None]

    own_out = lax.dynamic_slice_in_dim(out_grad[0, 0], own_chunk * patches, patches, 0)
    grad_stream = (
        jnp.concatenate(
            [
                own_out.astype(wide_type),
                extra_rows(out_grad[0, 0, patch_rows:].astype(wide_type)),
            ],
            axis=0,
        )
        * own_live
    )

    small = {}
    small["down", level_count - 1] = jnp.sum(grad_stream, axis=0)
    sums_list = []
    wide_part = model_width // 4
    later = None
    for layer in reversed(range(level_count)):
        (
            hat_one,
            inverse_one,
            own_all,
            cross_all,
            log_total,
            attn_wide,
            hat_two,
            inverse_two,
            hidden,
            first_all,
            second_all,
        ) = stored[layer]
        branch = first_branch if later is None else join_rows_tensor(branch_chunk)
        if later is not None:
            first_all = with_other_core(first_all, model_width, (branch,))
            second_all = with_other_core(second_all, model_width, (branch,))
        _, gelu_pull = jax.vjp(exact_gelu, hidden)
        grad_hidden = gelu_pull(dot_dims(branch, down_weight[layer], 1, 1))[0].astype(low_type)
        small["up", layer] = jnp.sum(grad_hidden.astype(wide_type), axis=0)
        parts = [branch, grad_hidden] + ([] if later is None else [later["proj_out"]])
        packs = pack_parts(clip_scalar, parts, False, ())
        grad_middle, proj_chunk, sums = norm_back(
            dot_dims(grad_hidden, up_weight[layer], 1, 1),
            mlp_gain[layer],
            hat_two,
            inverse_two,
            grad_stream,
            chunk_rows,
            (packs[0],) if later is None else (packs[0], later["tall_join"]),
            () if later is None else (later["heads_sum"],),
        )
        sums_list.append(sums)
        packs = swap_clips(packs)
        if later is None:
            second_all = (second_all, None)
            block_full = block_rows((proj_chunk,))
            block_out = block_in_order(block_full)
        proj_out = join_rows_tensor(proj_chunk)
        grad_attn = dot_dims(proj_out, proj_turned[layer], 1, 1).astype(low_type)
        grads = to_heads([grad_attn[:, head_cols(at)] for at in range(4)])

        if later is not None:
            later["heads_ring"] = ring_sum(
                ring_scalar, later["heads_sum"], later["heads_got"], (proj_chunk,)
            )

            later["tall_all"] = lax.all_gather(later["tall_join"], "clip")

        def attend_back(own, after, after_far=()):
            return call_kernel(
                functools.partial(attend_back_kernel, own),
                (key_bias, causal, log_total, attn_wide, own_all, *grads)
                + (() if own else (cross_all,)),
                (),
                (
                    jax.ShapeDtypeStruct((4 * rows, 2 * HEAD), wide_type),
                    jax.ShapeDtypeStruct((4 * rows, HEAD), wide_type),
                ),
                [
                    pltpu.VMEM((4 * rows, HEAD), low_type),
                    pltpu.VMEM((4 * rows, HEAD), low_type),
                ],
                5 * pair_work // 2,
                pair_exps // 2,
                after,
                after_far,
                (0, 1, 2, 3, 4) if own else (0, 1, 2, 3, 4, 9),
            )

        cross_pair, cross_query = attend_back(
            False, () if later is None else (later["heads_ring"],)
        )
        got_pair = lax.ppermute(cross_pair, "frame", DOWN_HALF)
        if later is None:
            first_all = with_other_core(
                gather_clips(*first_all, (cross_pair,)), model_width, (cross_pair,)
            )
        tall_sum = layer_grad(
            clip_scalar,
            second_all,
            packs,
            None if later is None else later["first_all"],
            (cross_pair,),
        )
        own_pair, own_query = attend_back(
            True, (), (tall_sum,) if later is None else (tall_sum, later["tall_all"], block_full)
        )
        tall_got = ring_sends(tall_sum, ring_at)
        if later is not None:
            later["heads_total"] = half_sum(later["heads_ring"], (own_pair,))
        tall_ring = ring_sum(ring_scalar, tall_sum, tall_got, ())
        tall_total = half_sum(tall_ring, ())
        turned = call_kernel(
            turn_back_kernel,
            (own_pair, got_pair, own_query, cross_query, cosine_four, sine_four, swap_one),
            (),
            tuple(jax.ShapeDtypeStruct((rows, 3 * HEAD), low_type) for _ in range(4)),
            [],
            24 * rows * HEAD * HEAD,
            0,
            (tall_ring,) if later is None else (tall_ring, later["heads_total"]),
            (),
            (4, 5, 6),
        )
        mixed = to_frames(list(turned))
        if later is not None:
            later["heads_join"] = join_frames(ring_scalar, later["heads_total"], (turned[0],))
        normed_part, mixed_stack, bias_sums = call_kernel(
            mix_back_kernel,
            (
                jnp.stack([ring_scalar, clip_scalar]),
                head_place,
                *weight_parts[layer],
                *mixed,
            ),
            (0,),
            (
                jax.ShapeDtypeStruct((rows, model_width), wide_type),
                jax.ShapeDtypeStruct((4, rows, 3 * HEAD), low_type),
                jax.ShapeDtypeStruct((8, width), wide_type),
            ),
            [],
            6 * rows * model_width * width,
            0,
            (tall_total,) if later is None else (tall_total, later["heads_join"]),
            (),
            (1, 2, 3, 4),
        )
        small["qkv", layer] = jnp.concatenate([bias_sums[2:3], bias_sums[:2]], axis=0)
        packs = swap_clips([mixed_stack[step] for step in range(4)])
        grad_stream, branch_chunk, sums = norm_back(
            normed_part,
            attn_gain[layer],
            hat_one,
            inverse_one,
            grad_middle,
            patches if layer == 0 else chunk_rows,
        )
        sums_list.append(sums)
        tall_join = join_frames(ring_scalar, tall_total, (branch_chunk,))

        heads_sum = plain_grad(clip_scalar, first_all, packs, (branch_chunk,))
        heads_got = ring_sends(heads_sum, ring_at)
        if layer > 0:
            later = {
                "proj_out": proj_out,
                "first_all": first_all,
                "tall_join": tall_join,
                "heads_sum": heads_sum,
                "heads_got": heads_got,
            }

    patch_chunk = branch_chunk[:patches]
    grad_patch = join_rows_tensor(patch_chunk)
    grad_features = call_kernel(
        feature_grad_kernel,
        (jnp.stack(chunk_ids).astype(jnp.int32), grad_patch, in_weight),
        (0,),
        jax.ShapeDtypeStruct((patch_rows, feat_width), wide_type),
        [],
        2 * patch_rows * feat_width * model_width,
        0,
        piped=(2,),
    )
    slot_row = grad_stream[patches : patches + 1] * own_live[patches : patches + 1]
    own_cond = lax.dynamic_slice_in_dim(
        cond_here, jnp.minimum(own_chunk, slot_count - 1), 1, 0
    )
    slot_part = jnp.concatenate([own_cond.T * slot_row, slot_row], axis=0)
    here = own_chunk < slot_count
    is_act = here & (own_chunk % 2 == 0)
    is_state = here & (own_chunk % 2 == 1)
    act_part = jnp.where(is_act, slot_part, 0.0)
    state_part = jnp.where(is_state, slot_part, 0.0)

    def at_tensor(value, total):
        return lax.dynamic_update_slice(
            jnp.zeros((value.shape[0], total), wide_type),
            value,
            (0, tensor_at * value.shape[1]),
        )

    layers = range(level_count)
    qkv_rows = at_tensor(
        jnp.concatenate([small["qkv", layer] for layer in layers], axis=0), 4 * width
    )
    mixed_rows = jnp.concatenate(
        [qkv_rows, small["down", level_count - 1][None], jnp.zeros_like(qkv_rows[:1])], axis=0
    )
    ups = at_tensor(jnp.stack([small["up", layer] for layer in layers]), 4 * hidden_width)
    parts = [*sums_list, act_part, state_part, mixed_rows, ups.reshape(-1, model_width)]
    vector = call_kernel(
        stack_kernel,
        tuple(parts),
        (),
        jax.ShapeDtypeStruct((8 * len(parts), model_width), wide_type),
        [],
        0,
        0,
    )
    vector = vector + core_swap(vector)
    later["heads_all"] = lax.all_gather(later["heads_join"], "clip")
    head_rows, patch_count, small_rows = proj_out.shape[0], grad_patch.shape[0], vector.shape[0]
    packs = call_kernel(
        last_pack_kernel,
        (clip_scalar[None], proj_out, grad_patch, vector, chip_swap(vector)),
        (0,),
        tuple(
            jax.ShapeDtypeStruct((head_rows + patch_count + 2 * small_rows, wide_part), low_type)
            for _ in range(4)
        ),
        [],
        0,
        0,
        (),
        (heads_sum,),
    )
    tall_all = lax.all_gather(tall_join, "clip")
    placed = place_layer(
        clip_scalar, level_count - 1, level_count, later["tall_all"], (), 0, (packs[0],)
    )
    packs = swap_clips(packs)
    heads_ring = ring_sum(ring_scalar, heads_sum, heads_got, tuple(packs[1:]))
    last_sum = last_grad(
        clip_scalar, first_all, feats, packs, (heads_ring,), (placed[0], grad_features)
    )
    last_ring = ring_sum(ring_scalar, last_sum, ring_sends(last_sum, ring_at), ())
    heads_total = half_sum(heads_ring, (mark(last_sum),))
    heads_join = join_frames(ring_scalar, heads_total, (last_ring,))
    heads_all = lax.all_gather(heads_join, "clip")
    heads_placed = place_heads(
        clip_scalar, level_count - 1, level_count, later["heads_all"], (), (packs[0],)
    )
    grad_down, grad_up, grad_proj = place_layer(
        clip_scalar, 0, level_count, tall_all, placed, level_count - 1, ()
    )
    last_join = join_frames(
        ring_scalar, half_sum(last_ring, ()), (), (grad_down, heads_placed)
    )
    last_pieces = clip_pieces(last_join)
    grad_in, vector, grad_proj = place_last(
        clip_scalar, feat_width, feat_wide, level_count, last_pieces, grad_proj
    )
    grad_heads = (place_heads(clip_scalar, 0, level_count, heads_all, (heads_placed,), ()),)


    def norm_sums(layer, first, row):
        return vector[8 * (2 * (level_count - 1 - layer) + first) + row]

    grad_mlp_gain = jnp.stack([norm_sums(layer, 0, 0) for layer in layers])
    grad_mlp_shift = jnp.stack([norm_sums(layer, 0, 1) for layer in layers])
    grad_proj_bias = jnp.stack([norm_sums(layer, 0, 2) for layer in layers])
    grad_attn_gain = jnp.stack([norm_sums(layer, 1, 0) for layer in layers])
    grad_attn_shift = jnp.stack([norm_sums(layer, 1, 1) for layer in layers])
    rest = vector[16 * level_count :]
    grad_down_bias = jnp.stack(
        [norm_sums(layer + 1, 1, 2) for layer in range(level_count - 1)]
        + [rest[16 + 3 * level_count]]
    )
    grad_qkv_bias = lax.dynamic_slice_in_dim(
        rest[16 : 16 + 3 * level_count], tensor_at * width, width, 1
    )
    grad_qkv_bias = grad_qkv_bias.reshape(level_count, 3, width)
    grad_up_bias = lax.dynamic_slice_in_dim(
        rest[24:].reshape(level_count, 4 * hidden_width), tensor_at * hidden_width, hidden_width, 1
    )
    act_count = cond_here.shape[1]
    return (
        block_out,
        grad_features[None, None],
        grad_in,
        norm_sums(0, 1, 2),
        rest[:act_count],
        rest[act_count],
        rest[8 : 8 + act_count],
        rest[8 + act_count],
        grad_attn_gain,
        grad_attn_shift,
        jnp.swapaxes(grad_heads[0], 1, 2),
        grad_qkv_bias,
        grad_proj,
        grad_proj_bias,
        grad_mlp_gain,
        grad_mlp_shift,
        grad_up,
        grad_up_bias,
        grad_down,
        grad_down_bias,
    )


def solution(mesh):
    return jax.shard_map(
        on_device,
        mesh=mesh,
        in_specs=(
            P("clip", "frame", None, "tensor"),
            P("clip", "frame", None, None),
            P("clip", None, None),
            P("tensor", None),
            P(),
            P(),
            P(),
            P(),
            P(),
            P(),
            P(),
            P(None, None, None, "tensor"),
            P(None, None, "tensor"),
            P(None, "tensor", None),
            P(),
            P(),
            P(),
            P(None, None, "tensor"),
            P(None, "tensor"),
            P(None, "tensor", None),
            P(),
            P("clip", "frame", None, None),
        ),
        out_specs=(
            P("clip", "frame", None, None),
            P("clip", "frame", None, "tensor"),
            P("tensor", None),
            P(),
            P(),
            P(),
            P(),
            P(),
            P(),
            P(),
            P(None, None, None, "tensor"),
            P(None, None, "tensor"),
            P(None, "tensor", None),
            P(),
            P(),
            P(),
            P(None, None, "tensor"),
            P(None, "tensor"),
            P(None, "tensor", None),
            P(),
        ),
        check_vma=False,
    )
```

```python
import functools

import jax
import jax.numpy as jnp
import numpy as np
from jax import lax
from jax.experimental import pallas as pl
from jax.experimental.pallas import tpu as pltpu
from jax.sharding import PartitionSpec as P

HEAD = 64
GRID_W = 16
EXTRA = 8

highest_precision = lax.Precision.HIGHEST
norm_epsilon = 1e-06
masked_score = -1000000000.0
low_type = jnp.bfloat16
wide_type = jnp.float32

CORE_SWAP = [(0, 1), (1, 0), (2, 3), (3, 2)]
CHIP_SWAP = [(0, 2), (2, 0), (1, 3), (3, 1)]
HALF_SWAP = [(i, (i + 4) % 8) for i in range(8)]


def clip_shift(step):
    return [(i, (i + step) % 4) for i in range(4)]


def frame_shift(halves, step):
    return [
        (4 * half + i, 4 * ((half + halves) % 2) + (i + step) % 4)
        for half in range(2)
        for i in range(4)
    ]


def core_swap(value):
    return lax.ppermute(value, "tensor", CORE_SWAP)


def chip_swap(value):
    return lax.ppermute(value, "tensor", CHIP_SWAP)


def halves_tensor(part):
    if not isinstance(part, tuple):
        half = part.shape[0] // 2
        part = (part[:half], part[half:])
    pair = part[0] + core_swap(part[1])
    quarter = pair.shape[0] // 2
    return pair[:quarter], chip_swap(pair[quarter:])


def join_rows_tensor(chunk):
    pair = jnp.concatenate([chunk, chip_swap(chunk)], axis=0)
    return jnp.concatenate([pair, core_swap(pair)], axis=0)


def to_heads(blocks):
    return [blocks[0]] + [
        lax.ppermute(blocks[step], "frame", frame_shift(0, step)) for step in range(1, 4)
    ]


def to_frames(blocks):
    return [blocks[0]] + [
        lax.ppermute(blocks[step], "frame", frame_shift(0, -step)) for step in range(1, 4)
    ]


def pairs_to_later_half(blocks):
    return [
        lax.ppermute(
            blocks[step],
            "frame",
            [(src, dst) for src, dst in frame_shift(1, step) if src < dst],
        )
        for step in range(4)
    ]


DOWN_HALF = [(i + 4, i) for i in range(4)]


def swap_clips(packs):
    return [packs[0]] + [
        lax.ppermute(packs[step], "clip", clip_shift(step)) for step in range(1, 4)
    ]


def ring_pieces(value):
    return [value] + [
        lax.ppermute(value, "frame", frame_shift(0, step)) for step in range(1, 4)
    ]


def ring_sends(part, ring):
    block = part.shape[0] // 4
    got = []
    for step in range(1, 4):
        sent = lax.dynamic_slice_in_dim(part, ((ring + step) % 4) * block, block, 0)
        got.append(lax.ppermute(sent.astype(low_type), "frame", frame_shift(0, step)))
    return got


def clip_pieces(joined):
    return [joined] + [
        lax.ppermute(joined, "clip", clip_shift(step)) for step in range(1, 4)
    ]


def rotary_tables(head_size, head_count):
    group_size = 2 * (head_size // 3 // 2)
    half_size = group_size // 2
    total_width = head_size * head_count
    swap_table = np.zeros((total_width, total_width), np.float32)
    rate_table = np.zeros((3, total_width), np.float32)
    for head_at in range(head_count):
        for axis_at in range(3):
            for pair_at in range(half_size):
                lower_at = head_at * head_size + axis_at * group_size + pair_at
                upper_at = lower_at + half_size
                swap_table[upper_at, lower_at] = -1.0
                swap_table[lower_at, upper_at] = 1.0
                rate_value = 10000.0 ** (-2.0 * pair_at / group_size)
                rate_table[axis_at, lower_at] = rate_value
                rate_table[axis_at, upper_at] = rate_value
    return swap_table, rate_table


def norm_rows(values):
    row_mean = jnp.mean(values, axis=-1, keepdims=True)
    centred = values - row_mean
    spread = jnp.mean(centred * centred, axis=-1, keepdims=True)
    inverse = lax.rsqrt(spread + norm_epsilon)
    return centred * inverse, inverse


def norm_kernel(gain_ref, shift_ref, *refs):
    terms, (stream_ref, hat_ref, inverse_ref, low_ref) = refs[:-4], refs[-4:]
    values = terms[0][...]
    if len(terms) > 1:
        values = values + (terms[1][...] + terms[2][...] + terms[3][...])
    hat, inverse = norm_rows(values)
    stream_ref[...] = values
    hat_ref[...] = hat
    inverse_ref[...] = jnp.broadcast_to(inverse, inverse_ref.shape)
    low_ref[...] = (hat * gain_ref[...] + shift_ref[...]).astype(low_type)


def block_kernel(stream_ref, kept_ref, got_ref, bias_ref, live_ref, out_ref):
    values = stream_ref[...] + (kept_ref[...] + got_ref[...] + bias_ref[...])
    out_ref[...] = (values * live_ref[:, 0:1]).astype(low_type)


def norm_back_kernel(count, kept_ref, got_ref, gain_ref, hat_ref, inverse_ref, grad_ref, out_ref, low_ref, sums_ref):
    grad = kept_ref[...] + got_ref[...]
    hat = hat_ref[...]
    scaled = grad * gain_ref[...]
    first = jnp.mean(scaled, axis=-1, keepdims=True)
    second = jnp.mean(scaled * hat, axis=-1, keepdims=True)
    out = grad_ref[...] + (scaled - first - hat * second) * inverse_ref[:, 0:1]
    low = out.astype(low_type)
    out_ref[...] = out
    low_ref[...] = low
    sums_ref[...] = jnp.zeros_like(sums_ref)
    sums_ref[0:1, :] = jnp.sum(grad * hat, axis=0, keepdims=True)
    sums_ref[1:2, :] = jnp.sum(grad, axis=0, keepdims=True)
    sums_ref[2:3, :] = jnp.sum(low[:count].astype(wide_type), axis=0, keepdims=True)


def exact_gelu(values):
    return jax.nn.gelu(values, approximate=False)


def dot_wide(left, right):
    return jnp.dot(left, right, preferred_element_type=wide_type)


def dot_dims(left, right, left_dim, right_dim):
    return lax.dot_general(
        left, right, (((left_dim,), (right_dim,)), ((), ())), preferred_element_type=wide_type
    )


def head_cols(at):
    return slice(at * HEAD, (at + 1) * HEAD)


def ring_back(place, step):
    return lax.rem(place - step + 4, 4)


def ring_ahead(place, step):
    return lax.rem(place + step, 4)


def project_kernel(heads, at_ref, rows_ref, key_w, value_w, query_w, bias_ref, cos_ref, sin_ref, swap_ref, *out_refs):
    rows = rows_ref[...]
    swap = swap_ref[...]
    cosine = jnp.concatenate([cos_ref[: rows.shape[0], :]] * heads, axis=1)
    sine = jnp.concatenate([sin_ref[: rows.shape[0], :]] * heads, axis=1)

    def turned(weight, bias):
        value = dot_wide(rows, weight[...]) + bias
        crossed = jnp.dot(value, swap, precision=highest_precision, preferred_element_type=wide_type)
        return value * cosine + crossed * sine

    key = turned(key_w, bias_ref[1:2, :]).astype(low_type)
    value = (dot_wide(rows, value_w[...]) + bias_ref[2:3, :]).astype(low_type)
    query = (turned(query_w, bias_ref[0:1, :]).astype(low_type).astype(wide_type) * HEAD ** (-0.5)).astype(low_type)

    def write(head, step):
        for at, part in enumerate((key, value, query)):
            out_refs[step][:, head_cols(at)] = part[:, head_cols(head)]
            if at < 2:
                out_refs[4 + step][:, head_cols(at)] = part[:, head_cols(head)]

    for ring in range(4):

        @pl.when(at_ref[0] == ring)
        def _(ring=ring):
            for step in range(4):
                write((ring + step) % 4, step)


def lane_tiles(total):
    size = 384 if total % 384 == 0 else total
    return [slice(at * size, (at + 1) * size) for at in range(total // size)]


def attend_kernel(bias_ref, mask_ref, *refs):
    own_refs, cross_refs = refs[:4], refs[4:8]
    out_ref, low_ref, total_ref, own_out, cross_out, query_ref, score_ref = refs[8:]
    rows = own_refs[0].shape[0]
    total_rows = 4 * rows
    for at in range(4):
        block = slice(at * rows, (at + 1) * rows)
        query_ref[block, :] = own_refs[at][:, head_cols(2)]
        own_out[block, :] = own_refs[at][...]
        cross_out[block, :] = cross_refs[at][...]
    total_ref[...] = jnp.zeros_like(total_ref)

    def pair(at, part):
        if at < 4:
            return own_refs[at][:, head_cols(part)]
        return cross_refs[at - 4][:, head_cols(part)]

    for tile in lane_tiles(total_rows):
        query = query_ref[tile, :]
        wide = tile.stop - tile.start
        top = jnp.full((1, wide), 2.0 * masked_score, wide_type)
        for at in range(8):
            scores = dot_dims(pair(at, 0), query, 1, 1) + bias_ref[:, at : at + 1]
            if at < 4:
                scores = scores + mask_ref[at : at + 1, tile]
            score_ref[at * rows : (at + 1) * rows, :] = scores
            top = jnp.maximum(top, jnp.max(scores, axis=0, keepdims=True))
        mass = jnp.zeros((1, wide), wide_type)
        out = jnp.zeros((HEAD, wide), wide_type)
        for at in range(8):
            weights = jnp.exp(score_ref[at * rows : (at + 1) * rows, :] - top)
            mass = mass + jnp.sum(weights, axis=0, keepdims=True)
            out = out + dot_dims(pair(at, 1), weights.astype(low_type), 0, 0)
        total_ref[0:1, tile] = top + jnp.log(mass)
        rows_out = (out / mass).T
        out_ref[tile, :] = rows_out
        low_ref[tile, :] = rows_out.astype(low_type)


def attend_back_kernel(own, bias_ref, mask_ref, total_ref, out_ref, own_ref, *refs):
    grad_refs, cross_refs = refs[:4], refs[4:-4]
    pair_sum, query_sum, query_ref, grad_ref = refs[-4:]
    rows = grad_refs[0].shape[0]
    query_ref[...] = own_ref[:, head_cols(2)]
    for at in range(4):
        grad_ref[at * rows : (at + 1) * rows, :] = grad_refs[at][...]
    ones = jnp.ones((8, HEAD), wide_type)
    pair_sum[...] = jnp.zeros_like(pair_sum)
    for tile in lane_tiles(4 * rows):
        query = query_ref[tile, :]
        grad = grad_ref[tile, :]
        centre = lax.dot_general(
            ones,
            grad.astype(wide_type) * out_ref[tile, :],
            (((1,), (1,)), ((), ())),
            precision=highest_precision,
            preferred_element_type=wide_type,
        )[0:1, :]
        total = total_ref[0:1, tile]
        query_part = jnp.zeros((HEAD, tile.stop - tile.start), wide_type)
        for at in range(4):
            block = slice(at * rows, (at + 1) * rows)
            if own:
                key, value = own_ref[block, head_cols(0)], own_ref[block, head_cols(1)]
                scores = dot_dims(key, query, 1, 1) + bias_ref[:, at : at + 1] + mask_ref[at : at + 1, tile]
            else:
                key, value = cross_refs[0][block, head_cols(0)], cross_refs[0][block, head_cols(1)]
                scores = dot_dims(key, query, 1, 1) + bias_ref[:, at + 4 : at + 5]
            weights = jnp.exp(scores - total)
            pair_sum[block, head_cols(1)] += dot_wide(weights.astype(low_type), grad)
            soft = dot_dims(value, grad, 1, 1)
            back = (weights * (soft - centre)).astype(low_type)
            pair_sum[block, head_cols(0)] += dot_wide(back, query)
            query_part = query_part + dot_dims(key, back, 0, 0)
        query_sum[tile, :] = query_part.T * HEAD ** (-0.5)


def head_grad_kernel(rows_ref, weight_ref, *out_refs):
    value = dot_dims(rows_ref[...], weight_ref[...], 1, 1).astype(low_type)
    for at, out_ref in enumerate(out_refs):
        out_ref[...] = value[:, head_cols(at)]


def turn_back_kernel(own_pair, other_pair, own_query, other_query, cos_ref, sin_ref, swap_ref, *out_refs):
    rows = out_refs[0].shape[0]
    swap = swap_ref[...]
    for at in range(4):
        block = slice(at * rows, (at + 1) * rows)
        cosine, sine = cos_ref[block, :], sin_ref[block, :]

        def turned(value):
            crossed = jnp.dot(value, swap, precision=highest_precision, preferred_element_type=wide_type)
            return (value * cosine - crossed * sine).astype(low_type)

        pair = own_pair[block, :] + other_pair[block, :]
        out_refs[at][:, head_cols(0)] = turned(pair[:, head_cols(0)])
        out_refs[at][:, head_cols(1)] = pair[:, head_cols(1)].astype(low_type)
        out_refs[at][:, head_cols(2)] = turned(own_query[block, :] + other_query[block, :])


def mix_back_kernel(at_ref, place_ref, key_w, value_w, query_w, *refs):
    mixed_refs = refs[:4]
    near_ref, far_ref, stack_ref, bias_ref = refs[4:]
    ring, clip = at_ref[0], at_ref[1]
    place = place_ref[...]
    total = None
    bias_ref[...] = jnp.zeros_like(bias_ref)
    for part, weight in ((0, key_w), (1, value_w), (2, query_w)):
        relative = jnp.concatenate([ref[:, head_cols(part)] for ref in mixed_refs], axis=1)
        ordered = dot_wide(relative, place)
        bias_ref[part : part + 1, :] = jnp.sum(ordered, axis=0, keepdims=True)
        term = dot_dims(ordered.astype(low_type), weight[...], 1, 1)
        total = term if total is None else total + term
    half = near_ref.shape[0]
    near_ref[...] = total[:half]
    far_ref[...] = total[half:]
    for at in range(4):
        stack_ref[lax.rem(ring + at - clip + 4, 4)] = mixed_refs[at][...]


def clip_products(at_ref, first_ref, second_ref, pack_refs, columns):
    out = None
    half = first_ref.shape[1]
    for step in range(4):
        place = ring_back(at_ref[0], step)
        pack = pack_refs[step]
        term = dot_dims(first_ref[place], pack[:half, columns], 0, 0)
        term = term + dot_dims(second_ref[place], pack[half : 2 * half, columns], 0, 0)
        out = term if out is None else out + term
    return out


def layer_grad_kernel(at_ref, act_a, act_b, norm_a, norm_b, *refs):
    head_refs, pack_refs, out_ref = refs[:-5], refs[-5:-1], refs[-1]
    part = out_ref.shape[1] // 2
    tiles = pl.num_programs(0) - (1 if head_refs else 0)

    @pl.when(pl.program_id(0) < tiles)
    def _():
        out_ref[:, :part] = clip_products(at_ref, act_a, act_b, pack_refs, slice(0, part))
        out_ref[:, part:] = clip_products(at_ref, norm_a, norm_b, pack_refs, slice(part, 2 * part))

    if head_refs:

        @pl.when(pl.program_id(0) == tiles)
        def _():
            columns = slice(2 * part, 3 * part)
            out_ref[:, :part] = clip_products(at_ref, head_refs[0], head_refs[2], pack_refs, columns)
            out_ref[:, part:] = clip_products(at_ref, head_refs[1], head_refs[3], pack_refs, columns)


def plain_grad_kernel(at_ref, rows_a, rows_b, *refs):
    pack_refs, out_ref = refs[:4], refs[4]
    out_ref[...] = clip_products(at_ref, rows_a, rows_b, pack_refs, slice(None))


def last_grad_kernel(tiles, at_ref, head_a, head_b, *refs):
    feat_refs, pack_refs, out_ref = refs[:4], refs[4:8], refs[8]
    head_rows = 2 * head_a.shape[1]
    feat_rows = head_rows + feat_refs[0].shape[0]

    @pl.when(pl.program_id(0) < tiles)
    def _():
        out = None
        for step in range(4):
            term = dot_dims(feat_refs[step][...], pack_refs[step][head_rows:feat_rows, :], 0, 0)
            out = term if out is None else out + term
        out_ref[...] = out

    @pl.when(pl.program_id(0) == tiles + 2)
    def _():
        out = None
        small = (pack_refs[0].shape[0] - feat_rows) // 2
        for step in range(4):
            high = pack_refs[step][feat_rows : feat_rows + small, :].astype(wide_type)
            term = high + pack_refs[step][feat_rows + small :, :].astype(wide_type)
            out = term if out is None else out + term
        high = out.astype(low_type).astype(wide_type)
        out_ref[:small, :] = high
        out_ref[small:, :] = out - high

    @pl.when((pl.program_id(0) >= tiles) & (pl.program_id(0) < tiles + 2))
    def _():
        out_ref[...] = clip_products(at_ref, head_a, head_b, pack_refs, slice(None))


def ring_sum_kernel(at_ref, part_ref, *refs):
    got_refs, out_ref = refs[:3], refs[3]
    block = out_ref.shape[0]
    out = part_ref[pl.ds(pl.multiple_of(at_ref[0] * block, 8), block), :]
    for got in got_refs:
        out = out + got[...].astype(wide_type)
    out_ref[...] = out


def ring_sum(ring_at, part, got, after):
    shape = (part.shape[0] // 4, part.shape[1])
    return call_kernel(
        ring_sum_kernel,
        (ring_at[None], part, *got),
        (0,),
        jax.ShapeDtypeStruct(shape, wide_type),
        [],
        4 * shape[0] * shape[1],
        0,
        after,
    )


def half_sum_kernel(own_ref, got_ref, out_ref):
    out_ref[...] = (own_ref[...] + got_ref[...]).astype(low_type)


def half_sum(own, after):
    got = lax.ppermute(own, "frame", HALF_SWAP)
    return call_kernel(
        half_sum_kernel,
        (own, got),
        (),
        jax.ShapeDtypeStruct(own.shape, low_type),
        [],
        own.size,
        0,
        after,
    )


def join_kernel(at_ref, *refs):
    out_ref = refs[4]
    block = refs[0].shape[0]
    for step in range(4):
        start = pl.multiple_of(ring_back(at_ref[0], step) * block, 16)
        out_ref[pl.ds(start, block), :] = refs[step][...]


def join_frames(ring_at, total, after, after_far=()):
    pieces = ring_pieces(total)
    return call_kernel(
        join_kernel,
        (ring_at[None], *pieces),
        (0,),
        jax.ShapeDtypeStruct((4 * total.shape[0], total.shape[1]), low_type),
        [],
        0,
        0,
        after,
        after_far,
    )


def beside_kernel(first_ref, second_ref, out_ref):
    half, wide, other = first_ref.shape[0] // 2, first_ref.shape[1], second_ref.shape[1]
    out_ref[:, :wide] = first_ref[:half, :]
    out_ref[:, wide : wide + other] = second_ref[:half, :]
    out_ref[:, wide + other :] = second_ref[half:, :]


def gather_clips(first, second, after):
    half, wide = first.shape[0] // 2, first.shape[1]
    beside = call_kernel(
        beside_kernel,
        (first, second),
        (),
        jax.ShapeDtypeStruct((half, wide + 2 * second.shape[1]), low_type),
        [],
        0,
        0,
        after,
    )
    return lax.all_gather(beside, "clip")


def take_kernel(whole_ref, out_ref):
    out_ref[...] = whole_ref[:, :, : out_ref.shape[2]]


def with_other_core(whole, wide, after):
    shape = (*whole.shape[:2], wide)
    columns = pl.pallas_call(
        without(take_kernel, 1, after),
        grid=(1,),
        out_shape=jax.ShapeDtypeStruct(shape, low_type),
        in_specs=[pl.BlockSpec(shape, lambda i: (0, 0, 0))] + any_specs(after),
        out_specs=pl.BlockSpec(shape, lambda i: (0, 0, 0)),
        compiler_params=kernel_params(),
    )(whole, *after)
    return whole, core_swap(columns)


def smem_spec():
    return pl.BlockSpec(memory_space=pltpu.SMEM)


def kernel_params():
    return pltpu.CompilerParams(vmem_limit_bytes=48 * 1024 * 1024)


def held_spec():
    return pl.BlockSpec(memory_space=pltpu.VMEM)


def any_specs(arrays):
    return [pl.BlockSpec(memory_space=pl.ANY)] * len(arrays)


def mark(value):
    while value.ndim > 2:
        value = value[0]
    return value[:8, :128]


def without(kernel, count, after):
    return lambda *refs: kernel(*refs[:count], *refs[count + len(after) :])


def layer_grad(clip_at, second_all, packs, first_all, after):
    whole, other = second_all
    half, wide = other.shape[1:]
    tiles = wide // 128
    part = 256
    block = (4, half, 128)
    heads = () if first_all is None else (first_all[0],) * 4
    held = [
        pl.BlockSpec(block, lambda i, at=at: (0, 0, tiles + at)) for at in range(len(heads))
    ]

    def moving(start):
        return pl.BlockSpec(block, lambda i: (0, 0, start + jnp.minimum(i, tiles - 1)))

    return pl.pallas_call(
        without(layer_grad_kernel, 9 + len(heads), after),
        grid=(tiles + (1 if heads else 0),),
        out_shape=jax.ShapeDtypeStruct((wide + (128 if heads else 0), 2 * part), wide_type),
        in_specs=[smem_spec(), moving(tiles), moving(2 * tiles), moving(0), moving(0)]
        + held
        + [held_spec()] * 4
        + any_specs(after),
        out_specs=pl.BlockSpec((128, 2 * part), lambda i: (i, 0)),
        compiler_params=kernel_params(),
        cost_estimate=pl.CostEstimate(
            flops=32 * half * wide * part,
            bytes_accessed=2 * whole.size + 8 * wide * part,
            transcendentals=0,
        ),
    )(clip_at[None], whole, whole, whole, other, *heads, *packs, *after)


def plain_grad(clip_at, rows_all, packs, after):
    whole, other = rows_all
    half, count = other.shape[1:]
    part = packs[0].shape[1]
    block = pl.BlockSpec((4, half, 128), lambda i: (0, 0, i))
    return pl.pallas_call(
        without(plain_grad_kernel, 7, after),
        grid=(count // 128,),
        out_shape=jax.ShapeDtypeStruct((count, part), wide_type),
        in_specs=[smem_spec(), block, block] + [held_spec()] * 4 + any_specs(after),
        out_specs=pl.BlockSpec((128, part), lambda i: (i, 0)),
        compiler_params=kernel_params(),
        cost_estimate=pl.CostEstimate(
            flops=16 * half * count * part,
            bytes_accessed=16 * half * count + 4 * count * part,
            transcendentals=0,
        ),
    )(clip_at[None], whole, other, *packs, *after)


def last_grad(clip_at, first_all, feats, packs, after, after_far):
    whole, other = first_all
    half, part = other.shape[1], packs[0].shape[1]
    first_block = other.shape[2] // 128
    tiles = feats[0].shape[1] // 128
    kernel = functools.partial(last_grad_kernel, tiles)
    after_far = tuple(mark(value) for value in after_far)

    def moving(start):
        return pl.BlockSpec(
            (4, half, 128), lambda i: (0, 0, start + jnp.clip(i - tiles, 0, 1))
        )

    return pl.pallas_call(
        without(kernel, 11, (*after, *after_far)),
        grid=(tiles + 3,),
        out_shape=jax.ShapeDtypeStruct(((tiles + 3) * 128, part), wide_type),
        in_specs=[smem_spec(), moving(first_block), moving(first_block + 2)]
        + [pl.BlockSpec((feats[0].shape[0], 128), lambda i: (0, jnp.minimum(i, tiles - 1)))] * 4
        + [held_spec()] * 4
        + any_specs(after)
        + any_specs(after_far),
        out_specs=pl.BlockSpec((128, part), lambda i: (i, 0)),
        compiler_params=kernel_params(),
    )(clip_at[None], whole, whole, *feats, *packs, *after, *after_far)


def by_clip(clip_at, write):
    for place in range(4):

        @pl.when(clip_at == place)
        def _(place=place):
            for step in range(4):
                write((place - step) % 4, step)


def place_layer_kernel(tiles, at_ref, all_ref, *outs):
    part = all_ref.shape[2] // 2
    is_last = pl.program_id(0) == tiles

    for place in range(4):
        columns = slice(place * part, (place + 1) * part)
        left = all_ref[place, :, :part].astype(wide_type)
        right = all_ref[place, :, part:].astype(wide_type)

        @pl.when(jnp.logical_not(is_last))
        def _(columns=columns, left=left, right=right):
            outs[0][0, :, columns] = left
            outs[1][0, :, columns] = right

        if len(outs) > 2:

            @pl.when(is_last)
            def _(columns=columns, left=left, right=right):
                outs[2][0, : outs[2].shape[1] // 2, columns] = left
                outs[2][0, outs[2].shape[1] // 2 :, columns] = right


def place_layer(clip_at, layer, levels, joined, earlier, heads_layer, after):
    part = joined.shape[2] // 2
    rows = 4 * part
    tiles = rows // 128
    heads = joined.shape[1] > rows
    out = [(levels, rows, 4 * part)] * 2 + [(levels, 256, 4 * part)] * heads
    tall = pl.BlockSpec((1, 128, 4 * part), lambda i: (layer, jnp.minimum(i, tiles - 1), 0))
    wide = pl.BlockSpec((1, 256, 4 * part), lambda i: (heads_layer, 0, 0))
    return pl.pallas_call(
        without(functools.partial(place_layer_kernel, tiles), 2, (*earlier, *after)),
        grid=(tiles + (1 if heads else 0),),
        out_shape=tuple(jax.ShapeDtypeStruct(shape, wide_type) for shape in out),
        in_specs=[smem_spec(), pl.BlockSpec((4, 128, 2 * part), lambda i: (0, i, 0))]
        + any_specs(earlier)
        + any_specs(after),
        out_specs=(tall, tall) + ((wide,) if heads else ()),
        input_output_aliases={2 + at: at for at in range(len(earlier))},
        compiler_params=kernel_params(),
    )(clip_at[None], joined, *earlier, *after)


def place_last_kernel(skip, at_ref, *refs):
    pieces = refs[:4]
    in_ref, small_ref, proj_ref = refs[-3:]
    part = pieces[0].shape[1]
    heads = skip + proj_ref.shape[1]
    small = small_ref.shape[0]

    def write(place, step):
        columns = slice(place * part, (place + 1) * part)
        piece = pieces[step]
        in_ref[:, columns] = piece[: in_ref.shape[0], :].astype(wide_type)
        proj_ref[0, :, columns] = piece[skip:heads, :].astype(wide_type)
        small_ref[:, columns] = piece[heads : heads + small, :].astype(wide_type) + piece[
            heads + small :, :
        ].astype(wide_type)

    by_clip(at_ref[0], write)


def place_last(clip_at, feat_rows, skip, levels, pieces, earlier):
    part = pieces[0].shape[1]
    return pl.pallas_call(
        functools.partial(place_last_kernel, skip),
        grid=(1,),
        out_shape=(
            jax.ShapeDtypeStruct((feat_rows, 4 * part), wide_type),
            jax.ShapeDtypeStruct((64, 4 * part), wide_type),
            jax.ShapeDtypeStruct((levels, 256, 4 * part), wide_type),
        ),
        in_specs=[smem_spec()]
        + [pl.BlockSpec(pieces[0].shape, lambda i: (0, 0))] * 4
        + [pl.BlockSpec(memory_space=pl.ANY)],
        out_specs=(
            pl.BlockSpec((feat_rows, 4 * part), lambda i: (0, 0)),
            pl.BlockSpec((64, 4 * part), lambda i: (0, 0)),
            pl.BlockSpec((1, 256, 4 * part), lambda i: (0, 0, 0)),
        ),
        input_output_aliases={5: 2},
        compiler_params=kernel_params(),
    )(clip_at[None], *pieces, earlier)


def pack_kernel(by_rows, count, at_ref, *refs):
    parts, outs = refs[:count], refs[count:]
    for clip in range(4):

        @pl.when(at_ref[0] == clip)
        def _(clip=clip):
            for step in range(4):
                place, start = (clip + step) % 4, 0
                for part in parts:
                    size = part.shape[1] // 4
                    value = part[:, place * size : (place + 1) * size]
                    if by_rows:
                        outs[step][start : start + part.shape[0], :] = value
                        start += part.shape[0]
                    else:
                        outs[step][:, start : start + size] = value
                        start += size


def pack_parts(clip_at, parts, by_rows, after):
    sizes = [part.shape[1] // 4 for part in parts]
    if by_rows:
        shape = (sum(part.shape[0] for part in parts), sizes[0])
    else:
        shape = (parts[0].shape[0], sum(sizes))
    return call_kernel(
        functools.partial(pack_kernel, by_rows, len(parts)),
        (clip_at[None], *parts),
        (0,),
        tuple(jax.ShapeDtypeStruct(shape, low_type) for _ in range(4)),
        [],
        0,
        0,
        after,
    )


def place_heads_kernel(at_ref, all_ref, *refs):
    out_ref = refs[-1]
    for place in range(4):
        piece = all_ref[place].astype(wide_type)
        for at, part in ((1, 0), (2, 1), (0, 2)):
            out_ref[0, at, :, head_cols(place)] = piece[:, head_cols(part)]


def place_heads(clip_at, layer, levels, joined, earlier, after):
    rows = joined.shape[1]
    tile = 256
    count = 2
    return pl.pallas_call(
        without(place_heads_kernel, count, (*earlier, *after)),
        grid=(rows // tile,),
        out_shape=jax.ShapeDtypeStruct((levels, 3, rows, 4 * HEAD), wide_type),
        in_specs=[smem_spec(), pl.BlockSpec((4, tile, 3 * HEAD), lambda i: (0, i, 0))]
        + any_specs(earlier)
        + any_specs(after),
        out_specs=pl.BlockSpec((1, 3, tile, 4 * HEAD), lambda i: (layer, 0, i, 0)),
        input_output_aliases={count + at: at for at in range(len(earlier))},
        compiler_params=kernel_params(),
    )(clip_at[None], joined, *earlier, *after)


def stack_kernel(*refs):
    out_ref = refs[-1]
    for at, ref in enumerate(refs[:-1]):
        out_ref[8 * at : 8 * (at + 1), :] = ref[...]


def feature_grad_kernel(ids_ref, rows_ref, weight_ref, out_ref):
    size = rows_ref.shape[0] // 4
    for at in range(4):
        start = pl.multiple_of(ids_ref[at] * size, 8)
        out_ref[pl.ds(start, size), :] = dot_dims(
            rows_ref[at * size : (at + 1) * size, :], weight_ref[...], 1, 1
        )


def last_pack_kernel(at_ref, head_ref, patch_ref, small_a, small_b, *outs):
    heads, patches, small = head_ref.shape[0], patch_ref.shape[0], small_a.shape[0]
    values = small_a[...] + small_b[...]
    high = values.astype(low_type)
    rest = (values - high.astype(wide_type)).astype(low_type)
    for clip in range(4):

        @pl.when(at_ref[0] == clip)
        def _(clip=clip):
            for step in range(4):
                size = outs[step].shape[1]
                place = (clip + step) % 4
                columns = slice(place * size, (place + 1) * size)
                outs[step][:heads, :] = head_ref[:, columns]
                outs[step][heads : heads + patches, :] = patch_ref[:, columns]
                outs[step][heads + patches : heads + patches + small, :] = high[:, columns]
                outs[step][heads + patches + small :, :] = rest[:, columns]


def call_kernel(kernel, args, in_smem, outs, scratch, flops, exps, after=(), after_far=(), piped=()):
    count = len(args)

    def spec(at):
        if at in piped:
            return pl.BlockSpec(args[at].shape, lambda i, rank=args[at].ndim: (0,) * rank)
        return pl.BlockSpec(memory_space=pltpu.SMEM if at in in_smem else pltpu.VMEM)

    specs = [spec(at) for at in range(count)]
    after = (*after, *(mark(value) for value in after_far))
    specs += any_specs(after)
    moved = sum(a.size * a.dtype.itemsize for a in args)
    return pl.pallas_call(
        without(kernel, count, after),
        grid=(1,),
        out_shape=outs,
        in_specs=specs,
        out_specs=jax.tree.map(lambda _: pl.BlockSpec(memory_space=pltpu.VMEM), outs),
        scratch_shapes=scratch,
        compiler_params=kernel_params(),
        cost_estimate=pl.CostEstimate(flops=flops, bytes_accessed=moved, transcendentals=exps),
    )(*args, *after)


def on_device(
    features,
    cond_values,
    cond_live,
    in_weight,
    in_bias,
    act_weight,
    act_bias,
    state_weight,
    state_bias,
    attn_gain,
    attn_shift,
    qkv_weight,
    qkv_bias,
    proj_weight,
    proj_bias,
    mlp_gain,
    mlp_shift,
    up_weight,
    up_bias,
    down_weight,
    down_bias,
    out_grad,
):
    patch_rows = features.shape[2]
    feat_width = features.shape[3]
    slot_count = cond_values.shape[2]
    all_frames = cond_live.shape[1]
    model_width = in_weight.shape[1]
    width = qkv_weight.shape[3]
    heads = width // HEAD
    level_count = attn_gain.shape[0]
    patches = patch_rows // 4
    chunk_rows = patches + EXTRA
    rows = 4 * chunk_rows
    hidden_width = up_weight.shape[2]

    tensor_at = lax.axis_index("tensor")
    chip_at, core_at = tensor_at // 2, tensor_at % 2
    frame_at = lax.axis_index("frame")
    half_at, ring_at = frame_at // 4, frame_at % 4
    clip_at = lax.axis_index("clip")

    chunk_ids = [
        2 * jnp.bitwise_xor(core_at, core_step) + jnp.bitwise_xor(chip_at, chip_step)
        for core_step in range(2)
        for chip_step in range(2)
    ]
    own_chunk = chunk_ids[0]
    own_frames = jnp.stack([4 * half_at + (ring_at - step) % 4 for step in range(4)])
    cross_frames = jnp.stack([4 * (1 - half_at) + (ring_at - step) % 4 for step in range(4)])

    within = lax.broadcasted_iota(jnp.int32, (chunk_rows, 1), 0)
    is_patch = within < patches
    heights, columns = [], []
    for chunk_id in chunk_ids:
        patch_id = chunk_id * patches + within
        heights.append(jnp.where(is_patch, patch_id // GRID_W, 0))
        columns.append(jnp.where(is_patch, patch_id % GRID_W, 0))
    heights = jnp.concatenate(heights, axis=0).astype(wide_type)
    columns = jnp.concatenate(columns, axis=0).astype(wide_type)
    swap_table, rate_table = rotary_tables(HEAD, heads)
    swap_heads = jnp.asarray(swap_table)
    swap_one = jnp.asarray(swap_table[:HEAD, :HEAD])
    rates = rate_table[:, :HEAD]
    place_angles = heights * rates[1] + columns * rates[2]
    angles = jnp.concatenate(
        [
            own_frames[step].astype(wide_type) * rates[0][None, :] + place_angles
            for step in range(4)
        ],
        axis=0,
    )
    cosine_four, sine_four = jnp.cos(angles), jnp.sin(angles)
    head_from = jnp.arange(width)
    head_to = ((head_from // HEAD + ring_at) % 4) * HEAD + head_from % HEAD
    head_place = (head_to[:, None] == head_from[None, :]).astype(low_type)
    proj_turned = [
        lax.dynamic_slice_in_dim(
            jnp.concatenate([proj_weight[layer], proj_weight[layer]], axis=0),
            ring_at * HEAD,
            width,
            0,
        )
        for layer in range(level_count)
    ]
    ring_scalar = ring_at.astype(jnp.int32)
    clip_scalar = clip_at.astype(jnp.int32)

    live_all = cond_live[0].astype(wide_type)
    own_slots = lax.dynamic_index_in_dim(live_all, frame_at, 0, False)

    def live_rows(slots, chunk_id):
        picked = jnp.where(
            chunk_id < slot_count,
            lax.dynamic_index_in_dim(slots, jnp.minimum(chunk_id, slot_count - 1), 1, False),
            0.0,
        )
        return jnp.where(is_patch, 1.0, jnp.where(within == patches, picked[None, :], 0.0))

    sources = jnp.concatenate([own_frames, cross_frames])
    source_live = jnp.take(live_all, sources, axis=0)
    key_live = jnp.concatenate([live_rows(source_live, c) for c in chunk_ids], axis=0)
    reached = jnp.concatenate([jnp.ones((4,), jnp.bool_), jnp.full((4,), half_at == 1)])
    key_bias = jnp.where((key_live > 0.5) & reached[None, :], 0.0, masked_score).astype(wide_type)
    seen = own_frames[:, None] <= own_frames[None, :]
    causal = jnp.where(seen, 0.0, masked_score).astype(wide_type)
    causal = jnp.pad(jnp.repeat(causal, rows, axis=1), ((0, 4), (0, 0)))
    own_live = live_rows(own_slots[None, :], own_chunk)

    def extra_rows(slot_rows):
        picked = lax.dynamic_slice_in_dim(
            slot_rows, jnp.minimum(own_chunk, slot_count - 1), 1, 0
        )
        picked = jnp.where(own_chunk < slot_count, picked, jnp.zeros_like(picked))
        return jnp.pad(picked, ((0, EXTRA - 1), (0, 0)))

    cond_here = cond_values[0, 0]
    act_rows = jnp.dot(cond_here, act_weight, precision=highest_precision) + act_bias
    state_rows = jnp.dot(cond_here, state_weight, precision=highest_precision) + state_bias
    even_slot = (jnp.arange(slot_count) % 2 == 0)[:, None]
    cond_x = jnp.where(even_slot, act_rows, state_rows) * own_slots[:, None]

    flat_feat = jnp.concatenate(
        [
            lax.dynamic_slice_in_dim(features[0, 0], c * patches, patches, 0)
            for c in chunk_ids
        ],
        axis=0,
    )
    kept, got = halves_tensor(dot_wide(flat_feat, in_weight))
    stream = jnp.concatenate([kept + got + in_bias, extra_rows(cond_x)], axis=0)

    feat_wide = -(-feat_width // 128) * 128
    feat_low = jnp.pad(flat_feat, ((0, 0), (0, feat_wide - feat_width)))
    feats = [feat_low] + [
        lax.ppermute(feat_low, "clip", clip_shift(step)) for step in range(1, 4)
    ]
    pair_work = 2 * 32 * rows * rows * HEAD
    pair_exps = 32 * rows * rows
    weight_parts = [
        [qkv_weight[layer, :, at] for at in (1, 2, 0)] for layer in range(level_count)
    ]

    def norm(terms, gain, shift, after_far=()):
        chunk = jax.ShapeDtypeStruct((chunk_rows, model_width), wide_type)
        return call_kernel(
            norm_kernel,
            (gain[None], shift[None], *terms),
            (),
            (
                chunk,
                chunk,
                jax.ShapeDtypeStruct((chunk_rows, 128), wide_type),
                jax.ShapeDtypeStruct((chunk_rows, model_width), low_type),
            ),
            [],
            12 * chunk_rows * model_width,
            0,
            (),
            after_far,
        )

    def norm_back(part, gain, hat, inverse, grad, count, after=(), after_far=()):
        kept, got = halves_tensor(part)
        return call_kernel(
            functools.partial(norm_back_kernel, count),
            (kept, got, gain[None], hat, inverse, grad),
            (),
            (
                jax.ShapeDtypeStruct((chunk_rows, model_width), wide_type),
                jax.ShapeDtypeStruct((chunk_rows, model_width), low_type),
                jax.ShapeDtypeStruct((8, model_width), wide_type),
            ),
            [],
            16 * chunk_rows * model_width,
            0,
            after,
            after_far,
            (2, 3, 4, 5),
        )

    slot_grads = out_grad[0, 0, patch_rows:] * own_slots[:, None].astype(low_type)
    slot_blocks = jnp.concatenate(
        [
            jnp.pad(slot_grads[:, None], ((0, 0), (0, EXTRA - 1), (0, 0))),
            jnp.zeros((4 - slot_count, EXTRA, model_width), low_type),
        ],
        axis=0,
    )
    branch_parts = []
    for chunk_id in chunk_ids:
        branch_parts.append(
            lax.dynamic_slice_in_dim(out_grad[0, 0], chunk_id * patches, patches, 0)
        )
        branch_parts.append(lax.dynamic_index_in_dim(slot_blocks, chunk_id, 0, False))
    first_branch = jnp.concatenate(branch_parts, axis=0)
    stored = []
    terms = (stream,)
    before = None
    for layer in range(level_count):
        stream, hat_one, inverse_one, first_chunk = norm(terms, attn_gain[layer], attn_shift[layer])
        first_in = join_rows_tensor(first_chunk)
        bias = jnp.pad(qkv_bias[layer], ((0, 5), (0, 0)))
        heads_out = call_kernel(
            functools.partial(project_kernel, heads),
            (
                ring_scalar[None],
                first_in,
                *weight_parts[layer],
                bias,
                cosine_four,
                sine_four,
                swap_heads,
            ),
            (0,),
            tuple(
                jax.ShapeDtypeStruct((rows, count * HEAD), low_type)
                for count in (3, 3, 3, 3, 2, 2, 2, 2)
            ),
            [],
            6 * rows * model_width * width,
            0,
            (),
            () if before is None else (before[0],),
            (2, 3, 4, 5, 6, 7, 8),
        )
        blocks = to_heads(heads_out[:4])
        cross = pairs_to_later_half(heads_out[4:])
        attn_wide, attn_turned, log_total, own_all, cross_all = call_kernel(
            attend_kernel,
            (key_bias, causal, *blocks, *cross),
            (),
            (
                jax.ShapeDtypeStruct((4 * rows, HEAD), wide_type),
                jax.ShapeDtypeStruct((4 * rows, HEAD), low_type),
                jax.ShapeDtypeStruct((8, 4 * rows), wide_type),
                jax.ShapeDtypeStruct((4 * rows, 3 * HEAD), low_type),
                jax.ShapeDtypeStruct((4 * rows, 2 * HEAD), low_type),
            ),
            [
                pltpu.VMEM((4 * rows, HEAD), low_type),
                pltpu.VMEM((8 * rows, lane_tiles(4 * rows)[0].stop), wide_type),
            ],
            2 * pair_work,
            pair_exps,
            tuple(feats[1:]) if layer == 0 else (),
        )
        attn_relative = jnp.concatenate(
            to_frames([attn_turned[at * rows : (at + 1) * rows] for at in range(4)]), axis=1
        )
        attn_low = dot_wide(attn_relative, head_place).astype(low_type)
        if layer < level_count - 1:
            first_all = gather_clips(first_in, attn_low, ())
        kept, got = halves_tensor(dot_wide(attn_relative, proj_turned[layer]))
        middle, hat_two, inverse_two, second_chunk = norm(
            (stream, kept, got, proj_bias[layer][None]), mlp_gain[layer], mlp_shift[layer],
            () if before is None else (before[1], first_branch),
        )
        second_in = join_rows_tensor(second_chunk)
        hidden = dot_wide(second_in, up_weight[layer]) + up_bias[layer]
        active_low = exact_gelu(hidden).astype(low_type)
        second_all = gather_clips(second_in, active_low, ())
        if layer == level_count - 1:
            first_all = (first_in, attn_low)
        before = (first_all, second_all)
        kept, got = halves_tensor(dot_wide(active_low, down_weight[layer]))
        terms = (middle, kept, got, down_bias[layer][None])
        stored.append(
            (
                hat_one,
                inverse_one,
                own_all,
                cross_all,
                log_total,
                attn_wide,
                hat_two,
                inverse_two,
                hidden,
                first_all,
                second_all,
            )
        )
    def in_order(full, count):
        out = jnp.zeros((4 * count,) + full.shape[1:], full.dtype)
        size = full.shape[0] // 4
        for at, chunk_id in enumerate(chunk_ids):
            out = lax.dynamic_update_slice_in_dim(
                out, full[at * size : at * size + count], chunk_id * count, 0
            )
        return out

    def block_rows(after):
        low = call_kernel(
            block_kernel,
            (*terms, jnp.broadcast_to(own_live, (chunk_rows, 128))),
            (),
            jax.ShapeDtypeStruct((chunk_rows, model_width), low_type),
            [],
            4 * chunk_rows * model_width,
            0,
            after,
        )
        return join_rows_tensor(low)

    def block_in_order(block_full):
        slot_full = jnp.concatenate(
            [
                block_full[at * chunk_rows + patches : at * chunk_rows + patches + 1]
                for at in range(4)
            ],
            axis=0,
        )
        return jnp.concatenate(
            [in_order(block_full, patches), in_order(slot_full, 1)[:slot_count]], axis=0
        )[None, None]

    own_out = lax.dynamic_slice_in_dim(out_grad[0, 0], own_chunk * patches, patches, 0)
    grad_stream = (
        jnp.concatenate(
            [
                own_out.astype(wide_type),
                extra_rows(out_grad[0, 0, patch_rows:].astype(wide_type)),
            ],
            axis=0,
        )
        * own_live
    )

    small = {}
    small["down", level_count - 1] = jnp.sum(grad_stream, axis=0)
    sums_list = []
    wide_part = model_width // 4
    later = None
    for layer in reversed(range(level_count)):
        (
            hat_one,
            inverse_one,
            own_all,
            cross_all,
            log_total,
            attn_wide,
            hat_two,
            inverse_two,
            hidden,
            first_all,
            second_all,
        ) = stored[layer]
        branch = first_branch if later is None else join_rows_tensor(branch_chunk)
        if later is not None:
            first_all = with_other_core(first_all, model_width, (branch,))
            second_all = with_other_core(second_all, model_width, (branch,))
        _, gelu_pull = jax.vjp(exact_gelu, hidden)
        grad_hidden = gelu_pull(dot_dims(branch, down_weight[layer], 1, 1))[0].astype(low_type)
        small["up", layer] = jnp.sum(grad_hidden.astype(wide_type), axis=0)
        parts = [branch, grad_hidden] + ([] if later is None else [later["proj_out"]])
        packs = pack_parts(clip_scalar, parts, False, ())
        grad_middle, proj_chunk, sums = norm_back(
            dot_dims(grad_hidden, up_weight[layer], 1, 1),
            mlp_gain[layer],
            hat_two,
            inverse_two,
            grad_stream,
            chunk_rows,
            (packs[0],) if later is None else (packs[0], later["tall_join"]),
            () if later is None else (later["heads_sum"],),
        )
        sums_list.append(sums)
        packs = swap_clips(packs)
        if later is None:
            second_all = with_other_core(second_all, model_width, (proj_chunk,))
            block_full = block_rows((proj_chunk,))
            block_out = block_in_order(block_full)
        proj_out = join_rows_tensor(proj_chunk)
        grads = to_heads(
            call_kernel(
                head_grad_kernel,
                (proj_out, proj_turned[layer]),
                (),
                tuple(jax.ShapeDtypeStruct((rows, HEAD), low_type) for _ in range(4)),
                [],
                2 * rows * model_width * width,
                0,
                piped=(1,),
            )
        )

        if later is not None:
            later["heads_ring"] = ring_sum(
                ring_scalar, later["heads_sum"], later["heads_got"], (proj_chunk,)
            )

            later["tall_all"] = lax.all_gather(later["tall_join"], "clip")

        def attend_back(own, after, after_far=()):
            return call_kernel(
                functools.partial(attend_back_kernel, own),
                (key_bias, causal, log_total, attn_wide, own_all, *grads)
                + (() if own else (cross_all,)),
                (),
                (
                    jax.ShapeDtypeStruct((4 * rows, 2 * HEAD), wide_type),
                    jax.ShapeDtypeStruct((4 * rows, HEAD), wide_type),
                ),
                [
                    pltpu.VMEM((4 * rows, HEAD), low_type),
                    pltpu.VMEM((4 * rows, HEAD), low_type),
                ],
                5 * pair_work // 2,
                pair_exps // 2,
                after,
                after_far,
                (0, 1, 2, 3, 4) if own else (0, 1, 2, 3, 4, 9),
            )

        cross_pair, cross_query = attend_back(
            False, () if later is None else (later["heads_ring"],)
        )
        got_pair = lax.ppermute(cross_pair, "frame", DOWN_HALF)
        if later is None:
            first_all = with_other_core(
                gather_clips(*first_all, (cross_pair,)), model_width, (cross_pair,)
            )
        tall_sum = layer_grad(
            clip_scalar,
            second_all,
            packs,
            None if later is None else later["first_all"],
            (cross_pair,),
        )
        own_pair, own_query = attend_back(
            True, (), (tall_sum,) if later is None else (tall_sum, later["tall_all"], block_full[rows // 2 :])
        )
        tall_got = ring_sends(tall_sum, ring_at)
        if later is not None:
            later["heads_total"] = half_sum(later["heads_ring"], (own_pair,))
        tall_ring = ring_sum(ring_scalar, tall_sum, tall_got, ())
        tall_total = half_sum(tall_ring, ())
        turned = call_kernel(
            turn_back_kernel,
            (own_pair, got_pair, own_query, cross_query, cosine_four, sine_four, swap_one),
            (),
            tuple(jax.ShapeDtypeStruct((rows, 3 * HEAD), low_type) for _ in range(4)),
            [],
            24 * rows * HEAD * HEAD,
            0,
            (tall_ring,) if later is None else (tall_ring, later["heads_total"]),
            (),
            (4, 5, 6),
        )
        mixed = to_frames(list(turned))
        if later is not None:
            later["heads_join"] = join_frames(ring_scalar, later["heads_total"], (turned[0],))
        normed_near, normed_far, mixed_stack, bias_sums = call_kernel(
            mix_back_kernel,
            (
                jnp.stack([ring_scalar, clip_scalar]),
                head_place,
                *weight_parts[layer],
                *mixed,
            ),
            (0,),
            (
                jax.ShapeDtypeStruct((rows // 2, model_width), wide_type),
                jax.ShapeDtypeStruct((rows // 2, model_width), wide_type),
                jax.ShapeDtypeStruct((4, rows, 3 * HEAD), low_type),
                jax.ShapeDtypeStruct((8, width), wide_type),
            ),
            [],
            6 * rows * model_width * width,
            0,
            (tall_total,) if later is None else (tall_total, later["heads_join"]),
            (),
            (1, 2, 3, 4),
        )
        small["qkv", layer] = jnp.concatenate([bias_sums[2:3], bias_sums[:2]], axis=0)
        packs = swap_clips([mixed_stack[step] for step in range(4)])
        grad_stream, branch_chunk, sums = norm_back(
            (normed_near, normed_far),
            attn_gain[layer],
            hat_one,
            inverse_one,
            grad_middle,
            patches if layer == 0 else chunk_rows,
        )
        sums_list.append(sums)
        tall_join = join_frames(ring_scalar, tall_total, (branch_chunk,))

        heads_sum = plain_grad(clip_scalar, first_all, packs, (branch_chunk,))
        heads_got = ring_sends(heads_sum, ring_at)
        if layer > 0:
            later = {
                "proj_out": proj_out,
                "first_all": first_all,
                "tall_join": tall_join,
                "heads_sum": heads_sum,
                "heads_got": heads_got,
            }

    patch_chunk = branch_chunk[:patches]
    grad_patch = join_rows_tensor(patch_chunk)
    grad_features = call_kernel(
        feature_grad_kernel,
        (jnp.stack(chunk_ids).astype(jnp.int32), grad_patch, in_weight),
        (0,),
        jax.ShapeDtypeStruct((patch_rows, feat_width), wide_type),
        [],
        2 * patch_rows * feat_width * model_width,
        0,
        piped=(2,),
    )
    slot_row = grad_stream[patches : patches + 1] * own_live[patches : patches + 1]
    own_cond = lax.dynamic_slice_in_dim(
        cond_here, jnp.minimum(own_chunk, slot_count - 1), 1, 0
    )
    slot_part = jnp.concatenate([own_cond.T * slot_row, slot_row], axis=0)
    here = own_chunk < slot_count
    is_act = here & (own_chunk % 2 == 0)
    is_state = here & (own_chunk % 2 == 1)
    act_part = jnp.where(is_act, slot_part, 0.0)
    state_part = jnp.where(is_state, slot_part, 0.0)

    def at_tensor(value, total):
        return lax.dynamic_update_slice(
            jnp.zeros((value.shape[0], total), wide_type),
            value,
            (0, tensor_at * value.shape[1]),
        )

    layers = range(level_count)
    qkv_rows = at_tensor(
        jnp.concatenate([small["qkv", layer] for layer in layers], axis=0), 4 * width
    )
    mixed_rows = jnp.concatenate(
        [qkv_rows, small["down", level_count - 1][None], jnp.zeros_like(qkv_rows[:1])], axis=0
    )
    ups = at_tensor(jnp.stack([small["up", layer] for layer in layers]), 4 * hidden_width)
    parts = [*sums_list, act_part, state_part, mixed_rows, ups.reshape(-1, model_width)]
    vector = call_kernel(
        stack_kernel,
        tuple(parts),
        (),
        jax.ShapeDtypeStruct((8 * len(parts), model_width), wide_type),
        [],
        0,
        0,
    )
    vector = vector + core_swap(vector)
    later["heads_all"] = lax.all_gather(later["heads_join"], "clip")
    head_rows, patch_count, small_rows = proj_out.shape[0], grad_patch.shape[0], vector.shape[0]
    packs = call_kernel(
        last_pack_kernel,
        (clip_scalar[None], proj_out, grad_patch, vector, chip_swap(vector)),
        (0,),
        tuple(
            jax.ShapeDtypeStruct((head_rows + patch_count + 2 * small_rows, wide_part), low_type)
            for _ in range(4)
        ),
        [],
        0,
        0,
        (),
        (heads_sum,),
    )
    tall_all = lax.all_gather(tall_join, "clip")
    placed = place_layer(
        clip_scalar, level_count - 1, level_count, later["tall_all"], (), 0, (packs[0],)
    )
    packs = swap_clips(packs)
    heads_ring = ring_sum(ring_scalar, heads_sum, heads_got, tuple(packs[1:]))
    last_sum = last_grad(
        clip_scalar, first_all, feats, packs, (heads_ring,), (placed[0], grad_features)
    )
    last_ring = ring_sum(ring_scalar, last_sum, ring_sends(last_sum, ring_at), ())
    heads_total = half_sum(heads_ring, (mark(last_sum),))
    heads_join = join_frames(ring_scalar, heads_total, (last_ring,))
    heads_all = lax.all_gather(heads_join, "clip")
    heads_placed = place_heads(
        clip_scalar, level_count - 1, level_count, later["heads_all"], (), (packs[0],)
    )
    last_join = join_frames(
        ring_scalar, half_sum(last_ring, ()), (), (tall_all, heads_placed)
    )
    last_pieces = clip_pieces(last_join)
    grad_down, grad_up, grad_proj = place_layer(
        clip_scalar, 0, level_count, tall_all, placed, level_count - 1, ()
    )
    grad_in, vector, grad_proj = place_last(
        clip_scalar, feat_width, feat_wide, level_count, last_pieces, grad_proj
    )
    grad_heads = (place_heads(clip_scalar, 0, level_count, heads_all, (heads_placed,), ()),)


    def norm_sums(layer, first, row):
        return vector[8 * (2 * (level_count - 1 - layer) + first) + row]

    grad_mlp_gain = jnp.stack([norm_sums(layer, 0, 0) for layer in layers])
    grad_mlp_shift = jnp.stack([norm_sums(layer, 0, 1) for layer in layers])
    grad_proj_bias = jnp.stack([norm_sums(layer, 0, 2) for layer in layers])
    grad_attn_gain = jnp.stack([norm_sums(layer, 1, 0) for layer in layers])
    grad_attn_shift = jnp.stack([norm_sums(layer, 1, 1) for layer in layers])
    rest = vector[16 * level_count :]
    grad_down_bias = jnp.stack(
        [norm_sums(layer + 1, 1, 2) for layer in range(level_count - 1)]
        + [rest[16 + 3 * level_count]]
    )
    grad_qkv_bias = lax.dynamic_slice_in_dim(
        rest[16 : 16 + 3 * level_count], tensor_at * width, width, 1
    )
    grad_qkv_bias = grad_qkv_bias.reshape(level_count, 3, width)
    grad_up_bias = lax.dynamic_slice_in_dim(
        rest[24:].reshape(level_count, 4 * hidden_width), tensor_at * hidden_width, hidden_width, 1
    )
    act_count = cond_here.shape[1]
    return (
        block_out,
        grad_features[None, None],
        grad_in,
        norm_sums(0, 1, 2),
        rest[:act_count],
        rest[act_count],
        rest[8 : 8 + act_count],
        rest[8 + act_count],
        grad_attn_gain,
        grad_attn_shift,
        jnp.swapaxes(grad_heads[0], 1, 2),
        grad_qkv_bias,
        grad_proj,
        grad_proj_bias,
        grad_mlp_gain,
        grad_mlp_shift,
        grad_up,
        grad_up_bias,
        grad_down,
        grad_down_bias,
    )


def solution(mesh):
    return jax.shard_map(
        on_device,
        mesh=mesh,
        in_specs=(
            P("clip", "frame", None, "tensor"),
            P("clip", "frame", None, None),
            P("clip", None, None),
            P("tensor", None),
            P(),
            P(),
            P(),
            P(),
            P(),
            P(),
            P(),
            P(None, None, None, "tensor"),
            P(None, None, "tensor"),
            P(None, "tensor", None),
            P(),
            P(),
            P(),
            P(None, None, "tensor"),
            P(None, "tensor"),
            P(None, "tensor", None),
            P(),
            P("clip", "frame", None, None),
        ),
        out_specs=(
            P("clip", "frame", None, None),
            P("clip", "frame", None, "tensor"),
            P("tensor", None),
            P(),
            P(),
            P(),
            P(),
            P(),
            P(),
            P(),
            P(None, None, None, "tensor"),
            P(None, None, "tensor"),
            P(None, "tensor", None),
            P(),
            P(),
            P(),
            P(None, None, "tensor"),
            P(None, "tensor"),
            P(None, "tensor", None),
            P(),
        ),
        check_vma=False,
    )
```
